32 devices in a mesh: ctx: 8 (over z, core), dp: 2 (over x), pipe: 2 (over y).
Axes of the slice: x: 2, y: 2, z: 4, core: 2. Of those that a mesh axis runs over, the one named last changes fastest.
Arguments:
- queries: bfloat16 [2, 2048, 4096], P('pipe', ('dp', 'ctx')), parts along dimension 1, may hold values from -6 to 6
- keys: bfloat16 [2, 2048, 4096], P('pipe', ('dp', 'ctx')), parts along dimension 1, may hold values from -6 to 6
- values: bfloat16 [2, 2048, 4096], P('pipe', ('dp', 'ctx')), parts along dimension 1, may hold values from -6 to 6
- residual: bfloat16 [2048, 4096], P(('dp', 'ctx')), parts along dimension 0, may hold values from -6 to 6
- filter_bank: bfloat16 [2, 256, 128], P('pipe'), may hold values from -0.5 to 0.5
- filter_scales: float32 [2, 256], P('pipe'), may hold values from 0.25 to 4
- group_filter: int32 [2, 256], P('pipe'), may hold values from 0 to 255
- context_start: int32 [2], P('dp'), parts along dimension 0, may hold values from 0 to 255
Outputs:
- section_out: bfloat16 [2, 2048, 4096], P('pipe', ('dp', 'ctx')), parts along dimension 1
The draws below stay inside these ranges and needn't reach their ends.
There are 2 independent parts, one for each index of `dp`. The reference program is written for one: setup_inputs(seed, part) draws one part's arguments, and reference() takes and returns one part's arrays. A program takes and returns all parts, laid end to end along the dimension named above; an argument that names none is the same for every part. Nothing has to cross between parts.
All inputs are finite; a program needn't handle non-finite values.
Results may differ from the reference program's by a relative error of at most 0.0058.
Values may be sent and summed in bfloat16 or wider, within the bound.
No kernel may reach another device: no remote copies, remote signals or barrier semaphores. Data moves between devices by JAX's collectives and lax.ppermute only.
A program may use at most 64 MiB of HBM per device.

```python
import math
import jax
import jax.numpy as jnp
from jax import lax

D = 4096
TAPS = 128
G = 256
NF = 256
TOK_DEV = 128
TOKENS = 1024


def set_ends(drawn, key, smallest, high):
    extent = drawn.shape
    place = [jax.random.randint(jax.random.fold_in(key, axis), (), 0, extent[axis]) for axis in range(len(extent))]
    drawn = drawn.at[tuple(place)].set(smallest)
    longest = extent.index(max(extent))
    place[longest] = (place[longest] + 1) % extent[longest]
    return drawn.at[tuple(place)].set(high)


def steps_of(key, extent, cuts, least, largest):
    gain, own = 1.0, jax.random.fold_in(key, 6)
    for dim, blocks in cuts:
        steps = jnp.exp(jax.random.uniform(jax.random.fold_in(own, dim), (blocks,), jnp.float32, least / len(cuts), largest / len(cuts)))
        gain = gain * jnp.repeat(steps, extent[dim] // blocks).reshape([-1 if axis == dim else 1 for axis in range(len(extent))])
    return gain


def centred(stream_key, shape, spread, limit, pieces=(), kind=jnp.bfloat16):
    factor_of = steps_of(stream_key, shape, pieces, -0.22, 0.18) if pieces else 1.0
    entries = jax.random.normal(stream_key, shape, jnp.float32) * spread * factor_of
    return jnp.minimum(jnp.maximum(entries, -limit), limit).astype(kind)


def setup_inputs(seed: int = 0, part: int = 0) -> dict:
    key_list = jax.random.split(jax.random.key(seed), 9)
    own_keys = jax.random.split(jax.random.fold_in(key_list[8], part), 9)
    queries = centred(own_keys[0], (2, TOKENS, D), 1.0, 6.0, ((0, 2), (1, 8)))
    keys = centred(own_keys[1], (2, TOKENS, D), 1.0, 6.0, ((0, 2), (1, 8)))
    values = centred(own_keys[2], (2, TOKENS, D), 1.0, 6.0, ((0, 2), (1, 8)))
    residual = centred(own_keys[3], (TOKENS, D), 1.0, 6.0, ((0, 8),))
    filter_bank = centred(key_list[4], (2, NF, TAPS), TAPS ** -0.5, 0.5, ((0, 2),))
    filter_scales = jnp.clip(jnp.exp(math.log(4.0) - 2.7725887 * jax.random.uniform(key_list[5], (2, G), jnp.float32) ** steps_of(key_list[5], (2, G), ((0, 2),), -0.2, 0.2)), 0.25, 4.0)
    group_filter = set_ends(jax.random.randint(key_list[6], (2, G), 0, NF), jax.random.fold_in(key_list[6], 1), 0, NF - 1).astype(jnp.int32)
    context_start = jax.random.randint(own_keys[7], (1,), 0, 2 * TOK_DEV).astype(jnp.int32)
    return dict(queries=queries, keys=keys, values=values, residual=residual, filter_bank=filter_bank, filter_scales=filter_scales, group_filter=group_filter, context_start=context_start)


def tap_table(bank_rows, scale_rows, assign_rows):
    bank_size = bank_rows.shape[0]
    onehot = (assign_rows[:, None] == jnp.arange(bank_size, dtype=jnp.int32)[None, :]).astype(jnp.bfloat16)
    tap_values = (jnp.dot(onehot, bank_rows, preferred_element_type=jnp.float32) * scale_rows[:, None]).astype(jnp.bfloat16)
    per_channel = jnp.repeat(tap_values, D // G, axis=0)
    return per_channel.T.astype(jnp.float32)


def causal_filter(extended, table):
    def add_tap(step, total):
        start = jnp.int32(TAPS - 1) - step
        rows = lax.dynamic_slice_in_dim(extended, start, TOKENS, 0)
        weight = lax.dynamic_slice_in_dim(table, step, 1, 0)
        return total + rows.astype(jnp.float32) * weight

    initial = jnp.zeros((TOKENS, D), jnp.float32)
    return lax.fori_loop(jnp.int32(0), jnp.int32(TAPS), add_tap, initial)


def reference(queries, keys, values, residual, filter_bank, filter_scales, group_filter, context_start):
    positions = jnp.arange(TOKENS, dtype=jnp.int32)
    inside = (positions >= context_start[0]).astype(jnp.float32)[:, None]
    padding = jnp.zeros((TAPS - 1, D), jnp.bfloat16)
    stream = residual
    results = []
    for section in range(2):
        table = tap_table(filter_bank[section], filter_scales[section], group_filter[section])
        product = (inside * keys[section].astype(jnp.float32) * values[section].astype(jnp.float32)).astype(jnp.bfloat16)
        mixed = causal_filter(jnp.concatenate([padding, product], axis=0), table)
        output = (stream.astype(jnp.float32) + queries[section].astype(jnp.float32) * mixed).astype(jnp.bfloat16)
        results.append(output)
        stream = output
    return jnp.stack(results)
```

```python
import functools

import jax
import jax.numpy as jnp
from jax import lax
from jax.experimental import pallas as pl
from jax.experimental.pallas import tpu as pltpu
from jax.sharding import PartitionSpec as P

LANES = 128
ROW_BLOCK = 32
CHUNKS = 4
F32 = jnp.float32
BF16 = jnp.bfloat16


def from_behind(value, axis, steps):
    count = lax.axis_size(axis)
    first, last = (max(0, -steps), min(count, count - steps))
    return lax.ppermute(value, axis, [(source, source + steps) for source in range(first, last)])


def smem():
    return pl.BlockSpec(memory_space=pltpu.SMEM)


def product_kernel(start_ref, keys_ref, values_ref, out_ref):
    rows, cols = out_ref.shape
    positions = lax.axis_index("ctx") * rows + lax.broadcasted_iota(jnp.int32, (rows, cols), 0)
    product = keys_ref[0].astype(F32) * values_ref[0].astype(F32)
    out_ref[...] = jnp.where(positions >= start_ref[0], product, 0.0).astype(BF16)


def product_of(context_start, keys, values, first, width, block):
    rows = keys.shape[1]
    offset = first // block
    spec = pl.BlockSpec((1, rows, block), lambda i: (0, 0, i + offset))
    return pl.pallas_call(
        product_kernel,
        grid=(width // block,),
        out_shape=jax.ShapeDtypeStruct((rows, width), BF16),
        in_specs=[smem(), spec, spec],
        out_specs=pl.BlockSpec((rows, block), lambda i: (0, i)),
        cost_estimate=pl.CostEstimate(flops=rows * width, bytes_accessed=rows * width * 6, transcendentals=0),
        name="product",
    )(context_start, keys, values)


def taps_kernel(bank_ref, scales_ref, assign_ref, out_ref):
    groups, taps = out_ref.shape
    size = bank_ref.shape[1]
    chosen = (lax.broadcasted_iota(jnp.int32, (size, groups), 0) == assign_ref[...]).astype(F32).astype(BF16)
    contract = (((0,), (0,)), ((), ()))
    picked = lax.dot_general(bank_ref[0], chosen, contract, preferred_element_type=F32)
    scaled = (picked * scales_ref[...]).astype(BF16)
    order = lax.broadcasted_iota(jnp.int32, (taps, taps), 0) + lax.broadcasted_iota(jnp.int32, (taps, taps), 1)
    flip = (order == taps - 1).astype(F32).astype(BF16)
    out_ref[...] = lax.dot_general(scaled, flip, contract, preferred_element_type=F32)


def reversed_taps(bank, scales, assign):
    groups, taps = assign.shape[1], bank.shape[2]
    return pl.pallas_call(
        taps_kernel,
        out_shape=jax.ShapeDtypeStruct((groups, taps), F32),
        cost_estimate=pl.CostEstimate(flops=groups * groups * taps * 4, bytes_accessed=300000, transcendentals=0),
        name="taps",
    )(bank, scales, assign)


def block_kernel(taps_ref, behind_ref, product_ref, queries_ref, residual_ref, out_ref):
    rows, cols = out_ref.shape
    taps = taps_ref.shape[1]
    per_lanes = taps_ref.shape[0] * LANES // cols
    chan = LANES // per_lanes
    is_first = lax.axis_index("pipe") == 0
    keep = jnp.where(is_first, 1.0, 0.0).astype(F32)
    row = lax.broadcasted_iota(jnp.int32, (ROW_BLOCK, taps), 0)
    lane = lax.broadcasted_iota(jnp.int32, (ROW_BLOCK, taps), 1)
    upper = lane > row
    member = lax.broadcasted_iota(jnp.int32, (ROW_BLOCK, LANES), 1) // chan
    for tile in range(cols // LANES):
        at = slice(tile * LANES, (tile + 1) * LANES)
        near, far = [], []
        for group in range(per_lanes):
            line = taps_ref[tile * per_lanes + group : tile * per_lanes + group + 1, :]
            turned = pltpu.roll(jnp.broadcast_to(line, (ROW_BLOCK, taps)), 1, 1, stride=1, stride_axis=0)
            far.append(jnp.where(upper, turned, 0.0).astype(BF16))
            near.append(jnp.where(upper, 0.0, turned)[:, :ROW_BLOCK].astype(BF16))
        table = jnp.concatenate([jnp.concatenate(far, axis=0), jnp.concatenate(near, axis=0)], axis=1)
        window = jnp.concatenate([behind_ref[:, at], product_ref[:, at]], axis=0)
        for first in range(0, rows, ROW_BLOCK):
            span = slice(first, first + ROW_BLOCK)
            sums = jnp.dot(table, window[first : first + taps + ROW_BLOCK], preferred_element_type=F32)
            mixed = sums[:ROW_BLOCK]
            for group in range(1, per_lanes):
                mixed = jnp.where(member == group, sums[group * ROW_BLOCK : (group + 1) * ROW_BLOCK], mixed)
            gated = queries_ref[0, span, at].astype(F32) * mixed
            out_ref[span, at] = (residual_ref[span, at].astype(F32) * keep + gated).astype(BF16)


def block_of(table, behind, product, queries, residual, first, width, local, block):
    rows, total = residual.shape
    taps = table.shape[1]
    groups = table.shape[0] * block // total
    offset, inner = first // block, local // block
    own = pl.BlockSpec((rows, block), lambda i: (0, i + inner))
    return pl.pallas_call(
        block_kernel,
        grid=(width // block,),
        out_shape=jax.ShapeDtypeStruct((rows, width), BF16),
        in_specs=[
            pl.BlockSpec((groups, taps), lambda i: (i + offset, 0)),
            own,
            own,
            pl.BlockSpec((1, rows, block), lambda i: (0, 0, i + offset)),
            pl.BlockSpec((rows, block), lambda i: (0, i + offset)),
        ],
        out_specs=pl.BlockSpec((rows, block), lambda i: (0, i)),
        cost_estimate=pl.CostEstimate(
            flops=2 * 2 * taps * rows * LANES * width // 16, bytes_accessed=rows * width * 10, transcendentals=0
        ),
        name="block",
    )(table, behind, product, queries, residual)


def finish_kernel(own_ref, received_ref, *refs):
    out_ref = refs[-1]
    out_ref[0] = (own_ref[...].astype(F32) + received_ref[...].astype(F32)).astype(BF16)


def finish(own, received, held, first, total):
    rows, width = own.shape
    offset = first // width
    spec = pl.BlockSpec((rows, width), lambda i: (0, 0))
    extra = [] if held is None else [held]
    return pl.pallas_call(
        finish_kernel,
        grid=(1,),
        out_shape=jax.ShapeDtypeStruct((1, rows, total), BF16),
        in_specs=[spec, spec] + [pl.BlockSpec(memory_space=pl.ANY)] * len(extra),
        out_specs=pl.BlockSpec((1, rows, width), lambda i: (0, 0, offset)),
        input_output_aliases={2: 0} if extra else {},
        cost_estimate=pl.CostEstimate(flops=rows * width, bytes_accessed=rows * width * 6, transcendentals=0),
        name="finish",
    )(own, received, *extra)


def body(queries, keys, values, residual, filter_bank, filter_scales, group_filter, context_start):
    total = queries.shape[2]
    width = total // CHUNKS
    block = min(width, 512)
    near = product_of(context_start, keys, values, 0, width, block)
    near_behind = from_behind(near, "ctx", 1)
    rest = product_of(context_start, keys, values, width, total - width, block)
    rest_behind = from_behind(rest, "ctx", 1)
    table = reversed_taps(filter_bank, filter_scales, group_filter)
    own, received = [], []
    for chunk in range(CHUNKS):
        first = chunk * width
        if chunk == 0:
            piece = block_of(table, near_behind, near, queries, residual, first, width, 0, block)
        else:
            piece = block_of(table, rest_behind, rest, queries, residual, first, width, first - width, block)
        own.append(piece)
        received.append(from_behind(piece, "pipe", 1))
    held = None
    for chunk in range(CHUNKS):
        held = finish(own[chunk], received[chunk], held, chunk * width, total)
    return held


def solution(mesh):
    return jax.shard_map(
        body,
        mesh=mesh,
        in_specs=(
            P("pipe", ("dp", "ctx"), None),
            P("pipe", ("dp", "ctx"), None),
            P("pipe", ("dp", "ctx"), None),
            P(("dp", "ctx"), None),
            P("pipe", None, None),
            P("pipe", None),
            P("pipe", None),
            P("dp"),
        ),
        out_specs=P("pipe", ("dp", "ctx"), None),
        check_vma=False,
    )
```

```python
import functools

import jax
import jax.numpy as jnp
from jax import lax
from jax.experimental import pallas as pl
from jax.experimental.pallas import tpu as pltpu
from jax.sharding import PartitionSpec as P

LANES = 128
ROW_BLOCK = 32
HALOS = (768, 1280, 2048)
CHUNKS = (768, 1280, 1024, 640, 384)
F32 = jnp.float32
BF16 = jnp.bfloat16
MIB = 1024 * 1024

SMEM = pl.BlockSpec(memory_space=pltpu.SMEM)
VMEM = pl.BlockSpec(memory_space=pltpu.VMEM)
ANY = pl.BlockSpec(memory_space=pl.ANY)
HBM = pl.BlockSpec(memory_space=pltpu.HBM)


def from_behind(value, axis, steps):
    count = lax.axis_size(axis)
    first, last = (max(0, -steps), min(count, count - steps))
    return lax.ppermute(value, axis, [(source, source + steps) for source in range(first, last)])


def params(limit=16):
    return pltpu.CompilerParams(vmem_limit_bytes=limit * MIB)


def cost(flops=1024):
    return pl.CostEstimate(flops=flops, bytes_accessed=1024, transcendentals=0)


def product_kernel(first, start_ref, keys_ref, values_ref, *refs):
    out_refs = refs[:-3]
    keys_in, values_in, sems = refs[-3:]
    rows, width = keys_in.shape
    copies = [
        pltpu.make_async_copy(keys_ref.at[0, :, pl.ds(first, width)], keys_in, sems.at[0]),
        pltpu.make_async_copy(values_ref.at[0, :, pl.ds(first, width)], values_in, sems.at[1]),
    ]
    for copy in copies:
        copy.start()
    for copy in copies:
        copy.wait()
    slab = lax.axis_index("ctx") * rows
    offset = 0
    for out_ref in out_refs:
        cols = out_ref.shape[1]
        for tile in range(0, cols, LANES):
            at = slice(offset + tile, offset + tile + LANES)
            positions = slab + lax.broadcasted_iota(jnp.int32, (rows, LANES), 0)
            product = keys_in[:, at].astype(F32) * values_in[:, at].astype(F32)
            out_ref[:, tile : tile + LANES] = jnp.where(positions >= start_ref[0], product, 0.0).astype(BF16)
        offset += cols


def products(context_start, keys, values, first, widths, after=()):
    rows, width = keys.shape[1], sum(widths)

    def kernel(start_ref, keys_ref, values_ref, *refs):
        product_kernel(first, start_ref, keys_ref, values_ref, *refs[len(after) :])

    return pl.pallas_call(
        kernel,
        out_shape=tuple(jax.ShapeDtypeStruct((rows, cols), BF16) for cols in widths),
        in_specs=[SMEM, HBM, HBM] + [ANY] * len(after),
        out_specs=tuple(VMEM for _ in widths),
        scratch_shapes=[
            pltpu.VMEM((rows, width), BF16),
            pltpu.VMEM((rows, width), BF16),
            pltpu.SemaphoreType.DMA((2,)),
        ],
        compiler_params=params(16),
        cost_estimate=cost(),
        name="product",
    )(context_start, keys, values, *after)


def turn_table(lines_ref, row, per_lanes, table_ref, at):
    taps = lines_ref.shape[1]
    upper = lax.broadcasted_iota(jnp.int32, (ROW_BLOCK, taps), 1) > lax.broadcasted_iota(
        jnp.int32, (ROW_BLOCK, taps), 0
    )
    for group in range(per_lanes):
        line = lines_ref[row + group : row + group + 1, :]
        turned = pltpu.roll(jnp.broadcast_to(line, (ROW_BLOCK, taps)), 1, 1, stride=1, stride_axis=0)
        span = slice(at + group * ROW_BLOCK, at + (group + 1) * ROW_BLOCK)
        table_ref[span, :taps] = jnp.where(upper, turned, 0.0).astype(BF16)
        table_ref[span, taps:] = jnp.where(upper, 0.0, turned)[:, :ROW_BLOCK].astype(BF16)


def taps_kernel(bank_ref, scales_ref, assign_ref, *refs):
    lines_ref, table_ref = refs[-2:]
    groups, taps = lines_ref.shape
    size = bank_ref.shape[1]
    per_lanes = LANES * groups // sum(CHUNKS)
    chosen = (lax.broadcasted_iota(jnp.int32, (size, groups), 0) == assign_ref[...]).astype(F32).astype(BF16)
    contract = (((0,), (0,)), ((), ()))
    picked = lax.dot_general(bank_ref[0], chosen, contract, preferred_element_type=F32)
    scaled = (picked * scales_ref[...]).astype(BF16)
    order = lax.broadcasted_iota(jnp.int32, (taps, taps), 0) + lax.broadcasted_iota(jnp.int32, (taps, taps), 1)
    flip = (order == taps - 1).astype(F32).astype(BF16)
    lines_ref[...] = lax.dot_general(scaled, flip, contract, preferred_element_type=F32)
    for tile in range(table_ref.shape[0] // (per_lanes * ROW_BLOCK)):
        turn_table(lines_ref, tile * per_lanes, per_lanes, table_ref, tile * per_lanes * ROW_BLOCK)


def tap_lines(bank, scales, assign, width, after=()):
    groups, taps = assign.shape[1], bank.shape[2]
    rows = width * groups // sum(CHUNKS) * ROW_BLOCK
    return pl.pallas_call(
        taps_kernel,
        out_shape=(
            jax.ShapeDtypeStruct((groups, taps), F32),
            jax.ShapeDtypeStruct((rows, taps + ROW_BLOCK), BF16),
        ),
        in_specs=[VMEM] * 3 + [ANY] * len(after),
        out_specs=(VMEM, VMEM),
        compiler_params=params(),
        cost_estimate=cost(),
        name="taps",
    )(bank, scales, assign, *after)


def mix(table_ref, row, per_lanes, window, queries_ref, cols, store):
    rows = queries_ref.shape[1]
    depth = table_ref.shape[1]
    member = lax.broadcasted_iota(jnp.int32, (ROW_BLOCK, LANES), 1) // (LANES // per_lanes)
    table = table_ref[row : row + per_lanes * ROW_BLOCK, :]
    for first in range(0, rows, ROW_BLOCK):
        span = slice(first, first + ROW_BLOCK)
        sums = jnp.dot(table, window[first : first + depth], preferred_element_type=F32)
        mixed = sums[:ROW_BLOCK]
        for group in range(1, per_lanes):
            mixed = jnp.where(member == group, sums[group * ROW_BLOCK : (group + 1) * ROW_BLOCK], mixed)
        store(span, queries_ref[0, span, cols].astype(F32) * mixed)


def gate(first, local, width, lines_ref, table_ref, made, behind_ref, product_ref, queries_ref, store):
    per_lanes = LANES * lines_ref.shape[0] // queries_ref.shape[2]
    for tile in range(width // LANES):
        at = slice(tile * LANES, (tile + 1) * LANES)
        inner = slice(local + at.start, local + at.stop)
        cols = slice(first + at.start, first + at.stop)
        row = tile * per_lanes * ROW_BLOCK
        if not made:
            turn_table(lines_ref, cols.start // LANES * per_lanes, per_lanes, table_ref, row)
        window = jnp.concatenate([behind_ref[:, inner], product_ref[:, inner]], axis=0)
        mix(table_ref, row, per_lanes, window, queries_ref, cols, functools.partial(store, at, cols))


def own_kernel(first, local, made, *refs):
    lines_ref, behind_ref, product_ref, queries_ref, residual_ref, table_ref, out_ref = refs[:7]
    if not made:
        table_ref = refs[-1]

    @pl.when(lax.axis_index("pipe") == 0)
    def _():
        def store(at, cols, span, gated):
            out_ref[span, at] = (residual_ref[span, cols].astype(F32) + gated).astype(BF16)

        gate(
            first, local, out_ref.shape[1], lines_ref, table_ref, made, behind_ref, product_ref, queries_ref, store
        )


def later_kernel(first, local, *refs):
    lines_ref, behind_ref, product_ref, queries_ref, _, out_ref, table_ref = refs

    @pl.when(lax.axis_index("pipe") != 0)
    def _():
        def store(at, cols, span, gated):
            out_ref[span, at] = gated

        gate(
            first, local, out_ref.shape[1], lines_ref, table_ref, False, behind_ref, product_ref, queries_ref, store
        )


def table_scratch(lines, width, total):
    groups, taps = lines.shape
    return pltpu.VMEM((width * groups // total * ROW_BLOCK, taps + ROW_BLOCK), BF16)


def own_of(lines, behind, product, queries, residual, first, local, width, made, after):
    rows, total = residual.shape
    return pl.pallas_call(
        functools.partial(own_kernel, first, local, made),
        out_shape=jax.ShapeDtypeStruct((rows, width), BF16),
        in_specs=[VMEM] * 5 + [VMEM if made else ANY],
        out_specs=VMEM,
        scratch_shapes=[] if made else [table_scratch(lines, width, total)],
        compiler_params=params(),
        cost_estimate=cost(20_000_000_000),
        name="own",
    )(lines, behind, product, queries, residual, after)


def later_of(lines, behind, product, queries, own, first, local, width):
    rows, total = queries.shape[1:]
    return pl.pallas_call(
        functools.partial(later_kernel, first, local),
        out_shape=jax.ShapeDtypeStruct((rows, width), F32),
        in_specs=[VMEM] * 4 + [ANY],
        out_specs=VMEM,
        scratch_shapes=[table_scratch(lines, width, total)],
        compiler_params=params(),
        cost_estimate=cost(),
        name="later",
    )(lines, behind, product, queries, own)


def send_out(buffer, out_ref, first, sem):
    width = buffer.shape[1]
    copy = pltpu.make_async_copy(buffer, out_ref.at[0, :, pl.ds(first, width)], sem)
    copy.start()
    copy.wait()


def finish_kernel(first, local, *refs):
    own_ref, received_ref, lines_ref, behind_ref, product_ref, queries_ref = refs[:6]
    out_ref, table_ref, buffer, sem = refs[-4:]
    is_first = lax.axis_index("pipe") == 0

    @pl.when(is_first)
    def _():
        send_out(own_ref, out_ref, first, sem)

    @pl.when(jnp.logical_not(is_first))
    def _():
        def store(at, cols, span, gated):
            buffer[span, at] = (received_ref[span, at].astype(F32) + gated).astype(BF16)

        gate(
            first, local, buffer.shape[1], lines_ref, table_ref, False, behind_ref, product_ref, queries_ref, store
        )
        send_out(buffer, out_ref, first, sem)


def last_kernel(first, own_ref, received_ref, gated_ref, *refs):
    out_ref, buffer, sem = refs[-3:]
    is_first = lax.axis_index("pipe") == 0

    @pl.when(is_first)
    def _():
        send_out(own_ref, out_ref, first, sem)

    @pl.when(jnp.logical_not(is_first))
    def _():
        buffer[...] = (received_ref[...].astype(F32) + gated_ref[...]).astype(BF16)
        send_out(buffer, out_ref, first, sem)


def finish(held, after, own, received, lines, behind, product, queries, first, local):
    rows, width = own.shape
    total = queries.shape[2]
    return pl.pallas_call(
        functools.partial(finish_kernel, first, local),
        out_shape=jax.ShapeDtypeStruct((1, rows, total), BF16),
        in_specs=[VMEM] * 6 + [ANY],
        out_specs=ANY,
        scratch_shapes=[
            table_scratch(lines, width, total),
            pltpu.VMEM((rows, width), BF16),
            pltpu.SemaphoreType.DMA(()),
        ],
        input_output_aliases={} if held is None else {6: 0},
        compiler_params=params(),
        cost_estimate=cost(20_000_000_000),
        name="finish",
    )(own, received, lines, behind, product, queries, after if held is None else held)


def last(held, own, received, gated, first):
    rows, width = own.shape
    return pl.pallas_call(
        functools.partial(last_kernel, first),
        out_shape=jax.ShapeDtypeStruct(held.shape, BF16),
        in_specs=[VMEM] * 3 + [ANY],
        out_specs=ANY,
        scratch_shapes=[pltpu.VMEM((rows, width), BF16), pltpu.SemaphoreType.DMA(())],
        input_output_aliases={3: 0},
        compiler_params=params(),
        cost_estimate=cost(20_000_000_000),
        name="last",
    )(own, received, gated, held)


def body(queries, keys, values, residual, filter_bank, filter_scales, group_filter, context_start):
    keys, values = (pltpu.with_memory_space_constraint(array, pltpu.HBM) for array in (keys, values))
    (near,) = products(context_start, keys, values, 0, HALOS[:1])
    pieces = [near, *products(context_start, keys, values, HALOS[0], HALOS[1:], (near,))]
    behinds = [from_behind(piece, "ctx", 1) for piece in pieces]
    lines, table = tap_lines(filter_bank, filter_scales, group_filter, CHUNKS[0], (pieces[1],))
    places = []
    first = 0
    for width in CHUNKS:
        start, piece = 0, 0
        while start + HALOS[piece] <= first:
            start, piece = start + HALOS[piece], piece + 1
        places.append((piece, first, first - start, width))
        first += width
    own, received = [], []
    for chunk, (piece, first, local, width) in enumerate(places):
        after = own[-1] if own else table
        own.append(
            own_of(lines, behinds[piece], pieces[piece], queries, residual, first, local, width, not own, after)
        )
        received.append(from_behind(own[-1], "pipe", 1))
    piece, first, local, width = places[-1]
    gated = later_of(lines, behinds[piece], pieces[piece], queries, own[-1], first, local, width)
    held = None
    for chunk, (piece, first, local, width) in enumerate(places[:-1]):
        held = finish(
            held, gated, own[chunk], received[chunk], lines, behinds[piece], pieces[piece], queries, first, local
        )
    return last(held, own[-1], received[-1], gated, places[-1][1])


def solution(mesh):
    return jax.shard_map(
        body,
        mesh=mesh,
        in_specs=(
            P("pipe", ("dp", "ctx"), None),
            P("pipe", ("dp", "ctx"), None),
            P("pipe", ("dp", "ctx"), None),
            P(("dp", "ctx"), None),
            P("pipe", None, None),
            P("pipe", None),
            P("pipe", None),
            P("dp"),
        ),
        out_specs=P("pipe", ("dp", "ctx"), None),
        check_vma=False,
    )
```

```python
import functools

import jax
import jax.numpy as jnp
from jax import lax
from jax.experimental import pallas as pl
from jax.experimental.pallas import tpu as pltpu
from jax.sharding import PartitionSpec as P

LANES = 128
ROW_BLOCK = 32
RAW = 1152
CHUNKS = (1408, 1024, 512)
F32 = jnp.float32
BF16 = jnp.bfloat16
MIB = 1024 * 1024
QUICK, SLOW = 1024, 20_000_000_000

SMEM = pl.BlockSpec(memory_space=pltpu.SMEM)
VMEM = pl.BlockSpec(memory_space=pltpu.VMEM)
ANY = pl.BlockSpec(memory_space=pl.ANY)
HBM = pl.BlockSpec(memory_space=pltpu.HBM)


def to_next_slab(value, pipes):
    slabs, depth = lax.axis_size("ctx"), lax.axis_size("pipe")
    pairs = [(slab * depth + pipe, (slab + 1) * depth + pipe) for slab in range(slabs - 1) for pipe in pipes]
    return lax.ppermute(value, ("ctx", "pipe"), pairs)


def to_next_section(value):
    return lax.ppermute(value, "pipe", [(0, 1)])


def call(kernel, name, out_shape, in_specs, out_specs, scratch=(), weight=QUICK, aliases=None):
    return pl.pallas_call(
        kernel,
        out_shape=out_shape,
        in_specs=in_specs,
        out_specs=out_specs,
        scratch_shapes=list(scratch),
        input_output_aliases=aliases or {},
        compiler_params=pltpu.CompilerParams(vmem_limit_bytes=16 * MIB),
        cost_estimate=pl.CostEstimate(flops=weight, bytes_accessed=1024, transcendentals=0),
        name=name,
    )


def is_first():
    return lax.axis_index("pipe") == 0


def array(rows, cols, kind=BF16):
    return jax.ShapeDtypeStruct((rows, cols), kind)


def multiply(start_ref, keys_ref, values_ref, keys_in, values_in, sems, first, targets):
    rows = keys_in.shape[0]
    slab = lax.axis_index("ctx") * rows
    positions = slab + lax.broadcasted_iota(jnp.int32, (rows, LANES), 0)
    inside = positions >= start_ref[0]
    pieces, offset = [], 0
    for piece, (out_ref, row, col, width) in enumerate(targets):
        at = pl.ds(offset, width)
        source = pl.ds(first + offset, width)
        copies = (
            pltpu.make_async_copy(keys_ref.at[0, :, source], keys_in.at[:, at], sems.at[2 * piece]),
            pltpu.make_async_copy(values_ref.at[0, :, source], values_in.at[:, at], sems.at[2 * piece + 1]),
        )
        for copy in copies:
            copy.start()
        pieces.append(copies)
        offset += width
    offset = 0
    for copies, (out_ref, row, col, width) in zip(pieces, targets):
        for copy in copies:
            copy.wait()
        for tile in range(0, width, LANES):
            at = slice(offset + tile, offset + tile + LANES)
            product = keys_in[:, at].astype(F32) * values_in[:, at].astype(F32)
            out_ref[row : row + rows, col + tile : col + tile + LANES] = jnp.where(inside, product, 0.0).astype(BF16)
        offset += width


def lead_kernel(start_ref, queries_ref, keys_ref, values_ref, raw_ref, near_ref, keys_in, values_in, sems, sem):
    rows, width = near_ref.shape

    @pl.when(is_first())
    def _():
        copy = pltpu.make_async_copy(queries_ref.at[0, :, pl.ds(0, RAW)], raw_ref.at[pl.ds(0, rows)], sem)
        copy.start()
        targets = [(raw_ref, rows, 0, RAW), (near_ref, 0, 0, width)]
        multiply(start_ref, keys_ref, values_ref, keys_in, values_in, sems, 0, targets)
        copy.wait()


def lead_of(start, queries, keys, values):
    rows, width = queries.shape[1], CHUNKS[0]
    return call(
        lead_kernel,
        "lead",
        (array(2 * rows, RAW), array(rows, width)),
        [SMEM, HBM, HBM, HBM],
        (VMEM, VMEM),
        [
            pltpu.VMEM((rows, RAW + width), BF16),
            pltpu.VMEM((rows, RAW + width), BF16),
            pltpu.SemaphoreType.DMA((4,)),
            pltpu.SemaphoreType.DMA(()),
        ],
    )(start, queries, keys, values)


def rest_kernel(start_ref, keys_ref, values_ref, _, rest_ref, later_ref, keys_in, values_in, sems):
    width, total = rest_ref.shape[1], later_ref.shape[1]
    half = total // 2

    @pl.when(is_first())
    def _():
        targets = [(rest_ref, 0, 0, width)]
        multiply(start_ref, keys_ref, values_ref, keys_in, values_in, sems, total - width, targets)

    @pl.when(jnp.logical_not(is_first()))
    def _():
        targets = [(later_ref, 0, 0, half), (later_ref, 0, half, total - half)]
        multiply(start_ref, keys_ref, values_ref, keys_in, values_in, sems, 0, targets)


def rest_of(start, keys, values, after):
    rows, total = keys.shape[1:]
    return call(
        rest_kernel,
        "rest",
        (array(rows, total - RAW - CHUNKS[0]), array(rows, total)),
        [SMEM, HBM, HBM, ANY],
        (VMEM, VMEM),
        [pltpu.VMEM((rows, total), BF16), pltpu.VMEM((rows, total), BF16), pltpu.SemaphoreType.DMA((4,))],
    )(start, keys, values, after)


def turn_table(lines_ref, row, count, table_ref, at):
    taps = lines_ref.shape[1]
    upper = lax.broadcasted_iota(jnp.int32, (ROW_BLOCK, taps), 1) > lax.broadcasted_iota(
        jnp.int32, (ROW_BLOCK, taps), 0
    )
    for group in range(count):
        line = lines_ref[row + group : row + group + 1, :]
        turned = pltpu.roll(jnp.broadcast_to(line, (ROW_BLOCK, taps)), 1, 1, stride=1, stride_axis=0)
        span = slice(at + group * ROW_BLOCK, at + (group + 1) * ROW_BLOCK)
        table_ref[span, :taps] = jnp.where(upper, turned, 0.0).astype(BF16)
        table_ref[span, taps:] = jnp.where(upper, 0.0, turned)[:, :ROW_BLOCK].astype(BF16)


def taps_kernel(share, bank_ref, scales_ref, assign_ref, _, lines_ref, table_ref):
    groups, taps = lines_ref.shape
    size = bank_ref.shape[1]
    chosen = (lax.broadcasted_iota(jnp.int32, (size, groups), 0) == assign_ref[...]).astype(F32).astype(BF16)
    contract = (((0,), (0,)), ((), ()))
    picked = lax.dot_general(bank_ref[0], chosen, contract, preferred_element_type=F32)
    scaled = (picked * scales_ref[...]).astype(BF16)
    order = lax.broadcasted_iota(jnp.int32, (taps, taps), 0) + lax.broadcasted_iota(jnp.int32, (taps, taps), 1)
    flip = (order == taps - 1).astype(F32).astype(BF16)
    lines_ref[...] = lax.dot_general(scaled, flip, contract, preferred_element_type=F32)

    @pl.when(is_first())
    def _():
        for tile in range(CHUNKS[0] // LANES):
            turn_table(lines_ref, (RAW // LANES + tile) * share, share, table_ref, tile * share * ROW_BLOCK)


def taps_of(bank, scales, assign, total, after):
    groups, taps = assign.shape[1], bank.shape[2]
    share = LANES * groups // total
    return call(
        functools.partial(taps_kernel, share),
        "taps",
        (array(groups, taps, F32), array(CHUNKS[0] // LANES * share * ROW_BLOCK, taps + ROW_BLOCK)),
        [VMEM] * 3 + [ANY],
        (VMEM, VMEM),
    )(bank, scales, assign, after)


def mix(table_ref, row, share, window, store):
    depth = table_ref.shape[1]
    rows = window.shape[0] - depth + ROW_BLOCK
    member = lax.broadcasted_iota(jnp.int32, (ROW_BLOCK, LANES), 1) // (LANES // share)
    table = table_ref[row : row + share * ROW_BLOCK, :]
    for first in range(0, rows, ROW_BLOCK):
        sums = jnp.dot(table, window[first : first + depth], preferred_element_type=F32)
        mixed = sums[:ROW_BLOCK]
        for group in range(1, share):
            mixed = jnp.where(member == group, sums[group * ROW_BLOCK : (group + 1) * ROW_BLOCK], mixed)
        store(slice(first, first + ROW_BLOCK), mixed)


def mix_all(width, share, lines_ref, line, table_ref, made, behind_ref, product_ref, local, store):
    for tile in range(width // LANES):
        at = slice(tile * LANES, (tile + 1) * LANES)
        inner = slice(local + at.start, local + at.stop)
        row = tile * share * ROW_BLOCK
        if not made:
            turn_table(lines_ref, line + tile * share, share, table_ref, row)
        window = jnp.concatenate([behind_ref[:, inner], product_ref[:, inner]], axis=0)
        mix(table_ref, row, share, window, functools.partial(store, at))


def share_of(lines_ref, total):
    return LANES * lines_ref.shape[0] // total


def own_kernel(first, local, made, *refs):
    lines_ref, behind_ref, product_ref, queries_ref, residual_ref, table_ref, out_ref = refs[:7]
    if not made:
        table_ref = refs[-1]
    width = out_ref.shape[1]
    rows, total = residual_ref.shape
    share = share_of(lines_ref, total)

    @pl.when(is_first())
    def _():
        def store(at, span, mixed):
            cols = slice(first + at.start, first + at.stop)
            gated = queries_ref[0, span, cols].astype(F32) * mixed
            out_ref[span, at] = (residual_ref[span, cols].astype(F32) + gated).astype(BF16)

        line = first // LANES * share
        mix_all(width, share, lines_ref, line, table_ref, made, behind_ref, product_ref, local, store)
        if made:
            extra = out_ref.shape[0] - rows
            for part in range(-(-(RAW // LANES * share) // extra)):
                taken = lines_ref[part * extra : (part + 1) * extra, :].astype(BF16)
                out_ref[rows:, part * LANES : (part + 1) * LANES] = taken


def table_scratch(lines, width, total):
    groups, taps = lines.shape
    return pltpu.VMEM((width * groups // total * ROW_BLOCK, taps + ROW_BLOCK), BF16)


def own_of(lines, behind, product, queries, residual, first, local, width, made, after):
    rows, total = residual.shape
    return call(
        functools.partial(own_kernel, first, local, made),
        "own",
        array(rows + 16 if made else rows, width),
        [VMEM] * 5 + [VMEM if made else ANY],
        VMEM,
        [] if made else [table_scratch(lines, width, total)],
        weight=QUICK if made else SLOW,
    )(lines, behind, product, queries, residual, after)


def pick_kernel(raw_ref, received_ref, _, queries_ref, product_ref):
    rows = queries_ref.shape[0]

    def take(source):
        queries_ref[...] = source[:rows, :]
        product_ref[...] = source[rows:, :]

    pl.when(is_first())(lambda: take(raw_ref))
    pl.when(jnp.logical_not(is_first()))(lambda: take(received_ref))


def pick_of(raw, received, after):
    rows, width = raw.shape[0] // 2, raw.shape[1]
    return call(
        pick_kernel, "pick", (array(rows, width),) * 2, [VMEM, VMEM, ANY], (VMEM, VMEM), weight=SLOW
    )(raw, received, after)


def later_kernel(first, lines_ref, behind_ref, product_ref, queries_ref, _, out_ref, table_ref):
    total = queries_ref.shape[2]
    share = share_of(lines_ref, total)

    @pl.when(jnp.logical_not(is_first()))
    def _():
        def store(at, span, mixed):
            cols = slice(first + at.start, first + at.stop)
            out_ref[span, at] = queries_ref[0, span, cols].astype(F32) * mixed

        line = first // LANES * share
        mix_all(total - first, share, lines_ref, line, table_ref, False, behind_ref, product_ref, first, store)


def later_of(lines, behind, product, queries, first, after):
    rows, total = product.shape
    return call(
        functools.partial(later_kernel, first),
        "later",
        array(rows, total - first, F32),
        [VMEM] * 4 + [ANY],
        VMEM,
        [table_scratch(lines, total - first, total)],
        weight=SLOW,
    )(lines, behind, product, queries, after)


def send_out(buffer, out_ref, first, sem):
    width = out_ref.shape[2] if buffer.shape[1] == out_ref.shape[2] else buffer.shape[1]
    copy = pltpu.make_async_copy(buffer, out_ref.at[0, :, pl.ds(first, width)], sem)
    copy.start()
    copy.wait()


def chunk_kernel(first, *refs):
    own_ref, received_ref, lines_ref, behind_ref, product_ref, queries_ref = refs[:6]
    out_ref, table_ref, buffer, sem = refs[-4:]
    rows, width = buffer.shape
    share = share_of(lines_ref, queries_ref.shape[2])

    @pl.when(is_first())
    def _():
        send_out(own_ref.at[pl.ds(0, rows)], out_ref, first, sem)

    @pl.when(jnp.logical_not(is_first()))
    def _():
        def store(at, span, mixed):
            cols = slice(first + at.start, first + at.stop)
            gated = queries_ref[0, span, cols].astype(F32) * mixed
            buffer[span, at] = (received_ref[span, at].astype(F32) + gated).astype(BF16)

        line = first // LANES * share
        mix_all(width, share, lines_ref, line, table_ref, False, behind_ref, product_ref, first, store)
        send_out(buffer, out_ref, first, sem)


def chunk_finish(own, received, lines, behind, product, queries, first, after):
    rows, total = product.shape
    width = own.shape[1]
    return call(
        functools.partial(chunk_kernel, first),
        "chunk",
        jax.ShapeDtypeStruct((1, rows, total), BF16),
        [VMEM] * 6 + [ANY],
        ANY,
        [table_scratch(lines, width, total), pltpu.VMEM((rows, width), BF16), pltpu.SemaphoreType.DMA(())],
        weight=SLOW,
    )(own, received, lines, behind, product, queries, after)


def raw_kernel(*refs):
    lines_ref, received_ref, raw_behind_ref, raw_product_ref, raw_queries_ref = refs[:5]
    behind_ref, product_ref, queries_ref, residual_ref, _ = refs[5:10]
    out_ref, chosen_ref, table_ref, buffer, sem = refs[10:]
    rows, width = buffer.shape
    share = share_of(lines_ref, queries_ref.shape[2])
    count = chosen_ref.shape[0]

    @pl.when(is_first())
    def _():
        chosen_ref[...] = lines_ref[:count, :]

    @pl.when(jnp.logical_not(is_first()))
    def _():
        extra = received_ref.shape[0] - rows
        for part in range(-(-count // extra)):
            span = slice(part * extra, min((part + 1) * extra, count))
            taken = received_ref[rows:, part * LANES : (part + 1) * LANES].astype(F32)
            chosen_ref[span, :] = taken[: span.stop - span.start]

    def store_first(at, span, mixed):
        gated = raw_queries_ref[span, at].astype(F32) * mixed
        buffer[span, at] = (residual_ref[span, at].astype(F32) + gated).astype(BF16)

    mix_all(width, share, chosen_ref, 0, table_ref, False, raw_behind_ref, raw_product_ref, 0, store_first)

    @pl.when(jnp.logical_not(is_first()))
    def _():
        def store_second(at, span, mixed):
            gated = queries_ref[0, span, at].astype(F32) * mixed
            buffer[span, at] = (buffer[span, at].astype(F32) + gated).astype(BF16)

        mix_all(width, share, lines_ref, 0, table_ref, False, behind_ref, product_ref, 0, store_second)

    send_out(buffer, out_ref, 0, sem)


def raw_finish(held, lines, received, raw_behind, raw_product, raw_queries, behind, product, queries, residual):
    rows, total = residual.shape
    groups, taps = lines.shape
    return call(
        raw_kernel,
        "raw",
        jax.ShapeDtypeStruct(held.shape, BF16),
        [VMEM] * 9 + [ANY],
        ANY,
        [
            pltpu.VMEM((RAW * groups // total, taps), F32),
            table_scratch(lines, RAW, total),
            pltpu.VMEM((rows, RAW), BF16),
            pltpu.SemaphoreType.DMA(()),
        ],
        weight=SLOW,
        aliases={9: 0},
    )(lines, received, raw_behind, raw_product, raw_queries, behind, product, queries, residual, held)


def last_kernel(first, local, own_ref, received_ref, gated_ref, _, out_ref, buffer, sem):
    width = buffer.shape[1]

    @pl.when(is_first())
    def _():
        send_out(own_ref, out_ref, first, sem)

    @pl.when(jnp.logical_not(is_first()))
    def _():
        buffer[...] = (received_ref[...].astype(F32) + gated_ref[:, local : local + width]).astype(BF16)
        send_out(buffer, out_ref, first, sem)


def last_finish(held, own, received, gated, first, local):
    rows, width = own.shape
    return call(
        functools.partial(last_kernel, first, local),
        "last",
        jax.ShapeDtypeStruct(held.shape, BF16),
        [VMEM] * 3 + [ANY],
        ANY,
        [pltpu.VMEM((rows, width), BF16), pltpu.SemaphoreType.DMA(())],
        weight=SLOW,
        aliases={3: 0},
    )(own, received, gated, held)


def body(queries, keys, values, residual, filter_bank, filter_scales, group_filter, context_start):
    total = queries.shape[2]
    far_queries, keys, values = (
        pltpu.with_memory_space_constraint(value, pltpu.HBM) for value in (queries, keys, values)
    )
    raw, near = lead_of(context_start, far_queries, keys, values)
    raw_received = to_next_section(raw)
    near_behind = to_next_slab(near, (0,))
    rest, product = rest_of(context_start, keys, values, near)
    rest_behind = to_next_slab(rest, (0,))
    behind = to_next_slab(product, (1,))
    lines, table = taps_of(filter_bank, filter_scales, group_filter, total, rest)
    own = [own_of(lines, near_behind, near, queries, residual, RAW, 0, CHUNKS[0], True, table)]
    received = [to_next_section(own[0])]
    raw_queries, raw_product = pick_of(raw, raw_received, own[0])
    raw_behind = to_next_slab(raw_product, (0, 1))
    second = RAW + CHUNKS[0]
    first, after = second, raw_product
    for width in CHUNKS[1:]:
        after = own_of(lines, rest_behind, rest, queries, residual, first, first - second, width, False, after)
        own.append(after)
        received.append(to_next_section(after))
        first += width
    gated = later_of(lines, behind, product, queries, second, after)
    held = chunk_finish(own[0], received[0], lines, behind, product, queries, RAW, gated)
    held = raw_finish(
        held, lines, received[0], raw_behind, raw_product, raw_queries, behind, product, queries, residual
    )
    first = second
    for chunk, width in enumerate(CHUNKS[1:], 1):
        held = last_finish(held, own[chunk], received[chunk], gated, first, first - second)
        first += width
    return held


def solution(mesh):
    return jax.shard_map(
        body,
        mesh=mesh,
        in_specs=(
            P("pipe", ("dp", "ctx"), None),
            P("pipe", ("dp", "ctx"), None),
            P("pipe", ("dp", "ctx"), None),
            P(("dp", "ctx"), None),
            P("pipe", None, None),
            P("pipe", None),
            P("pipe", None),
            P("dp"),
        ),
        out_specs=P("pipe", ("dp", "ctx"), None),
        check_vma=False,
    )
```

```python
import functools

import jax
import jax.numpy as jnp
from jax import lax
from jax.experimental import pallas as pl
from jax.experimental.pallas import tpu as pltpu
from jax.sharding import PartitionSpec as P

LANES = 128
ROW_BLOCK = 32
RAW = 896
CHUNKS = (896, 768, 1024, 512)
EXTRA = 8
F32 = jnp.float32
BF16 = jnp.bfloat16
MIB = 1024 * 1024
QUICK, SLOW = 1024, 20_000_000_000

SMEM = pl.BlockSpec(memory_space=pltpu.SMEM)
VMEM = pl.BlockSpec(memory_space=pltpu.VMEM)
ANY = pl.BlockSpec(memory_space=pl.ANY)
HBM = pl.BlockSpec(memory_space=pltpu.HBM)


def to_next_slab(value, pipes):
    slabs, depth = lax.axis_size("ctx"), lax.axis_size("pipe")
    pairs = [(slab * depth + pipe, (slab + 1) * depth + pipe) for slab in range(slabs - 1) for pipe in pipes]
    return lax.ppermute(value, ("ctx", "pipe"), pairs)


def to_next_section(value):
    return lax.ppermute(value, "pipe", [(0, 1)])


def call(kernel, name, out_shape, in_specs, out_specs, scratch=(), weight=QUICK, aliases=None):
    return pl.pallas_call(
        kernel,
        out_shape=out_shape,
        in_specs=in_specs,
        out_specs=out_specs,
        scratch_shapes=list(scratch),
        input_output_aliases=aliases or {},
        compiler_params=pltpu.CompilerParams(vmem_limit_bytes=16 * MIB),
        cost_estimate=pl.CostEstimate(flops=weight, bytes_accessed=1024, transcendentals=0),
        name=name,
    )


def is_first():
    return lax.axis_index("pipe") == 0


def array(rows, cols, kind=BF16):
    return jax.ShapeDtypeStruct((rows, cols), kind)


def multiply(keys_ref, values_ref, keys_in, values_in, sems, first, targets):
    rows = keys_in.shape[0]
    pieces, offset = [], 0
    for piece, (out_ref, row, col, width) in enumerate(targets):
        at = pl.ds(offset, width)
        source = pl.ds(first + offset, width)
        copies = (
            pltpu.make_async_copy(keys_ref.at[0, :, source], keys_in.at[:, at], sems.at[2 * piece]),
            pltpu.make_async_copy(values_ref.at[0, :, source], values_in.at[:, at], sems.at[2 * piece + 1]),
        )
        for copy in copies:
            copy.start()
        pieces.append(copies)
        offset += width
    offset = 0
    for copies, (out_ref, row, col, width) in zip(pieces, targets):
        for copy in copies:
            copy.wait()
        for tile in range(0, width, LANES):
            at = slice(offset + tile, offset + tile + LANES)
            product = keys_in[:, at].astype(F32) * values_in[:, at].astype(F32)
            out_ref[row : row + rows, col + tile : col + tile + LANES] = product.astype(BF16)
        offset += width


def lead_kernel(queries_ref, keys_ref, values_ref, raw_ref, near_ref, rest_ref, keys_in, values_in, sems, sem):
    rows, width = near_ref.shape

    @pl.when(is_first())
    def _():
        copy = pltpu.make_async_copy(queries_ref.at[0, :, pl.ds(0, RAW)], raw_ref.at[pl.ds(0, rows)], sem)
        copy.start()
        targets = [(raw_ref, rows, 0, RAW), (near_ref, 0, 0, width), (rest_ref, 0, 0, rest_ref.shape[1])]
        multiply(keys_ref, values_ref, keys_in, values_in, sems, 0, targets)
        copy.wait()


def product_scratch(rows, total, pieces):
    return [pltpu.VMEM((rows, total), BF16), pltpu.VMEM((rows, total), BF16), pltpu.SemaphoreType.DMA((2 * pieces,))]


def lead_of(queries, keys, values):
    rows, total = queries.shape[1:]
    return call(
        lead_kernel,
        "lead",
        (array(2 * rows, RAW), array(rows, CHUNKS[0]), array(rows, total - RAW - CHUNKS[0])),
        [HBM] * 3,
        (VMEM,) * 3,
        product_scratch(rows, total, 3) + [pltpu.SemaphoreType.DMA(())],
    )(queries, keys, values)


def product_kernel(keys_ref, values_ref, _, out_ref, keys_in, values_in, sems):
    half = out_ref.shape[1] // 2

    @pl.when(jnp.logical_not(is_first()))
    def _():
        targets = [(out_ref, 0, 0, half), (out_ref, 0, half, half)]
        multiply(keys_ref, values_ref, keys_in, values_in, sems, 0, targets)


def product_of(keys, values, after):
    rows, total = keys.shape[1:]
    return call(
        product_kernel, "product", array(rows, total), [HBM, HBM, ANY], VMEM, product_scratch(rows, total, 2)
    )(keys, values, after)


def turn_table(lines_ref, row, count, table_ref, at):
    taps = lines_ref.shape[1]
    upper = lax.broadcasted_iota(jnp.int32, (ROW_BLOCK, taps), 1) > lax.broadcasted_iota(
        jnp.int32, (ROW_BLOCK, taps), 0
    )
    for group in range(count):
        line = lines_ref[row + group : row + group + 1, :]
        turned = pltpu.roll(jnp.broadcast_to(line, (ROW_BLOCK, taps)), 1, 1, stride=1, stride_axis=0)
        span = slice(at + group * ROW_BLOCK, at + (group + 1) * ROW_BLOCK)
        table_ref[span, :taps] = jnp.where(upper, turned, 0.0).astype(BF16)
        table_ref[span, taps:] = jnp.where(upper, 0.0, turned)[:, :ROW_BLOCK].astype(BF16)


def taps_kernel(share, bank_ref, scales_ref, assign_ref, _, lines_ref, table_ref):
    groups, taps = lines_ref.shape
    size = bank_ref.shape[1]
    chosen = (lax.broadcasted_iota(jnp.int32, (size, groups), 0) == assign_ref[...]).astype(F32).astype(BF16)
    contract = (((0,), (0,)), ((), ()))
    picked = lax.dot_general(bank_ref[0], chosen, contract, preferred_element_type=F32)
    scaled = (picked * scales_ref[...]).astype(BF16)
    order = lax.broadcasted_iota(jnp.int32, (taps, taps), 0) + lax.broadcasted_iota(jnp.int32, (taps, taps), 1)
    flip = (order == taps - 1).astype(F32).astype(BF16)
    lines_ref[...] = lax.dot_general(scaled, flip, contract, preferred_element_type=F32)

    @pl.when(is_first())
    def _():
        for tile in range(CHUNKS[0] // LANES):
            turn_table(lines_ref, (RAW // LANES + tile) * share, share, table_ref, tile * share * ROW_BLOCK)


def taps_of(bank, scales, assign, total, after):
    groups, taps = assign.shape[1], bank.shape[2]
    share = LANES * groups // total
    return call(
        functools.partial(taps_kernel, share),
        "taps",
        (array(groups, taps, F32), array(CHUNKS[0] // LANES * share * ROW_BLOCK, taps + ROW_BLOCK)),
        [VMEM] * 3 + [ANY],
        (VMEM, VMEM),
    )(bank, scales, assign, after)


def mix(table_ref, row, share, window, store):
    depth = table_ref.shape[1]
    rows = window.shape[0] - depth + ROW_BLOCK
    member = lax.broadcasted_iota(jnp.int32, (ROW_BLOCK, LANES), 1) // (LANES // share)
    table = table_ref[row : row + share * ROW_BLOCK, :]
    for first in range(0, rows, ROW_BLOCK):
        sums = jnp.dot(table, window[first : first + depth], preferred_element_type=F32)
        mixed = sums[:ROW_BLOCK]
        for group in range(1, share):
            mixed = jnp.where(member == group, sums[group * ROW_BLOCK : (group + 1) * ROW_BLOCK], mixed)
        store(slice(first, first + ROW_BLOCK), mixed)


def mix_all(width, share, lines_ref, line, table_ref, made, start_ref, behind_ref, product_ref, local, store):
    rows = product_ref.shape[0]
    first = (lax.axis_index("ctx") - 1) * rows
    inside = first + lax.broadcasted_iota(jnp.int32, (2 * rows, LANES), 0) >= start_ref[0]
    for tile in range(width // LANES):
        at = slice(tile * LANES, (tile + 1) * LANES)
        inner = slice(local + at.start, local + at.stop)
        row = tile * share * ROW_BLOCK
        if not made:
            turn_table(lines_ref, line + tile * share, share, table_ref, row)
        window = jnp.concatenate([behind_ref[:, inner], product_ref[:, inner]], axis=0)
        window = jnp.where(inside, window, jnp.zeros_like(window))
        mix(table_ref, row, share, window, functools.partial(store, at))


def share_of(lines_ref, total):
    return LANES * lines_ref.shape[0] // total


def own_kernel(first, local, made, *refs):
    start_ref, lines_ref, behind_ref, product_ref, queries_ref, residual_ref, table_ref, out_ref = refs[:8]
    if not made:
        table_ref = refs[-1]
    width = out_ref.shape[1]
    rows, total = residual_ref.shape
    share = share_of(lines_ref, total)

    @pl.when(is_first())
    def _():
        def store(at, span, mixed):
            cols = slice(first + at.start, first + at.stop)
            gated = queries_ref[0, span, cols].astype(F32) * mixed
            out_ref[span, at] = (residual_ref[span, cols].astype(F32) + gated).astype(BF16)

        line = first // LANES * share
        mix_all(width, share, lines_ref, line, table_ref, made, start_ref, behind_ref, product_ref, local, store)
        if made:
            for part in range(-(-(RAW // LANES * share) // EXTRA)):
                taken = lines_ref[part * EXTRA : (part + 1) * EXTRA, :].astype(BF16)
                out_ref[rows:, part * LANES : (part + 1) * LANES] = taken


def table_scratch(lines, width, total):
    groups, taps = lines.shape
    return pltpu.VMEM((width * groups // total * ROW_BLOCK, taps + ROW_BLOCK), BF16)


def own_of(start, lines, behind, product, queries, residual, first, local, width, made, after):
    rows, total = residual.shape
    return call(
        functools.partial(own_kernel, first, local, made),
        "own",
        array(rows + EXTRA if made else rows, width),
        [SMEM] + [VMEM] * 5 + [VMEM if made else ANY],
        VMEM,
        [] if made else [table_scratch(lines, width, total)],
        weight=QUICK if made else SLOW,
    )(start, lines, behind, product, queries, residual, after)


def pick_kernel(raw_ref, received_ref, _, queries_ref, product_ref):
    rows = queries_ref.shape[0]

    def take(source):
        queries_ref[...] = source[:rows, :]
        product_ref[...] = source[rows:, :]

    pl.when(is_first())(lambda: take(raw_ref))
    pl.when(jnp.logical_not(is_first()))(lambda: take(received_ref))


def pick_of(raw, received, after):
    rows, width = raw.shape[0] // 2, raw.shape[1]
    return call(
        pick_kernel, "pick", (array(rows, width),) * 2, [VMEM, VMEM, ANY], (VMEM, VMEM), weight=SLOW
    )(raw, received, after)


def hold_kernel(value_ref, _, out_ref):
    pass


def held_back(value, after):
    return call(hold_kernel, "hold", array(*value.shape), [ANY, ANY], ANY, aliases={0: 0})(value, after)


def later_kernel(start_ref, lines_ref, behind_ref, product_ref, queries_ref, _, out_ref, table_ref):
    total = queries_ref.shape[2]
    share = share_of(lines_ref, total)

    @pl.when(jnp.logical_not(is_first()))
    def _():
        def store(at, span, mixed):
            out_ref[span, at] = queries_ref[0, span, at].astype(F32) * mixed

        mix_all(total, share, lines_ref, 0, table_ref, False, start_ref, behind_ref, product_ref, 0, store)


def later_of(start, lines, behind, product, queries, after):
    rows, total = product.shape
    return call(
        later_kernel,
        "later",
        array(rows, total, F32),
        [SMEM] + [VMEM] * 4 + [ANY],
        VMEM,
        [table_scratch(lines, total, total)],
        weight=SLOW,
    )(start, lines, behind, product, queries, after)


def send_out(buffer, out_ref, first, sem):
    copy = pltpu.make_async_copy(buffer, out_ref.at[0, :, pl.ds(first, buffer.shape[1])], sem)
    copy.start()
    copy.wait()


def raw_kernel(*refs):
    start_ref, lines_ref, received_ref, behind_ref, product_ref, queries_ref, gated_ref, residual_ref, _ = refs[:9]
    out_ref, chosen_ref, table_ref, buffer, sem = refs[9:]
    rows, width = buffer.shape
    share = share_of(lines_ref, residual_ref.shape[1])
    count = chosen_ref.shape[0]

    @pl.when(is_first())
    def _():
        chosen_ref[...] = lines_ref[:count, :]

    @pl.when(jnp.logical_not(is_first()))
    def _():
        for part in range(-(-count // EXTRA)):
            span = slice(part * EXTRA, min((part + 1) * EXTRA, count))
            taken = received_ref[rows:, part * LANES : (part + 1) * LANES].astype(F32)
            chosen_ref[span, :] = taken[: span.stop - span.start]

    def store(at, span, mixed):
        gated = queries_ref[span, at].astype(F32) * mixed
        buffer[span, at] = (residual_ref[span, at].astype(F32) + gated).astype(BF16)

    mix_all(width, share, chosen_ref, 0, table_ref, False, start_ref, behind_ref, product_ref, 0, store)

    @pl.when(jnp.logical_not(is_first()))
    def _():
        buffer[...] = (buffer[...].astype(F32) + gated_ref[:, :width]).astype(BF16)

    send_out(buffer, out_ref, 0, sem)


def raw_finish(held, start, lines, received, behind, product, queries, gated, residual):
    rows, total = residual.shape
    groups, taps = lines.shape
    return call(
        raw_kernel,
        "raw",
        jax.ShapeDtypeStruct(held.shape, BF16),
        [SMEM] + [VMEM] * 7 + [ANY],
        ANY,
        [
            pltpu.VMEM((RAW * groups // total, taps), F32),
            table_scratch(lines, RAW, total),
            pltpu.VMEM((rows, RAW), BF16),
            pltpu.SemaphoreType.DMA(()),
        ],
        weight=SLOW,
        aliases={8: 0},
    )(start, lines, received, behind, product, queries, gated, residual, held)


def chunk_kernel(first, own_ref, received_ref, gated_ref, *refs):
    out_ref, buffer, sem = refs[-3:]
    rows, width = buffer.shape

    @pl.when(is_first())
    def _():
        send_out(own_ref.at[pl.ds(0, rows)], out_ref, first, sem)

    @pl.when(jnp.logical_not(is_first()))
    def _():
        total = received_ref[:rows, :].astype(F32) + gated_ref[:, first : first + width]
        buffer[...] = total.astype(BF16)
        send_out(buffer, out_ref, first, sem)


def chunk_finish(held, own, received, gated, first):
    rows, total = gated.shape
    width = own.shape[1]
    return call(
        functools.partial(chunk_kernel, first),
        "chunk",
        jax.ShapeDtypeStruct((1, rows, total), BF16),
        [VMEM] * 3 + ([] if held is None else [ANY]),
        ANY,
        [pltpu.VMEM((rows, width), BF16), pltpu.SemaphoreType.DMA(())],
        weight=SLOW,
        aliases={} if held is None else {3: 0},
    )(own, received, gated, *([] if held is None else [held]))


def body(queries, keys, values, residual, filter_bank, filter_scales, group_filter, context_start):
    total = queries.shape[2]
    far_queries, keys, values = (
        pltpu.with_memory_space_constraint(value, pltpu.HBM) for value in (queries, keys, values)
    )
    raw, near, rest = lead_of(far_queries, keys, values)
    raw_received = to_next_section(raw)
    near_behind = to_next_slab(near, (0,))
    product = product_of(keys, values, near)
    rest_behind = to_next_slab(rest, (0,))
    behind = to_next_slab(product, (1,))
    lines, table = taps_of(filter_bank, filter_scales, group_filter, total, product)
    own = [own_of(context_start, lines, near_behind, near, queries, residual, RAW, 0, CHUNKS[0], True, table)]
    received = [to_next_section(own[0])]
    raw_queries, raw_product = pick_of(raw, raw_received, own[0])
    second = RAW + CHUNKS[0]
    first, after = second, raw_queries
    for chunk, width in enumerate(CHUNKS[1:], 1):
        if chunk == len(CHUNKS) - 1:
            raw_product = held_back(raw_product, after)
            raw_behind = to_next_slab(raw_product, (0, 1))
            after = raw_product
        after = own_of(
            context_start, lines, rest_behind, rest, queries, residual, first, first - second, width, False, after
        )
        own.append(after)
        received.append(to_next_section(after))
        first += width
    gated = later_of(context_start, lines, behind, product, queries, after)
    held, first = None, RAW
    for chunk, width in enumerate(CHUNKS):
        held = chunk_finish(held, own[chunk], received[chunk], gated, first)
        first += width
        if chunk == 0:
            held = raw_finish(
                held, context_start, lines, received[0], raw_behind, raw_product, raw_queries, gated, residual
            )
    return held


def solution(mesh):
    return jax.shard_map(
        body,
        mesh=mesh,
        in_specs=(
            P("pipe", ("dp", "ctx"), None),
            P("pipe", ("dp", "ctx"), None),
            P("pipe", ("dp", "ctx"), None),
            P(("dp", "ctx"), None),
            P("pipe", None, None),
            P("pipe", None),
            P("pipe", None),
            P("dp"),
        ),
        out_specs=P("pipe", ("dp", "ctx"), None),
        check_vma=False,
    )
```

```python
import functools

import jax
import jax.numpy as jnp
from jax import lax
from jax.experimental import pallas as pl
from jax.experimental.pallas import tpu as pltpu
from jax.sharding import PartitionSpec as P

LANES = 128
ROW_BLOCK = 32
RAW = 896
NEAR = (512, 512)
REST = (512, 1024, 640)
LINES = 8
F32 = jnp.float32
BF16 = jnp.bfloat16
MIB = 1024 * 1024
QUICK, SLOW = 1024, 20_000_000_000

SMEM = pl.BlockSpec(memory_space=pltpu.SMEM)
VMEM = pl.BlockSpec(memory_space=pltpu.VMEM)
ANY = pl.BlockSpec(memory_space=pl.ANY)
HBM = pl.BlockSpec(memory_space=pltpu.HBM)


def to_next_slab(value, pipes):
    slabs, depth = lax.axis_size("ctx"), lax.axis_size("pipe")
    pairs = [(slab * depth + pipe, (slab + 1) * depth + pipe) for slab in range(slabs - 1) for pipe in pipes]
    return lax.ppermute(value, ("ctx", "pipe"), pairs)


def to_next_section(value):
    return lax.ppermute(value, "pipe", [(0, 1)])


def call(kernel, name, out_shape, in_specs, out_specs, scratch=(), weight=QUICK, aliases=None):
    return pl.pallas_call(
        kernel,
        out_shape=out_shape,
        in_specs=in_specs,
        out_specs=out_specs,
        scratch_shapes=list(scratch),
        input_output_aliases=aliases or {},
        compiler_params=pltpu.CompilerParams(vmem_limit_bytes=16 * MIB),
        cost_estimate=pl.CostEstimate(flops=weight, bytes_accessed=1024, transcendentals=0),
        name=name,
    )


def is_first():
    return lax.axis_index("pipe") == 0


def array(rows, cols, kind=BF16):
    return jax.ShapeDtypeStruct((rows, cols), kind)


def multiply(keys_ref, values_ref, keys_in, values_in, sems, first, targets, meanwhile=None):
    rows = keys_in.shape[0]
    pieces, offset = [], 0
    for piece, (out_ref, row, col, width) in enumerate(targets):
        at = pl.ds(offset, width)
        source = pl.ds(first + offset, width)
        copies = (
            pltpu.make_async_copy(keys_ref.at[0, :, source], keys_in.at[:, at], sems.at[2 * piece]),
            pltpu.make_async_copy(values_ref.at[0, :, source], values_in.at[:, at], sems.at[2 * piece + 1]),
        )
        for copy in copies:
            copy.start()
        pieces.append(copies)
        offset += width
    if meanwhile is not None:
        meanwhile()
    offset = 0
    for copies, (out_ref, row, col, width) in zip(pieces, targets):
        for copy in copies:
            copy.wait()
        for tile in range(0, width, LANES):
            at = slice(offset + tile, offset + tile + LANES)
            product = keys_in[:, at].astype(F32) * values_in[:, at].astype(F32)
            out_ref[row : row + rows, col + tile : col + tile + LANES] = product.astype(BF16)
        offset += width


def fill_lines(bank, scales_ref, assign_ref, lines_ref):
    groups, taps = lines_ref.shape
    size = bank.shape[0]
    chosen = (lax.broadcasted_iota(jnp.int32, (size, groups), 0) == assign_ref[...]).astype(F32).astype(BF16)
    contract = (((0,), (0,)), ((), ()))
    picked = lax.dot_general(bank, chosen, contract, preferred_element_type=F32)
    scaled = (picked * scales_ref[...]).astype(BF16)
    order = lax.broadcasted_iota(jnp.int32, (taps, taps), 0) + lax.broadcasted_iota(jnp.int32, (taps, taps), 1)
    flip = (order == taps - 1).astype(F32).astype(BF16)
    lines_ref[...] = lax.dot_general(scaled, flip, contract, preferred_element_type=F32)


def lead_kernel(*refs):
    bank_ref, scales_ref, assign_ref, queries_ref, keys_ref, values_ref = refs[:6]
    raw_ref, near_ref, rest_ref, lines_ref = refs[6:10]
    bank_in, scales_in, assign_in, keys_in, values_in, sems, own_sems = refs[10:]
    rows, width = near_ref.shape
    far = rest_ref.shape[1]
    half = far // 2 // LANES * LANES

    @pl.when(is_first())
    def _():
        copies = [
            pltpu.make_async_copy(bank_ref, bank_in, own_sems.at[0]),
            pltpu.make_async_copy(scales_ref, scales_in, own_sems.at[1]),
            pltpu.make_async_copy(assign_ref, assign_in, own_sems.at[2]),
            pltpu.make_async_copy(queries_ref.at[0, :, pl.ds(0, RAW)], raw_ref.at[pl.ds(0, rows)], own_sems.at[3]),
        ]
        for copy in copies:
            copy.start()

        def taps():
            for copy in copies[:3]:
                copy.wait()
            fill_lines(bank_in[0], scales_in, assign_in, lines_ref)
            for part in range(RAW // LANES):
                taken = lines_ref[part * LINES : (part + 1) * LINES, :].astype(BF16)
                raw_ref[2 * rows :, part * LANES : (part + 1) * LANES] = taken

        targets = [
            (raw_ref, rows, 0, RAW),
            (near_ref, 0, 0, width),
            (rest_ref, 0, 0, half),
            (rest_ref, 0, half, far - half),
        ]
        multiply(keys_ref, values_ref, keys_in, values_in, sems, 0, targets, taps)
        copies[3].wait()


def product_scratch(rows, total, pieces):
    return [pltpu.VMEM((rows, total), BF16), pltpu.VMEM((rows, total), BF16), pltpu.SemaphoreType.DMA((2 * pieces,))]


def lead_of(bank, scales, assign, queries, keys, values):
    rows, total = queries.shape[1:]
    near = sum(NEAR)
    return call(
        lead_kernel,
        "lead",
        (
            array(2 * rows + LINES, RAW),
            array(rows, near),
            array(rows, total - RAW - near),
            array(assign.shape[1], bank.shape[2], F32),
        ),
        [HBM] * 6,
        (VMEM,) * 4,
        [pltpu.VMEM(bank.shape, BF16), pltpu.VMEM(scales.shape, F32), pltpu.VMEM(assign.shape, jnp.int32)]
        + product_scratch(rows, total, 4)
        + [pltpu.SemaphoreType.DMA((4,))],
    )(bank, scales, assign, queries, keys, values)


def turn_table(lines_ref, row, count, table_ref, at):
    taps = lines_ref.shape[1]
    upper = lax.broadcasted_iota(jnp.int32, (ROW_BLOCK, taps), 1) > lax.broadcasted_iota(
        jnp.int32, (ROW_BLOCK, taps), 0
    )
    for group in range(count):
        line = lines_ref[row + group : row + group + 1, :]
        turned = pltpu.roll(jnp.broadcast_to(line, (ROW_BLOCK, taps)), 1, 1, stride=1, stride_axis=0)
        span = slice(at + group * ROW_BLOCK, at + (group + 1) * ROW_BLOCK)
        table_ref[span, :taps] = jnp.where(upper, turned, 0.0).astype(BF16)
        table_ref[span, taps:] = jnp.where(upper, 0.0, turned)[:, :ROW_BLOCK].astype(BF16)


def product_kernel(share, *refs):
    keys_ref, values_ref, bank_ref, scales_ref, assign_ref, held_ref, _ = refs[:7]
    out_ref, lines_ref, table_ref, keys_in, values_in, sems = refs[7:]
    half = out_ref.shape[1] // 2

    @pl.when(is_first())
    def _():
        for tile in range(sum(NEAR) // LANES):
            turn_table(held_ref, (RAW // LANES + tile) * share, share, table_ref, tile * share * ROW_BLOCK)

    @pl.when(jnp.logical_not(is_first()))
    def _():
        targets = [(out_ref, 0, 0, half), (out_ref, 0, half, half)]
        multiply(
            keys_ref,
            values_ref,
            keys_in,
            values_in,
            sems,
            0,
            targets,
            lambda: fill_lines(bank_ref[0], scales_ref, assign_ref, lines_ref),
        )


def product_of(keys, values, bank, scales, assign, lines, after):
    rows, total = keys.shape[1:]
    groups, taps = lines.shape
    share = LANES * groups // total
    return call(
        functools.partial(product_kernel, share),
        "product",
        (
            array(rows, total),
            array(groups, taps, F32),
            array(sum(NEAR) // LANES * share * ROW_BLOCK, taps + ROW_BLOCK),
        ),
        [HBM, HBM] + [VMEM] * 4 + [ANY],
        (VMEM,) * 3,
        product_scratch(rows, total, 2),
        aliases={5: 1},
    )(keys, values, bank, scales, assign, lines, after)


def mix(table_ref, row, share, window, store):
    depth = table_ref.shape[1]
    rows = window.shape[0] - depth + ROW_BLOCK
    member = lax.broadcasted_iota(jnp.int32, (ROW_BLOCK, LANES), 1) // (LANES // share)
    table = table_ref[row : row + share * ROW_BLOCK, :]
    for first in range(0, rows, ROW_BLOCK):
        sums = jnp.dot(table, window[first : first + depth], preferred_element_type=F32)
        mixed = sums[:ROW_BLOCK]
        for group in range(1, share):
            mixed = jnp.where(member == group, sums[group * ROW_BLOCK : (group + 1) * ROW_BLOCK], mixed)
        store(slice(first, first + ROW_BLOCK), mixed)


def mix_all(width, share, lines_ref, line, table_ref, made, start_ref, behind_ref, product_ref, local, store):
    rows = product_ref.shape[0]
    first = (lax.axis_index("ctx") - 1) * rows
    inside = first + lax.broadcasted_iota(jnp.int32, (2 * rows, LANES), 0) >= start_ref[0]
    for tile in range(width // LANES):
        at = slice(tile * LANES, (tile + 1) * LANES)
        inner = slice(local + at.start, local + at.stop)
        row = tile * share * ROW_BLOCK
        if not made:
            turn_table(lines_ref, line + tile * share, share, table_ref, row)
        window = jnp.concatenate([behind_ref[:, inner], product_ref[:, inner]], axis=0)
        window = jnp.where(inside, window, jnp.zeros_like(window))
        mix(table_ref, row, share, window, functools.partial(store, at))


def share_of(lines_ref, total):
    return LANES * lines_ref.shape[0] // total


def own_kernel(first, local, made, *refs):
    start_ref, lines_ref, behind_ref, product_ref, queries_ref, residual_ref, table_ref = refs[:7]
    out_ref = refs[-1] if made else refs[-2]
    width = out_ref.shape[1]
    share = share_of(lines_ref, residual_ref.shape[1])
    if made:
        table_ref = table_ref.at[pl.ds(local // LANES * share * ROW_BLOCK, width // LANES * share * ROW_BLOCK)]
    else:
        table_ref = refs[-1]

    @pl.when(is_first())
    def _():
        def store(at, span, mixed):
            cols = slice(first + at.start, first + at.stop)
            gated = queries_ref[0, span, cols].astype(F32) * mixed
            out_ref[span, at] = (residual_ref[span, cols].astype(F32) + gated).astype(BF16)

        line = first // LANES * share
        mix_all(width, share, lines_ref, line, table_ref, made, start_ref, behind_ref, product_ref, local, store)


def table_scratch(lines, width, total):
    groups, taps = lines.shape
    return pltpu.VMEM((width * groups // total * ROW_BLOCK, taps + ROW_BLOCK), BF16)


def own_of(start, lines, behind, product, queries, residual, first, local, width, table, *after):
    rows, total = residual.shape
    made = table is not None
    return call(
        functools.partial(own_kernel, first, local, made),
        "own",
        array(rows, width),
        [SMEM] + [VMEM] * (6 if made else 5) + [ANY] * len(after),
        VMEM,
        [] if made else [table_scratch(lines, width, total)],
        weight=QUICK if made else SLOW,
    )(start, lines, behind, product, queries, residual, *([table] if made else []), *after)


def pick_kernel(raw_ref, received_ref, _, queries_ref, product_ref, lines_ref):
    rows = queries_ref.shape[0]

    def take(source):
        queries_ref[...] = source[:rows, :]
        product_ref[...] = source[rows : 2 * rows, :]
        for part in range(RAW // LANES):
            taken = source[2 * rows :, part * LANES : (part + 1) * LANES]
            lines_ref[part * LINES : (part + 1) * LINES, :] = taken.astype(F32)

    pl.when(is_first())(lambda: take(raw_ref))
    pl.when(jnp.logical_not(is_first()))(lambda: take(received_ref))


def pick_of(raw, received, taps, after):
    rows, width = (raw.shape[0] - LINES) // 2, raw.shape[1]
    return call(
        pick_kernel,
        "pick",
        (array(rows, width), array(rows, width), array(RAW // LANES * LINES, taps, F32)),
        [VMEM, VMEM, ANY],
        (VMEM,) * 3,
        weight=SLOW,
    )(raw, received, after)


def hold_kernel(value_ref, _, out_ref):
    pass


def held_back(value, after):
    return call(hold_kernel, "hold", array(*value.shape), [ANY, ANY], ANY, aliases={0: 0})(value, after)


def send_out(pieces, out_ref, sems):
    copies = [
        pltpu.make_async_copy(buffer, out_ref.at[0, :, pl.ds(first, buffer.shape[1])], sems.at[place])
        for place, (buffer, first) in enumerate(pieces)
    ]
    for copy in copies:
        copy.start()
    return copies


def wait_all(copies):
    for copy in copies:
        copy.wait()


def later_kernel(places, *refs):
    start_ref, lines_ref, behind_ref, product_ref, queries_ref = refs[:5]
    own_refs = refs[5 : 5 + len(places)]
    out_ref, gated_ref, table_ref, sems = refs[-4:]
    total = queries_ref.shape[2]
    share = share_of(lines_ref, total)

    @pl.when(is_first())
    def _():
        wait_all(send_out([(own_ref, first) for own_ref, (first, _) in zip(own_refs, places)], out_ref, sems))

    @pl.when(jnp.logical_not(is_first()))
    def _():
        def store(at, span, mixed):
            gated_ref[span, at] = queries_ref[0, span, at].astype(F32) * mixed

        mix_all(total, share, lines_ref, 0, table_ref, False, start_ref, behind_ref, product_ref, 0, store)


def later_of(start, lines, behind, product, queries, own, places):
    rows, total = product.shape
    return call(
        functools.partial(later_kernel, places),
        "later",
        (jax.ShapeDtypeStruct((1, rows, total), BF16), array(rows, total, F32)),
        [SMEM] + [VMEM] * (4 + len(own)),
        (ANY, VMEM),
        [table_scratch(lines, total, total), pltpu.SemaphoreType.DMA((len(own),))],
        weight=SLOW,
    )(start, lines, behind, product, queries, *own)


def raw_kernel(start_ref, lines_ref, behind_ref, product_ref, queries_ref, gated_ref, residual_ref, _, *refs):
    out_ref, table_ref, buffer, sems = refs
    width = buffer.shape[1]
    share = share_of(lines_ref, width)

    def store(at, span, mixed):
        gated = queries_ref[span, at].astype(F32) * mixed
        buffer[span, at] = (residual_ref[span, at].astype(F32) + gated).astype(BF16)

    mix_all(width, share, lines_ref, 0, table_ref, False, start_ref, behind_ref, product_ref, 0, store)

    @pl.when(jnp.logical_not(is_first()))
    def _():
        buffer[...] = (buffer[...].astype(F32) + gated_ref[:, :width]).astype(BF16)

    wait_all(send_out([(buffer, 0)], out_ref, sems))


def raw_finish(held, start, lines, behind, product, queries, gated, residual):
    rows, width = product.shape
    return call(
        raw_kernel,
        "raw",
        jax.ShapeDtypeStruct(held.shape, BF16),
        [SMEM] + [VMEM] * 6 + [ANY],
        ANY,
        [table_scratch(lines, width, width), pltpu.VMEM((rows, width), BF16), pltpu.SemaphoreType.DMA((1,))],
        weight=SLOW,
        aliases={7: 0},
    )(start, lines, behind, product, queries, gated, residual, held)


def finish_kernel(places, *refs):
    gated_ref, received_refs = refs[0], refs[1 : 1 + len(places)]
    out_ref, *buffers, sems = refs[2 + len(places) :]

    @pl.when(jnp.logical_not(is_first()))
    def _():
        copies = []
        for place, (first, width) in enumerate(places):
            buffer = buffers[place]
            total = received_refs[place][...].astype(F32) + gated_ref[:, first : first + width]
            buffer[...] = total.astype(BF16)
            copies += send_out([(buffer, first)], out_ref, sems.at[pl.ds(place, 1)])
        wait_all(copies)


def finish(held, gated, received, places):
    rows = gated.shape[0]
    count = len(places)
    return call(
        functools.partial(finish_kernel, places),
        "finish",
        jax.ShapeDtypeStruct(held.shape, BF16),
        [VMEM] * (1 + count) + [ANY],
        ANY,
        [pltpu.VMEM((rows, width), BF16) for _, width in places] + [pltpu.SemaphoreType.DMA((count,))],
        weight=SLOW,
        aliases={1 + count: 0},
    )(gated, *received, held)


def body(queries, keys, values, residual, filter_bank, filter_scales, group_filter, context_start):
    total = queries.shape[2]
    small = (filter_bank, filter_scales, group_filter)
    far_small = [pltpu.with_memory_space_constraint(value, pltpu.HBM) for value in small]
    far_queries, keys, values = (
        pltpu.with_memory_space_constraint(value, pltpu.HBM) for value in (queries, keys, values)
    )
    raw, near, rest, lines = lead_of(*far_small, far_queries, keys, values)
    raw_received = to_next_section(raw)
    near_behind = to_next_slab(near, (0,))
    product, lines, table = product_of(keys, values, *small, lines, near)
    rest_behind = to_next_slab(rest, (0,))
    behind = to_next_slab(product, (1,))
    own, received, places = [], [], []

    def send(made, source, source_behind, origin, first, width, *after):
        piece = own_of(
            context_start, lines, source_behind, source, queries, residual, first, first - origin, width, made, *after
        )
        own.append(piece)
        received.append(to_next_section(piece))
        places.append((first, width))
        return first + width, piece

    first, after = RAW, lines
    for width in NEAR:
        first, after = send(table, near, near_behind, RAW, first, width, after)
    raw_queries, raw_product, raw_lines = pick_of(raw, raw_received, lines.shape[1], after)
    origin, after = first, raw_queries
    for chunk, width in enumerate(REST):
        if chunk == len(REST) - 1:
            raw_product = held_back(raw_product, after)
            raw_behind = to_next_slab(raw_product, (0, 1))
            after = raw_product
        passed = received[chunk - 1 : chunk] if chunk else []
        first, after = send(None, rest, rest_behind, origin, first, width, after, *passed)
    held, gated = later_of(context_start, lines, behind, product, queries, own, places)
    held = finish(held, gated, received[:3], places[:3])
    held = raw_finish(held, context_start, raw_lines, raw_behind, raw_product, raw_queries, gated, residual)
    for chunk in range(3, len(places)):
        held = finish(held, gated, received[chunk : chunk + 1], places[chunk : chunk + 1])
    return held


def solution(mesh):
    return jax.shard_map(
        body,
        mesh=mesh,
        in_specs=(
            P("pipe", ("dp", "ctx"), None),
            P("pipe", ("dp", "ctx"), None),
            P("pipe", ("dp", "ctx"), None),
            P(("dp", "ctx"), None),
            P("pipe", None, None),
            P("pipe", None),
            P("pipe", None),
            P("dp"),
        ),
        out_specs=P("pipe", ("dp", "ctx"), None),
        check_vma=False,
    )
```

```python
import functools

import jax
import jax.numpy as jnp
from jax import lax
from jax.experimental import pallas as pl
from jax.experimental.pallas import tpu as pltpu
from jax.sharding import PartitionSpec as P

LANES = 128
ROW_BLOCK = 32
RAW = 896
NEAR = (512, 512)
REST = (512, 1024, 640)
LINES = 8
F32 = jnp.float32
BF16 = jnp.bfloat16
MIB = 1024 * 1024
QUICK, SLOW = 1024, 20_000_000_000

SMEM = pl.BlockSpec(memory_space=pltpu.SMEM)
VMEM = pl.BlockSpec(memory_space=pltpu.VMEM)
ANY = pl.BlockSpec(memory_space=pl.ANY)
HBM = pl.BlockSpec(memory_space=pltpu.HBM)


def to_next_slab(value, pipes):
    slabs, depth = lax.axis_size("ctx"), lax.axis_size("pipe")
    pairs = [(slab * depth + pipe, (slab + 1) * depth + pipe) for slab in range(slabs - 1) for pipe in pipes]
    return lax.ppermute(value, ("ctx", "pipe"), pairs)


def to_next_section(value):
    return lax.ppermute(value, "pipe", [(0, 1)])


def call(kernel, name, out_shape, in_specs, out_specs, scratch=(), weight=QUICK, aliases=None):
    return pl.pallas_call(
        kernel,
        out_shape=out_shape,
        in_specs=in_specs,
        out_specs=out_specs,
        scratch_shapes=list(scratch),
        input_output_aliases=aliases or {},
        compiler_params=pltpu.CompilerParams(vmem_limit_bytes=16 * MIB),
        cost_estimate=pl.CostEstimate(flops=weight, bytes_accessed=1024, transcendentals=0),
        name=name,
    )


def is_first():
    return lax.axis_index("pipe") == 0


def array(rows, cols, kind=BF16):
    return jax.ShapeDtypeStruct((rows, cols), kind)


def multiply(keys_ref, values_ref, keys_in, values_in, sems, first, targets, meanwhile=None):
    rows = keys_in.shape[0]
    pieces, offset = [], 0
    for piece, (out_ref, row, col, width) in enumerate(targets):
        at = pl.ds(offset, width)
        source = pl.ds(first + offset, width)
        copies = (
            pltpu.make_async_copy(keys_ref.at[0, :, source], keys_in.at[:, at], sems.at[2 * piece]),
            pltpu.make_async_copy(values_ref.at[0, :, source], values_in.at[:, at], sems.at[2 * piece + 1]),
        )
        for copy in copies:
            copy.start()
        pieces.append(copies)
        offset += width
    if meanwhile is not None:
        meanwhile()
    offset = 0
    for copies, (out_ref, row, col, width) in zip(pieces, targets):
        for copy in copies:
            copy.wait()
        for tile in range(0, width, LANES):
            at = slice(offset + tile, offset + tile + LANES)
            product = keys_in[:, at].astype(F32) * values_in[:, at].astype(F32)
            out_ref[row : row + rows, col + tile : col + tile + LANES] = product.astype(BF16)
        offset += width


def fill_lines(bank, scales_ref, assign_ref, lines_ref):
    groups, taps = lines_ref.shape
    size = bank.shape[0]
    chosen = (lax.broadcasted_iota(jnp.int32, (size, groups), 0) == assign_ref[...]).astype(F32).astype(BF16)
    contract = (((0,), (0,)), ((), ()))
    picked = lax.dot_general(bank, chosen, contract, preferred_element_type=F32)
    scaled = (picked * scales_ref[...]).astype(BF16)
    order = lax.broadcasted_iota(jnp.int32, (taps, taps), 0) + lax.broadcasted_iota(jnp.int32, (taps, taps), 1)
    flip = (order == taps - 1).astype(F32).astype(BF16)
    lines_ref[...] = lax.dot_general(scaled, flip, contract, preferred_element_type=F32)


def lead_kernel(*refs):
    bank_ref, scales_ref, assign_ref, queries_ref, keys_ref, values_ref = refs[:6]
    raw_ref, near_ref, rest_ref, lines_ref = refs[6:10]
    bank_in, scales_in, assign_in, keys_in, values_in, sems, own_sems = refs[10:]
    rows, width = near_ref.shape
    far = rest_ref.shape[1]
    half = far // 2 // LANES * LANES

    @pl.when(is_first())
    def _():
        copies = [
            pltpu.make_async_copy(bank_ref, bank_in, own_sems.at[0]),
            pltpu.make_async_copy(scales_ref, scales_in, own_sems.at[1]),
            pltpu.make_async_copy(assign_ref, assign_in, own_sems.at[2]),
            pltpu.make_async_copy(queries_ref.at[0, :, pl.ds(0, RAW)], raw_ref.at[pl.ds(0, rows)], own_sems.at[3]),
        ]
        for copy in copies:
            copy.start()

        def taps():
            for copy in copies[:3]:
                copy.wait()
            fill_lines(bank_in[0], scales_in, assign_in, lines_ref)
            for part in range(RAW // LANES):
                taken = lines_ref[part * LINES : (part + 1) * LINES, :].astype(BF16)
                raw_ref[2 * rows :, part * LANES : (part + 1) * LANES] = taken

        targets = [
            (raw_ref, rows, 0, RAW),
            (near_ref, 0, 0, width),
            (rest_ref, 0, 0, half),
            (rest_ref, 0, half, far - half),
        ]
        multiply(keys_ref, values_ref, keys_in, values_in, sems, 0, targets, taps)
        copies[3].wait()


def product_scratch(rows, total, pieces):
    return [pltpu.VMEM((rows, total), BF16), pltpu.VMEM((rows, total), BF16), pltpu.SemaphoreType.DMA((2 * pieces,))]


def lead_of(bank, scales, assign, queries, keys, values):
    rows, total = queries.shape[1:]
    near = sum(NEAR)
    return call(
        lead_kernel,
        "lead",
        (
            array(2 * rows + LINES, RAW),
            array(rows, near),
            array(rows, total - RAW - near),
            array(assign.shape[1], bank.shape[2], F32),
        ),
        [HBM] * 6,
        (VMEM,) * 4,
        [pltpu.VMEM(bank.shape, BF16), pltpu.VMEM(scales.shape, F32), pltpu.VMEM(assign.shape, jnp.int32)]
        + product_scratch(rows, total, 4)
        + [pltpu.SemaphoreType.DMA((4,))],
    )(bank, scales, assign, queries, keys, values)


def turn_table(lines_ref, row, count, table_ref, at):
    taps = lines_ref.shape[1]
    upper = lax.broadcasted_iota(jnp.int32, (ROW_BLOCK, taps), 1) > lax.broadcasted_iota(
        jnp.int32, (ROW_BLOCK, taps), 0
    )
    for group in range(count):
        line = lines_ref[row + group : row + group + 1, :]
        turned = pltpu.roll(jnp.broadcast_to(line, (ROW_BLOCK, taps)), 1, 1, stride=1, stride_axis=0)
        span = slice(at + group * ROW_BLOCK, at + (group + 1) * ROW_BLOCK)
        table_ref[span, :taps] = jnp.where(upper, turned, 0.0).astype(BF16)
        table_ref[span, taps:] = jnp.where(upper, 0.0, turned)[:, :ROW_BLOCK].astype(BF16)


def product_kernel(share, *refs):
    keys_ref, values_ref, bank_ref, scales_ref, assign_ref, held_ref, _ = refs[:7]
    out_ref, lines_ref, table_ref, keys_in, values_in, sems = refs[7:]
    half = out_ref.shape[1] // 2

    @pl.when(is_first())
    def _():
        for tile in range(sum(NEAR) // LANES):
            turn_table(held_ref, (RAW // LANES + tile) * share, share, table_ref, tile * share * ROW_BLOCK)

    @pl.when(jnp.logical_not(is_first()))
    def _():
        targets = [(out_ref, 0, 0, half), (out_ref, 0, half, half)]
        multiply(
            keys_ref,
            values_ref,
            keys_in,
            values_in,
            sems,
            0,
            targets,
            lambda: fill_lines(bank_ref[0], scales_ref, assign_ref, lines_ref),
        )


def product_of(keys, values, bank, scales, assign, lines, after):
    rows, total = keys.shape[1:]
    groups, taps = lines.shape
    share = LANES * groups // total
    return call(
        functools.partial(product_kernel, share),
        "product",
        (
            array(rows, total),
            array(groups, taps, F32),
            array(sum(NEAR) // LANES * share * ROW_BLOCK, taps + ROW_BLOCK),
        ),
        [HBM, HBM] + [VMEM] * 4 + [ANY],
        (VMEM,) * 3,
        product_scratch(rows, total, 2),
        aliases={5: 1},
    )(keys, values, bank, scales, assign, lines, after)


def mix(table_ref, row, share, window, store):
    depth = table_ref.shape[1]
    rows = window.shape[0] - depth + ROW_BLOCK
    member = lax.broadcasted_iota(jnp.int32, (ROW_BLOCK, LANES), 1) // (LANES // share)
    table = table_ref[row : row + share * ROW_BLOCK, :]
    for first in range(0, rows, 2 * ROW_BLOCK):
        starts = (first, first + ROW_BLOCK)
        pair = jnp.concatenate([window[begin : begin + depth] for begin in starts], axis=1)
        sums = jnp.dot(table, pair, preferred_element_type=F32)
        for place, begin in enumerate(starts):
            part = sums[:, place * LANES : (place + 1) * LANES]
            mixed = part[:ROW_BLOCK]
            for group in range(1, share):
                mixed = jnp.where(member == group, part[group * ROW_BLOCK : (group + 1) * ROW_BLOCK], mixed)
            store(slice(begin, begin + ROW_BLOCK), mixed)


def mix_all(width, share, lines_ref, line, table_ref, made, start_ref, behind_ref, product_ref, local, store):
    rows = product_ref.shape[0]
    first = (lax.axis_index("ctx") - 1) * rows
    inside = first + lax.broadcasted_iota(jnp.int32, (2 * rows, LANES), 0) >= start_ref[0]
    for tile in range(width // LANES):
        at = slice(tile * LANES, (tile + 1) * LANES)
        inner = slice(local + at.start, local + at.stop)
        row = tile * share * ROW_BLOCK
        if not made:
            turn_table(lines_ref, line + tile * share, share, table_ref, row)
        window = jnp.concatenate([behind_ref[:, inner], product_ref[:, inner]], axis=0)
        window = jnp.where(inside, window, jnp.zeros_like(window))
        mix(table_ref, row, share, window, functools.partial(store, at))


def share_of(lines_ref, total):
    return LANES * lines_ref.shape[0] // total


def own_kernel(first, local, made, *refs):
    start_ref, lines_ref, behind_ref, product_ref, queries_ref, residual_ref, table_ref = refs[:7]
    out_ref = refs[-1] if made else refs[-2]
    width = out_ref.shape[1]
    share = share_of(lines_ref, residual_ref.shape[1])
    if made:
        table_ref = table_ref.at[pl.ds(local // LANES * share * ROW_BLOCK, width // LANES * share * ROW_BLOCK)]
    else:
        table_ref = refs[-1]

    @pl.when(is_first())
    def _():
        def store(at, span, mixed):
            cols = slice(first + at.start, first + at.stop)
            gated = queries_ref[0, span, cols].astype(F32) * mixed
            out_ref[span, at] = (residual_ref[span, cols].astype(F32) + gated).astype(BF16)

        line = first // LANES * share
        mix_all(width, share, lines_ref, line, table_ref, made, start_ref, behind_ref, product_ref, local, store)


def table_scratch(lines, width, total):
    groups, taps = lines.shape
    return pltpu.VMEM((width * groups // total * ROW_BLOCK, taps + ROW_BLOCK), BF16)


def own_of(start, lines, behind, product, queries, residual, first, local, width, table, *after):
    rows, total = residual.shape
    made = table is not None
    return call(
        functools.partial(own_kernel, first, local, made),
        "own",
        array(rows, width),
        [SMEM] + [VMEM] * (6 if made else 5) + [ANY] * len(after),
        VMEM,
        [] if made else [table_scratch(lines, width, total)],
        weight=QUICK if made else SLOW,
    )(start, lines, behind, product, queries, residual, *([table] if made else []), *after)


def pick_kernel(raw_ref, received_ref, _, queries_ref, product_ref, lines_ref):
    rows = queries_ref.shape[0]

    def take(source):
        queries_ref[...] = source[:rows, :]
        product_ref[...] = source[rows : 2 * rows, :]
        for part in range(RAW // LANES):
            taken = source[2 * rows :, part * LANES : (part + 1) * LANES]
            lines_ref[part * LINES : (part + 1) * LINES, :] = taken.astype(F32)

    pl.when(is_first())(lambda: take(raw_ref))
    pl.when(jnp.logical_not(is_first()))(lambda: take(received_ref))


def pick_of(raw, received, taps, after):
    rows, width = (raw.shape[0] - LINES) // 2, raw.shape[1]
    return call(
        pick_kernel,
        "pick",
        (array(rows, width), array(rows, width), array(RAW // LANES * LINES, taps, F32)),
        [VMEM, VMEM, ANY],
        (VMEM,) * 3,
        weight=SLOW,
    )(raw, received, after)


def hold_kernel(value_ref, _, out_ref):
    pass


def held_back(value, after):
    return call(hold_kernel, "hold", array(*value.shape), [ANY, ANY], ANY, aliases={0: 0})(value, after)


def send_out(pieces, out_ref, sems):
    copies = [
        pltpu.make_async_copy(buffer, out_ref.at[0, :, pl.ds(first, buffer.shape[1])], sems.at[place])
        for place, (buffer, first) in enumerate(pieces)
    ]
    for copy in copies:
        copy.start()
    return copies


def wait_all(copies):
    for copy in copies:
        copy.wait()


def later_kernel(places, *refs):
    start_ref, lines_ref, behind_ref, product_ref, queries_ref = refs[:5]
    own_refs = refs[5 : 5 + len(places)]
    out_ref, gated_ref, table_ref, sems = refs[-4:]
    total = queries_ref.shape[2]
    share = share_of(lines_ref, total)

    @pl.when(is_first())
    def _():
        wait_all(send_out([(own_ref, first) for own_ref, (first, _) in zip(own_refs, places)], out_ref, sems))

    @pl.when(jnp.logical_not(is_first()))
    def _():
        def store(at, span, mixed):
            gated_ref[span, at] = queries_ref[0, span, at].astype(F32) * mixed

        mix_all(total, share, lines_ref, 0, table_ref, False, start_ref, behind_ref, product_ref, 0, store)


def later_of(start, lines, behind, product, queries, own, places):
    rows, total = product.shape
    return call(
        functools.partial(later_kernel, places),
        "later",
        (jax.ShapeDtypeStruct((1, rows, total), BF16), array(rows, total, F32)),
        [SMEM] + [VMEM] * (4 + len(own)),
        (ANY, VMEM),
        [table_scratch(lines, total, total), pltpu.SemaphoreType.DMA((len(own),))],
        weight=SLOW,
    )(start, lines, behind, product, queries, *own)


def raw_kernel(start_ref, lines_ref, behind_ref, product_ref, queries_ref, gated_ref, residual_ref, _, *refs):
    out_ref, table_ref, buffer, sems = refs
    width = buffer.shape[1]
    share = share_of(lines_ref, width)

    def store(at, span, mixed):
        gated = queries_ref[span, at].astype(F32) * mixed
        buffer[span, at] = (residual_ref[span, at].astype(F32) + gated).astype(BF16)

    mix_all(width, share, lines_ref, 0, table_ref, False, start_ref, behind_ref, product_ref, 0, store)

    @pl.when(jnp.logical_not(is_first()))
    def _():
        buffer[...] = (buffer[...].astype(F32) + gated_ref[:, :width]).astype(BF16)

    wait_all(send_out([(buffer, 0)], out_ref, sems))


def raw_finish(held, start, lines, behind, product, queries, gated, residual):
    rows, width = product.shape
    return call(
        raw_kernel,
        "raw",
        jax.ShapeDtypeStruct(held.shape, BF16),
        [SMEM] + [VMEM] * 6 + [ANY],
        ANY,
        [table_scratch(lines, width, width), pltpu.VMEM((rows, width), BF16), pltpu.SemaphoreType.DMA((1,))],
        weight=SLOW,
        aliases={7: 0},
    )(start, lines, behind, product, queries, gated, residual, held)


def finish_kernel(places, *refs):
    gated_ref, received_refs = refs[0], refs[1 : 1 + len(places)]
    out_ref, *buffers, sems = refs[2 + len(places) :]

    @pl.when(jnp.logical_not(is_first()))
    def _():
        copies = []
        for place, (first, width) in enumerate(places):
            buffer = buffers[place]
            total = received_refs[place][...].astype(F32) + gated_ref[:, first : first + width]
            buffer[...] = total.astype(BF16)
            copies += send_out([(buffer, first)], out_ref, sems.at[pl.ds(place, 1)])
        wait_all(copies)


def finish(held, gated, received, places):
    rows = gated.shape[0]
    count = len(places)
    return call(
        functools.partial(finish_kernel, places),
        "finish",
        jax.ShapeDtypeStruct(held.shape, BF16),
        [VMEM] * (1 + count) + [ANY],
        ANY,
        [pltpu.VMEM((rows, width), BF16) for _, width in places] + [pltpu.SemaphoreType.DMA((count,))],
        weight=SLOW,
        aliases={1 + count: 0},
    )(gated, *received, held)


def body(queries, keys, values, residual, filter_bank, filter_scales, group_filter, context_start):
    total = queries.shape[2]
    small = (filter_bank, filter_scales, group_filter)
    far_small = [pltpu.with_memory_space_constraint(value, pltpu.HBM) for value in small]
    far_queries, keys, values = (
        pltpu.with_memory_space_constraint(value, pltpu.HBM) for value in (queries, keys, values)
    )
    raw, near, rest, lines = lead_of(*far_small, far_queries, keys, values)
    raw_received = to_next_section(raw)
    near_behind = to_next_slab(near, (0,))
    product, lines, table = product_of(keys, values, *small, lines, near)
    rest_behind = to_next_slab(rest, (0,))
    behind = to_next_slab(product, (1,))
    own, received, places = [], [], []

    def send(made, source, source_behind, origin, first, width, *after):
        piece = own_of(
            context_start, lines, source_behind, source, queries, residual, first, first - origin, width, made, *after
        )
        own.append(piece)
        received.append(to_next_section(piece))
        places.append((first, width))
        return first + width, piece

    first, after = RAW, lines
    for width in NEAR:
        first, after = send(table, near, near_behind, RAW, first, width, after)
    raw_queries, raw_product, raw_lines = pick_of(raw, raw_received, lines.shape[1], after)
    origin, after = first, raw_queries
    for chunk, width in enumerate(REST):
        if chunk == len(REST) - 1:
            raw_product = held_back(raw_product, after)
            raw_behind = to_next_slab(raw_product, (0, 1))
            after = raw_product
        passed = received[chunk - 1 : chunk] if chunk else []
        first, after = send(None, rest, rest_behind, origin, first, width, after, *passed)
    held, gated = later_of(context_start, lines, behind, product, queries, own, places)
    held = finish(held, gated, received[:3], places[:3])
    held = raw_finish(held, context_start, raw_lines, raw_behind, raw_product, raw_queries, gated, residual)
    for chunk in range(3, len(places)):
        held = finish(held, gated, received[chunk : chunk + 1], places[chunk : chunk + 1])
    return held


def solution(mesh):
    return jax.shard_map(
        body,
        mesh=mesh,
        in_specs=(
            P("pipe", ("dp", "ctx"), None),
            P("pipe", ("dp", "ctx"), None),
            P("pipe", ("dp", "ctx"), None),
            P(("dp", "ctx"), None),
            P("pipe", None, None),
            P("pipe", None),
            P("pipe", None),
            P("dp"),
        ),
        out_specs=P("pipe", ("dp", "ctx"), None),
        check_vma=False,
    )
```

```python
import functools

import jax
import jax.numpy as jnp
from jax import lax
from jax.experimental import pallas as pl
from jax.experimental.pallas import tpu as pltpu
from jax.sharding import PartitionSpec as P

LANES = 128
ROW_BLOCK = 32
RAW = 512
ODD = (1536, 2048)
EVEN = (1408, 768, 768, 640)
LINES = 8
F32 = jnp.float32
BF16 = jnp.bfloat16
MIB = 1024 * 1024
QUICK, SLOW = 1024, 20_000_000_000

SMEM = pl.BlockSpec(memory_space=pltpu.SMEM)
VMEM = pl.BlockSpec(memory_space=pltpu.VMEM)
ANY = pl.BlockSpec(memory_space=pl.ANY)
HBM = pl.BlockSpec(memory_space=pltpu.HBM)


def to_next_slab(value, pipes, from_odd=(0, 1)):
    slabs, depth = lax.axis_size("ctx"), lax.axis_size("pipe")
    sources = [slab for slab in range(slabs - 1) if slab % 2 in from_odd]
    pairs = [(slab * depth + pipe, (slab + 1) * depth + pipe) for slab in sources for pipe in pipes]
    return lax.ppermute(value, ("ctx", "pipe"), pairs)


def to_next_section(value, slabs=(0, 1)):
    depth = lax.axis_size("pipe")
    pairs = [(slab * depth, slab * depth + 1) for slab in range(lax.axis_size("ctx")) if slab % 2 in slabs]
    return lax.ppermute(value, ("ctx", "pipe"), pairs)


def call(kernel, name, out_shape, in_specs, out_specs, scratch=(), weight=QUICK, aliases=None):
    return pl.pallas_call(
        kernel,
        out_shape=out_shape,
        in_specs=in_specs,
        out_specs=out_specs,
        scratch_shapes=list(scratch),
        input_output_aliases=aliases or {},
        compiler_params=pltpu.CompilerParams(vmem_limit_bytes=16 * MIB),
        cost_estimate=pl.CostEstimate(flops=weight, bytes_accessed=1024, transcendentals=0),
        name=name,
    )


def is_first():
    return lax.axis_index("pipe") == 0


def is_slab(odd):
    return lax.axis_index("ctx") % 2 == odd


def array(rows, cols, kind=BF16):
    return jax.ShapeDtypeStruct((rows, cols), kind)


def multiply(keys_ref, values_ref, keys_in, values_in, sems, first, targets, meanwhile=None):
    rows = keys_in.shape[0]
    pieces, offset = [], 0
    for piece, (out_ref, row, col, width) in enumerate(targets):
        at = pl.ds(offset, width)
        source = pl.ds(first + offset, width)
        copies = (
            pltpu.make_async_copy(keys_ref.at[0, :, source], keys_in.at[:, at], sems.at[2 * piece]),
            pltpu.make_async_copy(values_ref.at[0, :, source], values_in.at[:, at], sems.at[2 * piece + 1]),
        )
        for copy in copies:
            copy.start()
        pieces.append(copies)
        offset += width
    if meanwhile is not None:
        meanwhile()
    offset = 0
    for copies, (out_ref, row, col, width) in zip(pieces, targets):
        for copy in copies:
            copy.wait()
        for tile in range(0, width, LANES):
            at = slice(offset + tile, offset + tile + LANES)
            product = keys_in[:, at].astype(F32) * values_in[:, at].astype(F32)
            out_ref[row : row + rows, col + tile : col + tile + LANES] = product.astype(BF16)
        offset += width


def fill_lines(bank, scales_ref, assign_ref, lines_ref):
    groups, taps = lines_ref.shape
    size = bank.shape[0]
    chosen = (lax.broadcasted_iota(jnp.int32, (size, groups), 0) == assign_ref[...]).astype(F32).astype(BF16)
    contract = (((0,), (0,)), ((), ()))
    picked = lax.dot_general(bank, chosen, contract, preferred_element_type=F32)
    scaled = (picked * scales_ref[...]).astype(BF16)
    order = lax.broadcasted_iota(jnp.int32, (taps, taps), 0) + lax.broadcasted_iota(jnp.int32, (taps, taps), 1)
    flip = (order == taps - 1).astype(F32).astype(BF16)
    lines_ref[...] = lax.dot_general(scaled, flip, contract, preferred_element_type=F32)


def lead_kernel(*refs):
    bank_ref, scales_ref, assign_ref, queries_ref, keys_ref, values_ref = refs[:6]
    raw_ref, rest_ref, lines_ref = refs[6:9]
    bank_in, scales_in, assign_in, keys_in, values_in, sems, own_sems = refs[9:]
    rows, far = rest_ref.shape
    step = far // 3 // LANES * LANES

    @pl.when(is_first())
    def _():
        copies = [
            pltpu.make_async_copy(bank_ref, bank_in, own_sems.at[0]),
            pltpu.make_async_copy(scales_ref, scales_in, own_sems.at[1]),
            pltpu.make_async_copy(assign_ref, assign_in, own_sems.at[2]),
            pltpu.make_async_copy(queries_ref.at[0, :, pl.ds(0, RAW)], raw_ref.at[pl.ds(0, rows)], own_sems.at[3]),
        ]
        for copy in copies:
            copy.start()

        def taps():
            for copy in copies[:3]:
                copy.wait()
            fill_lines(bank_in[0], scales_in, assign_in, lines_ref)
            for part in range(RAW // LANES):
                taken = lines_ref[part * LINES : (part + 1) * LINES, :].astype(BF16)
                raw_ref[2 * rows :, part * LANES : (part + 1) * LANES] = taken

        targets = [
            (raw_ref, rows, 0, RAW),
            (rest_ref, 0, 0, step),
            (rest_ref, 0, step, step),
            (rest_ref, 0, 2 * step, far - 2 * step),
        ]
        multiply(keys_ref, values_ref, keys_in, values_in, sems, 0, targets, taps)
        copies[3].wait()


def product_scratch(rows, total, pieces):
    return [pltpu.VMEM((rows, total), BF16), pltpu.VMEM((rows, total), BF16), pltpu.SemaphoreType.DMA((2 * pieces,))]


def lead_of(bank, scales, assign, queries, keys, values):
    rows, total = queries.shape[1:]
    return call(
        lead_kernel,
        "lead",
        (
            array(2 * rows + LINES, RAW),
            array(rows, total - RAW),
            array(assign.shape[1], bank.shape[2], F32),
        ),
        [HBM] * 6,
        (VMEM,) * 3,
        [pltpu.VMEM(bank.shape, BF16), pltpu.VMEM(scales.shape, F32), pltpu.VMEM(assign.shape, jnp.int32)]
        + product_scratch(rows, total, 4)
        + [pltpu.SemaphoreType.DMA((4,))],
    )(bank, scales, assign, queries, keys, values)


def turn_table(lines_ref, row, count, table_ref, at):
    taps = lines_ref.shape[1]
    upper = lax.broadcasted_iota(jnp.int32, (ROW_BLOCK, taps), 1) > lax.broadcasted_iota(
        jnp.int32, (ROW_BLOCK, taps), 0
    )
    for group in range(count):
        line = lines_ref[row + group : row + group + 1, :]
        turned = pltpu.roll(jnp.broadcast_to(line, (ROW_BLOCK, taps)), 1, 1, stride=1, stride_axis=0)
        span = slice(at + group * ROW_BLOCK, at + (group + 1) * ROW_BLOCK)
        table_ref[span, :taps] = jnp.where(upper, turned, 0.0).astype(BF16)
        table_ref[span, taps:] = jnp.where(upper, 0.0, turned)[:, :ROW_BLOCK].astype(BF16)


def product_kernel(*refs):
    keys_ref, values_ref, bank_ref, scales_ref, assign_ref, _, rest_ref = refs[:7]
    out_ref, lines_ref, near_ref, far_ref, keys_in, values_in, sems = refs[7:]
    half = out_ref.shape[1] // 2
    near = near_ref.shape[1]

    @pl.when(jnp.logical_and(is_first(), is_slab(1)))
    def _():
        near_ref[...] = rest_ref[:, :near]
        far_ref[...] = rest_ref[:, near:]

    @pl.when(jnp.logical_not(is_first()))
    def _():
        targets = [(out_ref, 0, 0, half), (out_ref, 0, half, half)]
        multiply(
            keys_ref,
            values_ref,
            keys_in,
            values_in,
            sems,
            0,
            targets,
            lambda: fill_lines(bank_ref[0], scales_ref, assign_ref, lines_ref),
        )


def product_of(keys, values, bank, scales, assign, lines, rest):
    rows, total = keys.shape[1:]
    near = EVEN[0]
    return call(
        product_kernel,
        "product",
        (array(rows, total), array(*lines.shape, F32), array(rows, near), array(rows, total - RAW - near)),
        [HBM, HBM] + [VMEM] * 5,
        (VMEM,) * 4,
        product_scratch(rows, total, 2),
        aliases={5: 1},
    )(keys, values, bank, scales, assign, lines, rest)


def mix(table_ref, row, share, window, store):
    depth = table_ref.shape[1]
    rows = window.shape[0] - depth + ROW_BLOCK
    member = lax.broadcasted_iota(jnp.int32, (ROW_BLOCK, LANES), 1) // (LANES // share)
    table = table_ref[row : row + share * ROW_BLOCK, :]
    for first in range(0, rows, 2 * ROW_BLOCK):
        starts = (first, first + ROW_BLOCK)
        pair = jnp.concatenate([window[begin : begin + depth] for begin in starts], axis=1)
        sums = jnp.dot(table, pair, preferred_element_type=F32)
        for place, begin in enumerate(starts):
            part = sums[:, place * LANES : (place + 1) * LANES]
            mixed = part[:ROW_BLOCK]
            for group in range(1, share):
                mixed = jnp.where(member == group, part[group * ROW_BLOCK : (group + 1) * ROW_BLOCK], mixed)
            store(slice(begin, begin + ROW_BLOCK), mixed)


def mix_all(width, share, lines_ref, line, table_ref, start_ref, behind_ref, product_ref, local, store):
    rows = product_ref.shape[0]
    first = (lax.axis_index("ctx") - 1) * rows
    inside = first + lax.broadcasted_iota(jnp.int32, (2 * rows, LANES), 0) >= start_ref[0]
    for tile in range(width // LANES):
        at = slice(tile * LANES, (tile + 1) * LANES)
        near, inner = (slice(begin + at.start, begin + at.stop) for begin in local)
        row = tile * share * ROW_BLOCK
        turn_table(lines_ref, line + tile * share, share, table_ref, row)
        window = jnp.concatenate([behind_ref[:, near], product_ref[:, inner]], axis=0)
        window = jnp.where(inside, window, jnp.zeros_like(window))
        mix(table_ref, row, share, window, functools.partial(store, at))


def share_of(lines_ref, total):
    return LANES * lines_ref.shape[0] // total


def own_kernel(odd, first, shift, local, *refs):
    start_ref, lines_ref, behind_ref, product_ref, queries_ref, residual_ref = refs[:6]
    out_ref, table_ref = refs[-2:]
    width = out_ref.shape[1]
    share = share_of(lines_ref, residual_ref.shape[1])

    @pl.when(jnp.logical_and(is_first(), is_slab(odd)))
    def _():
        def store(at, span, mixed):
            cols = slice(first + at.start, first + at.stop)
            gated = queries_ref[0, span, cols].astype(F32) * mixed
            out_ref[span, at] = (residual_ref[span, cols].astype(F32) + gated).astype(BF16)

        line = first // LANES * share
        at = (shift, local)
        mix_all(width, share, lines_ref, line, table_ref, start_ref, behind_ref, product_ref, at, store)


def table_scratch(lines, width, total):
    groups, taps = lines.shape
    return pltpu.VMEM((width * groups // total * ROW_BLOCK, taps + ROW_BLOCK), BF16)


def own_of(odd, origin, start, lines, behind, product, queries, residual, first, width, weight, *after):
    rows, total = residual.shape
    return call(
        functools.partial(own_kernel, odd, first, first - origin, first - RAW),
        "own",
        array(rows, width),
        [SMEM] + [VMEM] * 5 + [ANY] * len(after),
        VMEM,
        [table_scratch(lines, width, total)],
        weight=weight,
    )(start, lines, behind, product, queries, residual, *after)


def pick_kernel(raw_ref, received_ref, _, queries_ref, product_ref, lines_ref):
    rows = queries_ref.shape[0]

    def take(source):
        queries_ref[...] = source[:rows, :]
        product_ref[...] = source[rows : 2 * rows, :]
        for part in range(RAW // LANES):
            taken = source[2 * rows :, part * LANES : (part + 1) * LANES]
            lines_ref[part * LINES : (part + 1) * LINES, :] = taken.astype(F32)

    pl.when(is_first())(lambda: take(raw_ref))
    pl.when(jnp.logical_not(is_first()))(lambda: take(received_ref))


def pick_of(raw, received, taps, after):
    rows, width = (raw.shape[0] - LINES) // 2, raw.shape[1]
    return call(
        pick_kernel,
        "pick",
        (array(rows, width), array(rows, width), array(RAW // LANES * LINES, taps, F32)),
        [VMEM, VMEM, ANY],
        (VMEM,) * 3,
        weight=SLOW,
    )(raw, received, after)


def hold_kernel(value_ref, _, out_ref):
    pass


def held_back(value, after, weight=QUICK):
    return call(
        hold_kernel, "hold", array(*value.shape), [ANY, ANY], ANY, weight=weight, aliases={0: 0}
    )(value, after)


def send_out(pieces, out_ref, sems):
    copies = [
        pltpu.make_async_copy(buffer, out_ref.at[0, :, pl.ds(first, buffer.shape[1])], sems.at[place])
        for place, (buffer, first) in enumerate(pieces)
    ]
    for copy in copies:
        copy.start()
    return copies


def wait_all(copies):
    for copy in copies:
        copy.wait()


def later_kernel(places, *refs):
    start_ref, lines_ref, behind_ref, product_ref, queries_ref = refs[:5]
    own_refs = refs[5 : 5 + len(places)]
    out_ref, gated_ref, table_ref, sems = refs[-4:]
    total = queries_ref.shape[2]
    share = share_of(lines_ref, total)

    for odd in (0, 1):

        @pl.when(jnp.logical_and(is_first(), is_slab(odd)))
        def _():
            pieces = [(own_ref, first) for own_ref, (side, first, _) in zip(own_refs, places) if side == odd]
            wait_all(send_out(pieces, out_ref, sems))

    @pl.when(jnp.logical_not(is_first()))
    def _():
        def store(at, span, mixed):
            gated_ref[span, at] = queries_ref[0, span, at].astype(F32) * mixed

        mix_all(total, share, lines_ref, 0, table_ref, start_ref, behind_ref, product_ref, (0, 0), store)


def later_of(start, lines, behind, product, queries, own, places):
    rows, total = product.shape
    return call(
        functools.partial(later_kernel, places),
        "later",
        (jax.ShapeDtypeStruct((1, rows, total), BF16), array(rows, total, F32)),
        [SMEM] + [VMEM] * (4 + len(own)),
        (ANY, VMEM),
        [table_scratch(lines, total, total), pltpu.SemaphoreType.DMA((len(own),))],
        weight=SLOW,
    )(start, lines, behind, product, queries, *own)


def raw_kernel(start_ref, lines_ref, behind_ref, product_ref, queries_ref, gated_ref, residual_ref, _, *refs):
    out_ref, table_ref, buffer, sems = refs
    width = buffer.shape[1]
    share = share_of(lines_ref, width)

    def store(at, span, mixed):
        gated = queries_ref[span, at].astype(F32) * mixed
        buffer[span, at] = (residual_ref[span, at].astype(F32) + gated).astype(BF16)

    mix_all(width, share, lines_ref, 0, table_ref, start_ref, behind_ref, product_ref, (0, 0), store)

    @pl.when(jnp.logical_not(is_first()))
    def _():
        buffer[...] = (buffer[...].astype(F32) + gated_ref[:, :width]).astype(BF16)

    wait_all(send_out([(buffer, 0)], out_ref, sems))


def raw_finish(held, start, lines, behind, product, queries, gated, residual):
    rows, width = product.shape
    return call(
        raw_kernel,
        "raw",
        jax.ShapeDtypeStruct(held.shape, BF16),
        [SMEM] + [VMEM] * 6 + [ANY],
        ANY,
        [table_scratch(lines, width, width), pltpu.VMEM((rows, width), BF16), pltpu.SemaphoreType.DMA((1,))],
        weight=SLOW,
        aliases={7: 0},
    )(start, lines, behind, product, queries, gated, residual, held)


def finish_kernel(odd, places, *refs):
    gated_ref, received_refs = refs[0], refs[1 : 1 + len(places)]
    out_ref, *buffers, sems = refs[2 + len(places) :]

    @pl.when(jnp.logical_and(jnp.logical_not(is_first()), is_slab(odd)))
    def _():
        copies = []
        for place, (_, first, width) in enumerate(places):
            buffer = buffers[place]
            total = received_refs[place][...].astype(F32) + gated_ref[:, first : first + width]
            buffer[...] = total.astype(BF16)
            copies += send_out([(buffer, first)], out_ref, sems.at[pl.ds(place, 1)])
        wait_all(copies)


def finish(held, gated, received, places):
    rows = gated.shape[0]
    count = len(places)
    return call(
        functools.partial(finish_kernel, places[0][0], places),
        "finish",
        jax.ShapeDtypeStruct(held.shape, BF16),
        [VMEM] * (1 + count) + [ANY],
        ANY,
        [pltpu.VMEM((rows, width), BF16) for _, _, width in places] + [pltpu.SemaphoreType.DMA((count,))],
        weight=SLOW,
        aliases={1 + count: 0},
    )(gated, *received, held)


def body(queries, keys, values, residual, filter_bank, filter_scales, group_filter, context_start):
    total = queries.shape[2]
    small = (filter_bank, filter_scales, group_filter)
    far_small = [pltpu.with_memory_space_constraint(value, pltpu.HBM) for value in small]
    far_queries, keys, values = (
        pltpu.with_memory_space_constraint(value, pltpu.HBM) for value in (queries, keys, values)
    )
    raw, rest, lines = lead_of(*far_small, far_queries, keys, values)
    raw_received = to_next_section(raw)
    chip_behind = to_next_slab(rest, (0,), (0,))
    product, lines, near, far = product_of(keys, values, *small, lines, rest)
    own, received, places = [], [], []

    def send(odd, behind, origin, first, width, weight, *after):
        piece = own_of(
            odd, origin, context_start, lines, behind, rest, queries, residual, first, width, weight, *after
        )
        own.append(piece)
        received.append(to_next_section(piece, (odd,)))
        places.append((odd, first, width))
        return first + width, piece

    first, after = send(1, chip_behind, RAW, RAW, ODD[0], QUICK, lines)
    near = held_back(near, after)
    near_behind = to_next_slab(near, (0,), (1,))
    first, after = send(1, chip_behind, RAW, first, ODD[1], QUICK, near)
    product = held_back(product, after)
    behind = to_next_slab(product, (1,))
    raw_queries, raw_product, raw_lines = pick_of(raw, raw_received, lines.shape[1], product)
    far_behind = to_next_slab(held_back(far, raw_queries), (0,), (1,))
    raw_queries = held_back(raw_queries, received[0], SLOW)
    first, after = send(0, near_behind, RAW, RAW, EVEN[0], SLOW, raw_queries)
    raw_product = held_back(raw_product, after)
    raw_behind = to_next_slab(raw_product, (0, 1))
    origin, after = first, raw_product
    for width, passed in zip(EVEN[1:], (received[1], after, behind)):
        first, after = send(0, far_behind, origin, first, width, SLOW, after, passed)
    held, gated = later_of(context_start, lines, behind, product, queries, own, places)
    odd = len(ODD)
    held = finish(held, gated, received[:odd], places[:odd])
    held = raw_finish(held, context_start, raw_lines, raw_behind, raw_product, raw_queries, gated, residual)
    for last in (odd + 2, odd + 3, odd + 4):
        begin = odd if last == odd + 2 else last - 1
        held = finish(held, gated, received[begin:last], places[begin:last])
    return held


def solution(mesh):
    return jax.shard_map(
        body,
        mesh=mesh,
        in_specs=(
            P("pipe", ("dp", "ctx"), None),
            P("pipe", ("dp", "ctx"), None),
            P("pipe", ("dp", "ctx"), None),
            P(("dp", "ctx"), None),
            P("pipe", None, None),
            P("pipe", None),
            P("pipe", None),
            P("dp"),
        ),
        out_specs=P("pipe", ("dp", "ctx"), None),
        check_vma=False,
    )
```

```python
import functools

import jax
import jax.numpy as jnp
from jax import lax
from jax.experimental import pallas as pl
from jax.experimental.pallas import tpu as pltpu
from jax.sharding import PartitionSpec as P

LANES = 128
ROW_BLOCK = 32
RAW = 384
ODD = (1536, 2176)
EVEN = (1024, 1024, 768, 896)
NEAR = 2048
LINES = 8
F32 = jnp.float32
BF16 = jnp.bfloat16
MIB = 1024 * 1024
QUICK, SLOW = 1024, 20_000_000_000

SMEM = pl.BlockSpec(memory_space=pltpu.SMEM)
VMEM = pl.BlockSpec(memory_space=pltpu.VMEM)
ANY = pl.BlockSpec(memory_space=pl.ANY)
HBM = pl.BlockSpec(memory_space=pltpu.HBM)


def to_next_slab(value, pipes, from_odd=(0, 1)):
    slabs, depth = lax.axis_size("ctx"), lax.axis_size("pipe")
    sources = [slab for slab in range(slabs - 1) if slab % 2 in from_odd]
    pairs = [(slab * depth + pipe, (slab + 1) * depth + pipe) for slab in sources for pipe in pipes]
    return lax.ppermute(value, ("ctx", "pipe"), pairs)


def to_next_section(value, slabs=(0, 1)):
    depth = lax.axis_size("pipe")
    pairs = [(slab * depth, slab * depth + 1) for slab in range(lax.axis_size("ctx")) if slab % 2 in slabs]
    return lax.ppermute(value, ("ctx", "pipe"), pairs)


def call(kernel, name, out_shape, in_specs, out_specs, scratch=(), weight=QUICK, aliases=None):
    return pl.pallas_call(
        kernel,
        out_shape=out_shape,
        in_specs=in_specs,
        out_specs=out_specs,
        scratch_shapes=list(scratch),
        input_output_aliases=aliases or {},
        compiler_params=pltpu.CompilerParams(vmem_limit_bytes=16 * MIB),
        cost_estimate=pl.CostEstimate(flops=weight, bytes_accessed=1024, transcendentals=0),
        name=name,
    )


def is_first():
    return lax.axis_index("pipe") == 0


def is_slab(odd):
    return lax.axis_index("ctx") % 2 == odd


def array(rows, cols, kind=BF16):
    return jax.ShapeDtypeStruct((rows, cols), kind)


def multiply(keys_ref, values_ref, keys_in, values_in, sems, first, targets, meanwhile=None):
    rows = keys_in.shape[0]
    pieces, offset = [], 0
    for piece, (out_ref, row, col, width) in enumerate(targets):
        at = pl.ds(offset, width)
        source = pl.ds(first + offset, width)
        copies = (
            pltpu.make_async_copy(keys_ref.at[0, :, source], keys_in.at[:, at], sems.at[2 * piece]),
            pltpu.make_async_copy(values_ref.at[0, :, source], values_in.at[:, at], sems.at[2 * piece + 1]),
        )
        for copy in copies:
            copy.start()
        pieces.append(copies)
        offset += width
    if meanwhile is not None:
        meanwhile()
    offset = 0
    for copies, (out_ref, row, col, width) in zip(pieces, targets):
        for copy in copies:
            copy.wait()
        for tile in range(0, width, LANES):
            at = slice(offset + tile, offset + tile + LANES)
            product = keys_in[:, at].astype(F32) * values_in[:, at].astype(F32)
            out_ref[row : row + rows, col + tile : col + tile + LANES] = product.astype(BF16)
        offset += width


def fill_lines(bank, scales_ref, assign_ref, lines_ref):
    groups, taps = lines_ref.shape
    size = bank.shape[0]
    chosen = (lax.broadcasted_iota(jnp.int32, (size, groups), 0) == assign_ref[...]).astype(F32).astype(BF16)
    contract = (((0,), (0,)), ((), ()))
    picked = lax.dot_general(bank, chosen, contract, preferred_element_type=F32)
    scaled = (picked * scales_ref[...]).astype(BF16)
    order = lax.broadcasted_iota(jnp.int32, (taps, taps), 0) + lax.broadcasted_iota(jnp.int32, (taps, taps), 1)
    flip = (order == taps - 1).astype(F32).astype(BF16)
    lines_ref[...] = lax.dot_general(scaled, flip, contract, preferred_element_type=F32)


def lead_kernel(*refs):
    bank_ref, scales_ref, assign_ref, queries_ref, keys_ref, values_ref = refs[:6]
    raw_ref, whole_ref, lines_ref = refs[6:9]
    bank_in, scales_in, assign_in, keys_in, values_in, sems, own_sems = refs[9:]
    rows, total = whole_ref.shape
    step = total // 4 // LANES * LANES

    @pl.when(is_first())
    def _():
        copies = [
            pltpu.make_async_copy(bank_ref, bank_in, own_sems.at[0]),
            pltpu.make_async_copy(scales_ref, scales_in, own_sems.at[1]),
            pltpu.make_async_copy(assign_ref, assign_in, own_sems.at[2]),
            pltpu.make_async_copy(queries_ref.at[0, :, pl.ds(0, RAW)], raw_ref.at[pl.ds(0, rows)], own_sems.at[3]),
        ]
        for copy in copies:
            copy.start()

        def taps():
            for copy in copies[:3]:
                copy.wait()
            fill_lines(bank_in[0], scales_in, assign_in, lines_ref)
            for part in range(RAW // LANES):
                taken = lines_ref[part * LINES : (part + 1) * LINES, :].astype(BF16)
                raw_ref[2 * rows :, part * LANES : (part + 1) * LANES] = taken

        targets = [
            (whole_ref, 0, 0, step),
            (whole_ref, 0, step, step),
            (whole_ref, 0, 2 * step, step),
            (whole_ref, 0, 3 * step, total - 3 * step),
        ]
        multiply(keys_ref, values_ref, keys_in, values_in, sems, 0, targets, taps)
        raw_ref[rows : 2 * rows, :] = whole_ref[:, :RAW]
        copies[3].wait()


def product_scratch(rows, total, pieces):
    return [pltpu.VMEM((rows, total), BF16), pltpu.VMEM((rows, total), BF16), pltpu.SemaphoreType.DMA((2 * pieces,))]


def lead_of(bank, scales, assign, queries, keys, values):
    rows, total = queries.shape[1:]
    return call(
        lead_kernel,
        "lead",
        (
            array(2 * rows + LINES, RAW),
            array(rows, total),
            array(assign.shape[1], bank.shape[2], F32),
        ),
        [HBM] * 6,
        (VMEM,) * 3,
        [pltpu.VMEM(bank.shape, BF16), pltpu.VMEM(scales.shape, F32), pltpu.VMEM(assign.shape, jnp.int32)]
        + product_scratch(rows, total, 4)
        + [pltpu.SemaphoreType.DMA((4,))],
    )(bank, scales, assign, queries, keys, values)


def turn_table(lines_ref, row, count, table_ref, at):
    taps = lines_ref.shape[1]
    upper = lax.broadcasted_iota(jnp.int32, (ROW_BLOCK, taps), 1) > lax.broadcasted_iota(
        jnp.int32, (ROW_BLOCK, taps), 0
    )
    for group in range(count):
        line = lines_ref[row + group : row + group + 1, :]
        turned = pltpu.roll(jnp.broadcast_to(line, (ROW_BLOCK, taps)), 1, 1, stride=1, stride_axis=0)
        span = slice(at + group * ROW_BLOCK, at + (group + 1) * ROW_BLOCK)
        table_ref[span, :taps] = jnp.where(upper, turned, 0.0).astype(BF16)
        table_ref[span, taps:] = jnp.where(upper, 0.0, turned)[:, :ROW_BLOCK].astype(BF16)


def product_kernel(*refs):
    keys_ref, values_ref, bank_ref, scales_ref, assign_ref, _, whole_ref = refs[:7]
    out_ref, lines_ref, near_ref, far_ref, keys_in, values_in, sems = refs[7:]
    half = out_ref.shape[1] // 2
    near = near_ref.shape[1]

    @pl.when(jnp.logical_and(is_first(), is_slab(1)))
    def _():
        near_ref[...] = whole_ref[:, RAW : RAW + near]
        far_ref[:, : far_ref.shape[1] - RAW] = whole_ref[:, RAW + near :]
        far_ref[:, far_ref.shape[1] - RAW :] = whole_ref[:, :RAW]

    @pl.when(jnp.logical_not(is_first()))
    def _():
        targets = [(out_ref, 0, 0, half), (out_ref, 0, half, half)]
        multiply(
            keys_ref,
            values_ref,
            keys_in,
            values_in,
            sems,
            0,
            targets,
            lambda: fill_lines(bank_ref[0], scales_ref, assign_ref, lines_ref),
        )


def product_of(keys, values, bank, scales, assign, lines, whole):
    rows, total = keys.shape[1:]
    return call(
        product_kernel,
        "product",
        (array(rows, total), array(*lines.shape, F32), array(rows, NEAR), array(rows, total - NEAR)),
        [HBM, HBM] + [VMEM] * 5,
        (VMEM,) * 4,
        product_scratch(rows, total, 2),
        aliases={5: 1},
    )(keys, values, bank, scales, assign, lines, whole)


def mix(table_ref, row, share, window, store):
    depth = table_ref.shape[1]
    rows = window.shape[0] - depth + ROW_BLOCK
    member = lax.broadcasted_iota(jnp.int32, (ROW_BLOCK, LANES), 1) // (LANES // share)
    table = table_ref[row : row + share * ROW_BLOCK, :]
    for first in range(0, rows, 2 * ROW_BLOCK):
        starts = (first, first + ROW_BLOCK)
        pair = jnp.concatenate([window[begin : begin + depth] for begin in starts], axis=1)
        sums = jnp.dot(table, pair, preferred_element_type=F32)
        for place, begin in enumerate(starts):
            part = sums[:, place * LANES : (place + 1) * LANES]
            mixed = part[:ROW_BLOCK]
            for group in range(1, share):
                mixed = jnp.where(member == group, part[group * ROW_BLOCK : (group + 1) * ROW_BLOCK], mixed)
            store(slice(begin, begin + ROW_BLOCK), mixed)


def mix_all(width, share, lines_ref, line, table_ref, start_ref, behind_ref, product_ref, local, store):
    rows = product_ref.shape[0]
    first = (lax.axis_index("ctx") - 1) * rows
    inside = first + lax.broadcasted_iota(jnp.int32, (2 * rows, LANES), 0) >= start_ref[0]
    for tile in range(width // LANES):
        at = slice(tile * LANES, (tile + 1) * LANES)
        near, inner = (slice(begin + at.start, begin + at.stop) for begin in local)
        row = tile * share * ROW_BLOCK
        turn_table(lines_ref, line + tile * share, share, table_ref, row)
        window = jnp.concatenate([behind_ref[:, near], product_ref[:, inner]], axis=0)
        window = jnp.where(inside, window, jnp.zeros_like(window))
        mix(table_ref, row, share, window, functools.partial(store, at))


def share_of(lines_ref, total):
    return LANES * lines_ref.shape[0] // total


def own_kernel(odd, first, shift, local, *refs):
    start_ref, lines_ref, behind_ref, product_ref, queries_ref, residual_ref = refs[:6]
    out_ref, table_ref = refs[-2:]
    width = out_ref.shape[1]
    share = share_of(lines_ref, residual_ref.shape[1])

    @pl.when(jnp.logical_and(is_first(), is_slab(odd)))
    def _():
        def store(at, span, mixed):
            cols = slice(first + at.start, first + at.stop)
            gated = queries_ref[0, span, cols].astype(F32) * mixed
            out_ref[span, at] = (residual_ref[span, cols].astype(F32) + gated).astype(BF16)

        line = first // LANES * share
        at = (shift, local)
        mix_all(width, share, lines_ref, line, table_ref, start_ref, behind_ref, product_ref, at, store)


def table_scratch(lines, width, total):
    groups, taps = lines.shape
    return pltpu.VMEM((width * groups // total * ROW_BLOCK, taps + ROW_BLOCK), BF16)


def own_of(odd, origin, start, lines, behind, product, queries, residual, first, width, weight, *after):
    rows, total = residual.shape
    return call(
        functools.partial(own_kernel, odd, first, first - origin, first),
        "own",
        array(rows, width),
        [SMEM] + [VMEM] * 5 + [ANY] * len(after),
        VMEM,
        [table_scratch(lines, width, total)],
        weight=weight,
    )(start, lines, behind, product, queries, residual, *after)


def pick_kernel(raw_ref, received_ref, _, queries_ref, product_ref, lines_ref):
    rows = queries_ref.shape[0]

    def take(source):
        queries_ref[...] = source[:rows, :]
        product_ref[...] = source[rows : 2 * rows, :]
        for part in range(RAW // LANES):
            taken = source[2 * rows :, part * LANES : (part + 1) * LANES]
            lines_ref[part * LINES : (part + 1) * LINES, :] = taken.astype(F32)

    pl.when(is_first())(lambda: take(raw_ref))
    pl.when(jnp.logical_not(is_first()))(lambda: take(received_ref))


def pick_of(raw, received, taps, after):
    rows, width = (raw.shape[0] - LINES) // 2, raw.shape[1]
    return call(
        pick_kernel,
        "pick",
        (array(rows, width), array(rows, width), array(RAW // LANES * LINES, taps, F32)),
        [VMEM, VMEM, ANY],
        (VMEM,) * 3,
        weight=SLOW,
    )(raw, received, after)


def hold_kernel(value_ref, _, out_ref):
    pass


def held_back(value, after, weight=QUICK):
    return call(
        hold_kernel, "hold", array(*value.shape), [ANY, ANY], ANY, weight=weight, aliases={0: 0}
    )(value, after)


def send_out(pieces, out_ref, sems):
    copies = [
        pltpu.make_async_copy(buffer, out_ref.at[0, :, pl.ds(first, buffer.shape[1])], sems.at[place])
        for place, (buffer, first) in enumerate(pieces)
    ]
    for copy in copies:
        copy.start()
    return copies


def wait_all(copies):
    for copy in copies:
        copy.wait()


def later_kernel(places, *refs):
    start_ref, lines_ref, behind_ref, product_ref, queries_ref = refs[:5]
    own_refs = refs[5 : 5 + len(places)]
    out_ref, gated_ref, table_ref, sems = refs[-4:]
    total = queries_ref.shape[2]
    share = share_of(lines_ref, total)

    for odd in (0, 1):

        @pl.when(jnp.logical_and(is_first(), is_slab(odd)))
        def _():
            pieces = [(own_ref, first) for own_ref, (side, first, _) in zip(own_refs, places) if side == odd]
            wait_all(send_out(pieces, out_ref, sems))

    @pl.when(jnp.logical_not(is_first()))
    def _():
        def store(at, span, mixed):
            gated_ref[span, at] = queries_ref[0, span, at].astype(F32) * mixed

        mix_all(total, share, lines_ref, 0, table_ref, start_ref, behind_ref, product_ref, (0, 0), store)


def later_of(start, lines, behind, product, queries, own, places):
    rows, total = product.shape
    return call(
        functools.partial(later_kernel, places),
        "later",
        (jax.ShapeDtypeStruct((1, rows, total), BF16), array(rows, total, F32)),
        [SMEM] + [VMEM] * (4 + len(own)),
        (ANY, VMEM),
        [table_scratch(lines, total, total), pltpu.SemaphoreType.DMA((len(own),))],
        weight=SLOW,
    )(start, lines, behind, product, queries, *own)


def raw_kernel(*refs):
    start_ref, lines_ref, behind_ref, chip_ref, far_ref, product_ref, queries_ref, gated_ref, residual_ref = refs[:9]
    out_ref, chosen_ref, table_ref, buffer, sems = refs[10:]
    width = buffer.shape[1]
    share = share_of(lines_ref, width)
    far = far_ref.shape[1]
    sources = (
        (jnp.logical_and(is_first(), is_slab(0)), far_ref, slice(far - width, far)),
        (jnp.logical_and(is_first(), is_slab(1)), chip_ref, slice(0, width)),
        (jnp.logical_not(is_first()), behind_ref, slice(0, width)),
    )
    for wanted, source, cols in sources:

        @pl.when(wanted)
        def _():
            chosen_ref[...] = source[:, cols]

    def store(at, span, mixed):
        gated = queries_ref[span, at].astype(F32) * mixed
        buffer[span, at] = (residual_ref[span, at].astype(F32) + gated).astype(BF16)

    mix_all(width, share, lines_ref, 0, table_ref, start_ref, chosen_ref, product_ref, (0, 0), store)

    @pl.when(jnp.logical_not(is_first()))
    def _():
        buffer[...] = (buffer[...].astype(F32) + gated_ref[:, :width]).astype(BF16)

    wait_all(send_out([(buffer, 0)], out_ref, sems))


def raw_finish(held, start, lines, behind, chip_behind, far_behind, product, queries, gated, residual):
    rows, width = product.shape
    return call(
        raw_kernel,
        "raw",
        jax.ShapeDtypeStruct(held.shape, BF16),
        [SMEM] + [VMEM] * 8 + [ANY],
        ANY,
        [
            pltpu.VMEM((rows, width), BF16),
            table_scratch(lines, width, width),
            pltpu.VMEM((rows, width), BF16),
            pltpu.SemaphoreType.DMA((1,)),
        ],
        weight=SLOW,
        aliases={9: 0},
    )(start, lines, behind, chip_behind, far_behind, product, queries, gated, residual, held)


def finish_kernel(odd, places, *refs):
    gated_ref, received_refs = refs[0], refs[1 : 1 + len(places)]
    out_ref, *buffers, sems = refs[2 + len(places) :]

    @pl.when(jnp.logical_and(jnp.logical_not(is_first()), is_slab(odd)))
    def _():
        copies = []
        for place, (_, first, width) in enumerate(places):
            buffer = buffers[place]
            total = received_refs[place][...].astype(F32) + gated_ref[:, first : first + width]
            buffer[...] = total.astype(BF16)
            copies += send_out([(buffer, first)], out_ref, sems.at[pl.ds(place, 1)])
        wait_all(copies)


def finish(held, gated, received, places):
    rows = gated.shape[0]
    count = len(places)
    return call(
        functools.partial(finish_kernel, places[0][0], places),
        "finish",
        jax.ShapeDtypeStruct(held.shape, BF16),
        [VMEM] * (1 + count) + [ANY],
        ANY,
        [pltpu.VMEM((rows, width), BF16) for _, _, width in places] + [pltpu.SemaphoreType.DMA((count,))],
        weight=SLOW,
        aliases={1 + count: 0},
    )(gated, *received, held)


def body(queries, keys, values, residual, filter_bank, filter_scales, group_filter, context_start):
    total = queries.shape[2]
    small = (filter_bank, filter_scales, group_filter)
    far_small = [pltpu.with_memory_space_constraint(value, pltpu.HBM) for value in small]
    far_queries, keys, values = (
        pltpu.with_memory_space_constraint(value, pltpu.HBM) for value in (queries, keys, values)
    )
    raw, whole, lines = lead_of(*far_small, far_queries, keys, values)
    raw_received = to_next_section(raw)
    chip_behind = to_next_slab(whole, (0,), (0,))
    product, lines, near, far = product_of(keys, values, *small, lines, whole)
    own, received, places = [], [], []

    def send(odd, behind, origin, first, width, weight, *after):
        piece = own_of(
            odd, origin, context_start, lines, behind, whole, queries, residual, first, width, weight, *after
        )
        own.append(piece)
        received.append(to_next_section(piece, (odd,)))
        places.append((odd, first, width))
        return first + width, piece

    first, after = send(1, chip_behind, 0, RAW, ODD[0], QUICK, lines)
    near = held_back(near, after)
    near_behind = to_next_slab(near, (0,), (1,))
    first, after = send(1, chip_behind, 0, first, ODD[1], QUICK, near)
    product = held_back(product, after)
    behind = to_next_slab(product, (1,))
    raw_queries, raw_product, raw_lines = pick_of(raw, raw_received, lines.shape[1], product)
    far_behind = to_next_slab(held_back(far, raw_queries), (0,), (1,))
    raw_queries = held_back(raw_queries, received[0], SLOW)
    first, after = send(0, near_behind, RAW, RAW, EVEN[0], SLOW, raw_queries)
    raw_product = held_back(raw_product, after)
    raw_behind = to_next_slab(raw_product, (1,))
    after = raw_product
    for width, passed in zip(EVEN[1:], (received[1], after, behind)):
        origin = RAW if first < RAW + NEAR else RAW + NEAR
        source = near_behind if first < RAW + NEAR else far_behind
        first, after = send(0, source, origin, first, width, SLOW, after, passed)
    held, gated = later_of(context_start, lines, behind, product, queries, own, places)
    odd = len(ODD)
    held = finish(held, gated, received[:odd], places[:odd])
    held = raw_finish(
        held,
        context_start,
        raw_lines,
        raw_behind,
        chip_behind,
        far_behind,
        raw_product,
        raw_queries,
        gated,
        residual,
    )
    for last in (odd + 2, odd + 3, odd + 4):
        begin = odd if last == odd + 2 else last - 1
        held = finish(held, gated, received[begin:last], places[begin:last])
    return held


def solution(mesh):
    return jax.shard_map(
        body,
        mesh=mesh,
        in_specs=(
            P("pipe", ("dp", "ctx"), None),
            P("pipe", ("dp", "ctx"), None),
            P("pipe", ("dp", "ctx"), None),
            P(("dp", "ctx"), None),
            P("pipe", None, None),
            P("pipe", None),
            P("pipe", None),
            P("dp"),
        ),
        out_specs=P("pipe", ("dp", "ctx"), None),
        check_vma=False,
    )
```

```python
import functools

import jax
import jax.numpy as jnp
from jax import lax
from jax.experimental import pallas as pl
from jax.experimental.pallas import tpu as pltpu
from jax.sharding import PartitionSpec as P

LANES = 128
ROW_BLOCK = 32
RAW = 384
ODD = (1536, 2176)
EVEN = (1280, 768, 768, 896)
PIECES = 4
NEAR = 2048
LINES = 8
F32 = jnp.float32
BF16 = jnp.bfloat16
MIB = 1024 * 1024
QUICK, SLOW = 1024, 20_000_000_000

SMEM = pl.BlockSpec(memory_space=pltpu.SMEM)
VMEM = pl.BlockSpec(memory_space=pltpu.VMEM)
ANY = pl.BlockSpec(memory_space=pl.ANY)
HBM = pl.BlockSpec(memory_space=pltpu.HBM)


def to_next_slab(value, pipes, from_odd=(0, 1)):
    slabs, depth = lax.axis_size("ctx"), lax.axis_size("pipe")
    sources = [slab for slab in range(slabs - 1) if slab % 2 in from_odd]
    pairs = [(slab * depth + pipe, (slab + 1) * depth + pipe) for slab in sources for pipe in pipes]
    return lax.ppermute(value, ("ctx", "pipe"), pairs)


def to_next_section(value, slabs=(0, 1)):
    depth = lax.axis_size("pipe")
    pairs = [(slab * depth, slab * depth + 1) for slab in range(lax.axis_size("ctx")) if slab % 2 in slabs]
    return lax.ppermute(value, ("ctx", "pipe"), pairs)


def call(kernel, name, out_shape, in_specs, out_specs, scratch=(), weight=QUICK, aliases=None):
    return pl.pallas_call(
        kernel,
        out_shape=out_shape,
        in_specs=in_specs,
        out_specs=out_specs,
        scratch_shapes=list(scratch),
        input_output_aliases=aliases or {},
        compiler_params=pltpu.CompilerParams(vmem_limit_bytes=16 * MIB),
        cost_estimate=pl.CostEstimate(flops=weight, bytes_accessed=1024, transcendentals=0),
        name=name,
    )


def is_first():
    return lax.axis_index("pipe") == 0


def is_slab(odd):
    return lax.axis_index("ctx") % 2 == odd


def array(rows, cols, kind=BF16):
    return jax.ShapeDtypeStruct((rows, cols), kind)


def multiply(keys_ref, values_ref, keys_in, values_in, sems, out_ref, meanwhile):
    rows, cols = out_ref.shape
    step = rows // PIECES
    spans = [pl.ds(piece * step, step) for piece in range(PIECES)]
    copies = []
    for piece, span in enumerate(spans):
        copies.append(
            (
                pltpu.make_async_copy(keys_ref.at[0, span], keys_in.at[span], sems.at[2 * piece]),
                pltpu.make_async_copy(values_ref.at[0, span], values_in.at[span], sems.at[2 * piece + 1]),
            )
        )
        for copy in copies[-1]:
            copy.start()
    meanwhile()
    for span, pair in zip(spans, copies):
        for copy in pair:
            copy.wait()
        for tile in range(0, cols, 4 * LANES):
            at = slice(tile, tile + 4 * LANES)
            out_ref[span, at] = (keys_in[span, at].astype(F32) * values_in[span, at].astype(F32)).astype(BF16)


def fill_lines(bank, scales_ref, assign_ref, lines_ref):
    groups, taps = lines_ref.shape
    size = bank.shape[0]
    chosen = (lax.broadcasted_iota(jnp.int32, (size, groups), 0) == assign_ref[...]).astype(F32).astype(BF16)
    contract = (((0,), (0,)), ((), ()))
    picked = lax.dot_general(bank, chosen, contract, preferred_element_type=F32)
    scaled = (picked * scales_ref[...]).astype(BF16)
    order = lax.broadcasted_iota(jnp.int32, (taps, taps), 0) + lax.broadcasted_iota(jnp.int32, (taps, taps), 1)
    flip = (order == taps - 1).astype(F32).astype(BF16)
    lines_ref[...] = lax.dot_general(scaled, flip, contract, preferred_element_type=F32)


def lead_kernel(*refs):
    bank_ref, scales_ref, assign_ref, queries_ref, keys_ref, values_ref = refs[:6]
    raw_ref, whole_ref, lines_ref = refs[6:9]
    bank_in, scales_in, assign_in, keys_in, values_in, sems, own_sems = refs[9:]
    rows = whole_ref.shape[0]

    @pl.when(is_first())
    def _():
        copies = [
            pltpu.make_async_copy(bank_ref, bank_in, own_sems.at[0]),
            pltpu.make_async_copy(scales_ref, scales_in, own_sems.at[1]),
            pltpu.make_async_copy(assign_ref, assign_in, own_sems.at[2]),
            pltpu.make_async_copy(queries_ref.at[0, :, pl.ds(0, RAW)], raw_ref.at[pl.ds(0, rows)], own_sems.at[3]),
        ]
        for copy in copies:
            copy.start()

        def taps():
            for copy in copies[:3]:
                copy.wait()
            fill_lines(bank_in[0], scales_in, assign_in, lines_ref)
            for part in range(RAW // LANES):
                taken = lines_ref[part * LINES : (part + 1) * LINES, :].astype(BF16)
                raw_ref[2 * rows :, part * LANES : (part + 1) * LANES] = taken

        multiply(keys_ref, values_ref, keys_in, values_in, sems, whole_ref, taps)
        raw_ref[rows : 2 * rows, :] = whole_ref[:, :RAW]
        copies[3].wait()


def product_scratch(rows, total):
    return [pltpu.VMEM((rows, total), BF16), pltpu.VMEM((rows, total), BF16), pltpu.SemaphoreType.DMA((2 * PIECES,))]


def lead_of(bank, scales, assign, queries, keys, values):
    rows, total = queries.shape[1:]
    return call(
        lead_kernel,
        "lead",
        (
            array(2 * rows + LINES, RAW),
            array(rows, total),
            array(assign.shape[1], bank.shape[2], F32),
        ),
        [HBM] * 6,
        (VMEM,) * 3,
        [pltpu.VMEM(bank.shape, BF16), pltpu.VMEM(scales.shape, F32), pltpu.VMEM(assign.shape, jnp.int32)]
        + product_scratch(rows, total)
        + [pltpu.SemaphoreType.DMA((4,))],
    )(bank, scales, assign, queries, keys, values)


def turn_table(lines_ref, row, count, table_ref, at):
    taps = lines_ref.shape[1]
    upper = lax.broadcasted_iota(jnp.int32, (ROW_BLOCK, taps), 1) > lax.broadcasted_iota(
        jnp.int32, (ROW_BLOCK, taps), 0
    )
    for group in range(count):
        line = lines_ref[row + group : row + group + 1, :]
        turned = pltpu.roll(jnp.broadcast_to(line, (ROW_BLOCK, taps)), 1, 1, stride=1, stride_axis=0)
        span = slice(at + group * ROW_BLOCK, at + (group + 1) * ROW_BLOCK)
        table_ref[span, :taps] = jnp.where(upper, turned, 0.0).astype(BF16)
        table_ref[span, taps:] = jnp.where(upper, 0.0, turned)[:, :ROW_BLOCK].astype(BF16)


def product_kernel(*refs):
    keys_ref, values_ref, bank_ref, scales_ref, assign_ref, _, whole_ref = refs[:7]
    out_ref, lines_ref, near_ref, far_ref, keys_in, values_in, sems = refs[7:]
    near = near_ref.shape[1]

    @pl.when(jnp.logical_and(is_first(), is_slab(1)))
    def _():
        near_ref[...] = whole_ref[:, RAW : RAW + near]
        far_ref[:, : far_ref.shape[1] - RAW] = whole_ref[:, RAW + near :]
        far_ref[:, far_ref.shape[1] - RAW :] = whole_ref[:, :RAW]

    @pl.when(jnp.logical_not(is_first()))
    def _():
        multiply(
            keys_ref,
            values_ref,
            keys_in,
            values_in,
            sems,
            out_ref,
            lambda: fill_lines(bank_ref[0], scales_ref, assign_ref, lines_ref),
        )


def product_of(keys, values, bank, scales, assign, lines, whole):
    rows, total = keys.shape[1:]
    return call(
        product_kernel,
        "product",
        (array(rows, total), array(*lines.shape, F32), array(rows, NEAR), array(rows, total - NEAR)),
        [HBM, HBM] + [VMEM] * 5,
        (VMEM,) * 4,
        product_scratch(rows, total),
        aliases={5: 1},
    )(keys, values, bank, scales, assign, lines, whole)


def mix(table_ref, row, share, window, store):
    depth = table_ref.shape[1]
    rows = window.shape[0] - depth + ROW_BLOCK
    member = lax.broadcasted_iota(jnp.int32, (ROW_BLOCK, LANES), 1) // (LANES // share)
    table = table_ref[row : row + share * ROW_BLOCK, :]
    for first in range(0, rows, 2 * ROW_BLOCK):
        starts = (first, first + ROW_BLOCK)
        pair = jnp.concatenate([window[begin : begin + depth] for begin in starts], axis=1)
        sums = jnp.dot(table, pair, preferred_element_type=F32)
        for place, begin in enumerate(starts):
            part = sums[:, place * LANES : (place + 1) * LANES]
            mixed = part[:ROW_BLOCK]
            for group in range(1, share):
                mixed = jnp.where(member == group, part[group * ROW_BLOCK : (group + 1) * ROW_BLOCK], mixed)
            store(slice(begin, begin + ROW_BLOCK), mixed)


def mix_all(width, share, lines_ref, line, table_ref, start_ref, behind_ref, product_ref, local, store):
    rows = product_ref.shape[0]
    first = (lax.axis_index("ctx") - 1) * rows
    inside = first + lax.broadcasted_iota(jnp.int32, (2 * rows, LANES), 0) >= start_ref[0]
    for tile in range(width // LANES):
        at = slice(tile * LANES, (tile + 1) * LANES)
        near, inner = (slice(begin + at.start, begin + at.stop) for begin in local)
        row = tile * share * ROW_BLOCK
        turn_table(lines_ref, line + tile * share, share, table_ref, row)
        window = jnp.concatenate([behind_ref[:, near], product_ref[:, inner]], axis=0)
        window = jnp.where(inside, window, jnp.zeros_like(window))
        mix(table_ref, row, share, window, functools.partial(store, at))


def share_of(lines_ref, total):
    return LANES * lines_ref.shape[0] // total


def own_kernel(odd, first, shift, local, *refs):
    start_ref, lines_ref, behind_ref, product_ref, queries_ref, residual_ref = refs[:6]
    out_ref, table_ref = refs[-2:]
    width = out_ref.shape[1]
    share = share_of(lines_ref, residual_ref.shape[1])

    @pl.when(jnp.logical_and(is_first(), is_slab(odd)))
    def _():
        def store(at, span, mixed):
            cols = slice(first + at.start, first + at.stop)
            gated = queries_ref[0, span, cols].astype(F32) * mixed
            out_ref[span, at] = (residual_ref[span, cols].astype(F32) + gated).astype(BF16)

        line = first // LANES * share
        at = (shift, local)
        mix_all(width, share, lines_ref, line, table_ref, start_ref, behind_ref, product_ref, at, store)


def table_scratch(lines, width, total):
    groups, taps = lines.shape
    return pltpu.VMEM((width * groups // total * ROW_BLOCK, taps + ROW_BLOCK), BF16)


def own_of(odd, origin, start, lines, behind, product, queries, residual, first, width, weight, *after):
    rows, total = residual.shape
    return call(
        functools.partial(own_kernel, odd, first, first - origin, first),
        "own",
        array(rows, width),
        [SMEM] + [VMEM] * 5 + [ANY] * len(after),
        VMEM,
        [table_scratch(lines, width, total)],
        weight=weight,
    )(start, lines, behind, product, queries, residual, *after)


def pick_kernel(raw_ref, received_ref, _, queries_ref, product_ref, lines_ref):
    rows = queries_ref.shape[0]

    def take(source):
        queries_ref[...] = source[:rows, :]
        product_ref[...] = source[rows : 2 * rows, :]
        for part in range(RAW // LANES):
            taken = source[2 * rows :, part * LANES : (part + 1) * LANES]
            lines_ref[part * LINES : (part + 1) * LINES, :] = taken.astype(F32)

    pl.when(is_first())(lambda: take(raw_ref))
    pl.when(jnp.logical_not(is_first()))(lambda: take(received_ref))


def pick_of(raw, received, taps, after):
    rows, width = (raw.shape[0] - LINES) // 2, raw.shape[1]
    return call(
        pick_kernel,
        "pick",
        (array(rows, width), array(rows, width), array(RAW // LANES * LINES, taps, F32)),
        [VMEM, VMEM, ANY],
        (VMEM,) * 3,
        weight=SLOW,
    )(raw, received, after)


def hold_kernel(value_ref, _, out_ref):
    pass


def held_back(value, after, weight=QUICK):
    return call(
        hold_kernel, "hold", array(*value.shape), [ANY, ANY], ANY, weight=weight, aliases={0: 0}
    )(value, after)


def send_out(pieces, out_ref, sems):
    copies = [
        pltpu.make_async_copy(buffer, out_ref.at[0, :, pl.ds(first, buffer.shape[1])], sems.at[place])
        for place, (buffer, first) in enumerate(pieces)
    ]
    for copy in copies:
        copy.start()
    return copies


def wait_all(copies):
    for copy in copies:
        copy.wait()


def later_kernel(places, *refs):
    start_ref, lines_ref, behind_ref, product_ref, queries_ref = refs[:5]
    own_refs = refs[5 : 5 + len(places)]
    out_ref, gated_ref, table_ref, sems = refs[-4:]
    total = queries_ref.shape[2]
    share = share_of(lines_ref, total)

    for odd in (0, 1):

        @pl.when(jnp.logical_and(is_first(), is_slab(odd)))
        def _():
            pieces = [(own_ref, first) for own_ref, (side, first, _) in zip(own_refs, places) if side == odd]
            wait_all(send_out(pieces, out_ref, sems))

    @pl.when(jnp.logical_not(is_first()))
    def _():
        def store(at, span, mixed):
            gated_ref[span, at] = queries_ref[0, span, at].astype(F32) * mixed

        mix_all(total, share, lines_ref, 0, table_ref, start_ref, behind_ref, product_ref, (0, 0), store)


def later_of(start, lines, behind, product, queries, own, places):
    rows, total = product.shape
    return call(
        functools.partial(later_kernel, places),
        "later",
        (jax.ShapeDtypeStruct((1, rows, total), BF16), array(rows, total, F32)),
        [SMEM] + [VMEM] * (4 + len(own)),
        (ANY, VMEM),
        [table_scratch(lines, total, total), pltpu.SemaphoreType.DMA((len(own),))],
        weight=SLOW,
    )(start, lines, behind, product, queries, *own)


def raw_kernel(*refs):
    start_ref, lines_ref, behind_ref, chip_ref, far_ref, product_ref, queries_ref, gated_ref, residual_ref = refs[:9]
    out_ref, chosen_ref, table_ref, buffer, sems = refs[10:]
    width = buffer.shape[1]
    share = share_of(lines_ref, width)
    far = far_ref.shape[1]
    sources = (
        (jnp.logical_and(is_first(), is_slab(0)), far_ref, slice(far - width, far)),
        (jnp.logical_and(is_first(), is_slab(1)), chip_ref, slice(0, width)),
        (jnp.logical_not(is_first()), behind_ref, slice(0, width)),
    )
    for wanted, source, cols in sources:

        @pl.when(wanted)
        def _():
            chosen_ref[...] = source[:, cols]

    def store(at, span, mixed):
        gated = queries_ref[span, at].astype(F32) * mixed
        buffer[span, at] = (residual_ref[span, at].astype(F32) + gated).astype(BF16)

    mix_all(width, share, lines_ref, 0, table_ref, start_ref, chosen_ref, product_ref, (0, 0), store)

    @pl.when(jnp.logical_not(is_first()))
    def _():
        buffer[...] = (buffer[...].astype(F32) + gated_ref[:, :width]).astype(BF16)

    wait_all(send_out([(buffer, 0)], out_ref, sems))


def raw_finish(held, start, lines, behind, chip_behind, far_behind, product, queries, gated, residual):
    rows, width = product.shape
    return call(
        raw_kernel,
        "raw",
        jax.ShapeDtypeStruct(held.shape, BF16),
        [SMEM] + [VMEM] * 8 + [ANY],
        ANY,
        [
            pltpu.VMEM((rows, width), BF16),
            table_scratch(lines, width, width),
            pltpu.VMEM((rows, width), BF16),
            pltpu.SemaphoreType.DMA((1,)),
        ],
        weight=SLOW,
        aliases={9: 0},
    )(start, lines, behind, chip_behind, far_behind, product, queries, gated, residual, held)


def finish_kernel(odd, places, *refs):
    gated_ref, received_refs = refs[0], refs[1 : 1 + len(places)]
    out_ref, *buffers, sems = refs[2 + len(places) :]

    @pl.when(jnp.logical_and(jnp.logical_not(is_first()), is_slab(odd)))
    def _():
        copies = []
        for place, (_, first, width) in enumerate(places):
            buffer = buffers[place]
            total = received_refs[place][...].astype(F32) + gated_ref[:, first : first + width]
            buffer[...] = total.astype(BF16)
            copies += send_out([(buffer, first)], out_ref, sems.at[pl.ds(place, 1)])
        wait_all(copies)


def finish(held, gated, received, places):
    rows = gated.shape[0]
    count = len(places)
    return call(
        functools.partial(finish_kernel, places[0][0], places),
        "finish",
        jax.ShapeDtypeStruct(held.shape, BF16),
        [VMEM] * (1 + count) + [ANY],
        ANY,
        [pltpu.VMEM((rows, width), BF16) for _, _, width in places] + [pltpu.SemaphoreType.DMA((count,))],
        weight=SLOW,
        aliases={1 + count: 0},
    )(gated, *received, held)


def body(queries, keys, values, residual, filter_bank, filter_scales, group_filter, context_start):
    total = queries.shape[2]
    small = (filter_bank, filter_scales, group_filter)
    far_small = [pltpu.with_memory_space_constraint(value, pltpu.HBM) for value in small]
    far_queries, keys, values = (
        pltpu.with_memory_space_constraint(value, pltpu.HBM) for value in (queries, keys, values)
    )
    raw, whole, lines = lead_of(*far_small, far_queries, keys, values)
    raw_received = to_next_section(raw)
    chip_behind = to_next_slab(whole, (0,), (0,))
    product, lines, near, far = product_of(keys, values, *small, lines, whole)
    own, received, places = [], [], []

    def send(odd, behind, origin, first, width, weight, *after):
        piece = own_of(
            odd, origin, context_start, lines, behind, whole, queries, residual, first, width, weight, *after
        )
        own.append(piece)
        received.append(to_next_section(piece, (odd,)))
        places.append((odd, first, width))
        return first + width, piece

    first, after = send(1, chip_behind, 0, RAW, ODD[0], QUICK, lines)
    near = held_back(near, after)
    near_behind = to_next_slab(near, (0,), (1,))
    first, after = send(1, chip_behind, 0, first, ODD[1], QUICK, near)
    product = held_back(product, after)
    behind = to_next_slab(product, (1,))
    raw_queries, raw_product, raw_lines = pick_of(raw, raw_received, lines.shape[1], product)
    far_behind = to_next_slab(held_back(far, raw_queries), (0,), (1,))
    raw_queries = held_back(raw_queries, received[0], SLOW)
    first, after = send(0, near_behind, RAW, RAW, EVEN[0], SLOW, raw_queries)
    raw_product = held_back(raw_product, after)
    raw_behind = to_next_slab(raw_product, (1,))
    after = raw_product
    for width, passed in zip(EVEN[1:], (received[1], after, behind)):
        origin = RAW if first < RAW + NEAR else RAW + NEAR
        source = near_behind if first < RAW + NEAR else far_behind
        first, after = send(0, source, origin, first, width, SLOW, after, passed)
    held, gated = later_of(context_start, lines, behind, product, queries, own, places)
    odd = len(ODD)
    held = finish(held, gated, received[:odd], places[:odd])
    held = raw_finish(
        held,
        context_start,
        raw_lines,
        raw_behind,
        chip_behind,
        far_behind,
        raw_product,
        raw_queries,
        gated,
        residual,
    )
    for last in (odd + 2, odd + 3, odd + 4):
        begin = odd if last == odd + 2 else last - 1
        held = finish(held, gated, received[begin:last], places[begin:last])
    return held


def solution(mesh):
    return jax.shard_map(
        body,
        mesh=mesh,
        in_specs=(
            P("pipe", ("dp", "ctx"), None),
            P("pipe", ("dp", "ctx"), None),
            P("pipe", ("dp", "ctx"), None),
            P(("dp", "ctx"), None),
            P("pipe", None, None),
            P("pipe", None),
            P("pipe", None),
            P("dp"),
        ),
        out_specs=P("pipe", ("dp", "ctx"), None),
        check_vma=False,
    )
```

```python
import functools

import jax
import jax.numpy as jnp
from jax import lax
from jax.experimental import pallas as pl
from jax.experimental.pallas import tpu as pltpu
from jax.sharding import PartitionSpec as P

LANES = 128
ROW_BLOCK = 32
RAW = 384
ODD = (1536, 2176)
EVEN = (1024, 1024, 768, 896)
PIECES = 4
NEAR = 2048
LINES = 8
F32 = jnp.float32
BF16 = jnp.bfloat16
MIB = 1024 * 1024
QUICK, SLOW = 1024, 20_000_000_000

SMEM = pl.BlockSpec(memory_space=pltpu.SMEM)
VMEM = pl.BlockSpec(memory_space=pltpu.VMEM)
ANY = pl.BlockSpec(memory_space=pl.ANY)
HBM = pl.BlockSpec(memory_space=pltpu.HBM)


def to_next_slab(value, *links):
    slabs, depth = lax.axis_size("ctx"), lax.axis_size("pipe")
    pairs = [
        (slab * depth + pipe, (slab + 1) * depth + pipe)
        for odd, pipe in links
        for slab in range(slabs - 1)
        if slab % 2 == odd
    ]
    return lax.ppermute(value, ("ctx", "pipe"), pairs)


def to_next_section(value, slabs=(0, 1)):
    depth = lax.axis_size("pipe")
    pairs = [(slab * depth, slab * depth + 1) for slab in range(lax.axis_size("ctx")) if slab % 2 in slabs]
    return lax.ppermute(value, ("ctx", "pipe"), pairs)


def call(kernel, name, out_shape, in_specs, out_specs, scratch=(), weight=QUICK, aliases=None):
    return pl.pallas_call(
        kernel,
        out_shape=out_shape,
        in_specs=in_specs,
        out_specs=out_specs,
        scratch_shapes=list(scratch),
        input_output_aliases=aliases or {},
        compiler_params=pltpu.CompilerParams(vmem_limit_bytes=16 * MIB),
        cost_estimate=pl.CostEstimate(flops=weight, bytes_accessed=1024, transcendentals=0),
        name=name,
    )


def is_first():
    return lax.axis_index("pipe") == 0


def is_slab(odd):
    return lax.axis_index("ctx") % 2 == odd


def array(rows, cols, kind=BF16):
    return jax.ShapeDtypeStruct((rows, cols), kind)


def multiply(keys_ref, values_ref, keys_in, values_in, sems, out_refs, meanwhile):
    rows = out_refs[0].shape[0]
    step = rows // PIECES
    spans = [pl.ds(piece * step, step) for piece in range(PIECES)]
    copies = []
    for piece, span in enumerate(spans):
        copies.append(
            (
                pltpu.make_async_copy(keys_ref.at[0, span], keys_in.at[span], sems.at[2 * piece]),
                pltpu.make_async_copy(values_ref.at[0, span], values_in.at[span], sems.at[2 * piece + 1]),
            )
        )
        for copy in copies[-1]:
            copy.start()
    meanwhile()
    for span, pair in zip(spans, copies):
        for copy in pair:
            copy.wait()
        first = 0
        for out_ref in out_refs:
            for tile in range(0, out_ref.shape[1], 4 * LANES):
                at = slice(first + tile, first + tile + 4 * LANES)
                product = keys_in[span, at].astype(F32) * values_in[span, at].astype(F32)
                out_ref[span, tile : tile + 4 * LANES] = product.astype(BF16)
            first += out_ref.shape[1]


def fill_lines(bank, scales_ref, assign_ref, lines_ref):
    groups, taps = lines_ref.shape
    size = bank.shape[0]
    chosen = (lax.broadcasted_iota(jnp.int32, (size, groups), 0) == assign_ref[...]).astype(F32).astype(BF16)
    contract = (((0,), (0,)), ((), ()))
    picked = lax.dot_general(bank, chosen, contract, preferred_element_type=F32)
    scaled = (picked * scales_ref[...]).astype(BF16)
    order = lax.broadcasted_iota(jnp.int32, (taps, taps), 0) + lax.broadcasted_iota(jnp.int32, (taps, taps), 1)
    flip = (order == taps - 1).astype(F32).astype(BF16)
    lines_ref[...] = lax.dot_general(scaled, flip, contract, preferred_element_type=F32)


def lead_kernel(*refs):
    bank_ref, scales_ref, assign_ref, queries_ref, keys_ref, values_ref = refs[:6]
    raw_ref, whole_ref, lines_ref = refs[6:9]
    bank_in, scales_in, assign_in, keys_in, values_in, sems, own_sems = refs[9:]
    rows = whole_ref.shape[0]

    @pl.when(is_first())
    def _():
        copies = [
            pltpu.make_async_copy(bank_ref, bank_in, own_sems.at[0]),
            pltpu.make_async_copy(scales_ref, scales_in, own_sems.at[1]),
            pltpu.make_async_copy(assign_ref, assign_in, own_sems.at[2]),
            pltpu.make_async_copy(queries_ref.at[0, :, pl.ds(0, RAW)], raw_ref.at[pl.ds(0, rows)], own_sems.at[3]),
        ]
        for copy in copies:
            copy.start()

        def taps():
            for copy in copies[:3]:
                copy.wait()
            fill_lines(bank_in[0], scales_in, assign_in, lines_ref)
            for part in range(RAW // LANES):
                taken = lines_ref[part * LINES : (part + 1) * LINES, :].astype(BF16)
                raw_ref[2 * rows :, part * LANES : (part + 1) * LANES] = taken

        multiply(keys_ref, values_ref, keys_in, values_in, sems, [whole_ref], taps)
        raw_ref[rows : 2 * rows, :] = whole_ref[:, :RAW]
        copies[3].wait()


def product_scratch(rows, total):
    return [pltpu.VMEM((rows, total), BF16), pltpu.VMEM((rows, total), BF16), pltpu.SemaphoreType.DMA((2 * PIECES,))]


def lead_of(bank, scales, assign, queries, keys, values):
    rows, total = queries.shape[1:]
    return call(
        lead_kernel,
        "lead",
        (
            array(2 * rows + LINES, RAW),
            array(rows, total),
            array(assign.shape[1], bank.shape[2], F32),
        ),
        [HBM] * 6,
        (VMEM,) * 3,
        [pltpu.VMEM(bank.shape, BF16), pltpu.VMEM(scales.shape, F32), pltpu.VMEM(assign.shape, jnp.int32)]
        + product_scratch(rows, total)
        + [pltpu.SemaphoreType.DMA((4,))],
    )(bank, scales, assign, queries, keys, values)


def turn_table(lines_ref, row, count, table_ref, at):
    taps = lines_ref.shape[1]
    upper = lax.broadcasted_iota(jnp.int32, (ROW_BLOCK, taps), 1) > lax.broadcasted_iota(
        jnp.int32, (ROW_BLOCK, taps), 0
    )
    for group in range(count):
        line = lines_ref[row + group : row + group + 1, :]
        turned = pltpu.roll(jnp.broadcast_to(line, (ROW_BLOCK, taps)), 1, 1, stride=1, stride_axis=0)
        span = slice(at + group * ROW_BLOCK, at + (group + 1) * ROW_BLOCK)
        table_ref[span, :taps] = jnp.where(upper, turned, 0.0).astype(BF16)
        table_ref[span, taps:] = jnp.where(upper, 0.0, turned)[:, :ROW_BLOCK].astype(BF16)


def product_kernel(*refs):
    keys_ref, values_ref, bank_ref, scales_ref, assign_ref, _, whole_ref = refs[:7]
    lines_ref, near_ref, far_ref, keys_in, values_in, sems = refs[7:]
    near = near_ref.shape[1]

    @pl.when(jnp.logical_and(is_first(), is_slab(1)))
    def _():
        near_ref[...] = whole_ref[:, RAW : RAW + near]
        far_ref[:, : far_ref.shape[1] - RAW] = whole_ref[:, RAW + near :]
        far_ref[:, far_ref.shape[1] - RAW :] = whole_ref[:, :RAW]

    @pl.when(jnp.logical_not(is_first()))
    def _():
        multiply(
            keys_ref,
            values_ref,
            keys_in,
            values_in,
            sems,
            [near_ref, far_ref],
            lambda: fill_lines(bank_ref[0], scales_ref, assign_ref, lines_ref),
        )


def product_of(keys, values, bank, scales, assign, lines, whole):
    rows, total = keys.shape[1:]
    return call(
        product_kernel,
        "product",
        (array(*lines.shape, F32), array(rows, NEAR), array(rows, total - NEAR)),
        [HBM, HBM] + [VMEM] * 5,
        (VMEM,) * 3,
        product_scratch(rows, total),
        aliases={5: 0},
    )(keys, values, bank, scales, assign, lines, whole)


def mix(table_ref, row, share, window, store):
    depth = table_ref.shape[1]
    rows = window.shape[0] - depth + ROW_BLOCK
    member = lax.broadcasted_iota(jnp.int32, (ROW_BLOCK, LANES), 1) // (LANES // share)
    table = table_ref[row : row + share * ROW_BLOCK, :]
    for first in range(0, rows, 2 * ROW_BLOCK):
        starts = (first, first + ROW_BLOCK)
        pair = jnp.concatenate([window[begin : begin + depth] for begin in starts], axis=1)
        sums = jnp.dot(table, pair, preferred_element_type=F32)
        for place, begin in enumerate(starts):
            part = sums[:, place * LANES : (place + 1) * LANES]
            mixed = part[:ROW_BLOCK]
            for group in range(1, share):
                mixed = jnp.where(member == group, part[group * ROW_BLOCK : (group + 1) * ROW_BLOCK], mixed)
            store(slice(begin, begin + ROW_BLOCK), mixed)


def mix_all(width, share, lines_ref, line, table_ref, start_ref, behind_ref, product_ref, local, store):
    rows = product_ref.shape[0]
    first = (lax.axis_index("ctx") - 1) * rows
    inside = first + lax.broadcasted_iota(jnp.int32, (2 * rows, LANES), 0) >= start_ref[0]
    for tile in range(width // LANES):
        at = slice(tile * LANES, (tile + 1) * LANES)
        near, inner = (slice(begin + at.start, begin + at.stop) for begin in local)
        row = tile * share * ROW_BLOCK
        turn_table(lines_ref, line + tile * share, share, table_ref, row)
        window = jnp.concatenate([behind_ref[:, near], product_ref[:, inner]], axis=0)
        window = jnp.where(inside, window, jnp.zeros_like(window))
        mix(table_ref, row, share, window, functools.partial(store, at))


def share_of(lines_ref, total):
    return LANES * lines_ref.shape[0] // total


def own_kernel(odd, first, shift, local, *refs):
    start_ref, lines_ref, behind_ref, product_ref, queries_ref, residual_ref = refs[:6]
    out_ref, table_ref = refs[-2:]
    width = out_ref.shape[1]
    share = share_of(lines_ref, residual_ref.shape[1])

    @pl.when(jnp.logical_and(is_first(), is_slab(odd)))
    def _():
        def store(at, span, mixed):
            cols = slice(first + at.start, first + at.stop)
            gated = queries_ref[0, span, cols].astype(F32) * mixed
            out_ref[span, at] = (residual_ref[span, cols].astype(F32) + gated).astype(BF16)

        line = first // LANES * share
        at = (shift, local)
        mix_all(width, share, lines_ref, line, table_ref, start_ref, behind_ref, product_ref, at, store)


def table_scratch(lines, width, total):
    groups, taps = lines.shape
    return pltpu.VMEM((width * groups // total * ROW_BLOCK, taps + ROW_BLOCK), BF16)


def own_of(odd, origin, start, lines, behind, product, queries, residual, first, width, weight, *after):
    rows, total = residual.shape
    return call(
        functools.partial(own_kernel, odd, first, first - origin, first),
        "own",
        array(rows, width),
        [SMEM] + [VMEM] * 5 + [ANY] * len(after),
        VMEM,
        [table_scratch(lines, width, total)],
        weight=weight,
    )(start, lines, behind, product, queries, residual, *after)


def pick_kernel(raw_ref, received_ref, _, queries_ref, product_ref, lines_ref):
    rows = queries_ref.shape[0]

    def take(source):
        queries_ref[...] = source[:rows, :]
        product_ref[...] = source[rows : 2 * rows, :]
        for part in range(RAW // LANES):
            taken = source[2 * rows :, part * LANES : (part + 1) * LANES]
            lines_ref[part * LINES : (part + 1) * LINES, :] = taken.astype(F32)

    pl.when(is_first())(lambda: take(raw_ref))
    pl.when(jnp.logical_not(is_first()))(lambda: take(received_ref))


def pick_of(raw, received, taps, after):
    rows, width = (raw.shape[0] - LINES) // 2, raw.shape[1]
    return call(
        pick_kernel,
        "pick",
        (array(rows, width), array(rows, width), array(RAW // LANES * LINES, taps, F32)),
        [VMEM, VMEM, ANY],
        (VMEM,) * 3,
        weight=SLOW,
    )(raw, received, after)


def hold_kernel(value_ref, _, out_ref):
    pass


def held_back(value, after, weight=QUICK):
    return call(
        hold_kernel, "hold", array(*value.shape), [ANY, ANY], ANY, weight=weight, aliases={0: 0}
    )(value, after)


def send_out(pieces, out_ref, sems):
    copies = [
        pltpu.make_async_copy(buffer, out_ref.at[0, :, pl.ds(first, buffer.shape[1])], sems.at[place])
        for place, (buffer, first) in enumerate(pieces)
    ]
    for copy in copies:
        copy.start()
    return copies


def wait_all(copies):
    for copy in copies:
        copy.wait()


def later_kernel(places, *refs):
    start_ref, lines_ref, near_behind, near_ref, far_behind, far_ref, queries_ref = refs[:7]
    own_refs = refs[7 : 7 + len(places)]
    out_ref, gated_ref, table_ref, sems = refs[-4:]
    total = queries_ref.shape[2]
    share = share_of(lines_ref, total)

    for odd in (0, 1):

        @pl.when(jnp.logical_and(is_first(), is_slab(odd)))
        def _():
            pieces = [(own_ref, first) for own_ref, (side, first, _) in zip(own_refs, places) if side == odd]
            wait_all(send_out(pieces, out_ref, sems))

    @pl.when(jnp.logical_not(is_first()))
    def _():
        for first, behind_ref, product_ref in ((0, near_behind, near_ref), (NEAR, far_behind, far_ref)):

            def store(at, span, mixed):
                cols = slice(first + at.start, first + at.stop)
                gated_ref[span, cols] = queries_ref[0, span, cols].astype(F32) * mixed

            width, line = product_ref.shape[1], first // LANES * share
            mix_all(width, share, lines_ref, line, table_ref, start_ref, behind_ref, product_ref, (0, 0), store)


def later_of(start, lines, near_behind, near, far_behind, far, queries, own, places):
    rows, total = queries.shape[1:]
    return call(
        functools.partial(later_kernel, places),
        "later",
        (jax.ShapeDtypeStruct((1, rows, total), BF16), array(rows, total, F32)),
        [SMEM] + [VMEM] * (6 + len(own)),
        (ANY, VMEM),
        [table_scratch(lines, NEAR, total), pltpu.SemaphoreType.DMA((len(own),))],
        weight=SLOW,
    )(start, lines, near_behind, near, far_behind, far, queries, *own)


def raw_kernel(*refs):
    start_ref, lines_ref, behind_ref, chip_ref, far_ref, product_ref, queries_ref, gated_ref, residual_ref = refs[:9]
    out_ref, chosen_ref, table_ref, buffer, sems = refs[10:]
    width = buffer.shape[1]
    share = share_of(lines_ref, width)
    far = far_ref.shape[1]
    sources = (
        (jnp.logical_and(is_first(), is_slab(0)), far_ref, slice(far - width, far)),
        (jnp.logical_and(is_first(), is_slab(1)), chip_ref, slice(0, width)),
        (jnp.logical_not(is_first()), behind_ref, slice(0, width)),
    )
    for wanted, source, cols in sources:

        @pl.when(wanted)
        def _():
            chosen_ref[...] = source[:, cols]

    def store(at, span, mixed):
        gated = queries_ref[span, at].astype(F32) * mixed
        buffer[span, at] = (residual_ref[span, at].astype(F32) + gated).astype(BF16)

    mix_all(width, share, lines_ref, 0, table_ref, start_ref, chosen_ref, product_ref, (0, 0), store)

    @pl.when(jnp.logical_not(is_first()))
    def _():
        buffer[...] = (buffer[...].astype(F32) + gated_ref[:, :width]).astype(BF16)

    wait_all(send_out([(buffer, 0)], out_ref, sems))


def raw_finish(held, start, lines, behind, chip_behind, far_behind, product, queries, gated, residual):
    rows, width = product.shape
    return call(
        raw_kernel,
        "raw",
        jax.ShapeDtypeStruct(held.shape, BF16),
        [SMEM] + [VMEM] * 8 + [ANY],
        ANY,
        [
            pltpu.VMEM((rows, width), BF16),
            table_scratch(lines, width, width),
            pltpu.VMEM((rows, width), BF16),
            pltpu.SemaphoreType.DMA((1,)),
        ],
        weight=SLOW,
        aliases={9: 0},
    )(start, lines, behind, chip_behind, far_behind, product, queries, gated, residual, held)


def finish_kernel(odd, places, *refs):
    gated_ref, received_refs = refs[0], refs[1 : 1 + len(places)]
    out_ref, *buffers, sems = refs[2 + len(places) :]

    @pl.when(jnp.logical_and(jnp.logical_not(is_first()), is_slab(odd)))
    def _():
        copies = []
        for place, (_, first, width) in enumerate(places):
            buffer = buffers[place]
            total = received_refs[place][...].astype(F32) + gated_ref[:, first : first + width]
            buffer[...] = total.astype(BF16)
            copies += send_out([(buffer, first)], out_ref, sems.at[pl.ds(place, 1)])
        wait_all(copies)


def finish(held, gated, received, places):
    rows = gated.shape[0]
    count = len(places)
    return call(
        functools.partial(finish_kernel, places[0][0], places),
        "finish",
        jax.ShapeDtypeStruct(held.shape, BF16),
        [VMEM] * (1 + count) + [ANY],
        ANY,
        [pltpu.VMEM((rows, width), BF16) for _, _, width in places] + [pltpu.SemaphoreType.DMA((count,))],
        weight=SLOW,
        aliases={1 + count: 0},
    )(gated, *received, held)


def body(queries, keys, values, residual, filter_bank, filter_scales, group_filter, context_start):
    total = queries.shape[2]
    small = (filter_bank, filter_scales, group_filter)
    far_small = [pltpu.with_memory_space_constraint(value, pltpu.HBM) for value in small]
    far_queries, keys, values = (
        pltpu.with_memory_space_constraint(value, pltpu.HBM) for value in (queries, keys, values)
    )
    raw, whole, lines = lead_of(*far_small, far_queries, keys, values)
    raw_received = to_next_section(raw)
    chip_behind = to_next_slab(whole, (0, 0))
    lines, near, far = product_of(keys, values, *small, lines, whole)
    own, received, places = [], [], []

    def send(odd, behind, origin, first, width, weight, *after):
        piece = own_of(
            odd, origin, context_start, lines, behind, whole, queries, residual, first, width, weight, *after
        )
        own.append(piece)
        received.append(to_next_section(piece, (odd,)))
        places.append((odd, first, width))
        return first + width, piece

    first, after = send(1, chip_behind, 0, RAW, ODD[0], QUICK, lines)
    near = held_back(near, after)
    near_behind = to_next_slab(near, (1, 0), (0, 1), (1, 1))
    first, after = send(1, chip_behind, 0, first, ODD[1], QUICK, near)
    raw_queries, raw_product, raw_lines = pick_of(raw, raw_received, lines.shape[1], after)
    far = held_back(far, raw_queries)
    far_behind = to_next_slab(far, (1, 0), (0, 1), (1, 1))
    raw_queries = held_back(raw_queries, received[0], SLOW)
    first, after = send(0, near_behind, RAW, RAW, EVEN[0], SLOW, raw_queries)
    raw_product = held_back(raw_product, after)
    raw_behind = to_next_slab(raw_product, (0, 1), (1, 1))
    after = raw_product
    for width, passed in zip(EVEN[1:], (after, received[1], after)):
        origin = RAW if first < RAW + NEAR else RAW + NEAR
        source = near_behind if first < RAW + NEAR else far_behind
        first, after = send(0, source, origin, first, width, SLOW, after, passed)
    held, gated = later_of(
        context_start, lines, near_behind, near, far_behind, far, queries, own, places
    )
    odd = len(ODD)
    held = finish(held, gated, received[:odd], places[:odd])
    held = raw_finish(
        held,
        context_start,
        raw_lines,
        raw_behind,
        chip_behind,
        far_behind,
        raw_product,
        raw_queries,
        gated,
        residual,
    )
    for last in (odd + 2, odd + 3, odd + 4):
        begin = odd if last == odd + 2 else last - 1
        held = finish(held, gated, received[begin:last], places[begin:last])
    return held


def solution(mesh):
    return jax.shard_map(
        body,
        mesh=mesh,
        in_specs=(
            P("pipe", ("dp", "ctx"), None),
            P("pipe", ("dp", "ctx"), None),
            P("pipe", ("dp", "ctx"), None),
            P(("dp", "ctx"), None),
            P("pipe", None, None),
            P("pipe", None),
            P("pipe", None),
            P("dp"),
        ),
        out_specs=P("pipe", ("dp", "ctx"), None),
        check_vma=False,
    )
```

```python
import functools

import jax
import jax.numpy as jnp
from jax import lax
from jax.experimental import pallas as pl
from jax.experimental.pallas import tpu as pltpu
from jax.sharding import PartitionSpec as P

LANES = 128
ROW_BLOCK = 32
RAW = 384
ODD = (1536, 2176)
EVEN = (1024, 1024, 768, 896)
PIECES = 4
NEAR = 2048
LINES = 8
F32 = jnp.float32
BF16 = jnp.bfloat16
MIB = 1024 * 1024
QUICK, SLOW = 1024, 20_000_000_000

SMEM = pl.BlockSpec(memory_space=pltpu.SMEM)
VMEM = pl.BlockSpec(memory_space=pltpu.VMEM)
ANY = pl.BlockSpec(memory_space=pl.ANY)
HBM = pl.BlockSpec(memory_space=pltpu.HBM)


def to_next_slab(value, *links):
    slabs, depth = lax.axis_size("ctx"), lax.axis_size("pipe")
    pairs = [
        (slab * depth + pipe, (slab + 1) * depth + pipe)
        for odd, pipe in links
        for slab in range(slabs - 1)
        if slab % 2 == odd
    ]
    return lax.ppermute(value, ("ctx", "pipe"), pairs)


def to_next_section(value, slabs=(0, 1)):
    depth = lax.axis_size("pipe")
    pairs = [(slab * depth, slab * depth + 1) for slab in range(lax.axis_size("ctx")) if slab % 2 in slabs]
    return lax.ppermute(value, ("ctx", "pipe"), pairs)


def call(kernel, name, out_shape, in_specs, out_specs, scratch=(), weight=QUICK, aliases=None):
    return pl.pallas_call(
        kernel,
        out_shape=out_shape,
        in_specs=in_specs,
        out_specs=out_specs,
        scratch_shapes=list(scratch),
        input_output_aliases=aliases or {},
        compiler_params=pltpu.CompilerParams(vmem_limit_bytes=16 * MIB),
        cost_estimate=pl.CostEstimate(flops=weight, bytes_accessed=1024, transcendentals=0),
        name=name,
    )


def is_first():
    return lax.axis_index("pipe") == 0


def is_slab(odd):
    return lax.axis_index("ctx") % 2 == odd


def array(rows, cols, kind=BF16):
    return jax.ShapeDtypeStruct((rows, cols), kind)


def send_out(pieces, out_ref, sems):
    copies = [
        pltpu.make_async_copy(buffer, out_ref.at[0, :, pl.ds(first, buffer.shape[1])], sems.at[place])
        for place, (buffer, first) in enumerate(pieces)
    ]
    for copy in copies:
        copy.start()
    return copies


def wait_all(copies):
    for copy in copies:
        copy.wait()


def multiply(keys_ref, values_ref, keys_in, values_in, sems, out_refs, meanwhile):
    rows = out_refs[0].shape[0]
    step = rows // PIECES
    spans = [pl.ds(piece * step, step) for piece in range(PIECES)]
    copies = []
    for piece, span in enumerate(spans):
        copies.append(
            (
                pltpu.make_async_copy(keys_ref.at[0, span], keys_in.at[span], sems.at[2 * piece]),
                pltpu.make_async_copy(values_ref.at[0, span], values_in.at[span], sems.at[2 * piece + 1]),
            )
        )
        for copy in copies[-1]:
            copy.start()

    def piece_product(span):
        first = 0
        for out_ref in out_refs:
            for tile in range(0, out_ref.shape[1], 4 * LANES):
                at = slice(first + tile, first + tile + 4 * LANES)
                product = keys_in[span, at].astype(F32) * values_in[span, at].astype(F32)
                out_ref[span, tile : tile + 4 * LANES] = product.astype(BF16)
            first += out_ref.shape[1]

    beside = PIECES // 2
    for piece in range(beside):
        wait_all(copies[piece])
        piece_product(spans[piece])
    for pair in copies[beside:]:
        wait_all(pair)
    meanwhile()
    for span in spans[beside:]:
        piece_product(span)


def fill_lines(bank, scales_ref, assign_ref, lines_ref):
    groups, taps = lines_ref.shape
    size = bank.shape[0]
    chosen = (lax.broadcasted_iota(jnp.int32, (size, groups), 0) == assign_ref[...]).astype(F32).astype(BF16)
    contract = (((0,), (0,)), ((), ()))
    picked = lax.dot_general(bank, chosen, contract, preferred_element_type=F32)
    scaled = (picked * scales_ref[...]).astype(BF16)
    order = lax.broadcasted_iota(jnp.int32, (taps, taps), 0) + lax.broadcasted_iota(jnp.int32, (taps, taps), 1)
    flip = (order == taps - 1).astype(F32).astype(BF16)
    lines_ref[...] = lax.dot_general(scaled, flip, contract, preferred_element_type=F32)


def lead_kernel(*refs):
    bank_ref, scales_ref, assign_ref, queries_ref, keys_ref, values_ref = refs[:6]
    raw_ref, whole_ref, lines_ref = refs[6:9]
    bank_in, scales_in, assign_in, keys_in, values_in, sems, own_sems = refs[9:]
    rows = whole_ref.shape[0]

    @pl.when(is_first())
    def _():
        copies = [
            pltpu.make_async_copy(bank_ref, bank_in, own_sems.at[0]),
            pltpu.make_async_copy(scales_ref, scales_in, own_sems.at[1]),
            pltpu.make_async_copy(assign_ref, assign_in, own_sems.at[2]),
            pltpu.make_async_copy(queries_ref.at[0, :, pl.ds(0, RAW)], raw_ref.at[pl.ds(0, rows)], own_sems.at[3]),
        ]
        for copy in copies:
            copy.start()

        def taps():
            for copy in copies[:3]:
                copy.wait()
            fill_lines(bank_in[0], scales_in, assign_in, lines_ref)
            for part in range(RAW // LANES):
                taken = lines_ref[part * LINES : (part + 1) * LINES, :].astype(BF16)
                raw_ref[2 * rows :, part * LANES : (part + 1) * LANES] = taken

        multiply(keys_ref, values_ref, keys_in, values_in, sems, [whole_ref], taps)
        raw_ref[rows : 2 * rows, :] = whole_ref[:, :RAW]
        copies[3].wait()


def product_scratch(rows, total):
    return [pltpu.VMEM((rows, total), BF16), pltpu.VMEM((rows, total), BF16), pltpu.SemaphoreType.DMA((2 * PIECES,))]


def lead_of(bank, scales, assign, queries, keys, values):
    rows, total = queries.shape[1:]
    return call(
        lead_kernel,
        "lead",
        (
            array(2 * rows + LINES, RAW),
            array(rows, total),
            array(assign.shape[1], bank.shape[2], F32),
        ),
        [HBM] * 6,
        (VMEM,) * 3,
        [pltpu.VMEM(bank.shape, BF16), pltpu.VMEM(scales.shape, F32), pltpu.VMEM(assign.shape, jnp.int32)]
        + product_scratch(rows, total)
        + [pltpu.SemaphoreType.DMA((4,))],
    )(bank, scales, assign, queries, keys, values)


def turn_table(lines_ref, row, count, table_ref, at):
    taps = lines_ref.shape[1]
    upper = lax.broadcasted_iota(jnp.int32, (ROW_BLOCK, taps), 1) > lax.broadcasted_iota(
        jnp.int32, (ROW_BLOCK, taps), 0
    )
    for group in range(count):
        line = lines_ref[row + group : row + group + 1, :]
        turned = pltpu.roll(jnp.broadcast_to(line, (ROW_BLOCK, taps)), 1, 1, stride=1, stride_axis=0)
        span = slice(at + group * ROW_BLOCK, at + (group + 1) * ROW_BLOCK)
        table_ref[span, :taps] = jnp.where(upper, turned, 0.0).astype(BF16)
        table_ref[span, taps:] = jnp.where(upper, 0.0, turned)[:, :ROW_BLOCK].astype(BF16)


def product_kernel(*refs):
    keys_ref, values_ref, bank_ref, scales_ref, assign_ref, _, whole_ref = refs[:7]
    lines_ref, near_ref, far_ref, keys_in, values_in, sems = refs[7:]
    near = near_ref.shape[1]

    @pl.when(jnp.logical_and(is_first(), is_slab(1)))
    def _():
        near_ref[...] = whole_ref[:, RAW : RAW + near]
        far_ref[:, : far_ref.shape[1] - RAW] = whole_ref[:, RAW + near :]
        far_ref[:, far_ref.shape[1] - RAW :] = whole_ref[:, :RAW]

    @pl.when(jnp.logical_not(is_first()))
    def _():
        multiply(
            keys_ref,
            values_ref,
            keys_in,
            values_in,
            sems,
            [near_ref, far_ref],
            lambda: fill_lines(bank_ref[0], scales_ref, assign_ref, lines_ref),
        )


def product_of(keys, values, bank, scales, assign, lines, whole):
    rows, total = keys.shape[1:]
    return call(
        product_kernel,
        "product",
        (array(*lines.shape, F32), array(rows, NEAR), array(rows, total - NEAR)),
        [HBM, HBM] + [VMEM] * 5,
        (VMEM,) * 3,
        product_scratch(rows, total),
        aliases={5: 0},
    )(keys, values, bank, scales, assign, lines, whole)


def mix(table_ref, row, share, window, store):
    depth = table_ref.shape[1]
    rows = window.shape[0] - depth + ROW_BLOCK
    member = lax.broadcasted_iota(jnp.int32, (ROW_BLOCK, LANES), 1) // (LANES // share)
    table = table_ref[row : row + share * ROW_BLOCK, :]
    for first in range(0, rows, 2 * ROW_BLOCK):
        starts = (first, first + ROW_BLOCK)
        pair = jnp.concatenate([window[begin : begin + depth] for begin in starts], axis=1)
        sums = jnp.dot(table, pair, preferred_element_type=F32)
        for place, begin in enumerate(starts):
            part = sums[:, place * LANES : (place + 1) * LANES]
            mixed = part[:ROW_BLOCK]
            for group in range(1, share):
                mixed = jnp.where(member == group, part[group * ROW_BLOCK : (group + 1) * ROW_BLOCK], mixed)
            store(slice(begin, begin + ROW_BLOCK), mixed)


def mix_all(width, share, lines_ref, line, table_ref, start_ref, behind_ref, product_ref, local, store):
    rows = product_ref.shape[0]
    first = (lax.axis_index("ctx") - 1) * rows
    inside = first + lax.broadcasted_iota(jnp.int32, (2 * rows, LANES), 0) >= start_ref[0]
    for tile in range(width // LANES):
        at = slice(tile * LANES, (tile + 1) * LANES)
        near, inner = (slice(begin + at.start, begin + at.stop) for begin in local)
        row = tile * share * ROW_BLOCK
        turn_table(lines_ref, line + tile * share, share, table_ref, row)
        window = jnp.concatenate([behind_ref[:, near], product_ref[:, inner]], axis=0)
        window = jnp.where(inside, window, jnp.zeros_like(window))
        mix(table_ref, row, share, window, functools.partial(store, at))


def share_of(lines_ref, total):
    return LANES * lines_ref.shape[0] // total


def own_kernel(odd, first, shift, local, *refs):
    start_ref, lines_ref, behind_ref, product_ref, queries_ref, residual_ref = refs[:6]
    out_ref, table_ref = refs[-2:]
    width = out_ref.shape[1]
    share = share_of(lines_ref, residual_ref.shape[1])

    @pl.when(jnp.logical_and(is_first(), is_slab(odd)))
    def _():
        def store(at, span, mixed):
            cols = slice(first + at.start, first + at.stop)
            gated = queries_ref[0, span, cols].astype(F32) * mixed
            out_ref[span, at] = (residual_ref[span, cols].astype(F32) + gated).astype(BF16)

        line = first // LANES * share
        at = (shift, local)
        mix_all(width, share, lines_ref, line, table_ref, start_ref, behind_ref, product_ref, at, store)


def table_scratch(lines, width, total):
    groups, taps = lines.shape
    return pltpu.VMEM((width * groups // total * ROW_BLOCK, taps + ROW_BLOCK), BF16)


def own_of(odd, origin, start, lines, behind, product, queries, residual, first, width, weight, *after):
    rows, total = residual.shape
    return call(
        functools.partial(own_kernel, odd, first, first - origin, first),
        "own",
        array(rows, width),
        [SMEM] + [VMEM] * 5 + [ANY] * len(after),
        VMEM,
        [table_scratch(lines, width, total)],
        weight=weight,
    )(start, lines, behind, product, queries, residual, *after)


def pick_kernel(raw_ref, received_ref, _, queries_ref, product_ref, lines_ref):
    rows = queries_ref.shape[0]

    def take(source):
        queries_ref[...] = source[:rows, :]
        product_ref[...] = source[rows : 2 * rows, :]
        for part in range(RAW // LANES):
            taken = source[2 * rows :, part * LANES : (part + 1) * LANES]
            lines_ref[part * LINES : (part + 1) * LINES, :] = taken.astype(F32)

    pl.when(is_first())(lambda: take(raw_ref))
    pl.when(jnp.logical_not(is_first()))(lambda: take(received_ref))


def pick_of(raw, received, taps, after):
    rows, width = (raw.shape[0] - LINES) // 2, raw.shape[1]
    return call(
        pick_kernel,
        "pick",
        (array(rows, width), array(rows, width), array(RAW // LANES * LINES, taps, F32)),
        [VMEM, VMEM, ANY],
        (VMEM,) * 3,
        weight=SLOW,
    )(raw, received, after)


def hold_kernel(value_ref, _, out_ref):
    pass


def held_back(value, after, weight=QUICK):
    return call(
        hold_kernel, "hold", array(*value.shape), [ANY, ANY], ANY, weight=weight, aliases={0: 0}
    )(value, after)


def later_kernel(places, *refs):
    start_ref, lines_ref, near_behind, near_ref, far_behind, far_ref, queries_ref = refs[:7]
    own_refs = refs[7 : 7 + len(places)]
    out_ref, gated_ref, table_ref, sems = refs[-4:]
    total = queries_ref.shape[2]
    share = share_of(lines_ref, total)

    for odd in (0, 1):

        @pl.when(jnp.logical_and(is_first(), is_slab(odd)))
        def _():
            pieces = [(own_ref, first) for own_ref, (side, first, _) in zip(own_refs, places) if side == odd]
            wait_all(send_out(pieces, out_ref, sems))

    @pl.when(jnp.logical_not(is_first()))
    def _():
        for first, behind_ref, product_ref in ((0, near_behind, near_ref), (NEAR, far_behind, far_ref)):

            def store(at, span, mixed):
                cols = slice(first + at.start, first + at.stop)
                gated_ref[span, cols] = queries_ref[0, span, cols].astype(F32) * mixed

            width, line = product_ref.shape[1], first // LANES * share
            mix_all(width, share, lines_ref, line, table_ref, start_ref, behind_ref, product_ref, (0, 0), store)


def later_of(start, lines, near_behind, near, far_behind, far, queries, own, places):
    rows, total = queries.shape[1:]
    return call(
        functools.partial(later_kernel, places),
        "later",
        (jax.ShapeDtypeStruct((1, rows, total), BF16), array(rows, total, F32)),
        [SMEM] + [VMEM] * (6 + len(own)),
        (ANY, VMEM),
        [table_scratch(lines, NEAR, total), pltpu.SemaphoreType.DMA((len(own),))],
        weight=SLOW,
    )(start, lines, near_behind, near, far_behind, far, queries, *own)


def raw_kernel(*refs):
    start_ref, lines_ref, behind_ref, chip_ref, far_ref, product_ref, queries_ref, gated_ref, residual_ref = refs[:9]
    out_ref, chosen_ref, table_ref, buffer, sems = refs[10:]
    width = buffer.shape[1]
    share = share_of(lines_ref, width)
    far = far_ref.shape[1]
    sources = (
        (jnp.logical_and(is_first(), is_slab(0)), far_ref, slice(far - width, far)),
        (jnp.logical_and(is_first(), is_slab(1)), chip_ref, slice(0, width)),
        (jnp.logical_not(is_first()), behind_ref, slice(0, width)),
    )
    for wanted, source, cols in sources:

        @pl.when(wanted)
        def _():
            chosen_ref[...] = source[:, cols]

    def store(at, span, mixed):
        gated = queries_ref[span, at].astype(F32) * mixed
        buffer[span, at] = (residual_ref[span, at].astype(F32) + gated).astype(BF16)

    mix_all(width, share, lines_ref, 0, table_ref, start_ref, chosen_ref, product_ref, (0, 0), store)

    @pl.when(jnp.logical_not(is_first()))
    def _():
        buffer[...] = (buffer[...].astype(F32) + gated_ref[:, :width]).astype(BF16)

    wait_all(send_out([(buffer, 0)], out_ref, sems))


def raw_finish(held, start, lines, behind, chip_behind, far_behind, product, queries, gated, residual):
    rows, width = product.shape
    return call(
        raw_kernel,
        "raw",
        jax.ShapeDtypeStruct(held.shape, BF16),
        [SMEM] + [VMEM] * 8 + [ANY],
        ANY,
        [
            pltpu.VMEM((rows, width), BF16),
            table_scratch(lines, width, width),
            pltpu.VMEM((rows, width), BF16),
            pltpu.SemaphoreType.DMA((1,)),
        ],
        weight=SLOW,
        aliases={9: 0},
    )(start, lines, behind, chip_behind, far_behind, product, queries, gated, residual, held)


def finish_kernel(odd, places, *refs):
    gated_ref, received_refs = refs[0], refs[1 : 1 + len(places)]
    out_ref, *buffers, sems = refs[2 + len(places) :]

    @pl.when(jnp.logical_and(jnp.logical_not(is_first()), is_slab(odd)))
    def _():
        copies = []
        for place, (_, first, width) in enumerate(places):
            buffer = buffers[place]
            half = buffer.shape[0] // 2
            for part in range(2):
                span = slice(part * half, (part + 1) * half)
                total = received_refs[place][span, :].astype(F32) + gated_ref[span, first : first + width]
                buffer[span, :] = total.astype(BF16)
                target = out_ref.at[0, pl.ds(part * half, half), pl.ds(first, width)]
                sem = sems.at[2 * place + part]
                copies.append(pltpu.make_async_copy(buffer.at[pl.ds(part * half, half)], target, sem))
                copies[-1].start()
        wait_all(copies)


def finish(held, gated, received, places):
    rows = gated.shape[0]
    count = len(places)
    return call(
        functools.partial(finish_kernel, places[0][0], places),
        "finish",
        jax.ShapeDtypeStruct(held.shape, BF16),
        [VMEM] * (1 + count) + [ANY],
        ANY,
        [pltpu.VMEM((rows, width), BF16) for _, _, width in places] + [pltpu.SemaphoreType.DMA((2 * count,))],
        weight=SLOW,
        aliases={1 + count: 0},
    )(gated, *received, held)


def body(queries, keys, values, residual, filter_bank, filter_scales, group_filter, context_start):
    total = queries.shape[2]
    small = (filter_bank, filter_scales, group_filter)
    far_small = [pltpu.with_memory_space_constraint(value, pltpu.HBM) for value in small]
    far_queries, keys, values = (
        pltpu.with_memory_space_constraint(value, pltpu.HBM) for value in (queries, keys, values)
    )
    raw, whole, lines = lead_of(*far_small, far_queries, keys, values)
    raw_received = to_next_section(raw)
    chip_behind = to_next_slab(whole, (0, 0))
    lines, near, far = product_of(keys, values, *small, lines, whole)
    own, received, places = [], [], []

    def send(odd, behind, origin, first, width, weight, *after):
        piece = own_of(
            odd, origin, context_start, lines, behind, whole, queries, residual, first, width, weight, *after
        )
        own.append(piece)
        received.append(to_next_section(piece, (odd,)))
        places.append((odd, first, width))
        return first + width, piece

    first, after = send(1, chip_behind, 0, RAW, ODD[0], QUICK, lines)
    near = held_back(near, after)
    near_behind = to_next_slab(near, (1, 0), (0, 1), (1, 1))
    first, after = send(1, chip_behind, 0, first, ODD[1], QUICK, near)
    raw_queries, raw_product, raw_lines = pick_of(raw, raw_received, lines.shape[1], after)
    far = held_back(far, raw_queries)
    far_behind = to_next_slab(far, (1, 0), (0, 1), (1, 1))
    raw_queries = held_back(raw_queries, received[0], SLOW)
    first, after = send(0, near_behind, RAW, RAW, EVEN[0], SLOW, raw_queries)
    raw_product = held_back(raw_product, after)
    raw_behind = to_next_slab(raw_product, (0, 1), (1, 1))
    after = raw_product
    for width, passed in zip(EVEN[1:], (after, received[1], after)):
        origin = RAW if first < RAW + NEAR else RAW + NEAR
        source = near_behind if first < RAW + NEAR else far_behind
        first, after = send(0, source, origin, first, width, SLOW, after, passed)
    held, gated = later_of(
        context_start, lines, near_behind, near, far_behind, far, queries, own, places
    )
    odd = len(ODD)
    held = finish(held, gated, received[:odd], places[:odd])
    held = raw_finish(
        held,
        context_start,
        raw_lines,
        raw_behind,
        chip_behind,
        far_behind,
        raw_product,
        raw_queries,
        gated,
        residual,
    )
    for last in (odd + 2, odd + 3, odd + 4):
        begin = odd if last == odd + 2 else last - 1
        held = finish(held, gated, received[begin:last], places[begin:last])
    return held


def solution(mesh):
    return jax.shard_map(
        body,
        mesh=mesh,
        in_specs=(
            P("pipe", ("dp", "ctx"), None),
            P("pipe", ("dp", "ctx"), None),
            P("pipe", ("dp", "ctx"), None),
            P(("dp", "ctx"), None),
            P("pipe", None, None),
            P("pipe", None),
            P("pipe", None),
            P("dp"),
        ),
        out_specs=P("pipe", ("dp", "ctx"), None),
        check_vma=False,
    )
```

```python
import functools

import jax
import jax.numpy as jnp
from jax import lax
from jax.experimental import pallas as pl
from jax.experimental.pallas import tpu as pltpu
from jax.sharding import PartitionSpec as P

LANES = 128
ROW_BLOCK = 32
RAW = 384
ODD = (1536, 2176)
EVEN = (1024, 1024, 768, 896)
PIECES = 4
NEAR = 2048
LINES = 8
F32 = jnp.float32
BF16 = jnp.bfloat16
MIB = 1024 * 1024
QUICK, SLOW = 1024, 20_000_000_000

SMEM = pl.BlockSpec(memory_space=pltpu.SMEM)
VMEM = pl.BlockSpec(memory_space=pltpu.VMEM)
ANY = pl.BlockSpec(memory_space=pl.ANY)
HBM = pl.BlockSpec(memory_space=pltpu.HBM)


def to_next_slab(value, *links):
    slabs, depth = lax.axis_size("ctx"), lax.axis_size("pipe")
    pairs = [
        (slab * depth + pipe, (slab + 1) * depth + pipe)
        for odd, pipe in links
        for slab in range(slabs - 1)
        if slab % 2 == odd
    ]
    return lax.ppermute(value, ("ctx", "pipe"), pairs)


def to_next_section(value, slabs=(0, 1)):
    depth = lax.axis_size("pipe")
    pairs = [(slab * depth, slab * depth + 1) for slab in range(lax.axis_size("ctx")) if slab % 2 in slabs]
    return lax.ppermute(value, ("ctx", "pipe"), pairs)


def call(kernel, name, out_shape, in_specs, out_specs, scratch=(), weight=QUICK, aliases=None):
    return pl.pallas_call(
        kernel,
        out_shape=out_shape,
        in_specs=in_specs,
        out_specs=out_specs,
        scratch_shapes=list(scratch),
        input_output_aliases=aliases or {},
        compiler_params=pltpu.CompilerParams(vmem_limit_bytes=16 * MIB),
        cost_estimate=pl.CostEstimate(flops=weight, bytes_accessed=1024, transcendentals=0),
        name=name,
    )


def is_first():
    return lax.axis_index("pipe") == 0


def is_slab(odd):
    return lax.axis_index("ctx") % 2 == odd


def array(rows, cols, kind=BF16):
    return jax.ShapeDtypeStruct((rows, cols), kind)


def multiply(keys_ref, values_ref, keys_in, values_in, sems, out_refs, meanwhile):
    rows = out_refs[0].shape[0]
    step = rows // PIECES
    spans = [pl.ds(piece * step, step) for piece in range(PIECES)]
    copies = []
    for piece, span in enumerate(spans):
        copies.append(
            (
                pltpu.make_async_copy(keys_ref.at[0, span], keys_in.at[span], sems.at[2 * piece]),
                pltpu.make_async_copy(values_ref.at[0, span], values_in.at[span], sems.at[2 * piece + 1]),
            )
        )
        for copy in copies[-1]:
            copy.start()
    meanwhile()
    for span, pair in zip(spans, copies):
        for copy in pair:
            copy.wait()
        first = 0
        for out_ref in out_refs:
            for tile in range(0, out_ref.shape[1], 4 * LANES):
                at = slice(first + tile, first + tile + 4 * LANES)
                product = keys_in[span, at].astype(F32) * values_in[span, at].astype(F32)
                out_ref[span, tile : tile + 4 * LANES] = product.astype(BF16)
            first += out_ref.shape[1]


def fill_lines(bank, scales, assign, lines_ref):
    groups, taps = lines_ref.shape
    size = bank.shape[0]
    chosen = (lax.broadcasted_iota(jnp.int32, (size, groups), 0) == assign).astype(F32).astype(BF16)
    contract = (((0,), (0,)), ((), ()))
    picked = lax.dot_general(bank, chosen, contract, preferred_element_type=F32)
    scaled = (picked * scales).astype(BF16)
    order = lax.broadcasted_iota(jnp.int32, (taps, taps), 0) + lax.broadcasted_iota(jnp.int32, (taps, taps), 1)
    flip = (order == taps - 1).astype(F32).astype(BF16)
    lines_ref[...] = lax.dot_general(scaled, flip, contract, preferred_element_type=F32)


def lead_kernel(*refs):
    bank_ref, scales_ref, assign_ref, queries_ref, keys_ref, values_ref = refs[:6]
    raw_ref, whole_ref = refs[6:8]
    bank_in, scales_in, assign_in, lines_ref, keys_in, values_in, sems, own_sems = refs[8:]
    count = lines_ref.shape[0]
    rows = whole_ref.shape[0]

    @pl.when(is_first())
    def _():
        copies = [
            pltpu.make_async_copy(bank_ref, bank_in, own_sems.at[0]),
            pltpu.make_async_copy(scales_ref, scales_in, own_sems.at[1]),
            pltpu.make_async_copy(assign_ref, assign_in, own_sems.at[2]),
            pltpu.make_async_copy(queries_ref.at[0, :, pl.ds(0, RAW)], raw_ref.at[pl.ds(0, rows)], own_sems.at[3]),
        ]
        for copy in copies:
            copy.start()

        def taps():
            for copy in copies[:3]:
                copy.wait()
            fill_lines(bank_in[0], scales_in[:, :count], assign_in[:, :count], lines_ref)
            for part in range(RAW // LANES):
                taken = lines_ref[part * LINES : (part + 1) * LINES, :].astype(BF16)
                raw_ref[2 * rows :, part * LANES : (part + 1) * LANES] = taken

        multiply(keys_ref, values_ref, keys_in, values_in, sems, [whole_ref], taps)
        raw_ref[rows : 2 * rows, :] = whole_ref[:, :RAW]
        copies[3].wait()


def product_scratch(rows, total):
    return [pltpu.VMEM((rows, total), BF16), pltpu.VMEM((rows, total), BF16), pltpu.SemaphoreType.DMA((2 * PIECES,))]


def lead_of(bank, scales, assign, queries, keys, values):
    rows, total = queries.shape[1:]
    return call(
        lead_kernel,
        "lead",
        (
            array(2 * rows + LINES, RAW),
            array(rows, total),
        ),
        [HBM] * 6,
        (VMEM,) * 2,
        [
            pltpu.VMEM(bank.shape, BF16),
            pltpu.VMEM(scales.shape, F32),
            pltpu.VMEM(assign.shape, jnp.int32),
            pltpu.VMEM((min(LANES, assign.shape[1]), bank.shape[2]), F32),
        ]
        + product_scratch(rows, total)
        + [pltpu.SemaphoreType.DMA((4,))],
    )(bank, scales, assign, queries, keys, values)


def turn_table(lines_ref, row, count, table_ref, at):
    taps = lines_ref.shape[1]
    upper = lax.broadcasted_iota(jnp.int32, (ROW_BLOCK, taps), 1) > lax.broadcasted_iota(
        jnp.int32, (ROW_BLOCK, taps), 0
    )
    for group in range(count):
        line = lines_ref[row + group : row + group + 1, :]
        turned = pltpu.roll(jnp.broadcast_to(line, (ROW_BLOCK, taps)), 1, 1, stride=1, stride_axis=0)
        span = slice(at + group * ROW_BLOCK, at + (group + 1) * ROW_BLOCK)
        table_ref[span, :taps] = jnp.where(upper, turned, 0.0).astype(BF16)
        table_ref[span, taps:] = jnp.where(upper, 0.0, turned)[:, :ROW_BLOCK].astype(BF16)


def product_kernel(*refs):
    keys_ref, values_ref, bank_ref, scales_ref, assign_ref, whole_ref = refs[:6]
    lines_ref, near_ref, far_ref, keys_in, values_in, sems = refs[6:]
    near = near_ref.shape[1]

    def taps():
        fill_lines(bank_ref[0], scales_ref[...], assign_ref[...], lines_ref)

    @pl.when(is_first())
    def _():
        taps()

    @pl.when(jnp.logical_and(is_first(), is_slab(1)))
    def _():
        near_ref[...] = whole_ref[:, RAW : RAW + near]
        far_ref[:, : far_ref.shape[1] - RAW] = whole_ref[:, RAW + near :]
        far_ref[:, far_ref.shape[1] - RAW :] = whole_ref[:, :RAW]

    @pl.when(jnp.logical_not(is_first()))
    def _():
        multiply(keys_ref, values_ref, keys_in, values_in, sems, [near_ref, far_ref], taps)


def product_of(keys, values, bank, scales, assign, whole):
    rows, total = keys.shape[1:]
    groups, taps = assign.shape[1], bank.shape[2]
    return call(
        product_kernel,
        "product",
        (array(groups, taps, F32), array(rows, NEAR), array(rows, total - NEAR)),
        [HBM, HBM] + [VMEM] * 4,
        (VMEM,) * 3,
        product_scratch(rows, total),
    )(keys, values, bank, scales, assign, whole)


def mix(table_ref, row, share, window, store):
    depth = table_ref.shape[1]
    rows = window.shape[0] - depth + ROW_BLOCK
    member = lax.broadcasted_iota(jnp.int32, (ROW_BLOCK, LANES), 1) // (LANES // share)
    table = table_ref[row : row + share * ROW_BLOCK, :]
    for first in range(0, rows, 2 * ROW_BLOCK):
        starts = (first, first + ROW_BLOCK)
        pair = jnp.concatenate([window[begin : begin + depth] for begin in starts], axis=1)
        sums = jnp.dot(table, pair, preferred_element_type=F32)
        for place, begin in enumerate(starts):
            part = sums[:, place * LANES : (place + 1) * LANES]
            mixed = part[:ROW_BLOCK]
            for group in range(1, share):
                mixed = jnp.where(member == group, part[group * ROW_BLOCK : (group + 1) * ROW_BLOCK], mixed)
            store(slice(begin, begin + ROW_BLOCK), mixed)


def mix_all(width, share, lines_ref, line, table_ref, start_ref, behind_ref, product_ref, local, store):
    rows = product_ref.shape[0]
    first = (lax.axis_index("ctx") - 1) * rows
    inside = first + lax.broadcasted_iota(jnp.int32, (2 * rows, LANES), 0) >= start_ref[0]
    for tile in range(width // LANES):
        at = slice(tile * LANES, (tile + 1) * LANES)
        near, inner = (slice(begin + at.start, begin + at.stop) for begin in local)
        row = tile * share * ROW_BLOCK
        turn_table(lines_ref, line + tile * share, share, table_ref, row)
        window = jnp.concatenate([behind_ref[:, near], product_ref[:, inner]], axis=0)
        window = jnp.where(inside, window, jnp.zeros_like(window))
        mix(table_ref, row, share, window, functools.partial(store, at))


def share_of(lines_ref, total):
    return LANES * lines_ref.shape[0] // total


def own_kernel(odd, first, shift, local, *refs):
    start_ref, lines_ref, behind_ref, product_ref, queries_ref, residual_ref = refs[:6]
    out_ref, table_ref = refs[-2:]
    width = out_ref.shape[1]
    share = share_of(lines_ref, residual_ref.shape[1])

    @pl.when(jnp.logical_and(is_first(), is_slab(odd)))
    def _():
        def store(at, span, mixed):
            cols = slice(first + at.start, first + at.stop)
            gated = queries_ref[0, span, cols].astype(F32) * mixed
            out_ref[span, at] = (residual_ref[span, cols].astype(F32) + gated).astype(BF16)

        line = first // LANES * share
        at = (shift, local)
        mix_all(width, share, lines_ref, line, table_ref, start_ref, behind_ref, product_ref, at, store)


def table_scratch(lines, width, total):
    groups, taps = lines.shape
    return pltpu.VMEM((width * groups // total * ROW_BLOCK, taps + ROW_BLOCK), BF16)


def own_of(odd, origin, start, lines, behind, product, queries, residual, first, width, weight, *after):
    rows, total = residual.shape
    return call(
        functools.partial(own_kernel, odd, first, first - origin, first),
        "own",
        array(rows, width),
        [SMEM] + [VMEM] * 5 + [ANY] * len(after),
        VMEM,
        [table_scratch(lines, width, total)],
        weight=weight,
    )(start, lines, behind, product, queries, residual, *after)


def pick_kernel(raw_ref, received_ref, _, queries_ref, product_ref, lines_ref):
    rows = queries_ref.shape[0]

    def take(source):
        queries_ref[...] = source[:rows, :]
        product_ref[...] = source[rows : 2 * rows, :]
        for part in range(RAW // LANES):
            taken = source[2 * rows :, part * LANES : (part + 1) * LANES]
            lines_ref[part * LINES : (part + 1) * LINES, :] = taken.astype(F32)

    pl.when(is_first())(lambda: take(raw_ref))
    pl.when(jnp.logical_not(is_first()))(lambda: take(received_ref))


def pick_of(raw, received, taps, after):
    rows, width = (raw.shape[0] - LINES) // 2, raw.shape[1]
    return call(
        pick_kernel,
        "pick",
        (array(rows, width), array(rows, width), array(RAW // LANES * LINES, taps, F32)),
        [VMEM, VMEM, ANY],
        (VMEM,) * 3,
        weight=SLOW,
    )(raw, received, after)


def hold_kernel(value_ref, _, out_ref):
    pass


def held_back(value, after, weight=QUICK):
    return call(
        hold_kernel, "hold", array(*value.shape), [ANY, ANY], ANY, weight=weight, aliases={0: 0}
    )(value, after)


def send_out(pieces, out_ref, sems):
    copies = [
        pltpu.make_async_copy(buffer, out_ref.at[0, :, pl.ds(first, buffer.shape[1])], sems.at[place])
        for place, (buffer, first) in enumerate(pieces)
    ]
    for copy in copies:
        copy.start()
    return copies


def wait_all(copies):
    for copy in copies:
        copy.wait()


def later_kernel(places, *refs):
    start_ref, lines_ref, near_behind, near_ref, far_behind, far_ref, queries_ref = refs[:7]
    own_refs = refs[7 : 7 + len(places)]
    out_ref, gated_ref, table_ref, sems = refs[-4:]
    total = queries_ref.shape[2]
    share = share_of(lines_ref, total)

    for odd in (0, 1):

        @pl.when(jnp.logical_and(is_first(), is_slab(odd)))
        def _():
            pieces = [(own_ref, first) for own_ref, (side, first, _) in zip(own_refs, places) if side == odd]
            wait_all(send_out(pieces, out_ref, sems))

    @pl.when(jnp.logical_not(is_first()))
    def _():
        for first, behind_ref, product_ref in ((0, near_behind, near_ref), (NEAR, far_behind, far_ref)):

            def store(at, span, mixed):
                cols = slice(first + at.start, first + at.stop)
                gated_ref[span, cols] = queries_ref[0, span, cols].astype(F32) * mixed

            width, line = product_ref.shape[1], first // LANES * share
            mix_all(width, share, lines_ref, line, table_ref, start_ref, behind_ref, product_ref, (0, 0), store)


def later_of(start, lines, near_behind, near, far_behind, far, queries, own, places):
    rows, total = queries.shape[1:]
    return call(
        functools.partial(later_kernel, places),
        "later",
        (jax.ShapeDtypeStruct((1, rows, total), BF16), array(rows, total, F32)),
        [SMEM] + [VMEM] * (6 + len(own)),
        (ANY, VMEM),
        [table_scratch(lines, NEAR, total), pltpu.SemaphoreType.DMA((len(own),))],
        weight=SLOW,
    )(start, lines, near_behind, near, far_behind, far, queries, *own)


def raw_kernel(*refs):
    start_ref, lines_ref, behind_ref, chip_ref, far_ref, product_ref, queries_ref, gated_ref, residual_ref = refs[:9]
    out_ref, chosen_ref, table_ref, buffer, sems = refs[10:]
    width = buffer.shape[1]
    share = share_of(lines_ref, width)
    far = far_ref.shape[1]
    sources = (
        (jnp.logical_and(is_first(), is_slab(0)), far_ref, slice(far - width, far)),
        (jnp.logical_and(is_first(), is_slab(1)), chip_ref, slice(0, width)),
        (jnp.logical_not(is_first()), behind_ref, slice(0, width)),
    )
    for wanted, source, cols in sources:

        @pl.when(wanted)
        def _():
            chosen_ref[...] = source[:, cols]

    def store(at, span, mixed):
        gated = queries_ref[span, at].astype(F32) * mixed
        buffer[span, at] = (residual_ref[span, at].astype(F32) + gated).astype(BF16)

    mix_all(width, share, lines_ref, 0, table_ref, start_ref, chosen_ref, product_ref, (0, 0), store)

    @pl.when(jnp.logical_not(is_first()))
    def _():
        buffer[...] = (buffer[...].astype(F32) + gated_ref[:, :width]).astype(BF16)

    wait_all(send_out([(buffer, 0)], out_ref, sems))


def raw_finish(held, start, lines, behind, chip_behind, far_behind, product, queries, gated, residual):
    rows, width = product.shape
    return call(
        raw_kernel,
        "raw",
        jax.ShapeDtypeStruct(held.shape, BF16),
        [SMEM] + [VMEM] * 8 + [ANY],
        ANY,
        [
            pltpu.VMEM((rows, width), BF16),
            table_scratch(lines, width, width),
            pltpu.VMEM((rows, width), BF16),
            pltpu.SemaphoreType.DMA((1,)),
        ],
        weight=SLOW,
        aliases={9: 0},
    )(start, lines, behind, chip_behind, far_behind, product, queries, gated, residual, held)


def finish_kernel(odd, places, *refs):
    gated_ref, received_refs = refs[0], refs[1 : 1 + len(places)]
    out_ref, *buffers, sems = refs[2 + len(places) :]

    @pl.when(jnp.logical_and(jnp.logical_not(is_first()), is_slab(odd)))
    def _():
        copies = []
        for place, (_, first, width) in enumerate(places):
            buffer = buffers[place]
            total = received_refs[place][...].astype(F32) + gated_ref[:, first : first + width]
            buffer[...] = total.astype(BF16)
            copies += send_out([(buffer, first)], out_ref, sems.at[pl.ds(place, 1)])
        wait_all(copies)


def finish(held, gated, received, places):
    rows = gated.shape[0]
    count = len(places)
    return call(
        functools.partial(finish_kernel, places[0][0], places),
        "finish",
        jax.ShapeDtypeStruct(held.shape, BF16),
        [VMEM] * (1 + count) + [ANY],
        ANY,
        [pltpu.VMEM((rows, width), BF16) for _, _, width in places] + [pltpu.SemaphoreType.DMA((count,))],
        weight=SLOW,
        aliases={1 + count: 0},
    )(gated, *received, held)


def body(queries, keys, values, residual, filter_bank, filter_scales, group_filter, context_start):
    total = queries.shape[2]
    small = (filter_bank, filter_scales, group_filter)
    far_small = [pltpu.with_memory_space_constraint(value, pltpu.HBM) for value in small]
    far_queries, keys, values = (
        pltpu.with_memory_space_constraint(value, pltpu.HBM) for value in (queries, keys, values)
    )
    raw, whole = lead_of(*far_small, far_queries, keys, values)
    raw_received = to_next_section(raw)
    chip_behind = to_next_slab(whole, (0, 0))
    lines, near, far = product_of(keys, values, *small, whole)
    own, received, places = [], [], []

    def send(odd, behind, origin, first, width, weight, *after):
        piece = own_of(
            odd, origin, context_start, lines, behind, whole, queries, residual, first, width, weight, *after
        )
        own.append(piece)
        received.append(to_next_section(piece, (odd,)))
        places.append((odd, first, width))
        return first + width, piece

    first, after = send(1, chip_behind, 0, RAW, ODD[0], QUICK, lines)
    near = held_back(near, after)
    near_behind = to_next_slab(near, (1, 0), (0, 1), (1, 1))
    first, after = send(1, chip_behind, 0, first, ODD[1], QUICK, near)
    raw_queries, raw_product, raw_lines = pick_of(raw, raw_received, lines.shape[1], after)
    far = held_back(far, raw_queries)
    far_behind = to_next_slab(far, (1, 0), (0, 1), (1, 1))
    raw_queries = held_back(raw_queries, received[0], SLOW)
    first, after = send(0, near_behind, RAW, RAW, EVEN[0], SLOW, raw_queries)
    first, after = send(0, near_behind, RAW, first, EVEN[1], SLOW, after)
    raw_product = held_back(raw_product, after)
    raw_behind = to_next_slab(raw_product, (0, 1), (1, 1))
    origin, after = first, raw_product
    for width in EVEN[2:]:
        first, after = send(0, far_behind, origin, first, width, SLOW, after, received[1])
    held, gated = later_of(
        context_start, lines, near_behind, near, far_behind, far, queries, own, places
    )
    odd = len(ODD)
    held = finish(held, gated, received[:odd], places[:odd])
    held = raw_finish(
        held,
        context_start,
        raw_lines,
        raw_behind,
        chip_behind,
        far_behind,
        raw_product,
        raw_queries,
        gated,
        residual,
    )
    for last in (odd + 2, odd + 3, odd + 4):
        begin = odd if last == odd + 2 else last - 1
        held = finish(held, gated, received[begin:last], places[begin:last])
    return held


def solution(mesh):
    return jax.shard_map(
        body,
        mesh=mesh,
        in_specs=(
            P("pipe", ("dp", "ctx"), None),
            P("pipe", ("dp", "ctx"), None),
            P("pipe", ("dp", "ctx"), None),
            P(("dp", "ctx"), None),
            P("pipe", None, None),
            P("pipe", None),
            P("pipe", None),
            P("dp"),
        ),
        out_specs=P("pipe", ("dp", "ctx"), None),
        check_vma=False,
    )
```

```python
import functools

import jax
import jax.numpy as jnp
from jax import lax
from jax.experimental import pallas as pl
from jax.experimental.pallas import tpu as pltpu
from jax.sharding import PartitionSpec as P

LANES = 128
ROW_BLOCK = 32
RAW = 384
ODD = (1536, 2176)
EVEN = (1024, 768, 896, 1024)
PIECES = 4
NEAR = 1792
LINES = 8
F32 = jnp.float32
BF16 = jnp.bfloat16
MIB = 1024 * 1024
QUICK, SLOW = 1024, 20_000_000_000

SMEM = pl.BlockSpec(memory_space=pltpu.SMEM)
VMEM = pl.BlockSpec(memory_space=pltpu.VMEM)
ANY = pl.BlockSpec(memory_space=pl.ANY)
HBM = pl.BlockSpec(memory_space=pltpu.HBM)


def to_next_slab(value, *links):
    slabs, depth = lax.axis_size("ctx"), lax.axis_size("pipe")
    pairs = [
        (slab * depth + pipe, (slab + 1) * depth + pipe)
        for odd, pipe in links
        for slab in range(slabs - 1)
        if slab % 2 == odd
    ]
    return lax.ppermute(value, ("ctx", "pipe"), pairs)


def to_next_section(value, slabs=(0, 1)):
    depth = lax.axis_size("pipe")
    pairs = [(slab * depth, slab * depth + 1) for slab in range(lax.axis_size("ctx")) if slab % 2 in slabs]
    return lax.ppermute(value, ("ctx", "pipe"), pairs)


def call(kernel, name, out_shape, in_specs, out_specs, scratch=(), weight=QUICK, aliases=None):
    return pl.pallas_call(
        kernel,
        out_shape=out_shape,
        in_specs=in_specs,
        out_specs=out_specs,
        scratch_shapes=list(scratch),
        input_output_aliases=aliases or {},
        compiler_params=pltpu.CompilerParams(vmem_limit_bytes=16 * MIB),
        cost_estimate=pl.CostEstimate(flops=weight, bytes_accessed=1024, transcendentals=0),
        name=name,
    )


def is_first():
    return lax.axis_index("pipe") == 0


def is_slab(odd):
    return lax.axis_index("ctx") % 2 == odd


def array(rows, cols, kind=BF16):
    return jax.ShapeDtypeStruct((rows, cols), kind)


def multiply(keys_ref, values_ref, keys_in, values_in, sems, out_refs, meanwhile):
    rows = out_refs[0].shape[0]
    step = rows // PIECES
    spans = [pl.ds(piece * step, step) for piece in range(PIECES)]
    copies = []
    for piece, span in enumerate(spans):
        copies.append(
            (
                pltpu.make_async_copy(keys_ref.at[0, span], keys_in.at[span], sems.at[2 * piece]),
                pltpu.make_async_copy(values_ref.at[0, span], values_in.at[span], sems.at[2 * piece + 1]),
            )
        )
        for copy in copies[-1]:
            copy.start()
    meanwhile()
    for span, pair in zip(spans, copies):
        for copy in pair:
            copy.wait()
        first = 0
        for out_ref in out_refs:
            for tile in range(0, out_ref.shape[1], LANES):
                at = slice(first + tile, first + tile + LANES)
                product = keys_in[span, at].astype(F32) * values_in[span, at].astype(F32)
                out_ref[span, tile : tile + LANES] = product.astype(BF16)
            first += out_ref.shape[1]


def fill_lines(bank, scales, assign, lines_ref):
    groups, taps = lines_ref.shape
    size = bank.shape[0]
    chosen = (lax.broadcasted_iota(jnp.int32, (size, groups), 0) == assign).astype(F32).astype(BF16)
    contract = (((0,), (0,)), ((), ()))
    picked = lax.dot_general(bank, chosen, contract, preferred_element_type=F32)
    scaled = (picked * scales).astype(BF16)
    order = lax.broadcasted_iota(jnp.int32, (taps, taps), 0) + lax.broadcasted_iota(jnp.int32, (taps, taps), 1)
    flip = (order == taps - 1).astype(F32).astype(BF16)
    lines_ref[...] = lax.dot_general(scaled, flip, contract, preferred_element_type=F32)


def lead_kernel(*refs):
    bank_ref, scales_ref, assign_ref, queries_ref, keys_ref, values_ref = refs[:6]
    raw_ref, rest_ref = refs[6:8]
    bank_in, scales_in, assign_in, lines_ref, keys_in, values_in, sems, own_sems = refs[8:]
    count = lines_ref.shape[0]
    rows = rest_ref.shape[0]

    @pl.when(is_first())
    def _():
        copies = [
            pltpu.make_async_copy(bank_ref, bank_in, own_sems.at[0]),
            pltpu.make_async_copy(scales_ref, scales_in, own_sems.at[1]),
            pltpu.make_async_copy(assign_ref, assign_in, own_sems.at[2]),
            pltpu.make_async_copy(queries_ref.at[0, :, pl.ds(0, RAW)], raw_ref.at[pl.ds(0, rows)], own_sems.at[3]),
        ]
        for copy in copies:
            copy.start()

        def taps():
            for copy in copies[:3]:
                copy.wait()
            fill_lines(bank_in[0], scales_in[:, :count], assign_in[:, :count], lines_ref)
            for part in range(RAW // LANES):
                taken = lines_ref[part * LINES : (part + 1) * LINES, :].astype(BF16)
                raw_ref[2 * rows :, part * LANES : (part + 1) * LANES] = taken

        multiply(keys_ref, values_ref, keys_in, values_in, sems, [raw_ref.at[pl.ds(rows, rows)], rest_ref], taps)
        copies[3].wait()


def product_scratch(rows, total):
    return [pltpu.VMEM((rows, total), BF16), pltpu.VMEM((rows, total), BF16), pltpu.SemaphoreType.DMA((2 * PIECES,))]


def lead_of(bank, scales, assign, queries, keys, values):
    rows, total = queries.shape[1:]
    return call(
        lead_kernel,
        "lead",
        (
            array(2 * rows + LINES, RAW),
            array(rows, total - RAW),
        ),
        [HBM] * 6,
        (VMEM,) * 2,
        [
            pltpu.VMEM(bank.shape, BF16),
            pltpu.VMEM(scales.shape, F32),
            pltpu.VMEM(assign.shape, jnp.int32),
            pltpu.VMEM((min(LANES, assign.shape[1]), bank.shape[2]), F32),
        ]
        + product_scratch(rows, total)
        + [pltpu.SemaphoreType.DMA((4,))],
    )(bank, scales, assign, queries, keys, values)


def turn_table(lines_ref, row, count, table_ref, at):
    taps = lines_ref.shape[1]
    upper = lax.broadcasted_iota(jnp.int32, (ROW_BLOCK, taps), 1) > lax.broadcasted_iota(
        jnp.int32, (ROW_BLOCK, taps), 0
    )
    for group in range(count):
        line = lines_ref[row + group : row + group + 1, :]
        turned = pltpu.roll(jnp.broadcast_to(line, (ROW_BLOCK, taps)), 1, 1, stride=1, stride_axis=0)
        span = slice(at + group * ROW_BLOCK, at + (group + 1) * ROW_BLOCK)
        table_ref[span, :taps] = jnp.where(upper, turned, 0.0).astype(BF16)
        table_ref[span, taps:] = jnp.where(upper, 0.0, turned)[:, :ROW_BLOCK].astype(BF16)


def product_kernel(*refs):
    keys_ref, values_ref, bank_ref, scales_ref, assign_ref, rest_ref = refs[:6]
    lines_ref, near_ref, far_ref, tail_ref, keys_in, values_in, sems = refs[6:]

    def taps():
        fill_lines(bank_ref[0], scales_ref[...], assign_ref[...], lines_ref)

    @pl.when(is_first())
    def _():
        taps()

    @pl.when(jnp.logical_and(is_first(), is_slab(1)))
    def _():
        near_ref[...] = rest_ref[:, :NEAR]
        far_ref[...] = rest_ref[:, NEAR:]

    @pl.when(jnp.logical_not(is_first()))
    def _():
        multiply(keys_ref, values_ref, keys_in, values_in, sems, [near_ref, far_ref, tail_ref], taps)


def product_of(keys, values, bank, scales, assign, rest):
    rows, total = keys.shape[1:]
    groups, taps = assign.shape[1], bank.shape[2]
    return call(
        product_kernel,
        "product",
        (array(groups, taps, F32), array(rows, NEAR), array(rows, total - RAW - NEAR), array(rows, RAW)),
        [HBM, HBM] + [VMEM] * 4,
        (VMEM,) * 4,
        product_scratch(rows, total),
    )(keys, values, bank, scales, assign, rest)


def mix(table_ref, row, share, window, store):
    depth = table_ref.shape[1]
    rows = window.shape[0] - depth + ROW_BLOCK
    member = lax.broadcasted_iota(jnp.int32, (ROW_BLOCK, LANES), 1) // (LANES // share)
    table = table_ref[row : row + share * ROW_BLOCK, :]
    for first in range(0, rows, 2 * ROW_BLOCK):
        starts = (first, first + ROW_BLOCK)
        pair = jnp.concatenate([window[begin : begin + depth] for begin in starts], axis=1)
        sums = jnp.dot(table, pair, preferred_element_type=F32)
        for place, begin in enumerate(starts):
            part = sums[:, place * LANES : (place + 1) * LANES]
            mixed = part[:ROW_BLOCK]
            for group in range(1, share):
                mixed = jnp.where(member == group, part[group * ROW_BLOCK : (group + 1) * ROW_BLOCK], mixed)
            store(slice(begin, begin + ROW_BLOCK), mixed)


def mix_all(width, share, lines_ref, line, table_ref, start_ref, behind_ref, product_ref, local, store):
    rows = product_ref.shape[0]
    first = (lax.axis_index("ctx") - 1) * rows
    inside = first + lax.broadcasted_iota(jnp.int32, (2 * rows, LANES), 0) >= start_ref[0]
    for tile in range(width // LANES):
        at = slice(tile * LANES, (tile + 1) * LANES)
        near, inner = (slice(begin + at.start, begin + at.stop) for begin in local)
        row = tile * share * ROW_BLOCK
        turn_table(lines_ref, line + tile * share, share, table_ref, row)
        window = jnp.concatenate([behind_ref[:, near], product_ref[:, inner]], axis=0)
        window = jnp.where(inside, window, jnp.zeros_like(window))
        mix(table_ref, row, share, window, functools.partial(store, at))


def share_of(lines_ref, total):
    return LANES * lines_ref.shape[0] // total


def own_kernel(odd, first, shift, local, *refs):
    start_ref, lines_ref, behind_ref, product_ref, queries_ref, residual_ref = refs[:6]
    out_ref, table_ref = refs[-2:]
    width = out_ref.shape[1]
    share = share_of(lines_ref, residual_ref.shape[1])

    @pl.when(jnp.logical_and(is_first(), is_slab(odd)))
    def _():
        def store(at, span, mixed):
            cols = slice(first + at.start, first + at.stop)
            gated = queries_ref[0, span, cols].astype(F32) * mixed
            out_ref[span, at] = (residual_ref[span, cols].astype(F32) + gated).astype(BF16)

        line = first // LANES * share
        at = (shift, local)
        mix_all(width, share, lines_ref, line, table_ref, start_ref, behind_ref, product_ref, at, store)


def table_scratch(lines, width, total):
    groups, taps = lines.shape
    return pltpu.VMEM((width * groups // total * ROW_BLOCK, taps + ROW_BLOCK), BF16)


def own_of(odd, origin, start, lines, behind, product, queries, residual, first, width, weight, *after):
    rows, total = residual.shape
    return call(
        functools.partial(own_kernel, odd, first, first - origin, first - RAW),
        "own",
        array(rows, width),
        [SMEM] + [VMEM] * 5 + [ANY] * len(after),
        VMEM,
        [table_scratch(lines, width, total)],
        weight=weight,
    )(start, lines, behind, product, queries, residual, *after)


def pick_kernel(raw_ref, received_ref, tail_ref, _, queries_ref, product_ref, lines_ref):
    rows = queries_ref.shape[0]

    def take(source):
        queries_ref[...] = source[:rows, :]
        product_ref[:, :RAW] = source[rows : 2 * rows, :]
        for part in range(RAW // LANES):
            taken = source[2 * rows :, part * LANES : (part + 1) * LANES]
            lines_ref[part * LINES : (part + 1) * LINES, :] = taken.astype(F32)

    pl.when(is_first())(lambda: take(raw_ref))

    @pl.when(jnp.logical_not(is_first()))
    def _():
        take(received_ref)
        product_ref[:, RAW:] = tail_ref[...]


def pick_of(raw, received, tail, taps, after):
    rows, width = (raw.shape[0] - LINES) // 2, raw.shape[1]
    return call(
        pick_kernel,
        "pick",
        (array(rows, width), array(rows, 2 * width), array(RAW // LANES * LINES, taps, F32)),
        [VMEM, VMEM, VMEM, ANY],
        (VMEM,) * 3,
        weight=SLOW,
    )(raw, received, tail, after)


def hold_kernel(value_ref, _, out_ref):
    pass


def held_back(value, after, weight=QUICK):
    return call(
        hold_kernel, "hold", array(*value.shape), [ANY, ANY], ANY, weight=weight, aliases={0: 0}
    )(value, after)


def send_out(pieces, out_ref, sems):
    copies = [
        pltpu.make_async_copy(buffer, out_ref.at[0, :, pl.ds(first, buffer.shape[1])], sems.at[place])
        for place, (buffer, first) in enumerate(pieces)
    ]
    for copy in copies:
        copy.start()
    return copies


def wait_all(copies):
    for copy in copies:
        copy.wait()


def later_kernel(places, *refs):
    start_ref, lines_ref, near_behind, near_ref, far_behind, far_ref, raw_behind, tail_ref, queries_ref = refs[:9]
    own_refs = refs[9 : 9 + len(places)]
    out_ref, gated_ref, table_ref, sems = refs[-4:]
    total = queries_ref.shape[2]
    share = share_of(lines_ref, total)

    for odd in (0, 1):

        @pl.when(jnp.logical_and(is_first(), is_slab(odd)))
        def _():
            pieces = [(own_ref, first) for own_ref, (side, first, _) in zip(own_refs, places) if side == odd]
            wait_all(send_out(pieces, out_ref, sems))

    @pl.when(jnp.logical_not(is_first()))
    def _():
        parts = (
            (0, 0, near_behind, near_ref),
            (NEAR, 0, far_behind, far_ref),
            (total - RAW, RAW, raw_behind, tail_ref),
        )
        for first, skip, behind_ref, product_ref in parts:

            def store(at, span, mixed):
                cols = slice(first + at.start, first + at.stop)
                gated_ref[span, cols] = queries_ref[0, span, cols].astype(F32) * mixed

            width, line = product_ref.shape[1], first // LANES * share
            at = (skip, 0)
            mix_all(width, share, lines_ref, line, table_ref, start_ref, behind_ref, product_ref, at, store)


def later_of(start, lines, near_behind, near, far_behind, far, raw_behind, tail, queries, own, places):
    rows, total = queries.shape[1:]
    return call(
        functools.partial(later_kernel, places),
        "later",
        (jax.ShapeDtypeStruct((1, rows, total), BF16), array(rows, total, F32)),
        [SMEM] + [VMEM] * (8 + len(own)),
        (ANY, VMEM),
        [table_scratch(lines, total - RAW - NEAR, total), pltpu.SemaphoreType.DMA((len(own),))],
        weight=SLOW,
    )(start, lines, near_behind, near, far_behind, far, raw_behind, tail, queries, *own)


def raw_kernel(start_ref, lines_ref, behind_ref, product_ref, queries_ref, gated_ref, residual_ref, _, *refs):
    out_ref, table_ref, buffer, sems = refs
    width = buffer.shape[1]
    share = share_of(lines_ref, width)

    def store(at, span, mixed):
        gated = queries_ref[span, at].astype(F32) * mixed
        buffer[span, at] = (residual_ref[span, at].astype(F32) + gated).astype(BF16)

    mix_all(width, share, lines_ref, 0, table_ref, start_ref, behind_ref, product_ref, (0, 0), store)

    @pl.when(jnp.logical_not(is_first()))
    def _():
        buffer[...] = (buffer[...].astype(F32) + gated_ref[:, :width]).astype(BF16)

    wait_all(send_out([(buffer, 0)], out_ref, sems))


def raw_finish(held, start, lines, behind, product, queries, gated, residual):
    rows, width = queries.shape
    return call(
        raw_kernel,
        "raw",
        jax.ShapeDtypeStruct(held.shape, BF16),
        [SMEM] + [VMEM] * 6 + [ANY],
        ANY,
        [table_scratch(lines, width, width), pltpu.VMEM((rows, width), BF16), pltpu.SemaphoreType.DMA((1,))],
        weight=SLOW,
        aliases={7: 0},
    )(start, lines, behind, product, queries, gated, residual, held)


def finish_kernel(odd, places, *refs):
    gated_ref, received_refs = refs[0], refs[1 : 1 + len(places)]
    out_ref, *buffers, sems = refs[2 + len(places) :]

    @pl.when(jnp.logical_and(jnp.logical_not(is_first()), is_slab(odd)))
    def _():
        copies = []
        for place, (_, first, width) in enumerate(places):
            buffer = buffers[place]
            total = received_refs[place][...].astype(F32) + gated_ref[:, first : first + width]
            buffer[...] = total.astype(BF16)
            copies += send_out([(buffer, first)], out_ref, sems.at[pl.ds(place, 1)])
        wait_all(copies)


def finish(held, gated, received, places):
    rows = gated.shape[0]
    count = len(places)
    return call(
        functools.partial(finish_kernel, places[0][0], places),
        "finish",
        jax.ShapeDtypeStruct(held.shape, BF16),
        [VMEM] * (1 + count) + [ANY],
        ANY,
        [pltpu.VMEM((rows, width), BF16) for _, _, width in places] + [pltpu.SemaphoreType.DMA((count,))],
        weight=SLOW,
        aliases={1 + count: 0},
    )(gated, *received, held)


def body(queries, keys, values, residual, filter_bank, filter_scales, group_filter, context_start):
    total = queries.shape[2]
    small = (filter_bank, filter_scales, group_filter)
    far_small = [pltpu.with_memory_space_constraint(value, pltpu.HBM) for value in small]
    far_queries, keys, values = (
        pltpu.with_memory_space_constraint(value, pltpu.HBM) for value in (queries, keys, values)
    )
    raw, rest = lead_of(*far_small, far_queries, keys, values)
    raw_received = to_next_section(raw)
    chip_behind = to_next_slab(rest, (0, 0))
    lines, near, far, tail = product_of(keys, values, *small, rest)
    own, received, places = [], [], []

    def send(odd, behind, origin, first, width, *after):
        piece = own_of(
            odd, origin, context_start, lines, behind, rest, queries, residual, first, width, QUICK, *after
        )
        own.append(piece)
        received.append(to_next_section(piece, (odd,)))
        places.append((odd, first, width))
        return first + width, piece

    links = ((1, 0), (0, 1), (1, 1))
    first, after = send(1, chip_behind, RAW, RAW, ODD[0], lines)
    near = held_back(near, after)
    near_behind = to_next_slab(near, *links)
    first, after = send(1, chip_behind, RAW, first, ODD[1], near)
    raw_queries, raw_product, raw_lines = pick_of(raw, raw_received, tail, lines.shape[1], after)
    far = held_back(far, raw_queries)
    far_behind = to_next_slab(far, *links)
    raw_product = held_back(raw_product, far)
    raw_behind = to_next_slab(raw_product, (0, 0), *links)
    raw_queries = held_back(raw_queries, received[0], SLOW)
    first, after = send(0, near_behind, RAW, RAW, EVEN[0], raw_queries)
    first, after = send(0, near_behind, RAW, first, EVEN[1], after)
    origin = first
    first, after = send(0, far_behind, origin, first, EVEN[2], after, received[1])
    first, after = send(0, far_behind, origin, first, EVEN[3], after, raw_behind)
    held, gated = later_of(
        context_start,
        lines,
        near_behind,
        near,
        far_behind,
        far,
        raw_behind,
        tail,
        queries,
        own,
        places,
    )
    odd = len(ODD)
    held = finish(held, gated, received[:odd], places[:odd])
    held = raw_finish(held, context_start, raw_lines, raw_behind, raw_product, raw_queries, gated, residual)
    for last in (odd + 2, odd + 3, odd + 4):
        begin = odd if last == odd + 2 else last - 1
        held = finish(held, gated, received[begin:last], places[begin:last])
    return held


def solution(mesh):
    return jax.shard_map(
        body,
        mesh=mesh,
        in_specs=(
            P("pipe", ("dp", "ctx"), None),
            P("pipe", ("dp", "ctx"), None),
            P("pipe", ("dp", "ctx"), None),
            P(("dp", "ctx"), None),
            P("pipe", None, None),
            P("pipe", None),
            P("pipe", None),
            P("dp"),
        ),
        out_specs=P("pipe", ("dp", "ctx"), None),
        check_vma=False,
    )
```

```python
import functools

import jax
import jax.numpy as jnp
from jax import lax
from jax.experimental import pallas as pl
from jax.experimental.pallas import tpu as pltpu
from jax.sharding import PartitionSpec as P

LANES = 128
ROW_BLOCK = 32
RAW = 384
ODD = (1536, 2176)
EVEN = (1024, 768, 896, 1024)
PIECES = 4
NEAR = 1792
F32 = jnp.float32
BF16 = jnp.bfloat16
MIB = 1024 * 1024
QUICK, SLOW = 1024, 20_000_000_000

SMEM = pl.BlockSpec(memory_space=pltpu.SMEM)
VMEM = pl.BlockSpec(memory_space=pltpu.VMEM)
ANY = pl.BlockSpec(memory_space=pl.ANY)
HBM = pl.BlockSpec(memory_space=pltpu.HBM)


def to_next_slab(value, *links):
    slabs, depth = lax.axis_size("ctx"), lax.axis_size("pipe")
    pairs = [
        (slab * depth + pipe, (slab + 1) * depth + pipe)
        for odd, pipe in links
        for slab in range(slabs - 1)
        if slab % 2 == odd
    ]
    return lax.ppermute(value, ("ctx", "pipe"), pairs)


def to_next_section(value, slabs=(0, 1)):
    depth = lax.axis_size("pipe")
    pairs = [(slab * depth, slab * depth + 1) for slab in range(lax.axis_size("ctx")) if slab % 2 in slabs]
    return lax.ppermute(value, ("ctx", "pipe"), pairs)


def call(kernel, name, out_shape, in_specs, out_specs, scratch=(), weight=QUICK, aliases=None):
    return pl.pallas_call(
        kernel,
        out_shape=out_shape,
        in_specs=in_specs,
        out_specs=out_specs,
        scratch_shapes=list(scratch),
        input_output_aliases=aliases or {},
        compiler_params=pltpu.CompilerParams(vmem_limit_bytes=16 * MIB),
        cost_estimate=pl.CostEstimate(flops=weight, bytes_accessed=1024, transcendentals=0),
        name=name,
    )


def is_first():
    return lax.axis_index("pipe") == 0


def is_slab(odd):
    return lax.axis_index("ctx") % 2 == odd


def array(rows, cols, kind=BF16):
    return jax.ShapeDtypeStruct((rows, cols), kind)


def multiply(keys_ref, values_ref, keys_in, values_in, sems, out_refs, meanwhile):
    rows = out_refs[0].shape[0]
    step = rows // PIECES
    spans = [pl.ds(piece * step, step) for piece in range(PIECES)]
    copies = []
    for piece, span in enumerate(spans):
        copies.append(
            (
                pltpu.make_async_copy(keys_ref.at[0, span], keys_in.at[span], sems.at[2 * piece]),
                pltpu.make_async_copy(values_ref.at[0, span], values_in.at[span], sems.at[2 * piece + 1]),
            )
        )
        for copy in copies[-1]:
            copy.start()
    meanwhile()
    for span, pair in zip(spans, copies):
        for copy in pair:
            copy.wait()
        first = 0
        for out_ref in out_refs:
            for tile in range(0, out_ref.shape[1], LANES):
                at = slice(first + tile, first + tile + LANES)
                product = keys_in[span, at].astype(F32) * values_in[span, at].astype(F32)
                out_ref[span, tile : tile + LANES] = product.astype(BF16)
            first += out_ref.shape[1]


def fill_lines(bank, scales, assign, lines_ref):
    groups, taps = lines_ref.shape
    size = bank.shape[0]
    chosen = (lax.broadcasted_iota(jnp.int32, (size, groups), 0) == assign).astype(F32).astype(BF16)
    contract = (((0,), (0,)), ((), ()))
    picked = lax.dot_general(bank, chosen, contract, preferred_element_type=F32)
    scaled = (picked * scales).astype(BF16)
    order = lax.broadcasted_iota(jnp.int32, (taps, taps), 0) + lax.broadcasted_iota(jnp.int32, (taps, taps), 1)
    flip = (order == taps - 1).astype(F32).astype(BF16)
    lines_ref[...] = lax.dot_general(scaled, flip, contract, preferred_element_type=F32)


def lead_kernel(queries_ref, keys_ref, values_ref, raw_ref, rest_ref, keys_in, values_in, sems, own_sem):
    rows = rest_ref.shape[0]

    @pl.when(is_first())
    def _():
        source = queries_ref.at[0, :, pl.ds(0, RAW)]
        copy = pltpu.make_async_copy(source, raw_ref.at[pl.ds(0, rows)], own_sem)
        targets = [raw_ref.at[pl.ds(rows, rows)], rest_ref]
        multiply(keys_ref, values_ref, keys_in, values_in, sems, targets, copy.start)
        copy.wait()


def product_scratch(rows, total):
    return [pltpu.VMEM((rows, total), BF16), pltpu.VMEM((rows, total), BF16), pltpu.SemaphoreType.DMA((2 * PIECES,))]


def lead_of(queries, keys, values):
    rows, total = queries.shape[1:]
    return call(
        lead_kernel,
        "lead",
        (array(2 * rows, RAW), array(rows, total - RAW)),
        [HBM] * 3,
        (VMEM,) * 2,
        product_scratch(rows, total) + [pltpu.SemaphoreType.DMA(())],
    )(queries, keys, values)


def turn_table(lines_ref, row, count, table_ref, at):
    taps = lines_ref.shape[1]
    upper = lax.broadcasted_iota(jnp.int32, (ROW_BLOCK, taps), 1) > lax.broadcasted_iota(
        jnp.int32, (ROW_BLOCK, taps), 0
    )
    for group in range(count):
        line = lines_ref[row + group : row + group + 1, :]
        turned = pltpu.roll(jnp.broadcast_to(line, (ROW_BLOCK, taps)), 1, 1, stride=1, stride_axis=0)
        span = slice(at + group * ROW_BLOCK, at + (group + 1) * ROW_BLOCK)
        table_ref[span, :taps] = jnp.where(upper, turned, 0.0).astype(BF16)
        table_ref[span, taps:] = jnp.where(upper, 0.0, turned)[:, :ROW_BLOCK].astype(BF16)


def product_kernel(*refs):
    keys_ref, values_ref, bank_ref, scales_ref, assign_ref, rest_ref = refs[:6]
    lines_ref, wire_ref, near_ref, far_ref, tail_ref, keys_in, values_in, sems = refs[6:]

    def taps():
        fill_lines(bank_ref[0], scales_ref[...], assign_ref[...], lines_ref)

    @pl.when(is_first())
    def _():
        taps()
        wire_ref[...] = lines_ref[: wire_ref.shape[0], :].astype(BF16)

    @pl.when(jnp.logical_and(is_first(), is_slab(1)))
    def _():
        near_ref[...] = rest_ref[:, :NEAR]
        far_ref[...] = rest_ref[:, NEAR:]

    @pl.when(jnp.logical_not(is_first()))
    def _():
        multiply(keys_ref, values_ref, keys_in, values_in, sems, [near_ref, far_ref, tail_ref], taps)


def wire_rows(groups, total):
    return -(-RAW * groups // (total * 16)) * 16


def product_of(keys, values, bank, scales, assign, rest):
    rows, total = keys.shape[1:]
    groups, taps = assign.shape[1], bank.shape[2]
    return call(
        product_kernel,
        "product",
        (
            array(groups, taps, F32),
            array(wire_rows(groups, total), taps),
            array(rows, NEAR),
            array(rows, total - RAW - NEAR),
            array(rows, RAW),
        ),
        [HBM, HBM] + [VMEM] * 4,
        (VMEM,) * 5,
        product_scratch(rows, total),
    )(keys, values, bank, scales, assign, rest)


def mix(table_ref, row, share, window, store):
    depth = table_ref.shape[1]
    rows = window.shape[0] - depth + ROW_BLOCK
    member = lax.broadcasted_iota(jnp.int32, (ROW_BLOCK, LANES), 1) // (LANES // share)
    table = table_ref[row : row + share * ROW_BLOCK, :]
    for first in range(0, rows, 2 * ROW_BLOCK):
        starts = (first, first + ROW_BLOCK)
        pair = jnp.concatenate([window[begin : begin + depth] for begin in starts], axis=1)
        sums = jnp.dot(table, pair, preferred_element_type=F32)
        for place, begin in enumerate(starts):
            part = sums[:, place * LANES : (place + 1) * LANES]
            mixed = part[:ROW_BLOCK]
            for group in range(1, share):
                mixed = jnp.where(member == group, part[group * ROW_BLOCK : (group + 1) * ROW_BLOCK], mixed)
            store(slice(begin, begin + ROW_BLOCK), mixed)


def mix_all(width, share, lines_ref, line, table_ref, start_ref, behind_ref, product_ref, local, store):
    rows = product_ref.shape[0]
    first = (lax.axis_index("ctx") - 1) * rows
    inside = first + lax.broadcasted_iota(jnp.int32, (2 * rows, LANES), 0) >= start_ref[0]
    for tile in range(width // LANES):
        at = slice(tile * LANES, (tile + 1) * LANES)
        near, inner = (slice(begin + at.start, begin + at.stop) for begin in local)
        row = tile * share * ROW_BLOCK
        turn_table(lines_ref, line + tile * share, share, table_ref, row)
        window = jnp.concatenate([behind_ref[:, near], product_ref[:, inner]], axis=0)
        window = jnp.where(inside, window, jnp.zeros_like(window))
        mix(table_ref, row, share, window, functools.partial(store, at))


def share_of(lines_ref, total):
    return LANES * lines_ref.shape[0] // total


def own_kernel(odd, first, shift, local, *refs):
    start_ref, lines_ref, behind_ref, product_ref, queries_ref, residual_ref = refs[:6]
    out_ref, table_ref = refs[-2:]
    width = out_ref.shape[1]
    share = share_of(lines_ref, residual_ref.shape[1])

    @pl.when(jnp.logical_and(is_first(), is_slab(odd)))
    def _():
        def store(at, span, mixed):
            cols = slice(first + at.start, first + at.stop)
            gated = queries_ref[0, span, cols].astype(F32) * mixed
            out_ref[span, at] = (residual_ref[span, cols].astype(F32) + gated).astype(BF16)

        line = first // LANES * share
        at = (shift, local)
        mix_all(width, share, lines_ref, line, table_ref, start_ref, behind_ref, product_ref, at, store)


def table_scratch(lines, width, total):
    groups, taps = lines.shape
    return pltpu.VMEM((width * groups // total * ROW_BLOCK, taps + ROW_BLOCK), BF16)


def own_of(odd, origin, start, lines, behind, product, queries, residual, first, width, weight, *after):
    rows, total = residual.shape
    return call(
        functools.partial(own_kernel, odd, first, first - origin, first - RAW),
        "own",
        array(rows, width),
        [SMEM] + [VMEM] * 5 + [ANY] * len(after),
        VMEM,
        [table_scratch(lines, width, total)],
        weight=weight,
    )(start, lines, behind, product, queries, residual, *after)


def pick_kernel(raw_ref, received_ref, tail_ref, _, queries_ref, product_ref):
    rows = queries_ref.shape[0]

    def take(source):
        queries_ref[...] = source[:rows, :]
        product_ref[:, :RAW] = source[rows:, :]

    pl.when(is_first())(lambda: take(raw_ref))

    @pl.when(jnp.logical_not(is_first()))
    def _():
        take(received_ref)
        product_ref[:, RAW:] = tail_ref[...]


def pick_of(raw, received, tail, after):
    rows, width = raw.shape[0] // 2, raw.shape[1]
    return call(
        pick_kernel,
        "pick",
        (array(rows, width), array(rows, 2 * width)),
        [VMEM, VMEM, VMEM, ANY],
        (VMEM,) * 2,
        weight=SLOW,
    )(raw, received, tail, after)


def hold_kernel(value_ref, _, out_ref):
    pass


def held_back(value, after, weight=QUICK):
    return call(
        hold_kernel, "hold", array(*value.shape), [ANY, ANY], ANY, weight=weight, aliases={0: 0}
    )(value, after)


def send_out(pieces, out_ref, sems):
    copies = [
        pltpu.make_async_copy(buffer, out_ref.at[0, :, pl.ds(first, buffer.shape[1])], sems.at[place])
        for place, (buffer, first) in enumerate(pieces)
    ]
    for copy in copies:
        copy.start()
    return copies


def wait_all(copies):
    for copy in copies:
        copy.wait()


def later_kernel(places, *refs):
    start_ref, lines_ref, near_behind, near_ref, far_behind, far_ref, raw_behind, tail_ref, queries_ref = refs[:9]
    own_refs = refs[9 : 9 + len(places)]
    out_ref, gated_ref, table_ref, sems = refs[-4:]
    total = queries_ref.shape[2]
    share = share_of(lines_ref, total)

    for odd in (0, 1):

        @pl.when(jnp.logical_and(is_first(), is_slab(odd)))
        def _():
            pieces = [(own_ref, first) for own_ref, (side, first, _) in zip(own_refs, places) if side == odd]
            wait_all(send_out(pieces, out_ref, sems))

    @pl.when(jnp.logical_not(is_first()))
    def _():
        parts = (
            (0, 0, near_behind, near_ref),
            (NEAR, 0, far_behind, far_ref),
            (total - RAW, RAW, raw_behind, tail_ref),
        )
        for first, skip, behind_ref, product_ref in parts:

            def store(at, span, mixed):
                cols = slice(first + at.start, first + at.stop)
                gated_ref[span, cols] = queries_ref[0, span, cols].astype(F32) * mixed

            width, line = product_ref.shape[1], first // LANES * share
            at = (skip, 0)
            mix_all(width, share, lines_ref, line, table_ref, start_ref, behind_ref, product_ref, at, store)


def later_of(start, lines, near_behind, near, far_behind, far, raw_behind, tail, queries, own, places):
    rows, total = queries.shape[1:]
    return call(
        functools.partial(later_kernel, places),
        "later",
        (jax.ShapeDtypeStruct((1, rows, total), BF16), array(rows, total, F32)),
        [SMEM] + [VMEM] * (8 + len(own)),
        (ANY, VMEM),
        [table_scratch(lines, total - RAW - NEAR, total), pltpu.SemaphoreType.DMA((len(own),))],
        weight=SLOW,
    )(start, lines, near_behind, near, far_behind, far, raw_behind, tail, queries, *own)


def raw_kernel(*refs):
    start_ref, lines_ref, wire_ref, behind_ref, product_ref, queries_ref, gated_ref, residual_ref = refs[:8]
    out_ref, chosen_ref, table_ref, buffer, sems = refs[9:]
    width = buffer.shape[1]
    share = share_of(lines_ref, residual_ref.shape[1])

    @pl.when(is_first())
    def _():
        chosen_ref[...] = lines_ref[: chosen_ref.shape[0], :]

    @pl.when(jnp.logical_not(is_first()))
    def _():
        chosen_ref[...] = wire_ref[...].astype(F32)

    def store(at, span, mixed):
        gated = queries_ref[span, at].astype(F32) * mixed
        buffer[span, at] = (residual_ref[span, at].astype(F32) + gated).astype(BF16)

    mix_all(width, share, chosen_ref, 0, table_ref, start_ref, behind_ref, product_ref, (0, 0), store)

    @pl.when(jnp.logical_not(is_first()))
    def _():
        buffer[...] = (buffer[...].astype(F32) + gated_ref[:, :width]).astype(BF16)

    wait_all(send_out([(buffer, 0)], out_ref, sems))


def raw_finish(held, start, lines, wire, behind, product, queries, gated, residual):
    rows, width = queries.shape
    total = residual.shape[1]
    return call(
        raw_kernel,
        "raw",
        jax.ShapeDtypeStruct(held.shape, BF16),
        [SMEM] + [VMEM] * 7 + [ANY],
        ANY,
        [
            pltpu.VMEM(wire.shape, F32),
            table_scratch(lines, width, total),
            pltpu.VMEM((rows, width), BF16),
            pltpu.SemaphoreType.DMA((1,)),
        ],
        weight=SLOW,
        aliases={8: 0},
    )(start, lines, wire, behind, product, queries, gated, residual, held)


def finish_kernel(odd, places, *refs):
    gated_ref, received_refs = refs[0], refs[1 : 1 + len(places)]
    out_ref, *buffers, sems = refs[2 + len(places) :]

    @pl.when(jnp.logical_and(jnp.logical_not(is_first()), is_slab(odd)))
    def _():
        copies = []
        for place, (_, first, width) in enumerate(places):
            buffer = buffers[place]
            total = received_refs[place][...].astype(F32) + gated_ref[:, first : first + width]
            buffer[...] = total.astype(BF16)
            copies += send_out([(buffer, first)], out_ref, sems.at[pl.ds(place, 1)])
        wait_all(copies)


def finish(held, gated, received, places):
    rows = gated.shape[0]
    count = len(places)
    return call(
        functools.partial(finish_kernel, places[0][0], places),
        "finish",
        jax.ShapeDtypeStruct(held.shape, BF16),
        [VMEM] * (1 + count) + [ANY],
        ANY,
        [pltpu.VMEM((rows, width), BF16) for _, _, width in places] + [pltpu.SemaphoreType.DMA((count,))],
        weight=SLOW,
        aliases={1 + count: 0},
    )(gated, *received, held)


def body(queries, keys, values, residual, filter_bank, filter_scales, group_filter, context_start):
    total = queries.shape[2]
    small = (filter_bank, filter_scales, group_filter)
    far_queries, keys, values = (
        pltpu.with_memory_space_constraint(value, pltpu.HBM) for value in (queries, keys, values)
    )
    raw, rest = lead_of(far_queries, keys, values)
    raw_received = to_next_section(raw)
    chip_behind = to_next_slab(rest, (0, 0))
    lines, wire, near, far, tail = product_of(keys, values, *small, rest)
    own, received, places = [], [], []

    def send(odd, behind, origin, first, width, *after):
        piece = own_of(
            odd, origin, context_start, lines, behind, rest, queries, residual, first, width, QUICK, *after
        )
        own.append(piece)
        received.append(to_next_section(piece, (odd,)))
        places.append((odd, first, width))
        return first + width, piece

    links = ((1, 0), (0, 1), (1, 1))
    first, after = send(1, chip_behind, RAW, RAW, ODD[0], lines)
    near = held_back(near, after)
    near_behind = to_next_slab(near, *links)
    first, after = send(1, chip_behind, RAW, first, ODD[1], near)
    raw_queries, raw_product = pick_of(raw, raw_received, tail, after)
    far = held_back(far, raw_queries)
    far_behind = to_next_slab(far, *links)
    raw_product = held_back(raw_product, far)
    raw_behind = to_next_slab(raw_product, (0, 0), *links)
    raw_queries = held_back(raw_queries, received[0], SLOW)
    first, after = send(0, near_behind, RAW, RAW, EVEN[0], raw_queries)
    first, after = send(0, near_behind, RAW, first, EVEN[1], after)
    origin = first
    first, after = send(0, far_behind, origin, first, EVEN[2], after, received[1])
    first, after = send(0, far_behind, origin, first, EVEN[3], after, raw_behind)
    wire_received = to_next_section(held_back(wire, after))
    held, gated = later_of(
        context_start,
        lines,
        near_behind,
        near,
        far_behind,
        far,
        raw_behind,
        tail,
        queries,
        own,
        places,
    )
    odd = len(ODD)
    held = finish(held, gated, received[:odd], places[:odd])
    held = finish(held, gated, received[odd : odd + 2], places[odd : odd + 2])
    held = raw_finish(
        held, context_start, lines, wire_received, raw_behind, raw_product, raw_queries, gated, residual
    )
    for last in (odd + 2, odd + 3):
        held = finish(held, gated, received[last : last + 1], places[last : last + 1])
    return held


def solution(mesh):
    return jax.shard_map(
        body,
        mesh=mesh,
        in_specs=(
            P("pipe", ("dp", "ctx"), None),
            P("pipe", ("dp", "ctx"), None),
            P("pipe", ("dp", "ctx"), None),
            P(("dp", "ctx"), None),
            P("pipe", None, None),
            P("pipe", None),
            P("pipe", None),
            P("dp"),
        ),
        out_specs=P("pipe", ("dp", "ctx"), None),
        check_vma=False,
    )
```

```python
import functools

import jax
import jax.numpy as jnp
from jax import lax
from jax.experimental import pallas as pl
from jax.experimental.pallas import tpu as pltpu
from jax.sharding import PartitionSpec as P

LANES = 128
ROW_BLOCK = 32
RAW = 384
ODD = (1536, 2176)
EVEN = (1024, 768, 896, 1024)
PIECES = 4
LINES = 8
NEAR = 1792
F32 = jnp.float32
BF16 = jnp.bfloat16
MIB = 1024 * 1024
QUICK, SLOW = 1024, 20_000_000_000

SMEM = pl.BlockSpec(memory_space=pltpu.SMEM)
VMEM = pl.BlockSpec(memory_space=pltpu.VMEM)
ANY = pl.BlockSpec(memory_space=pl.ANY)
HBM = pl.BlockSpec(memory_space=pltpu.HBM)


def to_next_slab(value, *links):
    slabs, depth = lax.axis_size("ctx"), lax.axis_size("pipe")
    pairs = [
        (slab * depth + pipe, (slab + 1) * depth + pipe)
        for odd, pipe in links
        for slab in range(slabs - 1)
        if slab % 2 == odd
    ]
    return lax.ppermute(value, ("ctx", "pipe"), pairs)


def to_next_section(value, slabs=(0, 1)):
    depth = lax.axis_size("pipe")
    pairs = [(slab * depth, slab * depth + 1) for slab in range(lax.axis_size("ctx")) if slab % 2 in slabs]
    return lax.ppermute(value, ("ctx", "pipe"), pairs)


def call(kernel, name, out_shape, in_specs, out_specs, scratch=(), weight=QUICK, aliases=None):
    return pl.pallas_call(
        kernel,
        out_shape=out_shape,
        in_specs=in_specs,
        out_specs=out_specs,
        scratch_shapes=list(scratch),
        input_output_aliases=aliases or {},
        compiler_params=pltpu.CompilerParams(vmem_limit_bytes=16 * MIB),
        cost_estimate=pl.CostEstimate(flops=weight, bytes_accessed=1024, transcendentals=0),
        name=name,
    )


def is_first():
    return lax.axis_index("pipe") == 0


def is_slab(odd):
    return lax.axis_index("ctx") % 2 == odd


def array(rows, cols, kind=BF16):
    return jax.ShapeDtypeStruct((rows, cols), kind)


def multiply(keys_ref, values_ref, keys_in, values_in, sems, out_refs, meanwhile):
    rows = out_refs[0].shape[0]
    step = rows // PIECES
    spans = [pl.ds(piece * step, step) for piece in range(PIECES)]
    copies = []
    for piece, span in enumerate(spans):
        copies.append(
            (
                pltpu.make_async_copy(keys_ref.at[0, span], keys_in.at[span], sems.at[2 * piece]),
                pltpu.make_async_copy(values_ref.at[0, span], values_in.at[span], sems.at[2 * piece + 1]),
            )
        )
        for copy in copies[-1]:
            copy.start()
    meanwhile()
    for span, pair in zip(spans, copies):
        for copy in pair:
            copy.wait()
        first = 0
        for out_ref in out_refs:
            for tile in range(0, out_ref.shape[1], LANES):
                at = slice(first + tile, first + tile + LANES)
                product = keys_in[span, at].astype(F32) * values_in[span, at].astype(F32)
                out_ref[span, tile : tile + LANES] = product.astype(BF16)
            first += out_ref.shape[1]


def fill_lines(bank, scales, assign, lines_ref):
    groups, taps = lines_ref.shape
    size = bank.shape[0]
    chosen = (lax.broadcasted_iota(jnp.int32, (size, groups), 0) == assign).astype(F32).astype(BF16)
    contract = (((0,), (0,)), ((), ()))
    picked = lax.dot_general(bank, chosen, contract, preferred_element_type=F32)
    scaled = (picked * scales).astype(BF16)
    order = lax.broadcasted_iota(jnp.int32, (taps, taps), 0) + lax.broadcasted_iota(jnp.int32, (taps, taps), 1)
    flip = (order == taps - 1).astype(F32).astype(BF16)
    lines_ref[...] = lax.dot_general(scaled, flip, contract, preferred_element_type=F32)


def lead_kernel(queries_ref, keys_ref, values_ref, raw_ref, rest_ref, keys_in, values_in, sems, own_sem):
    rows = rest_ref.shape[0]

    @pl.when(is_first())
    def _():
        source = queries_ref.at[0, :, pl.ds(0, RAW)]
        copy = pltpu.make_async_copy(source, raw_ref.at[pl.ds(0, rows)], own_sem)
        targets = [raw_ref.at[pl.ds(rows, rows)], rest_ref]
        multiply(keys_ref, values_ref, keys_in, values_in, sems, targets, copy.start)
        copy.wait()


def product_scratch(rows, total):
    return [pltpu.VMEM((rows, total), BF16), pltpu.VMEM((rows, total), BF16), pltpu.SemaphoreType.DMA((2 * PIECES,))]


def lead_of(queries, keys, values):
    rows, total = queries.shape[1:]
    return call(
        lead_kernel,
        "lead",
        (array(2 * rows, RAW), array(rows, total - RAW)),
        [HBM] * 3,
        (VMEM,) * 2,
        product_scratch(rows, total) + [pltpu.SemaphoreType.DMA(())],
    )(queries, keys, values)


def turn_table(lines_ref, row, count, table_ref, at):
    taps = lines_ref.shape[1]
    upper = lax.broadcasted_iota(jnp.int32, (ROW_BLOCK, taps), 1) > lax.broadcasted_iota(
        jnp.int32, (ROW_BLOCK, taps), 0
    )
    for group in range(count):
        line = lines_ref[row + group : row + group + 1, :]
        turned = pltpu.roll(jnp.broadcast_to(line, (ROW_BLOCK, taps)), 1, 1, stride=1, stride_axis=0)
        span = slice(at + group * ROW_BLOCK, at + (group + 1) * ROW_BLOCK)
        table_ref[span, :taps] = jnp.where(upper, turned, 0.0).astype(BF16)
        table_ref[span, taps:] = jnp.where(upper, 0.0, turned)[:, :ROW_BLOCK].astype(BF16)


def product_kernel(*refs):
    keys_ref, values_ref, bank_ref, scales_ref, assign_ref, rest_ref = refs[:6]
    lines_ref, wire_ref, near_ref, far_ref, tail_ref, keys_in, values_in, sems = refs[6:]

    def taps():
        fill_lines(bank_ref[0], scales_ref[...], assign_ref[...], lines_ref)

    @pl.when(is_first())
    def _():
        taps()
        wire_ref[...] = lines_ref[: wire_ref.shape[0], :].astype(BF16)

    @pl.when(jnp.logical_and(is_first(), is_slab(1)))
    def _():
        near_ref[...] = rest_ref[:, :NEAR]
        far_ref[...] = rest_ref[:, NEAR:]

    @pl.when(jnp.logical_not(is_first()))
    def _():
        multiply(keys_ref, values_ref, keys_in, values_in, sems, [near_ref, far_ref, tail_ref], taps)


def wire_rows(groups, total):
    return -(-RAW * groups // (total * 16)) * 16


def product_of(keys, values, bank, scales, assign, rest):
    rows, total = keys.shape[1:]
    groups, taps = assign.shape[1], bank.shape[2]
    return call(
        product_kernel,
        "product",
        (
            array(groups, taps, F32),
            array(wire_rows(groups, total), taps),
            array(rows, NEAR),
            array(rows, total - RAW - NEAR),
            array(rows, RAW),
        ),
        [HBM, HBM] + [VMEM] * 4,
        (VMEM,) * 5,
        product_scratch(rows, total),
    )(keys, values, bank, scales, assign, rest)


def mix(table_ref, row, share, window, store):
    depth = table_ref.shape[1]
    rows = window.shape[0] - depth + ROW_BLOCK
    member = lax.broadcasted_iota(jnp.int32, (ROW_BLOCK, LANES), 1) // (LANES // share)
    table = table_ref[row : row + share * ROW_BLOCK, :]
    for first in range(0, rows, 2 * ROW_BLOCK):
        starts = (first, first + ROW_BLOCK)
        pair = jnp.concatenate([window[begin : begin + depth] for begin in starts], axis=1)
        sums = jnp.dot(table, pair, preferred_element_type=F32)
        for place, begin in enumerate(starts):
            part = sums[:, place * LANES : (place + 1) * LANES]
            mixed = part[:ROW_BLOCK]
            for group in range(1, share):
                mixed = jnp.where(member == group, part[group * ROW_BLOCK : (group + 1) * ROW_BLOCK], mixed)
            store(slice(begin, begin + ROW_BLOCK), mixed)


def mix_all(width, share, lines_ref, line, table_ref, start_ref, behind_ref, product_ref, local, store):
    rows = product_ref.shape[0]
    first = (lax.axis_index("ctx") - 1) * rows
    inside = first + lax.broadcasted_iota(jnp.int32, (2 * rows, LANES), 0) >= start_ref[0]
    for tile in range(width // LANES):
        at = slice(tile * LANES, (tile + 1) * LANES)
        near, inner = (slice(begin + at.start, begin + at.stop) for begin in local)
        row = tile * share * ROW_BLOCK
        turn_table(lines_ref, line + tile * share, share, table_ref, row)
        window = jnp.concatenate([behind_ref[:, near], product_ref[:, inner]], axis=0)
        window = jnp.where(inside, window, jnp.zeros_like(window))
        mix(table_ref, row, share, window, functools.partial(store, at))


def share_of(lines_ref, total):
    return LANES * lines_ref.shape[0] // total


def own_kernel(odd, first, shift, local, extra, *refs):
    start_ref, lines_ref, behind_ref, product_ref, queries_ref, residual_ref = refs[:6]
    out_ref, table_ref = refs[-2:]
    width = out_ref.shape[1]
    share = share_of(lines_ref, residual_ref.shape[1])

    @pl.when(jnp.logical_and(is_first(), is_slab(odd)))
    def _():
        def store(at, span, mixed):
            cols = slice(first + at.start, first + at.stop)
            gated = queries_ref[0, span, cols].astype(F32) * mixed
            out_ref[span, at] = (residual_ref[span, cols].astype(F32) + gated).astype(BF16)

        line = first // LANES * share
        at = (shift, local)
        mix_all(width, share, lines_ref, line, table_ref, start_ref, behind_ref, product_ref, at, store)
        if extra:
            rows = out_ref.shape[0] - extra
            for part in range(RAW // LANES):
                taken = lines_ref[part * extra : (part + 1) * extra, :].astype(BF16)
                out_ref[rows:, part * LANES : (part + 1) * LANES] = taken


def table_scratch(lines, width, total):
    groups, taps = lines.shape
    return pltpu.VMEM((width * groups // total * ROW_BLOCK, taps + ROW_BLOCK), BF16)


def own_of(odd, origin, extra, start, lines, behind, product, queries, residual, first, width, *after):
    rows, total = residual.shape
    return call(
        functools.partial(own_kernel, odd, first, first - origin, first - RAW, extra),
        "own",
        array(rows + extra, width),
        [SMEM] + [VMEM] * 5 + [ANY] * len(after),
        VMEM,
        [table_scratch(lines, width, total)],
    )(start, lines, behind, product, queries, residual, *after)


def pick_kernel(raw_ref, received_ref, tail_ref, _, queries_ref, product_ref):
    rows = queries_ref.shape[0]

    def take(source):
        queries_ref[...] = source[:rows, :]
        product_ref[:, :RAW] = source[rows:, :]

    pl.when(is_first())(lambda: take(raw_ref))

    @pl.when(jnp.logical_not(is_first()))
    def _():
        take(received_ref)
        product_ref[:, RAW:] = tail_ref[...]


def pick_of(raw, received, tail, after):
    rows, width = raw.shape[0] // 2, raw.shape[1]
    return call(
        pick_kernel,
        "pick",
        (array(rows, width), array(rows, 2 * width)),
        [VMEM, VMEM, VMEM, ANY],
        (VMEM,) * 2,
        weight=SLOW,
    )(raw, received, tail, after)


def hold_kernel(value_ref, _, out_ref):
    pass


def held_back(value, after, weight=QUICK):
    return call(
        hold_kernel, "hold", array(*value.shape), [ANY, ANY], ANY, weight=weight, aliases={0: 0}
    )(value, after)


def send_out(pieces, out_ref, sems):
    copies = [
        pltpu.make_async_copy(buffer, out_ref.at[0, :, pl.ds(first, buffer.shape[1])], sems.at[place])
        for place, (buffer, first) in enumerate(pieces)
    ]
    for copy in copies:
        copy.start()
    return copies


def wait_all(copies):
    for copy in copies:
        copy.wait()


def later_kernel(places, *refs):
    start_ref, lines_ref, near_behind, near_ref, far_behind, far_ref, raw_behind, tail_ref, queries_ref = refs[:9]
    own_refs = refs[9 : 9 + len(places)]
    out_ref, gated_ref, table_ref, sems = refs[-4:]
    total = queries_ref.shape[2]
    share = share_of(lines_ref, total)

    for odd in (0, 1):

        @pl.when(jnp.logical_and(is_first(), is_slab(odd)))
        def _():
            pieces = [
                (own_ref.at[pl.ds(0, out_ref.shape[1])], first)
                for own_ref, (side, first, _) in zip(own_refs, places)
                if side == odd
            ]
            wait_all(send_out(pieces, out_ref, sems))

    @pl.when(jnp.logical_not(is_first()))
    def _():
        parts = (
            (0, 0, near_behind, near_ref),
            (NEAR, 0, far_behind, far_ref),
            (total - RAW, RAW, raw_behind, tail_ref),
        )
        for first, skip, behind_ref, product_ref in parts:

            def store(at, span, mixed):
                cols = slice(first + at.start, first + at.stop)
                gated_ref[span, cols] = queries_ref[0, span, cols].astype(F32) * mixed

            width, line = product_ref.shape[1], first // LANES * share
            at = (skip, 0)
            mix_all(width, share, lines_ref, line, table_ref, start_ref, behind_ref, product_ref, at, store)


def later_of(start, lines, near_behind, near, far_behind, far, raw_behind, tail, queries, own, places):
    rows, total = queries.shape[1:]
    return call(
        functools.partial(later_kernel, places),
        "later",
        (jax.ShapeDtypeStruct((1, rows, total), BF16), array(rows, total, F32)),
        [SMEM] + [VMEM] * (8 + len(own)),
        (ANY, VMEM),
        [table_scratch(lines, total - RAW - NEAR, total), pltpu.SemaphoreType.DMA((len(own),))],
        weight=SLOW,
    )(start, lines, near_behind, near, far_behind, far, raw_behind, tail, queries, *own)


def raw_kernel(*refs):
    start_ref, lines_ref, wire_ref, received_ref = refs[:4]
    behind_ref, product_ref, queries_ref, gated_ref, residual_ref = refs[4:9]
    out_ref, chosen_ref, table_ref, buffer, sems = refs[10:]
    rows, width = buffer.shape
    share = share_of(lines_ref, residual_ref.shape[1])

    @pl.when(is_first())
    def _():
        chosen_ref[...] = lines_ref[: chosen_ref.shape[0], :]

    @pl.when(jnp.logical_and(jnp.logical_not(is_first()), is_slab(1)))
    def _():
        chosen_ref[...] = wire_ref[...].astype(F32)

    @pl.when(jnp.logical_and(jnp.logical_not(is_first()), is_slab(0)))
    def _():
        for part in range(RAW // LANES):
            taken = received_ref[rows:, part * LANES : (part + 1) * LANES]
            chosen_ref[part * LINES : (part + 1) * LINES, :] = taken.astype(F32)

    def store(at, span, mixed):
        gated = queries_ref[span, at].astype(F32) * mixed
        buffer[span, at] = (residual_ref[span, at].astype(F32) + gated).astype(BF16)

    mix_all(width, share, chosen_ref, 0, table_ref, start_ref, behind_ref, product_ref, (0, 0), store)

    @pl.when(jnp.logical_not(is_first()))
    def _():
        buffer[...] = (buffer[...].astype(F32) + gated_ref[:, :width]).astype(BF16)

    wait_all(send_out([(buffer, 0)], out_ref, sems))


def raw_finish(held, start, lines, wire, received, behind, product, queries, gated, residual):
    rows, width = queries.shape
    total = residual.shape[1]
    return call(
        raw_kernel,
        "raw",
        jax.ShapeDtypeStruct(held.shape, BF16),
        [SMEM] + [VMEM] * 8 + [ANY],
        ANY,
        [
            pltpu.VMEM(wire.shape, F32),
            table_scratch(lines, width, total),
            pltpu.VMEM((rows, width), BF16),
            pltpu.SemaphoreType.DMA((1,)),
        ],
        weight=SLOW,
        aliases={9: 0},
    )(start, lines, wire, received, behind, product, queries, gated, residual, held)


def finish_kernel(odd, places, *refs):
    gated_ref, received_refs = refs[0], refs[1 : 1 + len(places)]
    out_ref, *buffers, sems = refs[2 + len(places) :]

    @pl.when(jnp.logical_and(jnp.logical_not(is_first()), is_slab(odd)))
    def _():
        copies = []
        for place, (_, first, width) in enumerate(places):
            buffer = buffers[place]
            total = received_refs[place][: buffer.shape[0], :].astype(F32) + gated_ref[:, first : first + width]
            buffer[...] = total.astype(BF16)
            copies += send_out([(buffer, first)], out_ref, sems.at[pl.ds(place, 1)])
        wait_all(copies)


def finish(held, gated, received, places):
    rows = gated.shape[0]
    count = len(places)
    return call(
        functools.partial(finish_kernel, places[0][0], places),
        "finish",
        jax.ShapeDtypeStruct(held.shape, BF16),
        [VMEM] * (1 + count) + [ANY],
        ANY,
        [pltpu.VMEM((rows, width), BF16) for _, _, width in places] + [pltpu.SemaphoreType.DMA((count,))],
        weight=SLOW,
        aliases={1 + count: 0},
    )(gated, *received, held)


def body(queries, keys, values, residual, filter_bank, filter_scales, group_filter, context_start):
    total = queries.shape[2]
    small = (filter_bank, filter_scales, group_filter)
    far_queries, keys, values = (
        pltpu.with_memory_space_constraint(value, pltpu.HBM) for value in (queries, keys, values)
    )
    raw, rest = lead_of(far_queries, keys, values)
    raw_received = to_next_section(raw)
    chip_behind = to_next_slab(rest, (0, 0))
    lines, wire, near, far, tail = product_of(keys, values, *small, rest)
    own, received, places = [], [], []

    def send(odd, behind, origin, first, width, *after, extra=0):
        piece = own_of(
            odd, origin, extra, context_start, lines, behind, rest, queries, residual, first, width, *after
        )
        own.append(piece)
        received.append(to_next_section(piece, (odd,)))
        places.append((odd, first, width))
        return first + width, piece

    links = ((1, 0), (0, 1), (1, 1))
    first, after = send(1, chip_behind, RAW, RAW, ODD[0], lines)
    near = held_back(near, after)
    near_behind = to_next_slab(near, *links)
    first, after = send(1, chip_behind, RAW, first, ODD[1], near)
    raw_queries, raw_product = pick_of(raw, raw_received, tail, after)
    far = held_back(far, raw_queries)
    far_behind = to_next_slab(far, *links)
    raw_product = held_back(raw_product, far)
    raw_behind = to_next_slab(raw_product, (0, 0), *links)
    raw_queries = held_back(raw_queries, received[0], SLOW)
    first, after = send(0, near_behind, RAW, RAW, EVEN[0], raw_queries)
    first, after = send(0, near_behind, RAW, first, EVEN[1], after, extra=LINES)
    origin = first
    first, after = send(0, far_behind, origin, first, EVEN[2], after, received[1])
    first, after = send(0, far_behind, origin, first, EVEN[3], after, raw_behind)
    wire_received = to_next_section(held_back(wire, after), (1,))
    held, gated = later_of(
        context_start,
        lines,
        near_behind,
        near,
        far_behind,
        far,
        raw_behind,
        tail,
        queries,
        own,
        places,
    )
    odd = len(ODD)
    held = finish(held, gated, received[:odd], places[:odd])
    held = finish(held, gated, received[odd : odd + 2], places[odd : odd + 2])
    held = raw_finish(
        held,
        context_start,
        lines,
        wire_received,
        received[odd + 1],
        raw_behind,
        raw_product,
        raw_queries,
        gated,
        residual,
    )
    for last in (odd + 2, odd + 3):
        held = finish(held, gated, received[last : last + 1], places[last : last + 1])
    return held


def solution(mesh):
    return jax.shard_map(
        body,
        mesh=mesh,
        in_specs=(
            P("pipe", ("dp", "ctx"), None),
            P("pipe", ("dp", "ctx"), None),
            P("pipe", ("dp", "ctx"), None),
            P(("dp", "ctx"), None),
            P("pipe", None, None),
            P("pipe", None),
            P("pipe", None),
            P("dp"),
        ),
        out_specs=P("pipe", ("dp", "ctx"), None),
        check_vma=False,
    )
```

```python
import functools

import jax
import jax.numpy as jnp
from jax import lax
from jax.experimental import pallas as pl
from jax.experimental.pallas import tpu as pltpu
from jax.sharding import PartitionSpec as P

LANES = 128
ROW_BLOCK = 32
RAW = 384
ODD = (1536, 2176)
EVEN = (1024, 896, 1280, 512)
PIECES = 4
LINES = 8
NEAR = 1920
F32 = jnp.float32
BF16 = jnp.bfloat16
MIB = 1024 * 1024
QUICK, SLOW = 1024, 20_000_000_000

SMEM = pl.BlockSpec(memory_space=pltpu.SMEM)
VMEM = pl.BlockSpec(memory_space=pltpu.VMEM)
ANY = pl.BlockSpec(memory_space=pl.ANY)
HBM = pl.BlockSpec(memory_space=pltpu.HBM)


def to_next_slab(value, *links):
    slabs, depth = lax.axis_size("ctx"), lax.axis_size("pipe")
    pairs = [
        (slab * depth + pipe, (slab + 1) * depth + pipe)
        for odd, pipe in links
        for slab in range(slabs - 1)
        if slab % 2 == odd
    ]
    return lax.ppermute(value, ("ctx", "pipe"), pairs)


def to_next_section(value, slabs=(0, 1)):
    depth = lax.axis_size("pipe")
    pairs = [(slab * depth, slab * depth + 1) for slab in range(lax.axis_size("ctx")) if slab % 2 in slabs]
    return lax.ppermute(value, ("ctx", "pipe"), pairs)


def call(kernel, name, out_shape, in_specs, out_specs, scratch=(), weight=QUICK, aliases=None):
    return pl.pallas_call(
        kernel,
        out_shape=out_shape,
        in_specs=in_specs,
        out_specs=out_specs,
        scratch_shapes=list(scratch),
        input_output_aliases=aliases or {},
        compiler_params=pltpu.CompilerParams(vmem_limit_bytes=16 * MIB),
        cost_estimate=pl.CostEstimate(flops=weight, bytes_accessed=1024, transcendentals=0),
        name=name,
    )


def is_first():
    return lax.axis_index("pipe") == 0


def is_slab(odd):
    return lax.axis_index("ctx") % 2 == odd


def array(rows, cols, kind=BF16):
    return jax.ShapeDtypeStruct((rows, cols), kind)


def multiply(keys_ref, values_ref, keys_in, values_in, sems, out_refs, meanwhile):
    rows = out_refs[0].shape[0]
    step = rows // PIECES
    spans = [pl.ds(piece * step, step) for piece in range(PIECES)]
    copies = []
    for piece, span in enumerate(spans):
        copies.append(
            (
                pltpu.make_async_copy(keys_ref.at[0, span], keys_in.at[span], sems.at[2 * piece]),
                pltpu.make_async_copy(values_ref.at[0, span], values_in.at[span], sems.at[2 * piece + 1]),
            )
        )
        for copy in copies[-1]:
            copy.start()
    meanwhile()
    for span, pair in zip(spans, copies):
        for copy in pair:
            copy.wait()
        first = 0
        for out_ref in out_refs:
            for tile in range(0, out_ref.shape[1], LANES):
                at = slice(first + tile, first + tile + LANES)
                product = keys_in[span, at].astype(F32) * values_in[span, at].astype(F32)
                out_ref[span, tile : tile + LANES] = product.astype(BF16)
            first += out_ref.shape[1]


def fill_lines(bank, scales, assign, lines_ref):
    groups, taps = lines_ref.shape
    size = bank.shape[0]
    chosen = (lax.broadcasted_iota(jnp.int32, (size, groups), 0) == assign).astype(F32).astype(BF16)
    contract = (((0,), (0,)), ((), ()))
    picked = lax.dot_general(bank, chosen, contract, preferred_element_type=F32)
    scaled = (picked * scales).astype(BF16)
    order = lax.broadcasted_iota(jnp.int32, (taps, taps), 0) + lax.broadcasted_iota(jnp.int32, (taps, taps), 1)
    flip = (order == taps - 1).astype(F32).astype(BF16)
    lines_ref[...] = lax.dot_general(scaled, flip, contract, preferred_element_type=F32)


def lead_kernel(queries_ref, keys_ref, values_ref, raw_ref, rest_ref, keys_in, values_in, sems, own_sem):
    rows = rest_ref.shape[0]

    @pl.when(is_first())
    def _():
        source = queries_ref.at[0, :, pl.ds(0, RAW)]
        copy = pltpu.make_async_copy(source, raw_ref.at[pl.ds(0, rows)], own_sem)
        targets = [raw_ref.at[pl.ds(rows, rows)], rest_ref]
        multiply(keys_ref, values_ref, keys_in, values_in, sems, targets, copy.start)
        copy.wait()


def product_scratch(rows, total):
    return [pltpu.VMEM((rows, total), BF16), pltpu.VMEM((rows, total), BF16), pltpu.SemaphoreType.DMA((2 * PIECES,))]


def lead_of(queries, keys, values):
    rows, total = queries.shape[1:]
    return call(
        lead_kernel,
        "lead",
        (array(2 * rows, RAW), array(rows, total - RAW)),
        [HBM] * 3,
        (VMEM,) * 2,
        product_scratch(rows, total) + [pltpu.SemaphoreType.DMA(())],
    )(queries, keys, values)


def turn_table(lines_ref, row, count, table_ref, at):
    taps = lines_ref.shape[1]
    upper = lax.broadcasted_iota(jnp.int32, (ROW_BLOCK, taps), 1) > lax.broadcasted_iota(
        jnp.int32, (ROW_BLOCK, taps), 0
    )
    for group in range(count):
        line = lines_ref[row + group : row + group + 1, :]
        turned = pltpu.roll(jnp.broadcast_to(line, (ROW_BLOCK, taps)), 1, 1, stride=1, stride_axis=0)
        span = slice(at + group * ROW_BLOCK, at + (group + 1) * ROW_BLOCK)
        table_ref[span, :taps] = jnp.where(upper, turned, 0.0).astype(BF16)
        table_ref[span, taps:] = jnp.where(upper, 0.0, turned)[:, :ROW_BLOCK].astype(BF16)


def product_kernel(*refs):
    keys_ref, values_ref, bank_ref, scales_ref, assign_ref, rest_ref = refs[:6]
    lines_ref, wire_ref, near_ref, far_ref, tail_ref, keys_in, values_in, sems = refs[6:]

    def taps():
        fill_lines(bank_ref[0], scales_ref[...], assign_ref[...], lines_ref)

    @pl.when(jnp.logical_and(is_first(), is_slab(1)))
    def _():
        taps()
        wire_ref[...] = lines_ref[: wire_ref.shape[0], :].astype(BF16)
        near_ref[...] = rest_ref[:, :NEAR]
        far_ref[...] = rest_ref[:, NEAR:]

    @pl.when(jnp.logical_not(is_first()))
    def _():
        multiply(keys_ref, values_ref, keys_in, values_in, sems, [near_ref, far_ref, tail_ref], taps)


def wire_rows(groups, total):
    return -(-RAW * groups // (total * 16)) * 16


def product_of(keys, values, bank, scales, assign, rest):
    rows, total = keys.shape[1:]
    groups, taps = assign.shape[1], bank.shape[2]
    return call(
        product_kernel,
        "product",
        (
            array(groups, taps, F32),
            array(wire_rows(groups, total), taps),
            array(rows, NEAR),
            array(rows, total - RAW - NEAR),
            array(rows, RAW),
        ),
        [HBM, HBM] + [VMEM] * 4,
        (VMEM,) * 5,
        product_scratch(rows, total),
    )(keys, values, bank, scales, assign, rest)


def mix(table_ref, row, share, window, store):
    depth = table_ref.shape[1]
    rows = window.shape[0] - depth + ROW_BLOCK
    member = lax.broadcasted_iota(jnp.int32, (ROW_BLOCK, LANES), 1) // (LANES // share)
    table = table_ref[row : row + share * ROW_BLOCK, :]
    for first in range(0, rows, 2 * ROW_BLOCK):
        starts = (first, first + ROW_BLOCK)
        pair = jnp.concatenate([window[begin : begin + depth] for begin in starts], axis=1)
        sums = jnp.dot(table, pair, preferred_element_type=F32)
        for place, begin in enumerate(starts):
            part = sums[:, place * LANES : (place + 1) * LANES]
            mixed = part[:ROW_BLOCK]
            for group in range(1, share):
                mixed = jnp.where(member == group, part[group * ROW_BLOCK : (group + 1) * ROW_BLOCK], mixed)
            store(slice(begin, begin + ROW_BLOCK), mixed)


def mix_all(width, share, lines_ref, line, table_ref, start_ref, behind_ref, product_ref, local, store):
    rows = product_ref.shape[0]
    first = (lax.axis_index("ctx") - 1) * rows
    inside = first + lax.broadcasted_iota(jnp.int32, (2 * rows, LANES), 0) >= start_ref[0]
    for tile in range(width // LANES):
        at = slice(tile * LANES, (tile + 1) * LANES)
        near, inner = (slice(begin + at.start, begin + at.stop) for begin in local)
        row = tile * share * ROW_BLOCK
        turn_table(lines_ref, line + tile * share, share, table_ref, row)
        window = jnp.concatenate([behind_ref[:, near], product_ref[:, inner]], axis=0)
        window = jnp.where(inside, window, jnp.zeros_like(window))
        mix(table_ref, row, share, window, functools.partial(store, at))


def share_of(lines_ref, total):
    return LANES * lines_ref.shape[0] // total


def own_kernel(odd, first, shift, local, extra, *refs):
    start_ref, lines_ref, behind_ref, product_ref, queries_ref, residual_ref = refs[:6]
    out_ref, table_ref = refs[-2:]
    width = out_ref.shape[1]
    share = share_of(lines_ref, residual_ref.shape[1])

    @pl.when(jnp.logical_and(is_first(), is_slab(odd)))
    def _():
        def store(at, span, mixed):
            cols = slice(first + at.start, first + at.stop)
            gated = queries_ref[0, span, cols].astype(F32) * mixed
            out_ref[span, at] = (residual_ref[span, cols].astype(F32) + gated).astype(BF16)

        line = first // LANES * share
        at = (shift, local)
        mix_all(width, share, lines_ref, line, table_ref, start_ref, behind_ref, product_ref, at, store)
        if extra:
            rows = out_ref.shape[0] - extra
            for part in range(RAW // LANES):
                taken = lines_ref[part * extra : (part + 1) * extra, :].astype(BF16)
                out_ref[rows:, part * LANES : (part + 1) * LANES] = taken


def table_scratch(lines, width, total):
    groups, taps = lines.shape
    return pltpu.VMEM((width * groups // total * ROW_BLOCK, taps + ROW_BLOCK), BF16)


def own_of(odd, origin, extra, start, lines, behind, product, queries, residual, first, width, *after):
    rows, total = residual.shape
    return call(
        functools.partial(own_kernel, odd, first, first - origin, first - RAW, extra),
        "own",
        array(rows + extra, width),
        [SMEM] + [VMEM] * 5 + [ANY] * len(after),
        VMEM,
        [table_scratch(lines, width, total)],
    )(start, lines, behind, product, queries, residual, *after)


def pick_kernel(*refs):
    raw_ref, received_ref, tail_ref, bank_ref, scales_ref, assign_ref = refs[:6]
    queries_ref, product_ref, lines_ref = refs[8:]
    rows = queries_ref.shape[0]

    @pl.when(jnp.logical_and(is_first(), is_slab(0)))
    def _():
        fill_lines(bank_ref[0], scales_ref[...], assign_ref[...], lines_ref)

    def take(source):
        queries_ref[...] = source[:rows, :]
        product_ref[:, :RAW] = source[rows:, :]

    pl.when(is_first())(lambda: take(raw_ref))

    @pl.when(jnp.logical_not(is_first()))
    def _():
        take(received_ref)
        product_ref[:, RAW:] = tail_ref[...]


def pick_of(raw, received, tail, bank, scales, assign, lines, after):
    rows, width = raw.shape[0] // 2, raw.shape[1]
    return call(
        pick_kernel,
        "pick",
        (array(rows, width), array(rows, 2 * width), array(*lines.shape, F32)),
        [VMEM] * 7 + [ANY],
        (VMEM,) * 3,
        weight=SLOW,
        aliases={6: 2},
    )(raw, received, tail, bank, scales, assign, lines, after)


def hold_kernel(value_ref, _, out_ref):
    pass


def held_back(value, after, weight=QUICK):
    return call(
        hold_kernel, "hold", array(*value.shape), [ANY, ANY], ANY, weight=weight, aliases={0: 0}
    )(value, after)


def send_out(pieces, out_ref, sems):
    copies = [
        pltpu.make_async_copy(buffer, out_ref.at[0, :, pl.ds(first, buffer.shape[1])], sems.at[place])
        for place, (buffer, first) in enumerate(pieces)
    ]
    for copy in copies:
        copy.start()
    return copies


def wait_all(copies):
    for copy in copies:
        copy.wait()


def later_kernel(places, *refs):
    start_ref, lines_ref, near_behind, near_ref, far_behind, far_ref, raw_behind, tail_ref, queries_ref = refs[:9]
    own_refs = refs[9 : 9 + len(places)]
    out_ref, gated_ref, table_ref, sems = refs[-4:]
    total = queries_ref.shape[2]
    share = share_of(lines_ref, total)

    for odd in (0, 1):

        @pl.when(jnp.logical_and(is_first(), is_slab(odd)))
        def _():
            pieces = [
                (own_ref.at[pl.ds(0, out_ref.shape[1])], first)
                for own_ref, (side, first, _) in zip(own_refs, places)
                if side == odd
            ]
            wait_all(send_out(pieces, out_ref, sems))

    @pl.when(jnp.logical_not(is_first()))
    def _():
        parts = (
            (0, 0, near_behind, near_ref),
            (NEAR, 0, far_behind, far_ref),
            (total - RAW, RAW, raw_behind, tail_ref),
        )
        for first, skip, behind_ref, product_ref in parts:

            def store(at, span, mixed):
                cols = slice(first + at.start, first + at.stop)
                gated_ref[span, cols] = queries_ref[0, span, cols].astype(F32) * mixed

            width, line = product_ref.shape[1], first // LANES * share
            at = (skip, 0)
            mix_all(width, share, lines_ref, line, table_ref, start_ref, behind_ref, product_ref, at, store)


def later_of(start, lines, near_behind, near, far_behind, far, raw_behind, tail, queries, own, places):
    rows, total = queries.shape[1:]
    return call(
        functools.partial(later_kernel, places),
        "later",
        (jax.ShapeDtypeStruct((1, rows, total), BF16), array(rows, total, F32)),
        [SMEM] + [VMEM] * (8 + len(own)),
        (ANY, VMEM),
        [table_scratch(lines, max(NEAR, total - RAW - NEAR), total), pltpu.SemaphoreType.DMA((len(own),))],
        weight=SLOW,
    )(start, lines, near_behind, near, far_behind, far, raw_behind, tail, queries, *own)


def raw_kernel(*refs):
    start_ref, lines_ref, wire_ref, received_ref = refs[:4]
    behind_ref, product_ref, queries_ref, gated_ref, residual_ref = refs[4:9]
    out_ref, chosen_ref, table_ref, buffer, sems = refs[10:]
    rows, width = buffer.shape
    share = share_of(lines_ref, residual_ref.shape[1])

    @pl.when(is_first())
    def _():
        chosen_ref[...] = lines_ref[: chosen_ref.shape[0], :]

    @pl.when(jnp.logical_and(jnp.logical_not(is_first()), is_slab(1)))
    def _():
        chosen_ref[...] = wire_ref[...].astype(F32)

    @pl.when(jnp.logical_and(jnp.logical_not(is_first()), is_slab(0)))
    def _():
        for part in range(RAW // LANES):
            taken = received_ref[rows:, part * LANES : (part + 1) * LANES]
            chosen_ref[part * LINES : (part + 1) * LINES, :] = taken.astype(F32)

    def store(at, span, mixed):
        gated = queries_ref[span, at].astype(F32) * mixed
        buffer[span, at] = (residual_ref[span, at].astype(F32) + gated).astype(BF16)

    mix_all(width, share, chosen_ref, 0, table_ref, start_ref, behind_ref, product_ref, (0, 0), store)

    @pl.when(jnp.logical_not(is_first()))
    def _():
        buffer[...] = (buffer[...].astype(F32) + gated_ref[:, :width]).astype(BF16)

    wait_all(send_out([(buffer, 0)], out_ref, sems))


def raw_finish(held, start, lines, wire, received, behind, product, queries, gated, residual):
    rows, width = queries.shape
    total = residual.shape[1]
    return call(
        raw_kernel,
        "raw",
        jax.ShapeDtypeStruct(held.shape, BF16),
        [SMEM] + [VMEM] * 8 + [ANY],
        ANY,
        [
            pltpu.VMEM(wire.shape, F32),
            table_scratch(lines, width, total),
            pltpu.VMEM((rows, width), BF16),
            pltpu.SemaphoreType.DMA((1,)),
        ],
        weight=SLOW,
        aliases={9: 0},
    )(start, lines, wire, received, behind, product, queries, gated, residual, held)


def finish_kernel(odd, places, *refs):
    gated_ref, received_refs = refs[0], refs[1 : 1 + len(places)]
    out_ref, *buffers, sems = refs[2 + len(places) :]

    @pl.when(jnp.logical_and(jnp.logical_not(is_first()), is_slab(odd)))
    def _():
        copies = []
        for place, (_, first, width) in enumerate(places):
            buffer = buffers[place]
            total = received_refs[place][: buffer.shape[0], :].astype(F32) + gated_ref[:, first : first + width]
            buffer[...] = total.astype(BF16)
            copies += send_out([(buffer, first)], out_ref, sems.at[pl.ds(place, 1)])
        wait_all(copies)


def finish(held, gated, received, places):
    rows = gated.shape[0]
    count = len(places)
    return call(
        functools.partial(finish_kernel, places[0][0], places),
        "finish",
        jax.ShapeDtypeStruct(held.shape, BF16),
        [VMEM] * (1 + count) + [ANY],
        ANY,
        [pltpu.VMEM((rows, width), BF16) for _, _, width in places] + [pltpu.SemaphoreType.DMA((count,))],
        weight=SLOW,
        aliases={1 + count: 0},
    )(gated, *received, held)


def body(queries, keys, values, residual, filter_bank, filter_scales, group_filter, context_start):
    total = queries.shape[2]
    small = (filter_bank, filter_scales, group_filter)
    far_queries, keys, values = (
        pltpu.with_memory_space_constraint(value, pltpu.HBM) for value in (queries, keys, values)
    )
    raw, rest = lead_of(far_queries, keys, values)
    raw_received = to_next_section(raw)
    chip_behind = to_next_slab(rest, (0, 0))
    lines, wire, near, far, tail = product_of(keys, values, *small, rest)
    own, received, places = [], [], []

    def send(odd, behind, origin, first, width, *after, extra=0):
        piece = own_of(
            odd, origin, extra, context_start, lines, behind, rest, queries, residual, first, width, *after
        )
        own.append(piece)
        received.append(to_next_section(piece, (odd,)))
        places.append((odd, first, width))
        return first + width, piece

    links = ((1, 0), (0, 1), (1, 1))
    first, after = send(1, chip_behind, RAW, RAW, ODD[0], lines)
    near = held_back(near, after)
    near_behind = to_next_slab(near, *links)
    first, after = send(1, chip_behind, RAW, first, ODD[1], near)
    raw_queries, raw_product, lines = pick_of(raw, raw_received, tail, *small, lines, after)
    far = held_back(far, raw_queries)
    far_behind = to_next_slab(far, *links)
    raw_product = held_back(raw_product, far)
    raw_behind = to_next_slab(raw_product, (0, 0), *links)
    raw_queries = held_back(raw_queries, received[0], SLOW)
    first, after = send(0, near_behind, RAW, RAW, EVEN[0], raw_queries)
    first, after = send(0, near_behind, RAW, first, EVEN[1], after, extra=LINES)
    origin = first
    first, after = send(0, far_behind, origin, first, EVEN[2], after, received[1])
    first, after = send(0, far_behind, origin, first, EVEN[3], after, raw_behind)
    wire_received = to_next_section(held_back(wire, after), (1,))
    held, gated = later_of(
        context_start,
        lines,
        near_behind,
        near,
        far_behind,
        far,
        raw_behind,
        tail,
        queries,
        own,
        places,
    )
    odd = len(ODD)
    held = finish(held, gated, received[:odd], places[:odd])
    held = finish(held, gated, received[odd : odd + 2], places[odd : odd + 2])
    held = raw_finish(
        held,
        context_start,
        lines,
        wire_received,
        received[odd + 1],
        raw_behind,
        raw_product,
        raw_queries,
        gated,
        residual,
    )
    for last in (odd + 2, odd + 3):
        held = finish(held, gated, received[last : last + 1], places[last : last + 1])
    return held


def solution(mesh):
    return jax.shard_map(
        body,
        mesh=mesh,
        in_specs=(
            P("pipe", ("dp", "ctx"), None),
            P("pipe", ("dp", "ctx"), None),
            P("pipe", ("dp", "ctx"), None),
            P(("dp", "ctx"), None),
            P("pipe", None, None),
            P("pipe", None),
            P("pipe", None),
            P("dp"),
        ),
        out_specs=P("pipe", ("dp", "ctx"), None),
        check_vma=False,
    )
```

```python
import functools

import jax
import jax.numpy as jnp
from jax import lax
from jax.experimental import pallas as pl
from jax.experimental.pallas import tpu as pltpu
from jax.sharding import PartitionSpec as P

LANES = 128
ROW_BLOCK = 32
RAW = 384
ODD = (1536, 2176)
EVEN = (1024, 768, 1280, 640)
PIECES = 4
LINES = 8
NEAR = 1792
F32 = jnp.float32
BF16 = jnp.bfloat16
MIB = 1024 * 1024
QUICK, SLOW = 1024, 20_000_000_000

SMEM = pl.BlockSpec(memory_space=pltpu.SMEM)
VMEM = pl.BlockSpec(memory_space=pltpu.VMEM)
ANY = pl.BlockSpec(memory_space=pl.ANY)
HBM = pl.BlockSpec(memory_space=pltpu.HBM)


def to_next_slab(value, *links):
    slabs, depth = lax.axis_size("ctx"), lax.axis_size("pipe")
    pairs = [
        (slab * depth + pipe, (slab + 1) * depth + pipe)
        for odd, pipe in links
        for slab in range(slabs - 1)
        if slab % 2 == odd
    ]
    return lax.ppermute(value, ("ctx", "pipe"), pairs)


def to_next_section(value, slabs=(0, 1)):
    depth = lax.axis_size("pipe")
    pairs = [(slab * depth, slab * depth + 1) for slab in range(lax.axis_size("ctx")) if slab % 2 in slabs]
    return lax.ppermute(value, ("ctx", "pipe"), pairs)


def call(kernel, name, out_shape, in_specs, out_specs, scratch=(), weight=QUICK, aliases=None):
    return pl.pallas_call(
        kernel,
        out_shape=out_shape,
        in_specs=in_specs,
        out_specs=out_specs,
        scratch_shapes=list(scratch),
        input_output_aliases=aliases or {},
        compiler_params=pltpu.CompilerParams(vmem_limit_bytes=16 * MIB),
        cost_estimate=pl.CostEstimate(flops=weight, bytes_accessed=1024, transcendentals=0),
        name=name,
    )


def is_first():
    return lax.axis_index("pipe") == 0


def is_slab(odd):
    return lax.axis_index("ctx") % 2 == odd


def array(rows, cols, kind=BF16):
    return jax.ShapeDtypeStruct((rows, cols), kind)


def multiply(keys_ref, values_ref, keys_in, values_in, sems, out_refs, meanwhile):
    rows = out_refs[0].shape[0]
    step = rows // PIECES
    spans = [pl.ds(piece * step, step) for piece in range(PIECES)]
    copies = []
    for piece, span in enumerate(spans):
        copies.append(
            (
                pltpu.make_async_copy(keys_ref.at[0, span], keys_in.at[span], sems.at[2 * piece]),
                pltpu.make_async_copy(values_ref.at[0, span], values_in.at[span], sems.at[2 * piece + 1]),
            )
        )
        for copy in copies[-1]:
            copy.start()
    meanwhile()
    for span, pair in zip(spans, copies):
        for copy in pair:
            copy.wait()
        first = 0
        for out_ref in out_refs:
            for tile in range(0, out_ref.shape[1], LANES):
                at = slice(first + tile, first + tile + LANES)
                product = keys_in[span, at].astype(F32) * values_in[span, at].astype(F32)
                out_ref[span, tile : tile + LANES] = product.astype(BF16)
            first += out_ref.shape[1]


def fill_lines(bank, scales, assign, lines_ref):
    groups, taps = lines_ref.shape
    size = bank.shape[0]
    chosen = (lax.broadcasted_iota(jnp.int32, (size, groups), 0) == assign).astype(F32).astype(BF16)
    contract = (((0,), (0,)), ((), ()))
    picked = lax.dot_general(bank, chosen, contract, preferred_element_type=F32)
    scaled = (picked * scales).astype(BF16)
    order = lax.broadcasted_iota(jnp.int32, (taps, taps), 0) + lax.broadcasted_iota(jnp.int32, (taps, taps), 1)
    flip = (order == taps - 1).astype(F32).astype(BF16)
    lines_ref[...] = lax.dot_general(scaled, flip, contract, preferred_element_type=F32)


def lead_kernel(queries_ref, keys_ref, values_ref, raw_ref, rest_ref, keys_in, values_in, sems, own_sem):
    rows = rest_ref.shape[0]

    @pl.when(is_first())
    def _():
        source = queries_ref.at[0, :, pl.ds(0, RAW)]
        copy = pltpu.make_async_copy(source, raw_ref.at[pl.ds(0, rows)], own_sem)
        targets = [raw_ref.at[pl.ds(rows, rows)], rest_ref]
        multiply(keys_ref, values_ref, keys_in, values_in, sems, targets, copy.start)
        copy.wait()


def product_scratch(rows, total):
    return [pltpu.VMEM((rows, total), BF16), pltpu.VMEM((rows, total), BF16), pltpu.SemaphoreType.DMA((2 * PIECES,))]


def lead_of(queries, keys, values):
    rows, total = queries.shape[1:]
    return call(
        lead_kernel,
        "lead",
        (array(2 * rows, RAW), array(rows, total - RAW)),
        [HBM] * 3,
        (VMEM,) * 2,
        product_scratch(rows, total) + [pltpu.SemaphoreType.DMA(())],
    )(queries, keys, values)


def turn_table(lines_ref, row, count, table_ref, at):
    taps = lines_ref.shape[1]
    upper = lax.broadcasted_iota(jnp.int32, (ROW_BLOCK, taps), 1) > lax.broadcasted_iota(
        jnp.int32, (ROW_BLOCK, taps), 0
    )
    for group in range(count):
        line = lines_ref[row + group : row + group + 1, :]
        turned = pltpu.roll(jnp.broadcast_to(line, (ROW_BLOCK, taps)), 1, 1, stride=1, stride_axis=0)
        span = slice(at + group * ROW_BLOCK, at + (group + 1) * ROW_BLOCK)
        table_ref[span, :taps] = jnp.where(upper, turned, 0.0).astype(BF16)
        table_ref[span, taps:] = jnp.where(upper, 0.0, turned)[:, :ROW_BLOCK].astype(BF16)


def product_kernel(*refs):
    keys_ref, values_ref, bank_ref, scales_ref, assign_ref, rest_ref = refs[:6]
    lines_ref, wire_ref, near_ref, far_ref, tail_ref, keys_in, values_in, sems = refs[6:]

    def taps():
        fill_lines(bank_ref[0], scales_ref[...], assign_ref[...], lines_ref)

    @pl.when(jnp.logical_and(is_first(), is_slab(1)))
    def _():
        taps()
        wire_ref[...] = lines_ref[: wire_ref.shape[0], :].astype(BF16)
        near_ref[...] = rest_ref[:, :NEAR]
        far_ref[...] = rest_ref[:, NEAR:]

    @pl.when(jnp.logical_not(is_first()))
    def _():
        multiply(keys_ref, values_ref, keys_in, values_in, sems, [near_ref, far_ref, tail_ref], taps)


def wire_rows(groups, total):
    return -(-RAW * groups // (total * 16)) * 16


def product_of(keys, values, bank, scales, assign, rest):
    rows, total = keys.shape[1:]
    groups, taps = assign.shape[1], bank.shape[2]
    return call(
        product_kernel,
        "product",
        (
            array(groups, taps, F32),
            array(wire_rows(groups, total), taps),
            array(rows, NEAR),
            array(rows, total - RAW - NEAR),
            array(rows, RAW),
        ),
        [HBM, HBM] + [VMEM] * 4,
        (VMEM,) * 5,
        product_scratch(rows, total),
    )(keys, values, bank, scales, assign, rest)


def mix(table_ref, row, share, window, store):
    depth = table_ref.shape[1]
    rows = window.shape[0] - depth + ROW_BLOCK
    member = lax.broadcasted_iota(jnp.int32, (ROW_BLOCK, LANES), 1) // (LANES // share)
    table = table_ref[row : row + share * ROW_BLOCK, :]
    for first in range(0, rows, 2 * ROW_BLOCK):
        starts = (first, first + ROW_BLOCK)
        pair = jnp.concatenate([window[begin : begin + depth] for begin in starts], axis=1)
        sums = jnp.dot(table, pair, preferred_element_type=F32)
        for place, begin in enumerate(starts):
            part = sums[:, place * LANES : (place + 1) * LANES]
            mixed = part[:ROW_BLOCK]
            for group in range(1, share):
                mixed = jnp.where(member == group, part[group * ROW_BLOCK : (group + 1) * ROW_BLOCK], mixed)
            store(slice(begin, begin + ROW_BLOCK), mixed)


def mix_all(width, share, lines_ref, line, table_ref, start_ref, behind_ref, product_ref, local, store):
    rows = product_ref.shape[0]
    first = (lax.axis_index("ctx") - 1) * rows
    inside = first + lax.broadcasted_iota(jnp.int32, (2 * rows, LANES), 0) >= start_ref[0]
    for tile in range(width // LANES):
        at = slice(tile * LANES, (tile + 1) * LANES)
        near, inner = (slice(begin + at.start, begin + at.stop) for begin in local)
        row = tile * share * ROW_BLOCK
        turn_table(lines_ref, line + tile * share, share, table_ref, row)
        window = jnp.concatenate([behind_ref[:, near], product_ref[:, inner]], axis=0)
        window = jnp.where(inside, window, jnp.zeros_like(window))
        mix(table_ref, row, share, window, functools.partial(store, at))


def share_of(lines_ref, total):
    return LANES * lines_ref.shape[0] // total


def own_kernel(odd, first, shift, local, extra, *refs):
    start_ref, lines_ref, behind_ref, product_ref, queries_ref, residual_ref = refs[:6]
    out_ref, table_ref = refs[-2:]
    width = out_ref.shape[1]
    share = share_of(lines_ref, residual_ref.shape[1])

    @pl.when(jnp.logical_and(is_first(), is_slab(odd)))
    def _():
        def store(at, span, mixed):
            cols = slice(first + at.start, first + at.stop)
            gated = queries_ref[0, span, cols].astype(F32) * mixed
            out_ref[span, at] = (residual_ref[span, cols].astype(F32) + gated).astype(BF16)

        line = first // LANES * share
        at = (shift, local)
        mix_all(width, share, lines_ref, line, table_ref, start_ref, behind_ref, product_ref, at, store)
        if extra:
            rows = out_ref.shape[0] - extra
            for part in range(RAW // LANES):
                taken = lines_ref[part * extra : (part + 1) * extra, :].astype(BF16)
                out_ref[rows:, part * LANES : (part + 1) * LANES] = taken


def table_scratch(lines, width, total):
    groups, taps = lines.shape
    return pltpu.VMEM((width * groups // total * ROW_BLOCK, taps + ROW_BLOCK), BF16)


def own_of(odd, origin, extra, start, lines, behind, product, queries, residual, first, width, *after):
    rows, total = residual.shape
    return call(
        functools.partial(own_kernel, odd, first, first - origin, first - RAW, extra),
        "own",
        array(rows + extra, width),
        [SMEM] + [VMEM] * 5 + [ANY] * len(after),
        VMEM,
        [table_scratch(lines, width, total)],
    )(start, lines, behind, product, queries, residual, *after)


def pick_kernel(*refs):
    raw_ref, received_ref, tail_ref, bank_ref, scales_ref, assign_ref = refs[:6]
    queries_ref, product_ref, lines_ref = refs[8:]
    rows = queries_ref.shape[0]

    @pl.when(jnp.logical_and(is_first(), is_slab(0)))
    def _():
        fill_lines(bank_ref[0], scales_ref[...], assign_ref[...], lines_ref)

    def take(source):
        queries_ref[...] = source[:rows, :]
        product_ref[:, :RAW] = source[rows:, :]

    pl.when(is_first())(lambda: take(raw_ref))

    @pl.when(jnp.logical_not(is_first()))
    def _():
        take(received_ref)
        product_ref[:, RAW:] = tail_ref[...]


def pick_of(raw, received, tail, bank, scales, assign, lines, after):
    rows, width = raw.shape[0] // 2, raw.shape[1]
    return call(
        pick_kernel,
        "pick",
        (array(rows, width), array(rows, 2 * width), array(*lines.shape, F32)),
        [VMEM] * 7 + [ANY],
        (VMEM,) * 3,
        weight=SLOW,
        aliases={6: 2},
    )(raw, received, tail, bank, scales, assign, lines, after)


def hold_kernel(value_ref, _, out_ref):
    pass


def held_back(value, after, weight=QUICK):
    return call(
        hold_kernel, "hold", array(*value.shape), [ANY, ANY], ANY, weight=weight, aliases={0: 0}
    )(value, after)


def send_out(pieces, out_ref, sems):
    copies = [
        pltpu.make_async_copy(buffer, out_ref.at[0, :, pl.ds(first, buffer.shape[1])], sems.at[place])
        for place, (buffer, first) in enumerate(pieces)
    ]
    for copy in copies:
        copy.start()
    return copies


def wait_all(copies):
    for copy in copies:
        copy.wait()


def later_kernel(places, *refs):
    start_ref, lines_ref, near_behind, near_ref, far_behind, far_ref, raw_behind, tail_ref, queries_ref = refs[:9]
    own_refs = refs[9 : 9 + len(places)]
    out_ref, gated_ref, table_ref, sems = refs[-4:]
    total = queries_ref.shape[2]
    share = share_of(lines_ref, total)

    for odd in (0, 1):

        @pl.when(jnp.logical_and(is_first(), is_slab(odd)))
        def _():
            pieces = [
                (own_ref.at[pl.ds(0, out_ref.shape[1])], first)
                for own_ref, (side, first, _) in zip(own_refs, places)
                if side == odd
            ]
            wait_all(send_out(pieces, out_ref, sems))

    @pl.when(jnp.logical_not(is_first()))
    def _():
        parts = (
            (0, 0, near_behind, near_ref),
            (NEAR, 0, far_behind, far_ref),
            (total - RAW, RAW, raw_behind, tail_ref),
        )
        for first, skip, behind_ref, product_ref in parts:

            def store(at, span, mixed):
                cols = slice(first + at.start, first + at.stop)
                gated_ref[span, cols] = queries_ref[0, span, cols].astype(F32) * mixed

            width, line = product_ref.shape[1], first // LANES * share
            at = (skip, 0)
            mix_all(width, share, lines_ref, line, table_ref, start_ref, behind_ref, product_ref, at, store)


def later_of(start, lines, near_behind, near, far_behind, far, raw_behind, tail, queries, own, places):
    rows, total = queries.shape[1:]
    return call(
        functools.partial(later_kernel, places),
        "later",
        (jax.ShapeDtypeStruct((1, rows, total), BF16), array(rows, total, F32)),
        [SMEM] + [VMEM] * (8 + len(own)),
        (ANY, VMEM),
        [table_scratch(lines, max(NEAR, total - RAW - NEAR), total), pltpu.SemaphoreType.DMA((len(own),))],
        weight=SLOW,
    )(start, lines, near_behind, near, far_behind, far, raw_behind, tail, queries, *own)


def raw_kernel(*refs):
    start_ref, lines_ref, wire_ref, received_ref = refs[:4]
    behind_ref, product_ref, queries_ref, gated_ref, residual_ref = refs[4:9]
    out_ref, chosen_ref, table_ref, buffer, sems = refs[10:]
    rows, width = buffer.shape
    share = share_of(lines_ref, residual_ref.shape[1])

    @pl.when(is_first())
    def _():
        chosen_ref[...] = lines_ref[: chosen_ref.shape[0], :]

    @pl.when(jnp.logical_and(jnp.logical_not(is_first()), is_slab(1)))
    def _():
        chosen_ref[...] = wire_ref[...].astype(F32)

    @pl.when(jnp.logical_and(jnp.logical_not(is_first()), is_slab(0)))
    def _():
        for part in range(RAW // LANES):
            taken = received_ref[rows:, part * LANES : (part + 1) * LANES]
            chosen_ref[part * LINES : (part + 1) * LINES, :] = taken.astype(F32)

    def store(at, span, mixed):
        gated = queries_ref[span, at].astype(F32) * mixed
        buffer[span, at] = (residual_ref[span, at].astype(F32) + gated).astype(BF16)

    mix_all(width, share, chosen_ref, 0, table_ref, start_ref, behind_ref, product_ref, (0, 0), store)

    @pl.when(jnp.logical_not(is_first()))
    def _():
        buffer[...] = (buffer[...].astype(F32) + gated_ref[:, :width]).astype(BF16)

    wait_all(send_out([(buffer, 0)], out_ref, sems))


def raw_finish(held, start, lines, wire, received, behind, product, queries, gated, residual):
    rows, width = queries.shape
    total = residual.shape[1]
    return call(
        raw_kernel,
        "raw",
        jax.ShapeDtypeStruct(held.shape, BF16),
        [SMEM] + [VMEM] * 8 + [ANY],
        ANY,
        [
            pltpu.VMEM(wire.shape, F32),
            table_scratch(lines, width, total),
            pltpu.VMEM((rows, width), BF16),
            pltpu.SemaphoreType.DMA((1,)),
        ],
        weight=SLOW,
        aliases={9: 0},
    )(start, lines, wire, received, behind, product, queries, gated, residual, held)


def finish_kernel(odd, places, *refs):
    gated_ref, received_refs = refs[0], refs[1 : 1 + len(places)]
    out_ref, *buffers, sems = refs[2 + len(places) :]

    @pl.when(jnp.logical_and(jnp.logical_not(is_first()), is_slab(odd)))
    def _():
        copies = []
        for place, (_, first, width) in enumerate(places):
            buffer = buffers[place]
            total = received_refs[place][: buffer.shape[0], :].astype(F32) + gated_ref[:, first : first + width]
            buffer[...] = total.astype(BF16)
            copies += send_out([(buffer, first)], out_ref, sems.at[pl.ds(place, 1)])
        wait_all(copies)


def finish(held, gated, received, places):
    rows = gated.shape[0]
    count = len(places)
    return call(
        functools.partial(finish_kernel, places[0][0], places),
        "finish",
        jax.ShapeDtypeStruct(held.shape, BF16),
        [VMEM] * (1 + count) + [ANY],
        ANY,
        [pltpu.VMEM((rows, width), BF16) for _, _, width in places] + [pltpu.SemaphoreType.DMA((count,))],
        weight=SLOW,
        aliases={1 + count: 0},
    )(gated, *received, held)


def body(queries, keys, values, residual, filter_bank, filter_scales, group_filter, context_start):
    total = queries.shape[2]
    small = (filter_bank, filter_scales, group_filter)
    far_queries, keys, values = (
        pltpu.with_memory_space_constraint(value, pltpu.HBM) for value in (queries, keys, values)
    )
    raw, rest = lead_of(far_queries, keys, values)
    raw_received = to_next_section(raw)
    chip_behind = to_next_slab(rest, (0, 0))
    lines, wire, near, far, tail = product_of(keys, values, *small, rest)
    own, received, places = [], [], []

    def send(odd, behind, origin, first, width, *after, extra=0):
        piece = own_of(
            odd, origin, extra, context_start, lines, behind, rest, queries, residual, first, width, *after
        )
        own.append(piece)
        received.append(to_next_section(piece, (odd,)))
        places.append((odd, first, width))
        return first + width, piece

    links = ((1, 0), (0, 1), (1, 1))
    first, after = send(1, chip_behind, RAW, RAW, ODD[0], lines)
    near = held_back(near, after)
    near_behind = to_next_slab(near, *links)
    first, after = send(1, chip_behind, RAW, first, ODD[1], near)
    raw_queries, raw_product, lines = pick_of(raw, raw_received, tail, *small, lines, after)
    far = held_back(far, raw_queries)
    far_behind = to_next_slab(far, *links)
    raw_product = held_back(raw_product, far)
    raw_behind = to_next_slab(raw_product, (0, 0), *links)
    raw_queries = held_back(raw_queries, received[0], SLOW)
    first, after = send(0, near_behind, RAW, RAW, EVEN[0], raw_queries)
    first, after = send(0, near_behind, RAW, first, EVEN[1], after, extra=LINES)
    origin = first
    first, after = send(0, far_behind, origin, first, EVEN[2], after, received[1])
    first, after = send(0, far_behind, origin, first, EVEN[3], after, raw_behind)
    wire_received = to_next_section(held_back(wire, after), (1,))
    held, gated = later_of(
        context_start,
        lines,
        near_behind,
        near,
        far_behind,
        far,
        raw_behind,
        tail,
        queries,
        own,
        places,
    )
    odd = len(ODD)
    held = finish(held, gated, received[:odd], places[:odd])
    held = finish(held, gated, received[odd : odd + 2], places[odd : odd + 2])
    held = raw_finish(
        held,
        context_start,
        lines,
        wire_received,
        received[odd + 1],
        raw_behind,
        raw_product,
        raw_queries,
        gated,
        residual,
    )
    for last in (odd + 2, odd + 3):
        held = finish(held, gated, received[last : last + 1], places[last : last + 1])
    return held


def solution(mesh):
    return jax.shard_map(
        body,
        mesh=mesh,
        in_specs=(
            P("pipe", ("dp", "ctx"), None),
            P("pipe", ("dp", "ctx"), None),
            P("pipe", ("dp", "ctx"), None),
            P(("dp", "ctx"), None),
            P("pipe", None, None),
            P("pipe", None),
            P("pipe", None),
            P("dp"),
        ),
        out_specs=P("pipe", ("dp", "ctx"), None),
        check_vma=False,
    )
```

```python
import functools

import jax
import jax.numpy as jnp
from jax import lax
from jax.experimental import pallas as pl
from jax.experimental.pallas import tpu as pltpu
from jax.sharding import PartitionSpec as P

LANES = 128
ROW_BLOCK = 32
RAW = 384
ODD = (1536, 2176)
EVEN = (1024, 896, 1280, 512)
PIECES = 8
NEAR = 1920
F32 = jnp.float32
BF16 = jnp.bfloat16
MIB = 1024 * 1024
QUICK, SLOW = 1024, 20_000_000_000

SMEM = pl.BlockSpec(memory_space=pltpu.SMEM)
VMEM = pl.BlockSpec(memory_space=pltpu.VMEM)
ANY = pl.BlockSpec(memory_space=pl.ANY)
HBM = pl.BlockSpec(memory_space=pltpu.HBM)


def to_next_slab(value, *links):
    slabs, depth = lax.axis_size("ctx"), lax.axis_size("pipe")
    pairs = [
        (slab * depth + pipe, (slab + 1) * depth + pipe)
        for odd, pipe in links
        for slab in range(slabs - 1)
        if slab % 2 == odd
    ]
    return lax.ppermute(value, ("ctx", "pipe"), pairs)


def to_next_section(value, slabs=(0, 1)):
    depth = lax.axis_size("pipe")
    pairs = [(slab * depth, slab * depth + 1) for slab in range(lax.axis_size("ctx")) if slab % 2 in slabs]
    return lax.ppermute(value, ("ctx", "pipe"), pairs)


def call(kernel, name, out_shape, in_specs, out_specs, scratch=(), weight=QUICK, aliases=None):
    return pl.pallas_call(
        kernel,
        out_shape=out_shape,
        in_specs=in_specs,
        out_specs=out_specs,
        scratch_shapes=list(scratch),
        input_output_aliases=aliases or {},
        compiler_params=pltpu.CompilerParams(vmem_limit_bytes=16 * MIB),
        cost_estimate=pl.CostEstimate(flops=weight, bytes_accessed=1024, transcendentals=0),
        name=name,
    )


def is_first():
    return lax.axis_index("pipe") == 0


def is_slab(odd):
    return lax.axis_index("ctx") % 2 == odd


def array(rows, cols, kind=BF16):
    return jax.ShapeDtypeStruct((rows, cols), kind)


def multiply(keys_ref, values_ref, keys_in, values_in, sems, out_refs, meanwhile):
    rows = out_refs[0].shape[0]
    step = rows // PIECES
    spans = [pl.ds(piece * step, step) for piece in range(PIECES)]
    copies = []
    for piece, span in enumerate(spans):
        copies.append(
            (
                pltpu.make_async_copy(keys_ref.at[0, span], keys_in.at[span], sems.at[2 * piece]),
                pltpu.make_async_copy(values_ref.at[0, span], values_in.at[span], sems.at[2 * piece + 1]),
            )
        )
        for copy in copies[-1]:
            copy.start()
    meanwhile()
    for span, pair in zip(spans, copies):
        for copy in pair:
            copy.wait()
        first = 0
        for out_ref in out_refs:
            for tile in range(0, out_ref.shape[1], LANES):
                at = slice(first + tile, first + tile + LANES)
                product = keys_in[span, at].astype(F32) * values_in[span, at].astype(F32)
                out_ref[span, tile : tile + LANES] = product.astype(BF16)
            first += out_ref.shape[1]


def fill_lines(bank, scales, assign, lines_ref):
    groups, taps = lines_ref.shape
    size = bank.shape[0]
    chosen = (lax.broadcasted_iota(jnp.int32, (size, groups), 0) == assign).astype(F32).astype(BF16)
    contract = (((0,), (0,)), ((), ()))
    picked = lax.dot_general(bank, chosen, contract, preferred_element_type=F32)
    scaled = (picked * scales).astype(BF16)
    order = lax.broadcasted_iota(jnp.int32, (taps, taps), 0) + lax.broadcasted_iota(jnp.int32, (taps, taps), 1)
    flip = (order == taps - 1).astype(F32).astype(BF16)
    lines_ref[...] = lax.dot_general(scaled, flip, contract, preferred_element_type=F32)


def lead_kernel(queries_ref, keys_ref, values_ref, raw_ref, rest_ref, keys_in, values_in, sems, own_sem):
    rows = rest_ref.shape[0]

    @pl.when(is_first())
    def _():
        source = queries_ref.at[0, :, pl.ds(0, RAW)]
        copy = pltpu.make_async_copy(source, raw_ref.at[pl.ds(0, rows)], own_sem)
        targets = [raw_ref.at[pl.ds(rows, rows)], rest_ref]
        multiply(keys_ref, values_ref, keys_in, values_in, sems, targets, copy.start)
        copy.wait()


def product_scratch(rows, total):
    return [pltpu.VMEM((rows, total), BF16), pltpu.VMEM((rows, total), BF16), pltpu.SemaphoreType.DMA((2 * PIECES,))]


def lead_of(queries, keys, values):
    rows, total = queries.shape[1:]
    return call(
        lead_kernel,
        "lead",
        (array(2 * rows, RAW), array(rows, total - RAW)),
        [HBM] * 3,
        (VMEM,) * 2,
        product_scratch(rows, total) + [pltpu.SemaphoreType.DMA(())],
    )(queries, keys, values)


def turn_table(lines_ref, row, count, table_ref, at):
    taps = lines_ref.shape[1]
    upper = lax.broadcasted_iota(jnp.int32, (ROW_BLOCK, taps), 1) > lax.broadcasted_iota(
        jnp.int32, (ROW_BLOCK, taps), 0
    )
    for group in range(count):
        line = lines_ref[row + group : row + group + 1, :]
        turned = pltpu.roll(jnp.broadcast_to(line, (ROW_BLOCK, taps)), 1, 1, stride=1, stride_axis=0)
        span = slice(at + group * ROW_BLOCK, at + (group + 1) * ROW_BLOCK)
        table_ref[span, :taps] = jnp.where(upper, turned, 0.0).astype(BF16)
        table_ref[span, taps:] = jnp.where(upper, 0.0, turned)[:, :ROW_BLOCK].astype(BF16)


def product_kernel(*refs):
    keys_ref, values_ref, bank_ref, scales_ref, assign_ref, rest_ref = refs[:6]
    lines_ref, near_ref, far_ref, tail_ref, keys_in, values_in, sems = refs[6:]

    def taps():
        fill_lines(bank_ref[0], scales_ref[...], assign_ref[...], lines_ref)

    @pl.when(jnp.logical_and(is_first(), is_slab(1)))
    def _():
        taps()
        near_ref[...] = rest_ref[:, :NEAR]
        far_ref[...] = rest_ref[:, NEAR:]

    @pl.when(jnp.logical_not(is_first()))
    def _():
        multiply(keys_ref, values_ref, keys_in, values_in, sems, [near_ref, far_ref, tail_ref], taps)


def wire_rows(groups, total):
    return -(-RAW * groups // (total * 16)) * 16


def product_of(keys, values, bank, scales, assign, rest):
    rows, total = keys.shape[1:]
    groups, taps = assign.shape[1], bank.shape[2]
    return call(
        product_kernel,
        "product",
        (
            array(groups, taps, F32),
            array(rows, NEAR),
            array(rows, total - RAW - NEAR),
            array(rows, RAW),
        ),
        [HBM, HBM] + [VMEM] * 4,
        (VMEM,) * 4,
        product_scratch(rows, total),
    )(keys, values, bank, scales, assign, rest)


def mix(table_ref, row, share, window, store):
    depth = table_ref.shape[1]
    rows = window.shape[0] - depth + ROW_BLOCK
    member = lax.broadcasted_iota(jnp.int32, (ROW_BLOCK, LANES), 1) // (LANES // share)
    table = table_ref[row : row + share * ROW_BLOCK, :]
    for first in range(0, rows, 2 * ROW_BLOCK):
        starts = (first, first + ROW_BLOCK)
        pair = jnp.concatenate([window[begin : begin + depth] for begin in starts], axis=1)
        sums = jnp.dot(table, pair, preferred_element_type=F32)
        for place, begin in enumerate(starts):
            part = sums[:, place * LANES : (place + 1) * LANES]
            mixed = part[:ROW_BLOCK]
            for group in range(1, share):
                mixed = jnp.where(member == group, part[group * ROW_BLOCK : (group + 1) * ROW_BLOCK], mixed)
            store(slice(begin, begin + ROW_BLOCK), mixed)


def mix_all(width, share, lines_ref, line, table_ref, start_ref, behind_ref, product_ref, local, store):
    rows = product_ref.shape[0]
    first = (lax.axis_index("ctx") - 1) * rows
    inside = first + lax.broadcasted_iota(jnp.int32, (2 * rows, LANES), 0) >= start_ref[0]
    for tile in range(width // LANES):
        at = slice(tile * LANES, (tile + 1) * LANES)
        near, inner = (slice(begin + at.start, begin + at.stop) for begin in local)
        row = tile * share * ROW_BLOCK
        turn_table(lines_ref, line + tile * share, share, table_ref, row)
        window = jnp.concatenate([behind_ref[:, near], product_ref[:, inner]], axis=0)
        window = jnp.where(inside, window, jnp.zeros_like(window))
        mix(table_ref, row, share, window, functools.partial(store, at))


def share_of(lines_ref, total):
    return LANES * lines_ref.shape[0] // total


def own_kernel(odd, first, shift, local, *refs):
    start_ref, lines_ref, behind_ref, product_ref, queries_ref, residual_ref = refs[:6]
    out_ref, table_ref = refs[-2:]
    width = out_ref.shape[1]
    share = share_of(lines_ref, residual_ref.shape[1])

    @pl.when(jnp.logical_and(is_first(), is_slab(odd)))
    def _():
        def store(at, span, mixed):
            cols = slice(first + at.start, first + at.stop)
            gated = queries_ref[0, span, cols].astype(F32) * mixed
            out_ref[span, at] = (residual_ref[span, cols].astype(F32) + gated).astype(BF16)

        line = first // LANES * share
        at = (shift, local)
        mix_all(width, share, lines_ref, line, table_ref, start_ref, behind_ref, product_ref, at, store)


def table_scratch(lines, width, total):
    groups, taps = lines.shape
    return pltpu.VMEM((width * groups // total * ROW_BLOCK, taps + ROW_BLOCK), BF16)


def own_of(odd, origin, start, lines, behind, product, queries, residual, first, width, *after):
    rows, total = residual.shape
    return call(
        functools.partial(own_kernel, odd, first, first - origin, first - RAW),
        "own",
        array(rows, width),
        [SMEM] + [VMEM] * 5 + [ANY] * len(after),
        VMEM,
        [table_scratch(lines, width, total)],
    )(start, lines, behind, product, queries, residual, *after)


def pick_kernel(*refs):
    raw_ref, received_ref, tail_ref, bank_ref, scales_ref, assign_ref = refs[:6]
    queries_ref, product_ref, lines_ref, wire_ref = refs[8:]
    rows = queries_ref.shape[0]

    @pl.when(jnp.logical_and(is_first(), is_slab(0)))
    def _():
        fill_lines(bank_ref[0], scales_ref[...], assign_ref[...], lines_ref)

    @pl.when(is_first())
    def _():
        wire_ref[...] = lines_ref[: wire_ref.shape[0], :].astype(BF16)

    def take(source):
        queries_ref[...] = source[:rows, :]
        product_ref[:, :RAW] = source[rows:, :]

    pl.when(is_first())(lambda: take(raw_ref))

    @pl.when(jnp.logical_not(is_first()))
    def _():
        take(received_ref)
        product_ref[:, RAW:] = tail_ref[...]


def pick_of(raw, received, tail, bank, scales, assign, lines, total, after):
    rows, width = raw.shape[0] // 2, raw.shape[1]
    groups, taps = lines.shape
    return call(
        pick_kernel,
        "pick",
        (
            array(rows, width),
            array(rows, 2 * width),
            array(groups, taps, F32),
            array(wire_rows(groups, total), taps),
        ),
        [VMEM] * 7 + [ANY],
        (VMEM,) * 4,
        weight=SLOW,
        aliases={6: 2},
    )(raw, received, tail, bank, scales, assign, lines, after)


def hold_kernel(value_ref, _, out_ref):
    pass


def held_back(value, after, weight=QUICK):
    return call(
        hold_kernel, "hold", array(*value.shape), [ANY, ANY], ANY, weight=weight, aliases={0: 0}
    )(value, after)


def send_out(pieces, out_ref, sems):
    copies = [
        pltpu.make_async_copy(buffer, out_ref.at[0, :, pl.ds(first, buffer.shape[1])], sems.at[place])
        for place, (buffer, first) in enumerate(pieces)
    ]
    for copy in copies:
        copy.start()
    return copies


def wait_all(copies):
    for copy in copies:
        copy.wait()


def later_kernel(places, *refs):
    start_ref, lines_ref, near_behind, near_ref, far_behind, far_ref, raw_behind, tail_ref, queries_ref = refs[:9]
    own_refs = refs[9 : 9 + len(places)]
    out_ref, gated_ref, table_ref, sems = refs[-4:]
    total = queries_ref.shape[2]
    share = share_of(lines_ref, total)

    for odd in (0, 1):

        @pl.when(jnp.logical_and(is_first(), is_slab(odd)))
        def _():
            pieces = [
                (own_ref.at[pl.ds(0, out_ref.shape[1])], first)
                for own_ref, (side, first, _) in zip(own_refs, places)
                if side == odd
            ]
            wait_all(send_out(pieces, out_ref, sems))

    @pl.when(jnp.logical_not(is_first()))
    def _():
        parts = (
            (0, 0, near_behind, near_ref),
            (NEAR, 0, far_behind, far_ref),
            (total - RAW, RAW, raw_behind, tail_ref),
        )
        for first, skip, behind_ref, product_ref in parts:

            def store(at, span, mixed):
                cols = slice(first + at.start, first + at.stop)
                gated_ref[span, cols] = queries_ref[0, span, cols].astype(F32) * mixed

            width, line = product_ref.shape[1], first // LANES * share
            at = (skip, 0)
            mix_all(width, share, lines_ref, line, table_ref, start_ref, behind_ref, product_ref, at, store)


def later_of(start, lines, near_behind, near, far_behind, far, raw_behind, tail, queries, own, places):
    rows, total = queries.shape[1:]
    return call(
        functools.partial(later_kernel, places),
        "later",
        (jax.ShapeDtypeStruct((1, rows, total), BF16), array(rows, total, F32)),
        [SMEM] + [VMEM] * (8 + len(own)),
        (ANY, VMEM),
        [table_scratch(lines, max(NEAR, total - RAW - NEAR), total), pltpu.SemaphoreType.DMA((len(own),))],
        weight=SLOW,
    )(start, lines, near_behind, near, far_behind, far, raw_behind, tail, queries, *own)


def raw_kernel(*refs):
    start_ref, lines_ref, wire_ref = refs[:3]
    behind_ref, product_ref, queries_ref, gated_ref, residual_ref = refs[3:8]
    out_ref, chosen_ref, table_ref, buffer, sems = refs[9:]
    width = buffer.shape[1]
    share = share_of(lines_ref, residual_ref.shape[1])

    @pl.when(is_first())
    def _():
        chosen_ref[...] = lines_ref[: chosen_ref.shape[0], :]

    @pl.when(jnp.logical_not(is_first()))
    def _():
        chosen_ref[...] = wire_ref[...].astype(F32)

    def store(at, span, mixed):
        gated = queries_ref[span, at].astype(F32) * mixed
        buffer[span, at] = (residual_ref[span, at].astype(F32) + gated).astype(BF16)

    mix_all(width, share, chosen_ref, 0, table_ref, start_ref, behind_ref, product_ref, (0, 0), store)

    @pl.when(jnp.logical_not(is_first()))
    def _():
        buffer[...] = (buffer[...].astype(F32) + gated_ref[:, :width]).astype(BF16)

    wait_all(send_out([(buffer, 0)], out_ref, sems))


def raw_finish(held, start, lines, wire, behind, product, queries, gated, residual):
    rows, width = queries.shape
    total = residual.shape[1]
    return call(
        raw_kernel,
        "raw",
        jax.ShapeDtypeStruct(held.shape, BF16),
        [SMEM] + [VMEM] * 7 + [ANY],
        ANY,
        [
            pltpu.VMEM(wire.shape, F32),
            table_scratch(lines, width, total),
            pltpu.VMEM((rows, width), BF16),
            pltpu.SemaphoreType.DMA((1,)),
        ],
        weight=SLOW,
        aliases={8: 0},
    )(start, lines, wire, behind, product, queries, gated, residual, held)


def finish_kernel(odd, places, *refs):
    gated_ref, received_refs = refs[0], refs[1 : 1 + len(places)]
    out_ref, *buffers, sems = refs[2 + len(places) :]

    @pl.when(jnp.logical_and(jnp.logical_not(is_first()), is_slab(odd)))
    def _():
        copies = []
        for place, (_, first, width) in enumerate(places):
            buffer = buffers[place]
            total = received_refs[place][: buffer.shape[0], :].astype(F32) + gated_ref[:, first : first + width]
            buffer[...] = total.astype(BF16)
            copies += send_out([(buffer, first)], out_ref, sems.at[pl.ds(place, 1)])
        wait_all(copies)


def finish(held, gated, received, places):
    rows = gated.shape[0]
    count = len(places)
    return call(
        functools.partial(finish_kernel, places[0][0], places),
        "finish",
        jax.ShapeDtypeStruct(held.shape, BF16),
        [VMEM] * (1 + count) + [ANY],
        ANY,
        [pltpu.VMEM((rows, width), BF16) for _, _, width in places] + [pltpu.SemaphoreType.DMA((count,))],
        weight=SLOW,
        aliases={1 + count: 0},
    )(gated, *received, held)


def body(queries, keys, values, residual, filter_bank, filter_scales, group_filter, context_start):
    total = queries.shape[2]
    small = (filter_bank, filter_scales, group_filter)
    far_queries, keys, values = (
        pltpu.with_memory_space_constraint(value, pltpu.HBM) for value in (queries, keys, values)
    )
    raw, rest = lead_of(far_queries, keys, values)
    raw_received = to_next_section(raw)
    chip_behind = to_next_slab(rest, (0, 0))
    lines, near, far, tail = product_of(keys, values, *small, rest)
    own, received, places = [], [], []

    def send(odd, behind, origin, first, width, *after):
        piece = own_of(
            odd, origin, context_start, lines, behind, rest, queries, residual, first, width, *after
        )
        own.append(piece)
        received.append(to_next_section(piece, (odd,)))
        places.append((odd, first, width))
        return first + width, piece

    links = ((1, 0), (0, 1), (1, 1))
    first, after = send(1, chip_behind, RAW, RAW, ODD[0], lines)
    near = held_back(near, after)
    near_behind = to_next_slab(near, *links)
    first, after = send(1, chip_behind, RAW, first, ODD[1], near)
    raw_queries, raw_product, lines, wire = pick_of(raw, raw_received, tail, *small, lines, total, after)
    far = held_back(far, raw_queries)
    far_behind = to_next_slab(far, *links)
    raw_product = held_back(raw_product, far)
    raw_behind = to_next_slab(raw_product, (0, 0), *links)
    raw_queries = held_back(raw_queries, received[0], SLOW)
    first, after = send(0, near_behind, RAW, RAW, EVEN[0], raw_queries)
    first, after = send(0, near_behind, RAW, first, EVEN[1], after)
    origin = first
    first, after = send(0, far_behind, origin, first, EVEN[2], after, received[1])
    wire = held_back(wire, after)
    wire_received = to_next_section(wire)
    first, after = send(0, far_behind, origin, first, EVEN[3], wire, raw_behind)
    held, gated = later_of(
        context_start,
        lines,
        near_behind,
        near,
        far_behind,
        far,
        raw_behind,
        tail,
        queries,
        own,
        places,
    )
    odd = len(ODD)
    held = finish(held, gated, received[:odd], places[:odd])
    held = finish(held, gated, received[odd : odd + 2], places[odd : odd + 2])
    held = raw_finish(
        held,
        context_start,
        lines,
        wire_received,
        raw_behind,
        raw_product,
        raw_queries,
        gated,
        residual,
    )
    for last in (odd + 2, odd + 3):
        held = finish(held, gated, received[last : last + 1], places[last : last + 1])
    return held


def solution(mesh):
    return jax.shard_map(
        body,
        mesh=mesh,
        in_specs=(
            P("pipe", ("dp", "ctx"), None),
            P("pipe", ("dp", "ctx"), None),
            P("pipe", ("dp", "ctx"), None),
            P(("dp", "ctx"), None),
            P("pipe", None, None),
            P("pipe", None),
            P("pipe", None),
            P("dp"),
        ),
        out_specs=P("pipe", ("dp", "ctx"), None),
        check_vma=False,
    )
```

```python
import functools

import jax
import jax.numpy as jnp
from jax import lax
from jax.experimental import pallas as pl
from jax.experimental.pallas import tpu as pltpu
from jax.sharding import PartitionSpec as P

LANES = 128
ROW_BLOCK = 32
RAW = 384
ODD = (1536, 2176)
EVEN = (1024, 896, 1280, 512)
PIECES = 2
LINES = 8
NEAR = 1920
F32 = jnp.float32
BF16 = jnp.bfloat16
MIB = 1024 * 1024
QUICK, SLOW = 1024, 20_000_000_000

SMEM = pl.BlockSpec(memory_space=pltpu.SMEM)
VMEM = pl.BlockSpec(memory_space=pltpu.VMEM)
ANY = pl.BlockSpec(memory_space=pl.ANY)
HBM = pl.BlockSpec(memory_space=pltpu.HBM)


def to_next_slab(value, *links):
    slabs, depth = lax.axis_size("ctx"), lax.axis_size("pipe")
    pairs = [
        (slab * depth + pipe, (slab + 1) * depth + pipe)
        for odd, pipe in links
        for slab in range(slabs - 1)
        if slab % 2 == odd
    ]
    return lax.ppermute(value, ("ctx", "pipe"), pairs)


def to_next_section(value, slabs=(0, 1)):
    depth = lax.axis_size("pipe")
    pairs = [(slab * depth, slab * depth + 1) for slab in range(lax.axis_size("ctx")) if slab % 2 in slabs]
    return lax.ppermute(value, ("ctx", "pipe"), pairs)


def call(kernel, name, out_shape, in_specs, out_specs, scratch=(), weight=QUICK, aliases=None):
    return pl.pallas_call(
        kernel,
        out_shape=out_shape,
        in_specs=in_specs,
        out_specs=out_specs,
        scratch_shapes=list(scratch),
        input_output_aliases=aliases or {},
        compiler_params=pltpu.CompilerParams(vmem_limit_bytes=16 * MIB),
        cost_estimate=pl.CostEstimate(flops=weight, bytes_accessed=1024, transcendentals=0),
        name=name,
    )


def is_first():
    return lax.axis_index("pipe") == 0


def is_slab(odd):
    return lax.axis_index("ctx") % 2 == odd


def array(rows, cols, kind=BF16):
    return jax.ShapeDtypeStruct((rows, cols), kind)


def multiply(keys_ref, values_ref, keys_in, values_in, sems, out_refs, meanwhile):
    rows = out_refs[0].shape[0]
    step = rows // PIECES
    spans = [pl.ds(piece * step, step) for piece in range(PIECES)]
    copies = []
    for piece, span in enumerate(spans):
        copies.append(
            (
                pltpu.make_async_copy(keys_ref.at[0, span], keys_in.at[span], sems.at[2 * piece]),
                pltpu.make_async_copy(values_ref.at[0, span], values_in.at[span], sems.at[2 * piece + 1]),
            )
        )
        for copy in copies[-1]:
            copy.start()
    meanwhile()
    for span, pair in zip(spans, copies):
        for copy in pair:
            copy.wait()
        first = 0
        for out_ref in out_refs:
            for tile in range(0, out_ref.shape[1], LANES):
                at = slice(first + tile, first + tile + LANES)
                product = keys_in[span, at].astype(F32) * values_in[span, at].astype(F32)
                out_ref[span, tile : tile + LANES] = product.astype(BF16)
            first += out_ref.shape[1]


def fill_lines(bank, scales, assign, lines_ref):
    groups, taps = lines_ref.shape
    size = bank.shape[0]
    chosen = (lax.broadcasted_iota(jnp.int32, (size, groups), 0) == assign).astype(F32).astype(BF16)
    contract = (((0,), (0,)), ((), ()))
    picked = lax.dot_general(bank, chosen, contract, preferred_element_type=F32)
    scaled = (picked * scales).astype(BF16)
    order = lax.broadcasted_iota(jnp.int32, (taps, taps), 0) + lax.broadcasted_iota(jnp.int32, (taps, taps), 1)
    flip = (order == taps - 1).astype(F32).astype(BF16)
    lines_ref[...] = lax.dot_general(scaled, flip, contract, preferred_element_type=F32)


def lead_kernel(queries_ref, keys_ref, values_ref, raw_ref, rest_ref, keys_in, values_in, sems, own_sem):
    rows = rest_ref.shape[0]

    @pl.when(is_first())
    def _():
        source = queries_ref.at[0, :, pl.ds(0, RAW)]
        copy = pltpu.make_async_copy(source, raw_ref.at[pl.ds(0, rows)], own_sem)
        targets = [raw_ref.at[pl.ds(rows, rows)], rest_ref]
        multiply(keys_ref, values_ref, keys_in, values_in, sems, targets, copy.start)
        copy.wait()


def product_scratch(rows, total):
    return [pltpu.VMEM((rows, total), BF16), pltpu.VMEM((rows, total), BF16), pltpu.SemaphoreType.DMA((2 * PIECES,))]


def lead_of(queries, keys, values):
    rows, total = queries.shape[1:]
    return call(
        lead_kernel,
        "lead",
        (array(2 * rows, RAW), array(rows, total - RAW)),
        [HBM] * 3,
        (VMEM,) * 2,
        product_scratch(rows, total) + [pltpu.SemaphoreType.DMA(())],
    )(queries, keys, values)


def turn_table(lines_ref, row, count, table_ref, at):
    taps = lines_ref.shape[1]
    upper = lax.broadcasted_iota(jnp.int32, (ROW_BLOCK, taps), 1) > lax.broadcasted_iota(
        jnp.int32, (ROW_BLOCK, taps), 0
    )
    for group in range(count):
        line = lines_ref[row + group : row + group + 1, :]
        turned = pltpu.roll(jnp.broadcast_to(line, (ROW_BLOCK, taps)), 1, 1, stride=1, stride_axis=0)
        span = slice(at + group * ROW_BLOCK, at + (group + 1) * ROW_BLOCK)
        table_ref[span, :taps] = jnp.where(upper, turned, 0.0).astype(BF16)
        table_ref[span, taps:] = jnp.where(upper, 0.0, turned)[:, :ROW_BLOCK].astype(BF16)


def product_kernel(*refs):
    keys_ref, values_ref, bank_ref, scales_ref, assign_ref, rest_ref = refs[:6]
    lines_ref, wire_ref, near_ref, far_ref, tail_ref, keys_in, values_in, sems = refs[6:]

    def taps():
        fill_lines(bank_ref[0], scales_ref[...], assign_ref[...], lines_ref)

    @pl.when(jnp.logical_and(is_first(), is_slab(1)))
    def _():
        taps()
        wire_ref[...] = lines_ref[: wire_ref.shape[0], :].astype(BF16)
        near_ref[...] = rest_ref[:, :NEAR]
        far_ref[...] = rest_ref[:, NEAR:]

    @pl.when(jnp.logical_not(is_first()))
    def _():
        multiply(keys_ref, values_ref, keys_in, values_in, sems, [near_ref, far_ref, tail_ref], taps)


def wire_rows(groups, total):
    return -(-RAW * groups // (total * 16)) * 16


def product_of(keys, values, bank, scales, assign, rest):
    rows, total = keys.shape[1:]
    groups, taps = assign.shape[1], bank.shape[2]
    return call(
        product_kernel,
        "product",
        (
            array(groups, taps, F32),
            array(wire_rows(groups, total), taps),
            array(rows, NEAR),
            array(rows, total - RAW - NEAR),
            array(rows, RAW),
        ),
        [HBM, HBM] + [VMEM] * 4,
        (VMEM,) * 5,
        product_scratch(rows, total),
    )(keys, values, bank, scales, assign, rest)


def mix(table_ref, row, share, window, store):
    depth = table_ref.shape[1]
    rows = window.shape[0] - depth + ROW_BLOCK
    member = lax.broadcasted_iota(jnp.int32, (ROW_BLOCK, LANES), 1) // (LANES // share)
    table = table_ref[row : row + share * ROW_BLOCK, :]
    for first in range(0, rows, 2 * ROW_BLOCK):
        starts = (first, first + ROW_BLOCK)
        pair = jnp.concatenate([window[begin : begin + depth] for begin in starts], axis=1)
        sums = jnp.dot(table, pair, preferred_element_type=F32)
        for place, begin in enumerate(starts):
            part = sums[:, place * LANES : (place + 1) * LANES]
            mixed = part[:ROW_BLOCK]
            for group in range(1, share):
                mixed = jnp.where(member == group, part[group * ROW_BLOCK : (group + 1) * ROW_BLOCK], mixed)
            store(slice(begin, begin + ROW_BLOCK), mixed)


def mix_all(width, share, lines_ref, line, table_ref, start_ref, behind_ref, product_ref, local, store):
    rows = product_ref.shape[0]
    first = (lax.axis_index("ctx") - 1) * rows
    inside = first + lax.broadcasted_iota(jnp.int32, (2 * rows, LANES), 0) >= start_ref[0]
    for tile in range(width // LANES):
        at = slice(tile * LANES, (tile + 1) * LANES)
        near, inner = (slice(begin + at.start, begin + at.stop) for begin in local)
        row = tile * share * ROW_BLOCK
        turn_table(lines_ref, line + tile * share, share, table_ref, row)
        window = jnp.concatenate([behind_ref[:, near], product_ref[:, inner]], axis=0)
        window = jnp.where(inside, window, jnp.zeros_like(window))
        mix(table_ref, row, share, window, functools.partial(store, at))


def share_of(lines_ref, total):
    return LANES * lines_ref.shape[0] // total


def own_kernel(odd, first, shift, local, extra, *refs):
    start_ref, lines_ref, behind_ref, product_ref, queries_ref, residual_ref = refs[:6]
    out_ref, table_ref = refs[-2:]
    width = out_ref.shape[1]
    share = share_of(lines_ref, residual_ref.shape[1])

    @pl.when(jnp.logical_and(is_first(), is_slab(odd)))
    def _():
        def store(at, span, mixed):
            cols = slice(first + at.start, first + at.stop)
            gated = queries_ref[0, span, cols].astype(F32) * mixed
            out_ref[span, at] = (residual_ref[span, cols].astype(F32) + gated).astype(BF16)

        line = first // LANES * share
        at = (shift, local)
        mix_all(width, share, lines_ref, line, table_ref, start_ref, behind_ref, product_ref, at, store)
        if extra:
            rows = out_ref.shape[0] - extra
            for part in range(RAW // LANES):
                taken = lines_ref[part * extra : (part + 1) * extra, :].astype(BF16)
                out_ref[rows:, part * LANES : (part + 1) * LANES] = taken


def table_scratch(lines, width, total):
    groups, taps = lines.shape
    return pltpu.VMEM((width * groups // total * ROW_BLOCK, taps + ROW_BLOCK), BF16)


def own_of(odd, origin, extra, start, lines, behind, product, queries, residual, first, width, *after):
    rows, total = residual.shape
    return call(
        functools.partial(own_kernel, odd, first, first - origin, first - RAW, extra),
        "own",
        array(rows + extra, width),
        [SMEM] + [VMEM] * 5 + [ANY] * len(after),
        VMEM,
        [table_scratch(lines, width, total)],
    )(start, lines, behind, product, queries, residual, *after)


def pick_kernel(*refs):
    raw_ref, received_ref, tail_ref, bank_ref, scales_ref, assign_ref = refs[:6]
    queries_ref, product_ref, lines_ref = refs[8:]
    rows = queries_ref.shape[0]

    @pl.when(jnp.logical_and(is_first(), is_slab(0)))
    def _():
        fill_lines(bank_ref[0], scales_ref[...], assign_ref[...], lines_ref)

    def take(source):
        queries_ref[...] = source[:rows, :]
        product_ref[:, :RAW] = source[rows:, :]

    pl.when(is_first())(lambda: take(raw_ref))

    @pl.when(jnp.logical_not(is_first()))
    def _():
        take(received_ref)
        product_ref[:, RAW:] = tail_ref[...]


def pick_of(raw, received, tail, bank, scales, assign, lines, after):
    rows, width = raw.shape[0] // 2, raw.shape[1]
    return call(
        pick_kernel,
        "pick",
        (array(rows, width), array(rows, 2 * width), array(*lines.shape, F32)),
        [VMEM] * 7 + [ANY],
        (VMEM,) * 3,
        weight=SLOW,
        aliases={6: 2},
    )(raw, received, tail, bank, scales, assign, lines, after)


def hold_kernel(value_ref, _, out_ref):
    pass


def held_back(value, after, weight=QUICK):
    return call(
        hold_kernel, "hold", array(*value.shape), [ANY, ANY], ANY, weight=weight, aliases={0: 0}
    )(value, after)


def send_out(pieces, out_ref, sems):
    copies = [
        pltpu.make_async_copy(buffer, out_ref.at[0, :, pl.ds(first, buffer.shape[1])], sems.at[place])
        for place, (buffer, first) in enumerate(pieces)
    ]
    for copy in copies:
        copy.start()
    return copies


def wait_all(copies):
    for copy in copies:
        copy.wait()


def later_kernel(places, *refs):
    start_ref, lines_ref, near_behind, near_ref, far_behind, far_ref, raw_behind, tail_ref, queries_ref = refs[:9]
    own_refs = refs[9 : 9 + len(places)]
    out_ref, gated_ref, table_ref, sems = refs[-4:]
    total = queries_ref.shape[2]
    share = share_of(lines_ref, total)

    for odd in (0, 1):

        @pl.when(jnp.logical_and(is_first(), is_slab(odd)))
        def _():
            pieces = [
                (own_ref.at[pl.ds(0, out_ref.shape[1])], first)
                for own_ref, (side, first, _) in zip(own_refs, places)
                if side == odd
            ]
            wait_all(send_out(pieces, out_ref, sems))

    @pl.when(jnp.logical_not(is_first()))
    def _():
        parts = (
            (0, 0, near_behind, near_ref),
            (NEAR, 0, far_behind, far_ref),
            (total - RAW, RAW, raw_behind, tail_ref),
        )
        for first, skip, behind_ref, product_ref in parts:

            def store(at, span, mixed):
                cols = slice(first + at.start, first + at.stop)
                gated_ref[span, cols] = queries_ref[0, span, cols].astype(F32) * mixed

            width, line = product_ref.shape[1], first // LANES * share
            at = (skip, 0)
            mix_all(width, share, lines_ref, line, table_ref, start_ref, behind_ref, product_ref, at, store)


def later_of(start, lines, near_behind, near, far_behind, far, raw_behind, tail, queries, own, places):
    rows, total = queries.shape[1:]
    return call(
        functools.partial(later_kernel, places),
        "later",
        (jax.ShapeDtypeStruct((1, rows, total), BF16), array(rows, total, F32)),
        [SMEM] + [VMEM] * (8 + len(own)),
        (ANY, VMEM),
        [table_scratch(lines, max(NEAR, total - RAW - NEAR), total), pltpu.SemaphoreType.DMA((len(own),))],
        weight=SLOW,
    )(start, lines, near_behind, near, far_behind, far, raw_behind, tail, queries, *own)


def raw_kernel(*refs):
    start_ref, lines_ref, wire_ref, received_ref = refs[:4]
    behind_ref, product_ref, queries_ref, gated_ref, residual_ref = refs[4:9]
    out_ref, chosen_ref, table_ref, buffer, sems = refs[10:]
    rows, width = buffer.shape
    share = share_of(lines_ref, residual_ref.shape[1])

    @pl.when(is_first())
    def _():
        chosen_ref[...] = lines_ref[: chosen_ref.shape[0], :]

    @pl.when(jnp.logical_and(jnp.logical_not(is_first()), is_slab(1)))
    def _():
        chosen_ref[...] = wire_ref[...].astype(F32)

    @pl.when(jnp.logical_and(jnp.logical_not(is_first()), is_slab(0)))
    def _():
        for part in range(RAW // LANES):
            taken = received_ref[rows:, part * LANES : (part + 1) * LANES]
            chosen_ref[part * LINES : (part + 1) * LINES, :] = taken.astype(F32)

    def store(at, span, mixed):
        gated = queries_ref[span, at].astype(F32) * mixed
        buffer[span, at] = (residual_ref[span, at].astype(F32) + gated).astype(BF16)

    mix_all(width, share, chosen_ref, 0, table_ref, start_ref, behind_ref, product_ref, (0, 0), store)

    @pl.when(jnp.logical_not(is_first()))
    def _():
        buffer[...] = (buffer[...].astype(F32) + gated_ref[:, :width]).astype(BF16)

    wait_all(send_out([(buffer, 0)], out_ref, sems))


def raw_finish(held, start, lines, wire, received, behind, product, queries, gated, residual):
    rows, width = queries.shape
    total = residual.shape[1]
    return call(
        raw_kernel,
        "raw",
        jax.ShapeDtypeStruct(held.shape, BF16),
        [SMEM] + [VMEM] * 8 + [ANY],
        ANY,
        [
            pltpu.VMEM(wire.shape, F32),
            table_scratch(lines, width, total),
            pltpu.VMEM((rows, width), BF16),
            pltpu.SemaphoreType.DMA((1,)),
        ],
        weight=SLOW,
        aliases={9: 0},
    )(start, lines, wire, received, behind, product, queries, gated, residual, held)


def finish_kernel(odd, places, *refs):
    gated_ref, received_refs = refs[0], refs[1 : 1 + len(places)]
    out_ref, *buffers, sems = refs[2 + len(places) :]

    @pl.when(jnp.logical_and(jnp.logical_not(is_first()), is_slab(odd)))
    def _():
        copies = []
        for place, (_, first, width) in enumerate(places):
            buffer = buffers[place]
            total = received_refs[place][: buffer.shape[0], :].astype(F32) + gated_ref[:, first : first + width]
            buffer[...] = total.astype(BF16)
            copies += send_out([(buffer, first)], out_ref, sems.at[pl.ds(place, 1)])
        wait_all(copies)


def finish(held, gated, received, places):
    rows = gated.shape[0]
    count = len(places)
    return call(
        functools.partial(finish_kernel, places[0][0], places),
        "finish",
        jax.ShapeDtypeStruct(held.shape, BF16),
        [VMEM] * (1 + count) + [ANY],
        ANY,
        [pltpu.VMEM((rows, width), BF16) for _, _, width in places] + [pltpu.SemaphoreType.DMA((count,))],
        weight=SLOW,
        aliases={1 + count: 0},
    )(gated, *received, held)


def body(queries, keys, values, residual, filter_bank, filter_scales, group_filter, context_start):
    total = queries.shape[2]
    small = (filter_bank, filter_scales, group_filter)
    far_queries, keys, values = (
        pltpu.with_memory_space_constraint(value, pltpu.HBM) for value in (queries, keys, values)
    )
    raw, rest = lead_of(far_queries, keys, values)
    raw_received = to_next_section(raw)
    chip_behind = to_next_slab(rest, (0, 0))
    lines, wire, near, far, tail = product_of(keys, values, *small, rest)
    own, received, places = [], [], []

    def send(odd, behind, origin, first, width, *after, extra=0):
        piece = own_of(
            odd, origin, extra, context_start, lines, behind, rest, queries, residual, first, width, *after
        )
        own.append(piece)
        received.append(to_next_section(piece, (odd,)))
        places.append((odd, first, width))
        return first + width, piece

    links = ((1, 0), (0, 1), (1, 1))
    first, after = send(1, chip_behind, RAW, RAW, ODD[0], lines)
    near = held_back(near, after)
    near_behind = to_next_slab(near, *links)
    first, after = send(1, chip_behind, RAW, first, ODD[1], near)
    raw_queries, raw_product, lines = pick_of(raw, raw_received, tail, *small, lines, after)
    far = held_back(far, raw_queries)
    far_behind = to_next_slab(far, *links)
    raw_product = held_back(raw_product, far)
    raw_behind = to_next_slab(raw_product, (0, 0), *links)
    raw_queries = held_back(raw_queries, received[0], SLOW)
    first, after = send(0, near_behind, RAW, RAW, EVEN[0], raw_queries)
    first, after = send(0, near_behind, RAW, first, EVEN[1], after, extra=LINES)
    origin = first
    first, after = send(0, far_behind, origin, first, EVEN[2], after, received[1])
    first, after = send(0, far_behind, origin, first, EVEN[3], after, raw_behind)
    wire_received = to_next_section(held_back(wire, after), (1,))
    held, gated = later_of(
        context_start,
        lines,
        near_behind,
        near,
        far_behind,
        far,
        raw_behind,
        tail,
        queries,
        own,
        places,
    )
    odd = len(ODD)
    held = finish(held, gated, received[:odd], places[:odd])
    held = finish(held, gated, received[odd : odd + 2], places[odd : odd + 2])
    held = raw_finish(
        held,
        context_start,
        lines,
        wire_received,
        received[odd + 1],
        raw_behind,
        raw_product,
        raw_queries,
        gated,
        residual,
    )
    for last in (odd + 2, odd + 3):
        held = finish(held, gated, received[last : last + 1], places[last : last + 1])
    return held


def solution(mesh):
    return jax.shard_map(
        body,
        mesh=mesh,
        in_specs=(
            P("pipe", ("dp", "ctx"), None),
            P("pipe", ("dp", "ctx"), None),
            P("pipe", ("dp", "ctx"), None),
            P(("dp", "ctx"), None),
            P("pipe", None, None),
            P("pipe", None),
            P("pipe", None),
            P("dp"),
        ),
        out_specs=P("pipe", ("dp", "ctx"), None),
        check_vma=False,
    )
```

```python
import functools

import jax
import jax.numpy as jnp
from jax import lax
from jax.experimental import pallas as pl
from jax.experimental.pallas import tpu as pltpu
from jax.sharding import PartitionSpec as P

LANES = 128
ROW_BLOCK = 32
RAW = 384
ODD = (1536, 2176)
EVEN = (1024, 896, 1280, 512)
PIECES = 4
LINES = 8
NEAR = 1920
F32 = jnp.float32
BF16 = jnp.bfloat16
MIB = 1024 * 1024
QUICK, SLOW = 1024, 20_000_000_000

SMEM = pl.BlockSpec(memory_space=pltpu.SMEM)
VMEM = pl.BlockSpec(memory_space=pltpu.VMEM)
ANY = pl.BlockSpec(memory_space=pl.ANY)
HBM = pl.BlockSpec(memory_space=pltpu.HBM)


def to_next_slab(value, *links):
    slabs, depth = lax.axis_size("ctx"), lax.axis_size("pipe")
    pairs = [
        (slab * depth + pipe, (slab + 1) * depth + pipe)
        for odd, pipe in links
        for slab in range(slabs - 1)
        if slab % 2 == odd
    ]
    return lax.ppermute(value, ("ctx", "pipe"), pairs)


def to_next_section(value, slabs=(0, 1)):
    depth = lax.axis_size("pipe")
    pairs = [(slab * depth, slab * depth + 1) for slab in range(lax.axis_size("ctx")) if slab % 2 in slabs]
    return lax.ppermute(value, ("ctx", "pipe"), pairs)


def call(kernel, name, out_shape, in_specs, out_specs, scratch=(), weight=QUICK, aliases=None):
    return pl.pallas_call(
        kernel,
        out_shape=out_shape,
        in_specs=in_specs,
        out_specs=out_specs,
        scratch_shapes=list(scratch),
        input_output_aliases=aliases or {},
        compiler_params=pltpu.CompilerParams(vmem_limit_bytes=16 * MIB),
        cost_estimate=pl.CostEstimate(flops=weight, bytes_accessed=1024, transcendentals=0),
        name=name,
    )


def is_first():
    return lax.axis_index("pipe") == 0


def is_slab(odd):
    return lax.axis_index("ctx") % 2 == odd


def array(rows, cols, kind=BF16):
    return jax.ShapeDtypeStruct((rows, cols), kind)


def multiply(keys_ref, values_ref, keys_in, values_in, sems, out_refs, meanwhile):
    rows = out_refs[0].shape[0]
    step = rows // PIECES
    spans = [pl.ds(piece * step, step) for piece in range(PIECES)]
    copies = []
    for piece, span in enumerate(spans):
        copies.append(
            (
                pltpu.make_async_copy(keys_ref.at[0, span], keys_in.at[span], sems.at[2 * piece]),
                pltpu.make_async_copy(values_ref.at[0, span], values_in.at[span], sems.at[2 * piece + 1]),
            )
        )
        for copy in copies[-1]:
            copy.start()
    meanwhile()
    for span, pair in zip(spans, copies):
        for copy in pair:
            copy.wait()
        first = 0
        for out_ref in out_refs:
            for tile in range(0, out_ref.shape[1], LANES):
                at = slice(first + tile, first + tile + LANES)
                out_ref[span, tile : tile + LANES] = keys_in[span, at] * values_in[span, at]
            first += out_ref.shape[1]


def fill_lines(bank, scales, assign, lines_ref):
    groups, taps = lines_ref.shape
    size = bank.shape[0]
    chosen = (lax.broadcasted_iota(jnp.int32, (size, groups), 0) == assign).astype(F32).astype(BF16)
    contract = (((0,), (0,)), ((), ()))
    picked = lax.dot_general(bank, chosen, contract, preferred_element_type=F32)
    scaled = (picked * scales).astype(BF16)
    order = lax.broadcasted_iota(jnp.int32, (taps, taps), 0) + lax.broadcasted_iota(jnp.int32, (taps, taps), 1)
    flip = (order == taps - 1).astype(F32).astype(BF16)
    lines_ref[...] = lax.dot_general(scaled, flip, contract, preferred_element_type=F32)


def lead_kernel(queries_ref, keys_ref, values_ref, raw_ref, rest_ref, keys_in, values_in, sems, own_sem):
    rows = rest_ref.shape[0]

    @pl.when(is_first())
    def _():
        source = queries_ref.at[0, :, pl.ds(0, RAW)]
        copy = pltpu.make_async_copy(source, raw_ref.at[pl.ds(0, rows)], own_sem)
        targets = [raw_ref.at[pl.ds(rows, rows)], rest_ref]
        multiply(keys_ref, values_ref, keys_in, values_in, sems, targets, copy.start)
        copy.wait()


def product_scratch(rows, total):
    return [pltpu.VMEM((rows, total), BF16), pltpu.VMEM((rows, total), BF16), pltpu.SemaphoreType.DMA((2 * PIECES,))]


def lead_of(queries, keys, values):
    rows, total = queries.shape[1:]
    return call(
        lead_kernel,
        "lead",
        (array(2 * rows, RAW), array(rows, total - RAW)),
        [HBM] * 3,
        (VMEM,) * 2,
        product_scratch(rows, total) + [pltpu.SemaphoreType.DMA(())],
    )(queries, keys, values)


def turn_table(lines_ref, row, count, table_ref, at):
    taps = lines_ref.shape[1]
    upper = lax.broadcasted_iota(jnp.int32, (ROW_BLOCK, taps), 1) > lax.broadcasted_iota(
        jnp.int32, (ROW_BLOCK, taps), 0
    )
    for group in range(count):
        line = lines_ref[row + group : row + group + 1, :]
        turned = pltpu.roll(jnp.broadcast_to(line, (ROW_BLOCK, taps)), 1, 1, stride=1, stride_axis=0)
        span = slice(at + group * ROW_BLOCK, at + (group + 1) * ROW_BLOCK)
        table_ref[span, :taps] = jnp.where(upper, turned, 0.0).astype(BF16)
        table_ref[span, taps:] = jnp.where(upper, 0.0, turned)[:, :ROW_BLOCK].astype(BF16)


def product_kernel(*refs):
    keys_ref, values_ref, bank_ref, scales_ref, assign_ref, rest_ref = refs[:6]
    lines_ref, wire_ref, near_ref, far_ref, tail_ref, keys_in, values_in, sems = refs[6:]

    def taps():
        fill_lines(bank_ref[0], scales_ref[...], assign_ref[...], lines_ref)

    @pl.when(jnp.logical_and(is_first(), is_slab(1)))
    def _():
        taps()
        wire_ref[...] = lines_ref[: wire_ref.shape[0], :].astype(BF16)
        near_ref[...] = rest_ref[:, :NEAR]
        far_ref[...] = rest_ref[:, NEAR:]

    @pl.when(jnp.logical_not(is_first()))
    def _():
        multiply(keys_ref, values_ref, keys_in, values_in, sems, [near_ref, far_ref, tail_ref], taps)


def wire_rows(groups, total):
    return -(-RAW * groups // (total * 16)) * 16


def product_of(keys, values, bank, scales, assign, rest):
    rows, total = keys.shape[1:]
    groups, taps = assign.shape[1], bank.shape[2]
    return call(
        product_kernel,
        "product",
        (
            array(groups, taps, F32),
            array(wire_rows(groups, total), taps),
            array(rows, NEAR),
            array(rows, total - RAW - NEAR),
            array(rows, RAW),
        ),
        [HBM, HBM] + [VMEM] * 4,
        (VMEM,) * 5,
        product_scratch(rows, total),
    )(keys, values, bank, scales, assign, rest)


def mix(table_ref, row, share, window, store):
    depth = table_ref.shape[1]
    rows = window.shape[0] - depth + ROW_BLOCK
    member = lax.broadcasted_iota(jnp.int32, (ROW_BLOCK, LANES), 1) // (LANES // share)
    table = table_ref[row : row + share * ROW_BLOCK, :]
    for first in range(0, rows, 2 * ROW_BLOCK):
        starts = (first, first + ROW_BLOCK)
        pair = jnp.concatenate([window[begin : begin + depth] for begin in starts], axis=1)
        sums = jnp.dot(table, pair, preferred_element_type=F32)
        for place, begin in enumerate(starts):
            part = sums[:, place * LANES : (place + 1) * LANES]
            mixed = part[:ROW_BLOCK]
            for group in range(1, share):
                mixed = jnp.where(member == group, part[group * ROW_BLOCK : (group + 1) * ROW_BLOCK], mixed)
            store(slice(begin, begin + ROW_BLOCK), mixed)


def mix_all(width, share, lines_ref, line, table_ref, start_ref, behind_ref, product_ref, local, store):
    rows = product_ref.shape[0]
    first = (lax.axis_index("ctx") - 1) * rows
    inside = first + lax.broadcasted_iota(jnp.int32, (2 * rows, LANES), 0) >= start_ref[0]
    for tile in range(width // LANES):
        at = slice(tile * LANES, (tile + 1) * LANES)
        near, inner = (slice(begin + at.start, begin + at.stop) for begin in local)
        row = tile * share * ROW_BLOCK
        turn_table(lines_ref, line + tile * share, share, table_ref, row)
        window = jnp.concatenate([behind_ref[:, near], product_ref[:, inner]], axis=0)
        window = jnp.where(inside, window, jnp.zeros_like(window))
        mix(table_ref, row, share, window, functools.partial(store, at))


def share_of(lines_ref, total):
    return LANES * lines_ref.shape[0] // total


def own_kernel(odd, first, shift, local, extra, *refs):
    start_ref, lines_ref, behind_ref, product_ref, queries_ref, residual_ref = refs[:6]
    out_ref, table_ref = refs[-2:]
    width = out_ref.shape[1]
    share = share_of(lines_ref, residual_ref.shape[1])

    @pl.when(jnp.logical_and(is_first(), is_slab(odd)))
    def _():
        def store(at, span, mixed):
            cols = slice(first + at.start, first + at.stop)
            gated = queries_ref[0, span, cols].astype(F32) * mixed
            out_ref[span, at] = (residual_ref[span, cols].astype(F32) + gated).astype(BF16)

        line = first // LANES * share
        at = (shift, local)
        mix_all(width, share, lines_ref, line, table_ref, start_ref, behind_ref, product_ref, at, store)
        if extra:
            rows = out_ref.shape[0] - extra
            for part in range(RAW // LANES):
                taken = lines_ref[part * extra : (part + 1) * extra, :].astype(BF16)
                out_ref[rows:, part * LANES : (part + 1) * LANES] = taken


def table_scratch(lines, width, total):
    groups, taps = lines.shape
    return pltpu.VMEM((width * groups // total * ROW_BLOCK, taps + ROW_BLOCK), BF16)


def own_of(odd, origin, extra, start, lines, behind, product, queries, residual, first, width, *after):
    rows, total = residual.shape
    return call(
        functools.partial(own_kernel, odd, first, first - origin, first - RAW, extra),
        "own",
        array(rows + extra, width),
        [SMEM] + [VMEM] * 5 + [ANY] * len(after),
        VMEM,
        [table_scratch(lines, width, total)],
    )(start, lines, behind, product, queries, residual, *after)


def pick_kernel(*refs):
    raw_ref, received_ref, tail_ref, bank_ref, scales_ref, assign_ref = refs[:6]
    queries_ref, product_ref, lines_ref = refs[8:]
    rows = queries_ref.shape[0]

    @pl.when(jnp.logical_and(is_first(), is_slab(0)))
    def _():
        fill_lines(bank_ref[0], scales_ref[...], assign_ref[...], lines_ref)

    def take(source):
        queries_ref[...] = source[:rows, :]
        product_ref[:, :RAW] = source[rows:, :]

    pl.when(is_first())(lambda: take(raw_ref))

    @pl.when(jnp.logical_not(is_first()))
    def _():
        take(received_ref)
        product_ref[:, RAW:] = tail_ref[...]


def pick_of(raw, received, tail, bank, scales, assign, lines, after):
    rows, width = raw.shape[0] // 2, raw.shape[1]
    return call(
        pick_kernel,
        "pick",
        (array(rows, width), array(rows, 2 * width), array(*lines.shape, F32)),
        [VMEM] * 7 + [ANY],
        (VMEM,) * 3,
        weight=SLOW,
        aliases={6: 2},
    )(raw, received, tail, bank, scales, assign, lines, after)


def hold_kernel(value_ref, _, out_ref):
    pass


def held_back(value, after, weight=QUICK):
    return call(
        hold_kernel, "hold", array(*value.shape), [ANY, ANY], ANY, weight=weight, aliases={0: 0}
    )(value, after)


def send_out(pieces, out_ref, sems):
    copies = [
        pltpu.make_async_copy(buffer, out_ref.at[0, :, pl.ds(first, buffer.shape[1])], sems.at[place])
        for place, (buffer, first) in enumerate(pieces)
    ]
    for copy in copies:
        copy.start()
    return copies


def wait_all(copies):
    for copy in copies:
        copy.wait()


def later_kernel(places, *refs):
    start_ref, lines_ref, near_behind, near_ref, far_behind, far_ref, raw_behind, tail_ref, queries_ref = refs[:9]
    own_refs = refs[9 : 9 + len(places)]
    out_ref, gated_ref, table_ref, sems = refs[-4:]
    total = queries_ref.shape[2]
    share = share_of(lines_ref, total)

    for odd in (0, 1):

        @pl.when(jnp.logical_and(is_first(), is_slab(odd)))
        def _():
            pieces = [
                (own_ref.at[pl.ds(0, out_ref.shape[1])], first)
                for own_ref, (side, first, _) in zip(own_refs, places)
                if side == odd
            ]
            wait_all(send_out(pieces, out_ref, sems))

    @pl.when(jnp.logical_not(is_first()))
    def _():
        parts = (
            (0, 0, near_behind, near_ref),
            (NEAR, 0, far_behind, far_ref),
            (total - RAW, RAW, raw_behind, tail_ref),
        )
        for first, skip, behind_ref, product_ref in parts:

            def store(at, span, mixed):
                cols = slice(first + at.start, first + at.stop)
                gated_ref[span, cols] = queries_ref[0, span, cols].astype(F32) * mixed

            width, line = product_ref.shape[1], first // LANES * share
            at = (skip, 0)
            mix_all(width, share, lines_ref, line, table_ref, start_ref, behind_ref, product_ref, at, store)


def later_of(start, lines, near_behind, near, far_behind, far, raw_behind, tail, queries, own, places):
    rows, total = queries.shape[1:]
    return call(
        functools.partial(later_kernel, places),
        "later",
        (jax.ShapeDtypeStruct((1, rows, total), BF16), array(rows, total, F32)),
        [SMEM] + [VMEM] * (8 + len(own)),
        (ANY, VMEM),
        [table_scratch(lines, max(NEAR, total - RAW - NEAR), total), pltpu.SemaphoreType.DMA((len(own),))],
        weight=SLOW,
    )(start, lines, near_behind, near, far_behind, far, raw_behind, tail, queries, *own)


def raw_kernel(*refs):
    start_ref, lines_ref, wire_ref, received_ref = refs[:4]
    behind_ref, product_ref, queries_ref, gated_ref, residual_ref = refs[4:9]
    out_ref, chosen_ref, table_ref, buffer, sems = refs[10:]
    rows, width = buffer.shape
    share = share_of(lines_ref, residual_ref.shape[1])

    @pl.when(is_first())
    def _():
        chosen_ref[...] = lines_ref[: chosen_ref.shape[0], :]

    @pl.when(jnp.logical_and(jnp.logical_not(is_first()), is_slab(1)))
    def _():
        chosen_ref[...] = wire_ref[...].astype(F32)

    @pl.when(jnp.logical_and(jnp.logical_not(is_first()), is_slab(0)))
    def _():
        for part in range(RAW // LANES):
            taken = received_ref[rows:, part * LANES : (part + 1) * LANES]
            chosen_ref[part * LINES : (part + 1) * LINES, :] = taken.astype(F32)

    def store(at, span, mixed):
        gated = queries_ref[span, at].astype(F32) * mixed
        buffer[span, at] = (residual_ref[span, at].astype(F32) + gated).astype(BF16)

    mix_all(width, share, chosen_ref, 0, table_ref, start_ref, behind_ref, product_ref, (0, 0), store)

    @pl.when(jnp.logical_not(is_first()))
    def _():
        buffer[...] = (buffer[...].astype(F32) + gated_ref[:, :width]).astype(BF16)

    wait_all(send_out([(buffer, 0)], out_ref, sems))


def raw_finish(held, start, lines, wire, received, behind, product, queries, gated, residual):
    rows, width = queries.shape
    total = residual.shape[1]
    return call(
        raw_kernel,
        "raw",
        jax.ShapeDtypeStruct(held.shape, BF16),
        [SMEM] + [VMEM] * 8 + [ANY],
        ANY,
        [
            pltpu.VMEM(wire.shape, F32),
            table_scratch(lines, width, total),
            pltpu.VMEM((rows, width), BF16),
            pltpu.SemaphoreType.DMA((1,)),
        ],
        weight=SLOW,
        aliases={9: 0},
    )(start, lines, wire, received, behind, product, queries, gated, residual, held)


def finish_kernel(odd, places, *refs):
    gated_ref, received_refs = refs[0], refs[1 : 1 + len(places)]
    out_ref, *buffers, sems = refs[2 + len(places) :]

    @pl.when(jnp.logical_and(jnp.logical_not(is_first()), is_slab(odd)))
    def _():
        copies = []
        for place, (_, first, width) in enumerate(places):
            buffer = buffers[place]
            total = received_refs[place][: buffer.shape[0], :].astype(F32) + gated_ref[:, first : first + width]
            buffer[...] = total.astype(BF16)
            copies += send_out([(buffer, first)], out_ref, sems.at[pl.ds(place, 1)])
        wait_all(copies)


def finish(held, gated, received, places):
    rows = gated.shape[0]
    count = len(places)
    return call(
        functools.partial(finish_kernel, places[0][0], places),
        "finish",
        jax.ShapeDtypeStruct(held.shape, BF16),
        [VMEM] * (1 + count) + [ANY],
        ANY,
        [pltpu.VMEM((rows, width), BF16) for _, _, width in places] + [pltpu.SemaphoreType.DMA((count,))],
        weight=SLOW,
        aliases={1 + count: 0},
    )(gated, *received, held)


def body(queries, keys, values, residual, filter_bank, filter_scales, group_filter, context_start):
    total = queries.shape[2]
    small = (filter_bank, filter_scales, group_filter)
    far_queries, keys, values = (
        pltpu.with_memory_space_constraint(value, pltpu.HBM) for value in (queries, keys, values)
    )
    raw, rest = lead_of(far_queries, keys, values)
    raw_received = to_next_section(raw)
    chip_behind = to_next_slab(rest, (0, 0))
    lines, wire, near, far, tail = product_of(keys, values, *small, rest)
    own, received, places = [], [], []

    def send(odd, behind, origin, first, width, *after, extra=0):
        piece = own_of(
            odd, origin, extra, context_start, lines, behind, rest, queries, residual, first, width, *after
        )
        own.append(piece)
        received.append(to_next_section(piece, (odd,)))
        places.append((odd, first, width))
        return first + width, piece

    links = ((1, 0), (0, 1), (1, 1))
    first, after = send(1, chip_behind, RAW, RAW, ODD[0], lines)
    near = held_back(near, after)
    near_behind = to_next_slab(near, *links)
    first, after = send(1, chip_behind, RAW, first, ODD[1], near)
    raw_queries, raw_product, lines = pick_of(raw, raw_received, tail, *small, lines, after)
    far = held_back(far, raw_queries)
    far_behind = to_next_slab(far, *links)
    raw_product = held_back(raw_product, far)
    raw_behind = to_next_slab(raw_product, (0, 0), *links)
    raw_queries = held_back(raw_queries, received[0], SLOW)
    first, after = send(0, near_behind, RAW, RAW, EVEN[0], raw_queries)
    first, after = send(0, near_behind, RAW, first, EVEN[1], after, extra=LINES)
    origin = first
    first, after = send(0, far_behind, origin, first, EVEN[2], after, received[1])
    first, after = send(0, far_behind, origin, first, EVEN[3], after, raw_behind)
    wire_received = to_next_section(held_back(wire, after), (1,))
    held, gated = later_of(
        context_start,
        lines,
        near_behind,
        near,
        far_behind,
        far,
        raw_behind,
        tail,
        queries,
        own,
        places,
    )
    odd = len(ODD)
    held = finish(held, gated, received[:odd], places[:odd])
    held = finish(held, gated, received[odd : odd + 2], places[odd : odd + 2])
    held = raw_finish(
        held,
        context_start,
        lines,
        wire_received,
        received[odd + 1],
        raw_behind,
        raw_product,
        raw_queries,
        gated,
        residual,
    )
    for last in (odd + 2, odd + 3):
        held = finish(held, gated, received[last : last + 1], places[last : last + 1])
    return held


def solution(mesh):
    return jax.shard_map(
        body,
        mesh=mesh,
        in_specs=(
            P("pipe", ("dp", "ctx"), None),
            P("pipe", ("dp", "ctx"), None),
            P("pipe", ("dp", "ctx"), None),
            P(("dp", "ctx"), None),
            P("pipe", None, None),
            P("pipe", None),
            P("pipe", None),
            P("dp"),
        ),
        out_specs=P("pipe", ("dp", "ctx"), None),
        check_vma=False,
    )
```

```python
import functools

import jax
import jax.numpy as jnp
from jax import lax
from jax.experimental import pallas as pl
from jax.experimental.pallas import tpu as pltpu
from jax.sharding import PartitionSpec as P

LANES = 128
ROW_BLOCK = 32
RAW = 384
ODD = (1792, 1920)
EVEN = (1024, 896, 1280, 512)
PIECES = 4
LINES = 8
NEAR = 1920
F32 = jnp.float32
BF16 = jnp.bfloat16
MIB = 1024 * 1024
QUICK, SLOW = 1024, 20_000_000_000

SMEM = pl.BlockSpec(memory_space=pltpu.SMEM)
VMEM = pl.BlockSpec(memory_space=pltpu.VMEM)
ANY = pl.BlockSpec(memory_space=pl.ANY)
HBM = pl.BlockSpec(memory_space=pltpu.HBM)


def to_next_slab(value, *links):
    slabs, depth = lax.axis_size("ctx"), lax.axis_size("pipe")
    pairs = [
        (slab * depth + pipe, (slab + 1) * depth + pipe)
        for odd, pipe in links
        for slab in range(slabs - 1)
        if slab % 2 == odd
    ]
    return lax.ppermute(value, ("ctx", "pipe"), pairs)


def to_next_section(value, slabs=(0, 1)):
    depth = lax.axis_size("pipe")
    pairs = [(slab * depth, slab * depth + 1) for slab in range(lax.axis_size("ctx")) if slab % 2 in slabs]
    return lax.ppermute(value, ("ctx", "pipe"), pairs)


def call(kernel, name, out_shape, in_specs, out_specs, scratch=(), weight=QUICK, aliases=None):
    return pl.pallas_call(
        kernel,
        out_shape=out_shape,
        in_specs=in_specs,
        out_specs=out_specs,
        scratch_shapes=list(scratch),
        input_output_aliases=aliases or {},
        compiler_params=pltpu.CompilerParams(vmem_limit_bytes=16 * MIB),
        cost_estimate=pl.CostEstimate(flops=weight, bytes_accessed=1024, transcendentals=0),
        name=name,
    )


def is_first():
    return lax.axis_index("pipe") == 0


def is_slab(odd):
    return lax.axis_index("ctx") % 2 == odd


def array(rows, cols, kind=BF16):
    return jax.ShapeDtypeStruct((rows, cols), kind)


def multiply(keys_ref, values_ref, keys_in, values_in, sems, out_refs, meanwhile):
    rows = out_refs[0].shape[0]
    step = rows // PIECES
    spans = [pl.ds(piece * step, step) for piece in range(PIECES)]
    copies = []
    for piece, span in enumerate(spans):
        copies.append(
            (
                pltpu.make_async_copy(keys_ref.at[0, span], keys_in.at[span], sems.at[2 * piece]),
                pltpu.make_async_copy(values_ref.at[0, span], values_in.at[span], sems.at[2 * piece + 1]),
            )
        )
        for copy in copies[-1]:
            copy.start()
    meanwhile()
    for span, pair in zip(spans, copies):
        for copy in pair:
            copy.wait()
        first = 0
        for out_ref in out_refs:
            for tile in range(0, out_ref.shape[1], LANES):
                at = slice(first + tile, first + tile + LANES)
                out_ref[span, tile : tile + LANES] = keys_in[span, at] * values_in[span, at]
            first += out_ref.shape[1]


def fill_lines(bank, scales, assign, lines_ref):
    groups, taps = lines_ref.shape
    size = bank.shape[0]
    chosen = (lax.broadcasted_iota(jnp.int32, (size, groups), 0) == assign).astype(F32).astype(BF16)
    contract = (((0,), (0,)), ((), ()))
    picked = lax.dot_general(bank, chosen, contract, preferred_element_type=F32)
    scaled = (picked * scales).astype(BF16)
    order = lax.broadcasted_iota(jnp.int32, (taps, taps), 0) + lax.broadcasted_iota(jnp.int32, (taps, taps), 1)
    flip = (order == taps - 1).astype(F32).astype(BF16)
    lines_ref[...] = lax.dot_general(scaled, flip, contract, preferred_element_type=F32)


def lead_kernel(queries_ref, keys_ref, values_ref, raw_ref, rest_ref, keys_in, values_in, sems, own_sem):
    rows = rest_ref.shape[0]

    @pl.when(is_first())
    def _():
        source = queries_ref.at[0, :, pl.ds(0, RAW)]
        copy = pltpu.make_async_copy(source, raw_ref.at[pl.ds(0, rows)], own_sem)
        targets = [raw_ref.at[pl.ds(rows, rows)], rest_ref]
        multiply(keys_ref, values_ref, keys_in, values_in, sems, targets, copy.start)
        copy.wait()


def product_scratch(rows, total):
    return [pltpu.VMEM((rows, total), BF16), pltpu.VMEM((rows, total), BF16), pltpu.SemaphoreType.DMA((2 * PIECES,))]


def lead_of(queries, keys, values):
    rows, total = queries.shape[1:]
    return call(
        lead_kernel,
        "lead",
        (array(2 * rows, RAW), array(rows, total - RAW)),
        [HBM] * 3,
        (VMEM,) * 2,
        product_scratch(rows, total) + [pltpu.SemaphoreType.DMA(())],
    )(queries, keys, values)


def turn_table(lines_ref, row, count, table_ref, at):
    taps = lines_ref.shape[1]
    upper = lax.broadcasted_iota(jnp.int32, (ROW_BLOCK, taps), 1) > lax.broadcasted_iota(
        jnp.int32, (ROW_BLOCK, taps), 0
    )
    for group in range(count):
        line = lines_ref[row + group : row + group + 1, :]
        turned = pltpu.roll(jnp.broadcast_to(line, (ROW_BLOCK, taps)), 1, 1, stride=1, stride_axis=0)
        span = slice(at + group * ROW_BLOCK, at + (group + 1) * ROW_BLOCK)
        table_ref[span, :taps] = jnp.where(upper, turned, 0.0).astype(BF16)
        table_ref[span, taps:] = jnp.where(upper, 0.0, turned)[:, :ROW_BLOCK].astype(BF16)


def product_kernel(*refs):
    keys_ref, values_ref, bank_ref, scales_ref, assign_ref, rest_ref = refs[:6]
    lines_ref, wire_ref, near_ref, far_ref, tail_ref, keys_in, values_in, sems = refs[6:]

    def taps():
        fill_lines(bank_ref[0], scales_ref[...], assign_ref[...], lines_ref)

    @pl.when(jnp.logical_and(is_first(), is_slab(1)))
    def _():
        taps()
        wire_ref[...] = lines_ref[: wire_ref.shape[0], :].astype(BF16)
        near_ref[...] = rest_ref[:, :NEAR]
        far_ref[...] = rest_ref[:, NEAR:]

    @pl.when(jnp.logical_not(is_first()))
    def _():
        multiply(keys_ref, values_ref, keys_in, values_in, sems, [near_ref, far_ref, tail_ref], taps)


def wire_rows(groups, total):
    return -(-RAW * groups // (total * 16)) * 16


def product_of(keys, values, bank, scales, assign, rest):
    rows, total = keys.shape[1:]
    groups, taps = assign.shape[1], bank.shape[2]
    return call(
        product_kernel,
        "product",
        (
            array(groups, taps, F32),
            array(wire_rows(groups, total), taps),
            array(rows, NEAR),
            array(rows, total - RAW - NEAR),
            array(rows, RAW),
        ),
        [HBM, HBM] + [VMEM] * 4,
        (VMEM,) * 5,
        product_scratch(rows, total),
    )(keys, values, bank, scales, assign, rest)


def mix(table_ref, row, share, window, store):
    depth = table_ref.shape[1]
    rows = window.shape[0] - depth + ROW_BLOCK
    member = lax.broadcasted_iota(jnp.int32, (ROW_BLOCK, LANES), 1) // (LANES // share)
    table = table_ref[row : row + share * ROW_BLOCK, :]
    for first in range(0, rows, 2 * ROW_BLOCK):
        starts = (first, first + ROW_BLOCK)
        pair = jnp.concatenate([window[begin : begin + depth] for begin in starts], axis=1)
        sums = jnp.dot(table, pair, preferred_element_type=F32)
        for place, begin in enumerate(starts):
            part = sums[:, place * LANES : (place + 1) * LANES]
            mixed = part[:ROW_BLOCK]
            for group in range(1, share):
                mixed = jnp.where(member == group, part[group * ROW_BLOCK : (group + 1) * ROW_BLOCK], mixed)
            store(slice(begin, begin + ROW_BLOCK), mixed)


def mix_all(width, share, lines_ref, line, table_ref, start_ref, behind_ref, product_ref, local, store):
    rows = product_ref.shape[0]
    first = (lax.axis_index("ctx") - 1) * rows
    inside = first + lax.broadcasted_iota(jnp.int32, (2 * rows, LANES), 0) >= start_ref[0]
    for tile in range(width // LANES):
        at = slice(tile * LANES, (tile + 1) * LANES)
        near, inner = (slice(begin + at.start, begin + at.stop) for begin in local)
        row = tile * share * ROW_BLOCK
        turn_table(lines_ref, line + tile * share, share, table_ref, row)
        window = jnp.concatenate([behind_ref[:, near], product_ref[:, inner]], axis=0)
        window = jnp.where(inside, window, jnp.zeros_like(window))
        mix(table_ref, row, share, window, functools.partial(store, at))


def share_of(lines_ref, total):
    return LANES * lines_ref.shape[0] // total


def own_kernel(odd, first, shift, local, extra, *refs):
    start_ref, lines_ref, behind_ref, product_ref, queries_ref, residual_ref = refs[:6]
    out_ref, table_ref = refs[-2:]
    width = out_ref.shape[1]
    share = share_of(lines_ref, residual_ref.shape[1])

    @pl.when(jnp.logical_and(is_first(), is_slab(odd)))
    def _():
        def store(at, span, mixed):
            cols = slice(first + at.start, first + at.stop)
            gated = queries_ref[0, span, cols].astype(F32) * mixed
            out_ref[span, at] = (residual_ref[span, cols].astype(F32) + gated).astype(BF16)

        line = first // LANES * share
        at = (shift, local)
        mix_all(width, share, lines_ref, line, table_ref, start_ref, behind_ref, product_ref, at, store)
        if extra:
            rows = out_ref.shape[0] - extra
            for part in range(RAW // LANES):
                taken = lines_ref[part * extra : (part + 1) * extra, :].astype(BF16)
                out_ref[rows:, part * LANES : (part + 1) * LANES] = taken


def table_scratch(lines, width, total):
    groups, taps = lines.shape
    return pltpu.VMEM((width * groups // total * ROW_BLOCK, taps + ROW_BLOCK), BF16)


def own_of(odd, origin, extra, start, lines, behind, product, queries, residual, first, width, *after):
    rows, total = residual.shape
    return call(
        functools.partial(own_kernel, odd, first, first - origin, first - RAW, extra),
        "own",
        array(rows + extra, width),
        [SMEM] + [VMEM] * 5 + [ANY] * len(after),
        VMEM,
        [table_scratch(lines, width, total)],
    )(start, lines, behind, product, queries, residual, *after)


def pick_kernel(*refs):
    raw_ref, received_ref, tail_ref, bank_ref, scales_ref, assign_ref = refs[:6]
    queries_ref, product_ref, lines_ref = refs[8:]
    rows = queries_ref.shape[0]

    @pl.when(jnp.logical_and(is_first(), is_slab(0)))
    def _():
        fill_lines(bank_ref[0], scales_ref[...], assign_ref[...], lines_ref)

    def take(source):
        queries_ref[...] = source[:rows, :]
        product_ref[:, :RAW] = source[rows:, :]

    pl.when(is_first())(lambda: take(raw_ref))

    @pl.when(jnp.logical_not(is_first()))
    def _():
        take(received_ref)
        product_ref[:, RAW:] = tail_ref[...]


def pick_of(raw, received, tail, bank, scales, assign, lines, after):
    rows, width = raw.shape[0] // 2, raw.shape[1]
    return call(
        pick_kernel,
        "pick",
        (array(rows, width), array(rows, 2 * width), array(*lines.shape, F32)),
        [VMEM] * 7 + [ANY],
        (VMEM,) * 3,
        weight=SLOW,
        aliases={6: 2},
    )(raw, received, tail, bank, scales, assign, lines, after)


def hold_kernel(value_ref, _, out_ref):
    pass


def held_back(value, after, weight=QUICK):
    return call(
        hold_kernel, "hold", array(*value.shape), [ANY, ANY], ANY, weight=weight, aliases={0: 0}
    )(value, after)


def send_out(pieces, out_ref, sems):
    copies = [
        pltpu.make_async_copy(buffer, out_ref.at[0, :, pl.ds(first, buffer.shape[1])], sems.at[place])
        for place, (buffer, first) in enumerate(pieces)
    ]
    for copy in copies:
        copy.start()
    return copies


def wait_all(copies):
    for copy in copies:
        copy.wait()


def later_kernel(places, *refs):
    start_ref, lines_ref, near_behind, near_ref, far_behind, far_ref, raw_behind, tail_ref, queries_ref = refs[:9]
    own_refs = refs[9 : 9 + len(places)]
    out_ref, gated_ref, table_ref, sems = refs[-4:]
    total = queries_ref.shape[2]
    share = share_of(lines_ref, total)

    for odd in (0, 1):

        @pl.when(jnp.logical_and(is_first(), is_slab(odd)))
        def _():
            pieces = [
                (own_ref.at[pl.ds(0, out_ref.shape[1])], first)
                for own_ref, (side, first, _) in zip(own_refs, places)
                if side == odd
            ]
            wait_all(send_out(pieces, out_ref, sems))

    @pl.when(jnp.logical_not(is_first()))
    def _():
        parts = (
            (0, 0, near_behind, near_ref),
            (NEAR, 0, far_behind, far_ref),
            (total - RAW, RAW, raw_behind, tail_ref),
        )
        for first, skip, behind_ref, product_ref in parts:

            def store(at, span, mixed):
                cols = slice(first + at.start, first + at.stop)
                gated_ref[span, cols] = queries_ref[0, span, cols].astype(F32) * mixed

            width, line = product_ref.shape[1], first // LANES * share
            at = (skip, 0)
            mix_all(width, share, lines_ref, line, table_ref, start_ref, behind_ref, product_ref, at, store)


def later_of(start, lines, near_behind, near, far_behind, far, raw_behind, tail, queries, own, places):
    rows, total = queries.shape[1:]
    return call(
        functools.partial(later_kernel, places),
        "later",
        (jax.ShapeDtypeStruct((1, rows, total), BF16), array(rows, total, F32)),
        [SMEM] + [VMEM] * (8 + len(own)),
        (ANY, VMEM),
        [table_scratch(lines, max(NEAR, total - RAW - NEAR), total), pltpu.SemaphoreType.DMA((len(own),))],
        weight=SLOW,
    )(start, lines, near_behind, near, far_behind, far, raw_behind, tail, queries, *own)


def raw_kernel(*refs):
    start_ref, lines_ref, wire_ref, received_ref = refs[:4]
    behind_ref, product_ref, queries_ref, gated_ref, residual_ref = refs[4:9]
    out_ref, chosen_ref, table_ref, buffer, sems = refs[10:]
    rows, width = buffer.shape
    share = share_of(lines_ref, residual_ref.shape[1])

    @pl.when(is_first())
    def _():
        chosen_ref[...] = lines_ref[: chosen_ref.shape[0], :]

    @pl.when(jnp.logical_and(jnp.logical_not(is_first()), is_slab(1)))
    def _():
        chosen_ref[...] = wire_ref[...].astype(F32)

    @pl.when(jnp.logical_and(jnp.logical_not(is_first()), is_slab(0)))
    def _():
        for part in range(RAW // LANES):
            taken = received_ref[rows:, part * LANES : (part + 1) * LANES]
            chosen_ref[part * LINES : (part + 1) * LINES, :] = taken.astype(F32)

    def store(at, span, mixed):
        gated = queries_ref[span, at].astype(F32) * mixed
        buffer[span, at] = (residual_ref[span, at].astype(F32) + gated).astype(BF16)

    mix_all(width, share, chosen_ref, 0, table_ref, start_ref, behind_ref, product_ref, (0, 0), store)

    @pl.when(jnp.logical_not(is_first()))
    def _():
        buffer[...] = (buffer[...].astype(F32) + gated_ref[:, :width]).astype(BF16)

    wait_all(send_out([(buffer, 0)], out_ref, sems))


def raw_finish(held, start, lines, wire, received, behind, product, queries, gated, residual):
    rows, width = queries.shape
    total = residual.shape[1]
    return call(
        raw_kernel,
        "raw",
        jax.ShapeDtypeStruct(held.shape, BF16),
        [SMEM] + [VMEM] * 8 + [ANY],
        ANY,
        [
            pltpu.VMEM(wire.shape, F32),
            table_scratch(lines, width, total),
            pltpu.VMEM((rows, width), BF16),
            pltpu.SemaphoreType.DMA((1,)),
        ],
        weight=SLOW,
        aliases={9: 0},
    )(start, lines, wire, received, behind, product, queries, gated, residual, held)


def finish_kernel(odd, places, *refs):
    gated_ref, received_refs = refs[0], refs[1 : 1 + len(places)]
    out_ref, *buffers, sems = refs[2 + len(places) :]

    @pl.when(jnp.logical_and(jnp.logical_not(is_first()), is_slab(odd)))
    def _():
        copies = []
        for place, (_, first, width) in enumerate(places):
            buffer = buffers[place]
            total = received_refs[place][: buffer.shape[0], :].astype(F32) + gated_ref[:, first : first + width]
            buffer[...] = total.astype(BF16)
            copies += send_out([(buffer, first)], out_ref, sems.at[pl.ds(place, 1)])
        wait_all(copies)


def finish(held, gated, received, places):
    rows = gated.shape[0]
    count = len(places)
    return call(
        functools.partial(finish_kernel, places[0][0], places),
        "finish",
        jax.ShapeDtypeStruct(held.shape, BF16),
        [VMEM] * (1 + count) + [ANY],
        ANY,
        [pltpu.VMEM((rows, width), BF16) for _, _, width in places] + [pltpu.SemaphoreType.DMA((count,))],
        weight=SLOW,
        aliases={1 + count: 0},
    )(gated, *received, held)


def body(queries, keys, values, residual, filter_bank, filter_scales, group_filter, context_start):
    total = queries.shape[2]
    small = (filter_bank, filter_scales, group_filter)
    far_queries, keys, values = (
        pltpu.with_memory_space_constraint(value, pltpu.HBM) for value in (queries, keys, values)
    )
    raw, rest = lead_of(far_queries, keys, values)
    raw_received = to_next_section(raw)
    chip_behind = to_next_slab(rest, (0, 0))
    lines, wire, near, far, tail = product_of(keys, values, *small, rest)
    own, received, places = [], [], []

    def send(odd, behind, origin, first, width, *after, extra=0):
        piece = own_of(
            odd, origin, extra, context_start, lines, behind, rest, queries, residual, first, width, *after
        )
        own.append(piece)
        received.append(to_next_section(piece, (odd,)))
        places.append((odd, first, width))
        return first + width, piece

    links = ((1, 0), (0, 1), (1, 1))
    first, after = send(1, chip_behind, RAW, RAW, ODD[0], lines)
    near = held_back(near, after)
    near_behind = to_next_slab(near, *links)
    first, after = send(1, chip_behind, RAW, first, ODD[1], near)
    raw_queries, raw_product, lines = pick_of(raw, raw_received, tail, *small, lines, after)
    far = held_back(far, raw_queries)
    far_behind = to_next_slab(far, *links)
    raw_product = held_back(raw_product, far)
    raw_behind = to_next_slab(raw_product, (0, 0), *links)
    raw_queries = held_back(raw_queries, received[0], SLOW)
    first, after = send(0, near_behind, RAW, RAW, EVEN[0], raw_queries)
    first, after = send(0, near_behind, RAW, first, EVEN[1], after, extra=LINES)
    origin = first
    first, after = send(0, far_behind, origin, first, EVEN[2], after, received[1])
    first, after = send(0, far_behind, origin, first, EVEN[3], after, raw_behind)
    wire_received = to_next_section(held_back(wire, after), (1,))
    held, gated = later_of(
        context_start,
        lines,
        near_behind,
        near,
        far_behind,
        far,
        raw_behind,
        tail,
        queries,
        own,
        places,
    )
    odd = len(ODD)
    held = finish(held, gated, received[:odd], places[:odd])
    held = finish(held, gated, received[odd : odd + 2], places[odd : odd + 2])
    held = raw_finish(
        held,
        context_start,
        lines,
        wire_received,
        received[odd + 1],
        raw_behind,
        raw_product,
        raw_queries,
        gated,
        residual,
    )
    for last in (odd + 2, odd + 3):
        held = finish(held, gated, received[last : last + 1], places[last : last + 1])
    return held


def solution(mesh):
    return jax.shard_map(
        body,
        mesh=mesh,
        in_specs=(
            P("pipe", ("dp", "ctx"), None),
            P("pipe", ("dp", "ctx"), None),
            P("pipe", ("dp", "ctx"), None),
            P(("dp", "ctx"), None),
            P("pipe", None, None),
            P("pipe", None),
            P("pipe", None),
            P("dp"),
        ),
        out_specs=P("pipe", ("dp", "ctx"), None),
        check_vma=False,
    )
```
